32 devices in a mesh: stream: 2 (over x), dp: 16 (over z, y, core).
Axes of the slice: x: 2, y: 2, z: 4, core: 2. Of those that a mesh axis runs over, the one named last changes fastest.
Arguments:
- tokens: bfloat16 [2, 4096, 512], P('stream', 'dp'), may hold values from -6 to 6
- qkv_weight: bfloat16 [2, 512, 1536], P('stream'), may hold values from -0.25 to 0.25
- qkv_bias: bfloat16 [2, 1536], P('stream'), may hold values from -1.5 to 1.5
- out_weight: bfloat16 [2, 512, 512], P('stream'), may hold values from -1.5 to 1.5
- out_bias: bfloat16 [2, 512], P('stream'), may hold values from -1.5 to 1.5
- first_gain: bfloat16 [2, 512], P('stream'), may hold values from 0.25 to 1.75
- first_shift: bfloat16 [2, 512], P('stream'), may hold values from -1.5 to 1.5
- up_weight: bfloat16 [2, 512, 2048], P('stream'), may hold values from -0.25 to 0.25
- up_bias: bfloat16 [2, 2048], P('stream'), may hold values from -1.5 to 1.5
- down_weight: bfloat16 [2, 2048, 512], P('stream'), may hold values from -0.25 to 0.25
- down_bias: bfloat16 [2, 512], P('stream'), may hold values from -1.5 to 1.5
- second_gain: bfloat16 [2, 512], P('stream'), may hold values from 0.25 to 1.75
- second_shift: bfloat16 [2, 512], P('stream'), may hold values from -1.5 to 1.5
- proj_weight: bfloat16 [2, 512, 128], P('stream'), may hold values from -0.25 to 0.25
- log_scale: float32 [], replicated, may hold values from 2.5 to 3.5
- doc_lengths: int32 [16, 5], replicated, may hold values from 1 to 128, 256 in all within a row
- labels: int32 [128], P('dp'), may hold values from 0 to 63
Outputs:
- loss: float32 [], replicated
- tokens_grad: float32 [2, 4096, 512], P('stream', 'dp')
- qkv_weight_grad: float32 [2, 512, 1536], P('stream')
- qkv_bias_grad: float32 [2, 1536], P('stream')
- out_weight_grad: float32 [2, 512, 512], P('stream')
- out_bias_grad: float32 [2, 512], P('stream')
- first_gain_grad: float32 [2, 512], P('stream')
- first_shift_grad: float32 [2, 512], P('stream')
- up_weight_grad: float32 [2, 512, 2048], P('stream')
- up_bias_grad: float32 [2, 2048], P('stream')
- down_weight_grad: float32 [2, 2048, 512], P('stream')
- down_bias_grad: float32 [2, 512], P('stream')
- second_gain_grad: float32 [2, 512], P('stream')
- second_shift_grad: float32 [2, 512], P('stream')
- proj_weight_grad: float32 [2, 512, 128], P('stream')
- log_scale_grad: float32 [], replicated
The draws below stay inside these ranges and needn't reach their ends.
Inputs may be any that keep to these rules, and one draw needn't show every extreme that they name: Each row of doc_lengths sums to 256; its last entry is the padding; its largest entry is 128.
All inputs are finite; a program needn't handle non-finite values.
Results may differ from the reference program's by a relative error of at most 0.023.
Values may be sent and summed in bfloat16 or wider, within the bound.
No kernel may reach another device: no remote copies, remote signals or barrier semaphores. Data moves between devices by JAX's collectives and lax.ppermute only.
A program may use at most 128 MiB of HBM per device.

```python
import math
from functools import partial
import jax
import jax.numpy as jnp
import numpy as np
from jax import lax

D = 512
HEADS = 8
HD = 64
FF = 2048
PROJ = 128
QLEN = 32
DOCS_ROW = 4
ROW = 256
ROWS = 16
TOKENS = 4096
QUERIES = 128
DOCS = 64
N_DP = 16


def with_ends(result, own_key, least, high):
    longest = result.shape.index(max(result.shape))
    spots = []
    for shift in (0, 1):
        where = [jax.random.randint(jax.random.fold_in(own_key, axis), (), 0, length) for axis, length in enumerate(result.shape)]
        where[longest] = (where[longest] + shift) % result.shape[longest]
        spots.append(tuple(where))
    return result.at[spots[0]].set(least).at[spots[1]].set(high)


def block_levels(key, shape, split, least, largest):
    gain = 1.0
    for axis_at, shards_of in split:
        draws = jax.random.uniform(jax.random.fold_in(jax.random.fold_in(key, 6), axis_at), (shards_of,), jnp.float32, least / len(split), largest / len(split))
        gain = gain * jnp.repeat(jnp.exp(draws), shape[axis_at] // shards_of).reshape((-1,) + (1,) * (len(shape) - 1 - axis_at))
    return gain


def length_profile(count, total, most, slope):
    portions = [(1 << 20) // math.isqrt(rank ** slope) + 1 for rank in range(2, count + 1)]
    spare, holding = total - most - (count - 1), [1] * (count - 1)
    while spare > 0:
        candidates = [i for i in range(count - 1) if holding[i] < most]
        pool, remaining = sum([portions[i] for i in candidates]), spare
        for i in candidates:
            addition = min(most - holding[i], max(1, remaining * portions[i] // pool), spare)
            holding[i] = holding[i] + addition
            spare = spare - addition
    return np.array([most] + holding)


def ragged_sizes(rng, count, total, most, slope):
    if count == 2:
        one = jax.random.randint(rng, (), max(1, total - most), min(most, total - 1) + 1)
        return jnp.stack([one, total - one])
    sizes = jnp.asarray(length_profile(count, total, most, slope), jnp.int32)
    twos = (count - 1) // 2
    giver, taker = sizes[1:1 + 2 * twos:2], sizes[2:2 + 2 * twos:2]
    slack = jnp.minimum(giver - 1, most - taker)
    shifted = jax.random.randint(jax.random.fold_in(rng, 1), (twos,), 0, 1 << 20) % (slack + 1)
    sizes = sizes.at[1:1 + 2 * twos:2].set(giver - shifted).at[2:2 + 2 * twos:2].set(taker + shifted)
    return sizes[jax.random.permutation(jax.random.fold_in(rng, 2), count)]


def gaussian(key, dims, deviation, limit, split=(), held_as=jnp.bfloat16):
    level = block_levels(key, dims, split, -0.22, 0.18) if split else 1.0
    drawn = jax.random.normal(key, dims, jnp.float32) * deviation * level
    return jnp.minimum(jnp.maximum(drawn, -limit), limit).astype(held_as)


def setup_inputs(seed: int = 0) -> dict:
    key_of = jax.random.split(jax.random.key(seed), 18)
    return {
        "tokens": gaussian(key_of[0], (2, TOKENS, D), 1.0, 6.0, ((0, 2), (1, 16))),
        "qkv_weight": gaussian(key_of[1], (2, D, 3 * D), D ** -0.5, 0.25, ((0, 2),)),
        "qkv_bias": gaussian(key_of[2], (2, 3 * D), 0.3, 1.5, ((0, 2),)),
        "out_weight": gaussian(key_of[3], (2, D, D), (D // 32) ** -0.5, 1.5, ((0, 2),)),
        "out_bias": gaussian(key_of[4], (2, D), 0.3, 1.5, ((0, 2),)),
        "first_gain": jnp.clip(1.0 + 0.15 * jax.random.normal(key_of[5], (2, D), jnp.float32), 0.25, 1.75).astype(jnp.bfloat16),
        "first_shift": gaussian(key_of[6], (2, D), 0.3, 1.5, ((0, 2),)),
        "up_weight": gaussian(key_of[7], (2, D, FF), D ** -0.5, 0.25, ((0, 2),)),
        "up_bias": gaussian(key_of[8], (2, FF), 0.3, 1.5, ((0, 2),)),
        "down_weight": gaussian(key_of[9], (2, FF, D), (FF // 4) ** -0.5, 0.25, ((0, 2),)),
        "down_bias": gaussian(key_of[10], (2, D), 0.3, 1.5, ((0, 2),)),
        "second_gain": jnp.clip(1.0 + 0.15 * jax.random.normal(key_of[11], (2, D), jnp.float32), 0.25, 1.75).astype(jnp.bfloat16),
        "second_shift": gaussian(key_of[12], (2, D), 0.3, 1.5, ((0, 2),)),
        "proj_weight": gaussian(key_of[13], (2, D, PROJ), D ** -0.5, 0.25, ((0, 2),)),
        "log_scale": jnp.clip(jax.random.uniform(key_of[14], (), jnp.float32, 2.5, 3.5), 2.5, 3.5),
        "doc_lengths": jax.vmap(lambda own: ragged_sizes(own, DOCS_ROW + 1, ROW, ROW // 2, 2))(jax.random.split(key_of[15], ROWS)).reshape((ROWS, DOCS_ROW + 1)).astype(jnp.int32),
        "labels": with_ends(jax.random.randint(key_of[16], (QUERIES,), 0, DOCS), jax.random.fold_in(key_of[16], 1), 0, DOCS - 1).astype(jnp.int32),
    }


@jax.custom_vjp
def low(v):
    return lax.optimization_barrier(v.astype(jnp.bfloat16)).astype(jnp.float32)

@jax.custom_vjp
def low_back(v):
    return v

def low_keep(v):
    return (low(v), None)

def low_pass(kept, grad):
    return (grad,)

def back_keep(v):
    return (v, None)

def back_low(kept, grad):
    return (low(grad),)
low.defvjp(low_keep, low_pass)
low_back.defvjp(back_keep, back_low)
sharpness = 8.0
eps_norm = 1e-06
eps_layer = 1e-05

def product(left_op, right_op):
    return jnp.dot(left_op, right_op, precision=lax.Precision.HIGHEST, preferred_element_type=jnp.float32)

def layer_norm(values, gain_vec, shift_vec):
    centred = values - lax.optimization_barrier(jnp.mean(values, axis=-1, keepdims=True))
    spread = lax.optimization_barrier(jnp.mean(centred * centred, axis=-1, keepdims=True))
    return centred * lax.rsqrt(spread + eps_layer) * gain_vec + shift_vec

def angles(position):
    half_len = HD // 2
    freqs = 10000.0 ** (-jnp.arange(half_len, dtype=jnp.float32) / half_len)
    turned = position.astype(jnp.float32)[..., None] * freqs
    return (jnp.cos(turned)[..., None, :], jnp.sin(turned)[..., None, :])

def rotate(values, cosine, sine):
    half_len = HD // 2
    first_half = values[..., :half_len]
    second_half = values[..., half_len:]
    return jnp.concatenate([first_half * cosine - second_half * sine, second_half * cosine + first_half * sine], axis=-1)

def inverse_norms(values):
    cut_a = PROJ // 2
    cut_b = 3 * PROJ // 4
    squared = values * values
    part_a = lax.optimization_barrier(jnp.sum(squared[:, :cut_a], axis=1))
    part_b = part_a + lax.optimization_barrier(jnp.sum(squared[:, cut_a:cut_b], axis=1))
    part_c = part_b + lax.optimization_barrier(jnp.sum(squared[:, cut_b:], axis=1))
    return lax.rsqrt(jnp.stack([part_a, part_b, part_c]) + eps_norm)

def row_layout(doc_lengths, row_len):
    ends = jnp.cumsum(doc_lengths, axis=1)
    spots = jnp.arange(row_len, dtype=jnp.int32)
    finished = (spots[None, :, None] >= ends[:, None, :DOCS_ROW]).astype(jnp.int32)
    doc_table = lax.optimization_barrier(jnp.sum(finished, axis=2))
    offsets = lax.optimization_barrier(jnp.sum(finished * doc_lengths[:, None, :DOCS_ROW], axis=2))
    return (doc_table, spots[None, :] - offsets)

def encode_rows(weights, item):
    qkv_weight, qkv_bias, out_weight, out_bias, first_gain, first_shift, up_weight, up_bias, down_weight, down_bias, second_gain, second_shift, proj_weight = weights
    inputs, segment, position = item
    count = inputs.shape[0]
    joined = low_back(product(inputs, qkv_weight) + qkv_bias)
    cosine, sine = angles(position)
    query_rot = low(rotate(joined[..., :D].reshape(count, ROW, HEADS, HD), cosine, sine))
    key_rot = low(rotate(joined[..., D:2 * D].reshape(count, ROW, HEADS, HD), cosine, sine))
    value_low = low(joined[..., 2 * D:].reshape(count, ROW, HEADS, HD))
    att_scale = 1.0 / math.sqrt(HD)
    scores = low_back(jnp.einsum('gqhd,gkhd->ghqk', query_rot, key_rot, precision=lax.Precision.HIGHEST) * att_scale)
    same_seg = segment[:, None, :, None] == segment[:, None, None, :]
    scores = jnp.where(same_seg, scores, -1e+30)
    row_top = lax.optimization_barrier(jnp.max(scores, axis=-1, keepdims=True))
    exp_scores = jnp.exp(scores - row_top)
    probs_low = low(exp_scores / lax.optimization_barrier(jnp.sum(exp_scores, axis=-1, keepdims=True)))
    mixed = jnp.einsum('ghqk,gkhd->gqhd', probs_low, value_low, precision=lax.Precision.HIGHEST).reshape(count, ROW, D)
    mixed = low(low_back(mixed))
    attended = low_back(product(mixed, out_weight) + out_bias)
    first_out = layer_norm(inputs + attended, first_gain, first_shift)
    inner_pre = low_back(product(low(first_out), up_weight) + up_bias)
    branch = low_back(product(low(jax.nn.gelu(inner_pre, approximate=False)), down_weight) + down_bias)
    second = layer_norm(first_out + branch, second_gain, second_shift)
    return low(low_back(product(low(second), proj_weight)))

def match_block(documents, doc_inv, onehot, log_length, item):
    block_rows, block_inv = item
    count = block_rows.shape[0]
    cut_a = PROJ // 2
    cut_b = 3 * PROJ // 4
    part_a = low_back(product(block_rows[:, :cut_a], documents[:, :cut_a].T))
    part_b = low_back(product(block_rows[:, cut_a:cut_b], documents[:, cut_a:cut_b].T))
    part_c = low_back(product(block_rows[:, cut_b:], documents[:, cut_b:].T))
    sums = jnp.stack([part_a, part_a + part_b, part_a + part_b + part_c])
    scaled = sums * block_inv[:, :, None] * doc_inv[:, None, :]
    exp_sims = jnp.exp(sharpness * scaled).reshape(3, count, N_DP, ROW)
    totals = jnp.einsum('mqnr,nrd->mqnd', exp_sims, onehot, precision=lax.Precision.HIGHEST).reshape(3, count, DOCS)
    matched = (jnp.log(totals) - log_length) / sharpness
    return lax.optimization_barrier(jnp.sum(matched.reshape(3, count // QLEN, QLEN, DOCS), axis=2))

def reference(tokens, qkv_weight, qkv_bias, out_weight, out_bias, first_gain, first_shift, up_weight, up_bias, down_weight, down_bias, second_gain, second_shift, proj_weight, log_scale, doc_lengths, labels):
    doc_table, doc_position = row_layout(doc_lengths, ROW)
    spots = jnp.arange(ROW, dtype=jnp.int32)
    query_table = jnp.broadcast_to(spots // QLEN, (N_DP, ROW))
    query_position = jnp.broadcast_to(spots % QLEN, (N_DP, ROW))
    layouts = ((query_table, query_position), (doc_table, doc_position))
    group = math.gcd(N_DP, max(1, 4096 // ROW))
    onehot = (doc_table[..., None] == jnp.arange(DOCS_ROW, dtype=jnp.int32)).astype(jnp.float32)
    log_length = jnp.log(doc_lengths[:, :DOCS_ROW].astype(jnp.float32)).reshape(DOCS)
    block = math.gcd(N_DP * ROW, 512)
    blocks = N_DP * ROW // block

    def forward(inputs, *params):
        weights_all = params[:13]
        scale_log = params[13]
        encoded = []
        for stream_idx in range(2):
            weights = tuple((item[stream_idx] for item in weights_all))
            table, position = layouts[stream_idx]
            grouped = (inputs[stream_idx].reshape(N_DP // group, group, ROW, D), table.reshape(N_DP // group, group, ROW), position.reshape(N_DP // group, group, ROW))
            vectors = lax.map(jax.checkpoint(partial(encode_rows, weights)), grouped)
            encoded.append(vectors.reshape(N_DP * ROW, PROJ))
        queries, documents = encoded
        doc_inv = inverse_norms(documents)
        query_inv = inverse_norms(queries)
        items = (queries.reshape(blocks, block, PROJ), query_inv.reshape(3, blocks, block).transpose(1, 0, 2))
        scores = lax.map(jax.checkpoint(partial(match_block, documents, doc_inv, onehot, log_length)), items)
        scores = scores.transpose(1, 0, 2, 3).reshape(3, QUERIES, DOCS)
        logits = jnp.exp(scale_log) * scores / QLEN
        log_totals = jax.nn.logsumexp(logits, axis=2)
        picked = jnp.take_along_axis(logits, jnp.broadcast_to(labels[None, :, None], (3, QUERIES, 1)), axis=2)[..., 0]
        return jnp.sum(log_totals - picked) / QUERIES
    floats = tuple((item.astype(jnp.float32) for item in (tokens, qkv_weight, qkv_bias, out_weight, out_bias, first_gain, first_shift, up_weight, up_bias, down_weight, down_bias, second_gain, second_shift, proj_weight, log_scale)))
    loss, pullback = jax.vjp(forward, *floats)
    grads = pullback(jnp.ones_like(loss))
    return (loss, grads[0], grads[1], grads[2], grads[3], grads[4], grads[5], grads[6], grads[7], grads[8], grads[9], grads[10], grads[11], grads[12], grads[13], grads[14])
```

```python
from functools import partial
import math

import jax
import jax.numpy as jnp
import numpy as np
from jax import lax
from jax.experimental import pallas as pl
from jax.experimental.pallas import tpu as pltpu
from jax.sharding import PartitionSpec as P

D = 512
HEADS = 8
HD = 64
FF = 2048
PROJ = 128
QLEN = 32
DOCS_ROW = 4
ROW = 256
EXT = 16
RANGES = (64, 96, 128)

SHARPNESS = 8.0
EPS_NORM = 1e-06
EPS_LAYER = 1e-05
LOG2E = 1.4426950408889634

F32 = jnp.float32
BF16 = jnp.bfloat16
REST = 2304
VLIMIT = 56 * 1024 * 1024

VMEM = pl.BlockSpec(memory_space=pltpu.VMEM)
SMEM = pl.BlockSpec(memory_space=pltpu.SMEM)


def mm(a, b):
    return lax.dot_general(a, b, (((1,), (0,)), ((), ())), preferred_element_type=F32)


def mm_nt(a, b):
    return lax.dot_general(a, b, (((1,), (1,)), ((), ())), preferred_element_type=F32)


def mm_tn(a, b):
    return lax.dot_general(a, b, (((0,), (0,)), ((), ())), preferred_element_type=F32)


def iota(shape, axis):
    return lax.broadcasted_iota(jnp.int32, shape, axis)


def rope_table():
    half = HD // 2
    freqs = (10000.0 ** (-np.arange(half, dtype=np.float32) / np.float32(half))).astype(np.float32)
    turned = np.arange(ROW, dtype=np.float32)[:, None] * freqs[None, :]
    cosine = np.cos(turned.astype(np.float64))
    sine = np.sin(turned.astype(np.float64))
    cosine = np.concatenate([cosine, cosine, cosine, cosine], axis=1).astype(np.float32)
    sine = np.concatenate([-sine, sine, -sine, sine], axis=1).astype(np.float32)
    parts = []
    for table in (cosine, sine):
        high = table.astype(jnp.bfloat16)
        low = (table - high.astype(np.float32)).astype(jnp.bfloat16)
        parts += [high, low]
    return np.concatenate(parts, axis=1)


def swap_halves(block):
    lane = iota(block.shape, 1)
    return jnp.where(lane % HD < HD // 2, pltpu.roll(block, 96, 1), pltpu.roll(block, 32, 1))


def bounds_of(lens_ref, row):
    ends, total = [], jnp.int32(0)
    for k in range(DOCS_ROW):
        total = total + lens_ref[row, k]
        ends.append(total)
    return ends


def segment_of(spot, ends):
    seg = jnp.zeros_like(spot)
    for end in ends:
        seg = seg + (spot >= end).astype(jnp.int32)
    return seg


def norm_rows(values):
    mean = jnp.mean(values, axis=1, keepdims=True)
    centred = values - mean
    spread = jnp.mean(centred * centred, axis=1, keepdims=True)
    rstd = lax.rsqrt(spread + EPS_LAYER)
    return centred * rstd, rstd


def norm_back(d_out, xhat, rstd, gain):
    scaled = d_out * gain
    first = jnp.mean(scaled, axis=1, keepdims=True)
    second = jnp.mean(scaled * xhat, axis=1, keepdims=True)
    return rstd * (scaled - first - xhat * second)


def col_sum(values):
    return jnp.sum(values, axis=0, keepdims=True)


def encoder_forward(
    where_ref, lens_ref, labels_ref, table_ref, x_ref, wqkv_ref, bqkv_ref, wout_ref, bout_ref,
    g1_ref, s1_ref, wup_ref, bup_ref, wdown_ref, bdown_ref, g2_ref, s2_ref, wproj_ref,
    vec_ref, qkv_ref, rope_ref, probs_ref, mixed_ref, xh1_ref, rs1_ref, act_ref, slope_ref,
    xh2_ref, rs2_ref,
):
    me, is_query = where_ref[0], where_ref[1] == 0
    ends = bounds_of(lens_ref, me)

    def layout(spot):
        seg_doc = segment_of(spot, ends)
        start_doc = jnp.zeros_like(spot)
        for k in range(DOCS_ROW):
            start_doc = jnp.where(seg_doc == k + 1, ends[k], start_doc)
        seg_query = spot // QLEN
        seg = jnp.where(is_query, seg_query, seg_doc)
        start = jnp.where(is_query, seg_query * QLEN, start_doc)
        return seg, start

    shape = (ROW, ROW)
    seg_q, start_q = layout(iota(shape, 0))
    seg_k, _ = layout(iota(shape, 1))
    same = seg_q == seg_k
    onehot = (iota(shape, 1) == iota(shape, 0) - start_q).astype(F32).astype(BF16)
    turned = mm(onehot, table_ref[...])
    cosine = turned[:, :128] + turned[:, 128:256]
    sine = turned[:, 256:384] + turned[:, 384:]
    rope_ref[:, :128] = cosine
    rope_ref[:, 128:] = sine

    x = x_ref[...]
    joined = mm(x, wqkv_ref[...]) + bqkv_ref[...].astype(F32)
    for g in range(2 * D // 128):
        block = joined[:, g * 128 : (g + 1) * 128]
        qkv_ref[:, g * 128 : (g + 1) * 128] = (
            block * cosine + swap_halves(block) * sine
        ).astype(BF16)
    qkv_ref[:, 2 * D :] = joined[:, 2 * D :].astype(BF16)

    low_half = iota((ROW, 128), 1) < HD
    for g in range(HEADS // 2):
        q_g = qkv_ref[:, g * 128 : (g + 1) * 128]
        k_g = qkv_ref[:, D + g * 128 : D + (g + 1) * 128]
        v_g = qkv_ref[:, 2 * D + g * 128 : 2 * D + (g + 1) * 128]
        outs = []
        for h in range(2):
            pick = low_half if h == 0 else jnp.logical_not(low_half)
            scores = mm_nt(jnp.where(pick, q_g, jnp.zeros_like(q_g)), k_g) * (1.0 / math.sqrt(HD))
            scores = jnp.where(same, scores, -1e30)
            top = jnp.max(scores, axis=1, keepdims=True)
            exps = jnp.exp(scores - top)
            probs = (exps / jnp.sum(exps, axis=1, keepdims=True)).astype(BF16)
            probs_ref[2 * g + h] = probs
            outs.append(mm(probs, v_g))
        mixed_ref[:, g * 128 : (g + 1) * 128] = jnp.where(low_half, outs[0], outs[1]).astype(BF16)

    attended = mm(mixed_ref[...], wout_ref[...]) + bout_ref[...].astype(F32)
    xhat, rstd = norm_rows(x.astype(F32) + attended)
    xh1_ref[...] = xhat
    rs1_ref[...] = jnp.broadcast_to(rstd, (ROW, 128))
    first = xhat * g1_ref[...].astype(F32) + s1_ref[...].astype(F32)
    first_low = first.astype(BF16)
    branch = bdown_ref[...].astype(F32) + first
    step = 512
    for c in range(FF // step):
        cols = slice(c * step, (c + 1) * step)
        inner = mm(first_low, wup_ref[:, cols]) + bup_ref[:, cols].astype(F32)
        gate = 0.5 + 0.5 * lax.erf(inner * math.sqrt(0.5))
        bell = jnp.exp(inner * inner * -0.5) * (1.0 / math.sqrt(2.0 * math.pi))
        act = (inner * gate).astype(BF16)
        act_ref[:, cols] = act
        slope_ref[:, cols] = (gate + inner * bell).astype(BF16)
        branch = branch + mm(act, wdown_ref[cols, :])
    xhat, rstd = norm_rows(branch)
    xh2_ref[...] = xhat
    rs2_ref[...] = jnp.broadcast_to(rstd, (ROW, 128))
    second = xhat * g2_ref[...].astype(F32) + s2_ref[...].astype(F32)
    vec_ref[:ROW, :] = mm(second.astype(BF16), wproj_ref[...]).astype(BF16)
    line = iota((EXT, PROJ), 0)
    tag = jnp.zeros((EXT, PROJ), jnp.int32)
    for k in range(labels_ref.shape[0]):
        label = labels_ref[k]
        tag = jnp.where(line == k, label >> 6, tag)
        tag = jnp.where(line == k + 8, label & 63, tag)
    vec_ref[ROW:, :] = tag.astype(F32).astype(BF16)


def prefix_norms(values, axis):
    place = iota(values.shape, axis)
    squared = values * values
    sums = [
        jnp.sum(jnp.where(place < cut, squared, 0.0), axis=axis, keepdims=True) for cut in RANGES
    ]
    return [lax.rsqrt(s + EPS_NORM) for s in sums]


def load_queries(near_ref, far_ref):
    span = ROW + EXT
    rows = []
    for ref in (near_ref, far_ref):
        for k in range(ref.shape[0] // span):
            rows.append(ref[k * span : k * span + ROW, :])
    return jnp.concatenate(rows, axis=0).astype(F32)


def unit_queries(queries, scale):
    lane = iota(queries.shape, 1)
    inverse = prefix_norms(queries, 1)
    unit = [
        jnp.where(lane < cut, queries * (inv * scale), 0.0) for cut, inv in zip(RANGES, inverse)
    ]
    return unit, inverse


def unit_docs(doc_refs, scratch_ref):
    at = 0
    for ref in doc_refs:
        for k in range(ref.shape[0] // ROW):
            scratch_ref[:, at * ROW : (at + 1) * ROW] = ref[
                k * ROW : (k + 1) * ROW, :
            ].astype(F32).T
            at += 1
    turned = scratch_ref[...]
    inverse = prefix_norms(turned, 0)
    place = iota(turned.shape, 0)
    unit = [jnp.where(place < cut, turned * inv, 0.0) for cut, inv in zip(RANGES, inverse)]
    return unit, inverse


def row_ids(base, masks, doc_rows):
    ids = []
    for p in range(doc_rows):
        offset = 0
        for k, mask in enumerate(masks):
            if (p >> k) & 1:
                offset ^= mask
        ids.append(base ^ offset)
    return ids


def doc_marks(lens_ref, ids, lanes, transposed):
    docs = len(ids) * DOCS_ROW
    shape = (lanes, ROW) if transposed else (ROW, lanes)
    spot, lane = (iota(shape, 1), iota(shape, 0)) if transposed else (iota(shape, 0), iota(shape, 1))
    marks = []
    for p, row in enumerate(ids):
        seg = segment_of(spot, bounds_of(lens_ref, row))
        local = jnp.where(seg < DOCS_ROW, seg + p * DOCS_ROW, -1 - lanes)
        marks.append(
            [(lane == local + m * docs).astype(F32).astype(BF16) for m in range(len(RANGES))]
        )
    return marks


def matching_stats(
    masks, lanes, where_ref, scale_ref, lens_ref, near_ref, far_ref, *refs
):
    doc_refs = refs[:-6]
    totals_ref, el_ref, hot_ref, stats_ref, turn_ref, unit_ref = refs[-6:]
    base, near_at = where_ref[2], where_ref[3]
    span = ROW + EXT
    queries = load_queries(near_ref, far_ref)
    count = queries.shape[0]
    unit_q, _ = unit_queries(queries, SHARPNESS * LOG2E)
    unit_q = [u.astype(BF16) for u in unit_q]
    unit_d, _ = unit_docs(doc_refs, turn_ref)
    for m in range(len(RANGES)):
        unit_ref[m] = unit_d[m].astype(BF16)
    doc_rows = turn_ref.shape[1] // ROW
    docs = doc_rows * DOCS_ROW
    ids = row_ids(base, masks, doc_rows)
    marks = doc_marks(lens_ref, ids, lanes, False)
    totals = jnp.zeros((count, lanes), F32)
    for p in range(doc_rows):
        for m in range(len(RANGES)):
            sims = mm(unit_q[m], unit_ref[m, :, p * ROW : (p + 1) * ROW])
            totals = totals + mm(jnp.exp2(sims).astype(BF16), marks[p][m])
    lane_t = iota((count, lanes), 1)
    totals = jnp.where(lane_t < len(RANGES) * docs, totals, 1.0)
    totals_ref[...] = totals
    shape = (8, lanes)
    lane = iota(shape, 1)
    length = jnp.ones(shape, jnp.int32)
    name = jnp.full(shape, -1, jnp.int32)
    for p in range(doc_rows):
        for k in range(DOCS_ROW):
            own = jnp.zeros(shape, jnp.bool_)
            for m in range(len(RANGES)):
                own = jnp.logical_or(own, lane == m * docs + p * DOCS_ROW + k)
            length = jnp.where(own, lens_ref[ids[p], k], length)
            name = jnp.where(own, ids[p] * DOCS_ROW + k, name)
    log_length = jnp.log(length.astype(F32))
    matched = (jnp.log(totals) - log_length[:1]) * (1.0 / SHARPNESS)
    per_query = jnp.sum(matched.reshape(count // QLEN, QLEN, lanes), axis=1)
    scale = jnp.exp(jnp.full(shape, scale_ref[0], F32))[:1]
    logits = per_query * (scale * (1.0 / QLEN))
    groups = count // ROW
    tags = []
    for ref in (near_ref, far_ref):
        for k in range(ref.shape[0] // span):
            high = ref[k * span + ROW : k * span + ROW + 8, :].astype(F32).astype(jnp.int32)
            low = ref[k * span + ROW + 8 : k * span + ROW + 16, :].astype(F32).astype(jnp.int32)
            tag = high * 64 + low
            tags.append(jnp.concatenate([tag] * (lanes // 128), axis=1))
    tag = jnp.concatenate(tags, axis=0)
    lane_q = iota(logits.shape, 1)
    valid = lane_q < len(RANGES) * docs
    el = jnp.where(valid, jnp.exp(logits), 0.0)
    hot = jnp.where(jnp.logical_and(valid, jnp.concatenate([name] * groups, axis=0) == tag), 1.0, 0.0)
    el_ref[...] = el
    hot_ref[...] = hot
    place = iota((groups * 8, 128), 1)
    stats = jnp.zeros((groups * 8, 128), F32)
    for k, values in enumerate((el, el * logits, hot * logits)):
        for m in range(len(RANGES)):
            inside = jnp.logical_and(lane_q >= m * docs, lane_q < (m + 1) * docs)
            one = jnp.sum(jnp.where(inside, values, 0.0), axis=1, keepdims=True)
            stats = jnp.where(place == k * 3 + m, one, stats)
    for a in range(groups):
        at = pl.multiple_of((near_at ^ a) * 8, 8)
        stats_ref[pl.ds(at, 8), :] = stats[a * 8 : (a + 1) * 8, :]


def matching_back(
    masks, lanes, total_queries, where_ref, scale_ref, lens_ref, near_ref, far_ref, totals_ref,
    el_ref, hot_ref, stats_ref, *refs
):
    doc_refs = refs[:-8]
    dq_ref, dd_ref, loss_ref, turn_ref, unit_ref, qt_ref, dot_ref, dt_ref = refs[-8:]
    base, near_at = where_ref[2], where_ref[3]
    temper = SHARPNESS * LOG2E
    queries = load_queries(near_ref, far_ref)
    count = queries.shape[0]
    unit_q, inv_q = unit_queries(queries, temper)
    unit_q = [u.astype(BF16) for u in unit_q]
    unit_d, inv_d = unit_docs(doc_refs, turn_ref)
    for m in range(len(RANGES)):
        unit_ref[m] = unit_d[m].astype(BF16)
        qt_ref[m] = unit_q[m].astype(F32).T.astype(BF16)
    doc_rows = turn_ref.shape[1] // ROW
    docs = doc_rows * DOCS_ROW
    ids = row_ids(base, masks, doc_rows)
    marks = doc_marks(lens_ref, ids, lanes, True)
    groups = count // ROW
    rows = []
    for a in range(groups):
        at = pl.multiple_of((near_at ^ a) * 8, 8)
        rows.append(stats_ref[pl.ds(at, 8), :])
    stats = jnp.concatenate(rows, axis=0)
    place = iota(stats.shape, 1)

    def column(k):
        return jnp.sum(jnp.where(place == k, stats, 0.0), axis=1, keepdims=True)

    shape = (groups * 8, lanes)
    lane_q = iota(shape, 1)
    sums = jnp.ones(shape, F32)
    loss = jnp.zeros((groups * 8, 1), F32)
    moved = jnp.zeros((groups * 8, 1), F32)
    for m in range(len(RANGES)):
        whole, weighted, picked = column(m), column(3 + m), column(6 + m)
        inside = jnp.logical_and(lane_q >= m * docs, lane_q < (m + 1) * docs)
        sums = jnp.where(inside, whole, sums)
        loss = loss + (jnp.log(whole) - picked)
        moved = moved + (weighted / whole - picked)
    line = iota((8, 128), 0)
    loss_ref[...] = jnp.where(
        line == 0,
        jnp.sum(loss, axis=0, keepdims=True) * (1.0 / total_queries),
        jnp.where(line == 1, jnp.sum(moved, axis=0, keepdims=True) * (1.0 / total_queries), 0.0),
    )
    scale = jnp.exp(jnp.full((8, lanes), scale_ref[0], F32))[:1]
    coeff = (el_ref[...] / sums - hot_ref[...]) * (scale * (1.0 / (QLEN * total_queries)))
    coeff = jnp.broadcast_to(coeff[:, None, :], (groups * 8, QLEN, lanes)).reshape(count, lanes)
    ratio = coeff / totals_ref[...]
    ratio_high = ratio.astype(BF16)
    ratio_low = (ratio - ratio_high.astype(F32)).astype(BF16)
    ratio = jnp.concatenate([ratio_high, ratio_low], axis=1)
    for m in range(len(RANGES)):
        grad = jnp.zeros((count, PROJ), F32)
        for p in range(doc_rows):
            block = unit_ref[m, :, p * ROW : (p + 1) * ROW]
            mark = marks[p][m]
            exps = jnp.exp2(mm(unit_q[m], block))
            d_sims = (exps * mm(ratio, jnp.concatenate([mark, mark], axis=0))).astype(BF16)
            grad = grad + mm_nt(d_sims, block)
            dt_ref[m, :, p * ROW : (p + 1) * ROW] = mm(qt_ref[m], d_sims)
        unit = unit_q[m].astype(F32) * (1.0 / temper)
        along = jnp.sum(grad * unit, axis=1, keepdims=True)
        part = inv_q[m] * (grad - unit * along)
        if m == 0:
            dot_ref[...] = part
        else:
            dot_ref[...] += part
    dq_ref[...] = dot_ref[...].astype(BF16)
    total = jnp.zeros(turn_ref.shape, F32)
    for m in range(len(RANGES)):
        grad = dt_ref[m] * (1.0 / temper)
        unit = unit_ref[m].astype(F32)
        along = jnp.sum(grad * unit, axis=0, keepdims=True)
        total = total + inv_d[m] * (grad - unit * along)
    for p in range(doc_rows):
        dd_ref[p * ROW : (p + 1) * ROW, :] = total[:, p * ROW : (p + 1) * ROW].T.astype(BF16)


def store_block(refs, at, value):
    keep_ref, send_ref = refs
    half = keep_ref.shape[0]

    @pl.when(at < half)
    def _():
        keep_ref[at] = value

    @pl.when(at >= half)
    def _():
        send_ref[at - half] = value


def feed_back(
    where_ref, dq_ref, dd_ref, got_ref, xh2_ref, rs2_ref, g2_ref, s2_ref, xh1_ref, g1_ref, s1_ref,
    act_ref, slope_ref, wproj_ref, wdown_ref, wup_ref,
    down_keep, down_send, up_keep, up_send, dfirst_ref, gproj_ref, small_ref, dinner_ref,
):
    is_query, docs_there = where_ref[1] == 0, where_ref[4] == 0
    down_at, up_at = where_ref[5], where_ref[6]
    got = got_ref[...].astype(F32)
    d_vec = jnp.where(
        is_query,
        dq_ref[...].astype(F32) + got,
        jnp.where(docs_there, got, dd_ref[...].astype(F32)),
    )
    d_proj = d_vec.astype(BF16)
    xhat = xh2_ref[...]
    gain = g2_ref[...].astype(F32)
    second = (xhat * gain + s2_ref[...].astype(F32)).astype(BF16)
    gproj_ref[...] = mm_tn(second, d_proj)
    d_second = mm_nt(d_proj, wproj_ref[...])
    small_ref[...] = jnp.zeros_like(small_ref)
    small_ref[5:6, :] = col_sum(d_second * xhat)
    small_ref[6:7, :] = col_sum(d_second)
    d_sum = norm_back(d_second, xhat, rs2_ref[:, :1], gain)
    d_branch = d_sum.astype(BF16)
    small_ref[4:5, :] = col_sum(d_branch.astype(F32))
    step = 512
    blocks = 2 * down_keep.shape[0]
    size = down_keep.shape[1]
    d_first = d_sum
    for c in range(FF // step):
        cols = slice(c * step, (c + 1) * step)
        d_act = mm_nt(d_branch, wdown_ref[cols, :])
        d_inner = (d_act * slope_ref[:, cols].astype(F32)).astype(BF16)
        dinner_ref[:, cols] = d_inner
        small_ref[c : c + 1, :] = col_sum(d_inner.astype(F32))
        grad = mm_tn(act_ref[:, cols], d_branch).astype(BF16)
        for k in range(step // size):
            store_block(
                (down_keep, down_send),
                (c * (step // size) + k) ^ down_at,
                grad[k * size : (k + 1) * size, :],
            )
        d_first = d_first + mm_nt(d_inner, wup_ref[:, cols])
    dfirst_ref[...] = d_first
    first = (xh1_ref[...] * g1_ref[...].astype(F32) + s1_ref[...].astype(F32)).astype(BF16)
    for c in range(FF // step):
        cols = slice(c * step, (c + 1) * step)
        grad = mm_tn(first, dinner_ref[:, cols]).astype(BF16)
        for k in range(D // size):
            store_block(
                (up_keep, up_send),
                (c * (D // size) + k) ^ up_at,
                grad[k * size : (k + 1) * size, :],
            )


def attend_back(
    where_ref, dfirst_ref, xh1_ref, rs1_ref, g1_ref, mixed_ref, wout_ref, qkv_ref, probs_ref,
    rope_ref, x_ref, wqkv_ref, gproj_ref, small_ref,
    keep_ref, send_ref, tokens_ref, djoined_ref, rest_ref,
):
    at = where_ref[7]
    d_first = dfirst_ref[...]
    xhat = xh1_ref[...]
    gain = g1_ref[...].astype(F32)
    gain_grad = col_sum(d_first * xhat)
    shift_grad = col_sum(d_first)
    d_sum = norm_back(d_first, xhat, rs1_ref[:, :1], gain)
    d_att = d_sum.astype(BF16)
    bias_out = col_sum(d_att.astype(F32))
    rest_ref[3 * D : 4 * D, :] = mm_tn(mixed_ref[...], d_att).astype(BF16)
    d_mixed = mm_nt(d_att, wout_ref[...]).astype(BF16)
    cosine, sine = rope_ref[:, :128], rope_ref[:, 128:]
    low_half = iota((ROW, 128), 1) < HD

    def unrotate(values):
        values = values * (1.0 / math.sqrt(HD))
        return (values * cosine - swap_halves(values) * sine).astype(BF16)

    for g in range(HEADS // 2):
        span = slice(g * 128, (g + 1) * 128)
        q_g = qkv_ref[:, g * 128 : (g + 1) * 128]
        k_g = qkv_ref[:, D + g * 128 : D + (g + 1) * 128]
        v_g = qkv_ref[:, 2 * D + g * 128 : 2 * D + (g + 1) * 128]
        m_g = d_mixed[:, span]
        d_q = jnp.zeros((ROW, 128), F32)
        d_k = jnp.zeros((ROW, 128), F32)
        d_v = jnp.zeros((ROW, 128), F32)
        zero = jnp.zeros((ROW, 128), BF16)
        for h in range(2):
            pick = low_half if h == 0 else jnp.logical_not(low_half)
            probs_low = probs_ref[2 * g + h]
            probs = probs_low.astype(F32)
            m_h = jnp.where(pick, m_g, zero)
            d_probs = mm_nt(m_h, v_g)
            d_v = d_v + mm_tn(probs_low, m_h)
            inner = jnp.sum(d_probs * probs, axis=1, keepdims=True)
            d_scores = (probs * (d_probs - inner)).astype(BF16)
            d_q = d_q + mm(d_scores, jnp.where(pick, k_g, zero))
            d_k = d_k + mm_tn(d_scores, jnp.where(pick, q_g, zero))
        djoined_ref[:, g * 128 : (g + 1) * 128] = unrotate(d_q)
        djoined_ref[:, D + g * 128 : D + (g + 1) * 128] = unrotate(d_k)
        djoined_ref[:, 2 * D + g * 128 : 2 * D + (g + 1) * 128] = d_v.astype(BF16)
    x = x_ref[...]
    tokens = d_sum
    rest_ref[4 * D + 128 :, :] = jnp.zeros((REST - 4 * D - 128, D), BF16)
    smalls = []
    for c in range(3):
        cols = slice(c * D, (c + 1) * D)
        d_part = djoined_ref[:, cols]
        rest_ref[c * D : (c + 1) * D, :] = mm_tn(x, d_part).astype(BF16)
        smalls.append(col_sum(d_part.astype(F32)))
        tokens = tokens + mm_nt(d_part, wqkv_ref[:, cols])
    tokens_ref[...] = tokens
    for k in range(4):
        rest_ref[4 * D : 4 * D + 128, k * 128 : (k + 1) * 128] = gproj_ref[
            k * 128 : (k + 1) * 128, :
        ].astype(BF16)
    smalls += [bias_out, gain_grad, shift_grad] + [small_ref[k : k + 1, :] for k in range(7)]
    smalls += [jnp.zeros((EXT - len(smalls), D), F32)]
    rest_ref[4 * D + 128 : 4 * D + 128 + EXT, :] = jnp.concatenate(smalls, axis=0).astype(BF16)
    half, size = keep_ref.shape[0], keep_ref.shape[1]
    for p in range(half):
        for ref, offset in ((keep_ref, p), (send_ref, p + half)):
            start = pl.multiple_of((offset ^ at) * size, 16)
            ref[p] = rest_ref[pl.ds(start, size), :]


def spread_out(at_index, order, where_ref, near_ref, far_ref, out_ref):
    p = pl.program_id(0)
    half = pl.num_programs(0) // 2

    @pl.when(p < half)
    def _():
        out_ref[...] = near_ref[0].astype(F32)

    @pl.when(p >= half)
    def _():
        out_ref[...] = far_ref[0].astype(F32)


def spread_call(near, far, where, at_index, columns):
    half, size, width = near.shape
    blocks = 2 * half
    per_column = blocks // columns

    def out_index(p, where_ref):
        b = p ^ where_ref[at_index]
        return (b % per_column, b // per_column)

    return pl.pallas_call(
        partial(spread_out, at_index, None),
        out_shape=jax.ShapeDtypeStruct((blocks * size // columns, width * columns), F32),
        grid_spec=pltpu.PrefetchScalarGridSpec(
            num_scalar_prefetch=1,
            grid=(blocks,),
            in_specs=[
                pl.BlockSpec((1, size, width), lambda p, w: (jnp.minimum(p, half - 1), 0, 0)),
                pl.BlockSpec((1, size, width), lambda p, w: (jnp.maximum(p - half, 0), 0, 0)),
            ],
            out_specs=pl.BlockSpec((size, width), out_index),
        ),
    )(where, near, far)


def spread_rest(
    where_ref, near_ref, far_ref, qkv_ref, out_ref, proj_ref, bqkv_ref, bout_ref, g1_ref, s1_ref,
    bup_ref, bdown_ref, g2_ref, s2_ref, rest_ref,
):
    at = where_ref[7]
    half, size = near_ref.shape[0], near_ref.shape[1]
    for p in range(half):
        for ref, offset in ((near_ref, p), (far_ref, p + half)):
            start = pl.multiple_of((offset ^ at) * size, 16)
            rest_ref[pl.ds(start, size), :] = ref[p]
    for c in range(3):
        qkv_ref[:, c * D : (c + 1) * D] = rest_ref[c * D : (c + 1) * D, :].astype(F32)
    out_ref[...] = rest_ref[3 * D : 4 * D, :].astype(F32)
    for k in range(4):
        proj_ref[k * 128 : (k + 1) * 128, :] = rest_ref[
            4 * D : 4 * D + 128, k * 128 : (k + 1) * 128
        ].astype(F32)
    small = rest_ref[4 * D + 128 : 4 * D + 128 + EXT, :].astype(F32)
    row = [small[k : k + 1, :] for k in range(13)]
    for c in range(3):
        bqkv_ref[:, c * D : (c + 1) * D] = row[c]
    bout_ref[...] = row[3]
    g1_ref[...] = row[4]
    s1_ref[...] = row[5]
    for c in range(4):
        bup_ref[:, c * D : (c + 1) * D] = row[6 + c]
    bdown_ref[...] = row[10]
    g2_ref[...] = row[11]
    s2_ref[...] = row[12]


def shape_of(shape, dtype=F32):
    return jax.ShapeDtypeStruct(tuple(shape), dtype)


def call(kernel, args, specs, outs, scratch=(), flops=0):
    return pl.pallas_call(
        kernel,
        out_shape=outs,
        in_specs=specs,
        out_specs=[VMEM] * len(outs),
        scratch_shapes=list(scratch),
        compiler_params=pltpu.CompilerParams(vmem_limit_bytes=VLIMIT),
        cost_estimate=pl.CostEstimate(flops=flops, bytes_accessed=10**6, transcendentals=0),
    )(*args)


def swapped(value, mask, axis="dp"):
    size = lax.axis_size(axis)
    return lax.ppermute(value, axis, [(k, k ^ mask) for k in range(size)])


def added(a, b):
    return (a.astype(F32) + b.astype(F32)).astype(BF16)


def block_place(me, order):
    place = jnp.int32(0)
    for k, mask in enumerate(order):
        place = place | jnp.where((me & mask) != 0, 1 << (len(order) - 1 - k), 0)
    return place


def reduce_gather(keep, send, order, others):
    got = swapped(send, order[0])
    for mask in order[1:]:
        half = keep.shape[0] // 2
        send = added(keep[half:], got[half:])
        keep = added(keep[:half], got[:half])
        got = swapped(send, mask)
    own = added(keep, got)
    for mask in others:
        own = added(own, swapped(own, mask))
    for mask in reversed(order[1:]):
        own = jnp.concatenate([own, swapped(own, mask)], axis=0)
    return own, swapped(own, order[0])


def per_device(
    tokens, qkv_weight, qkv_bias, out_weight, out_bias, first_gain, first_shift, up_weight,
    up_bias, down_weight, down_bias, second_gain, second_shift, proj_weight, log_scale,
    doc_lengths, labels,
):
    size = lax.axis_size("dp")
    bits = [1 << k for k in range(size.bit_length() - 1)]
    near_masks, doc_masks = bits[:2], bits[2:]
    top_mask, doc_masks = doc_masks[-1], doc_masks[:-1]
    orders = [
        (bits[0], bits[1], bits[2], bits[3]),
        (bits[0], bits[2], bits[1], bits[3]),
        (bits[0], bits[1], bits[2], bits[3]),
    ]
    others = bits[4:]
    blocks = 16
    me = lax.axis_index("dp")
    stream = lax.axis_index("stream")
    is_query = stream == 0
    has_top = (me & top_mask) != 0
    base = jnp.where(is_query, me & ~top_mask, me | top_mask)
    near_at = jnp.where((me & near_masks[1]) != 0, 1, 0) + jnp.where((me & near_masks[0]) != 0, 2, 0)
    where = jnp.stack(
        [me, stream, base, near_at, has_top.astype(jnp.int32)]
        + [block_place(me, order) for order in orders]
    ).astype(jnp.int32)
    scale = log_scale.reshape(1)

    vec, qkv, rope, probs, mixed, xh1, rs1, act, slope, xh2, rs2 = call(
        encoder_forward,
        (
            where, doc_lengths, labels, jnp.asarray(rope_table()), tokens[0], qkv_weight[0], qkv_bias,
            out_weight[0], out_bias, first_gain, first_shift, up_weight[0], up_bias,
            down_weight[0], down_bias, second_gain, second_shift, proj_weight[0],
        ),
        [SMEM] * 3 + [VMEM] * 15,
        [
            shape_of((ROW + EXT, PROJ), BF16),
            shape_of((ROW, 3 * D), BF16),
            shape_of((ROW, 256)),
            shape_of((HEADS, ROW, ROW), BF16),
            shape_of((ROW, D), BF16),
            shape_of((ROW, D)),
            shape_of((ROW, 128)),
            shape_of((ROW, FF), BF16),
            shape_of((ROW, FF), BF16),
            shape_of((ROW, D)),
            shape_of((ROW, 128)),
        ],
    )

    other = swapped(vec, 1, "stream")
    near = jnp.where(is_query, vec, other)
    rows = jnp.where(is_query, other, vec)[:ROW]
    moved = swapped(rows, top_mask)
    near = jnp.concatenate([near, swapped(near, near_masks[1])], axis=0)
    rows = jnp.where(has_top == is_query, moved, rows)
    far = swapped(near, near_masks[0])
    pieces = []
    for k, mask in enumerate(doc_masks):
        pieces.append(rows)
        got = swapped(rows, mask)
        if k + 1 < len(doc_masks):
            rows = jnp.concatenate([rows, got], axis=0)
        else:
            pieces = [rows, got]
    doc_rows = sum(p.shape[0] for p in pieces) // ROW
    tokens_d = doc_rows * ROW
    tokens_q = 4 * ROW
    lanes = -(-3 * doc_rows * DOCS_ROW // 128) * 128
    total_queries = size * (ROW // QLEN)
    totals, el, hot, stats = call(
        partial(matching_stats, doc_masks, lanes),
        (where, scale, doc_lengths, near, far, *pieces),
        [SMEM] * 3 + [VMEM] * (2 + len(pieces)),
        [
            shape_of((tokens_q, lanes)),
            shape_of((tokens_q // QLEN, lanes)),
            shape_of((tokens_q // QLEN, lanes)),
            shape_of((tokens_q // QLEN, 128)),
        ],
        [pltpu.VMEM((PROJ, tokens_d), F32), pltpu.VMEM((3, PROJ, tokens_d), BF16)],
    )
    stats = stats + swapped(stats, near_masks[0])
    stats = stats + swapped(stats, near_masks[1])
    stats = stats + swapped(stats, 1, "stream")
    dq, dd, loss = call(
        partial(matching_back, doc_masks, lanes, total_queries),
        (where, scale, doc_lengths, near, far, totals, el, hot, stats, *pieces),
        [SMEM] * 3 + [VMEM] * (6 + len(pieces)),
        [shape_of((tokens_q, PROJ), BF16), shape_of((tokens_d, PROJ), BF16), shape_of((8, 128))],
        [
            pltpu.VMEM((PROJ, tokens_d), F32),
            pltpu.VMEM((3, PROJ, tokens_d), BF16),
            pltpu.VMEM((3, PROJ, tokens_q), BF16),
            pltpu.VMEM((tokens_q, PROJ), F32),
            pltpu.VMEM((3, PROJ, tokens_d), F32),
        ],
    )
    for mask in reversed(doc_masks):
        half = dd.shape[0] // 2
        dd = added(dd[:half], swapped(dd[half:], mask))
    for mask in near_masks:
        half = dq.shape[0] // 2
        dq = added(dq[:half], swapped(dq[half:], mask))
    dd = added(dd, swapped(dd, top_mask))
    got = swapped(jnp.where(is_query, dd, dq), 1, "stream")

    down_keep, down_send, up_keep, up_send, d_first, gproj, small = call(
        feed_back,
        (
            where, dq, dd, got, xh2, rs2, second_gain, second_shift, xh1, first_gain, first_shift,
            act, slope, proj_weight[0], down_weight[0], up_weight[0],
        ),
        [SMEM] + [VMEM] * 15,
        [shape_of((blocks // 2, FF // blocks, D), BF16)] * 4
        + [shape_of((ROW, D)), shape_of((D, PROJ)), shape_of((8, D))],
        [pltpu.VMEM((ROW, FF), BF16)],
    )
    rest_keep, rest_send, tokens_grad = call(
        attend_back,
        (
            where, d_first, xh1, rs1, first_gain, mixed, out_weight[0], qkv, probs, rope,
            tokens[0], qkv_weight[0], gproj, small,
        ),
        [SMEM] + [VMEM] * 13,
        [shape_of((blocks // 2, REST // blocks, D), BF16)] * 2 + [shape_of((ROW, D))],
        [pltpu.VMEM((ROW, 3 * D), BF16), pltpu.VMEM((REST, D), BF16)],
    )
    down_near, down_far = reduce_gather(down_keep, down_send, orders[0], others)
    up_near, up_far = reduce_gather(up_keep, up_send, orders[1], others)
    rest_near, rest_far = reduce_gather(rest_keep, rest_send, orders[2], others)
    for mask in doc_masks + [top_mask]:
        loss = loss + swapped(loss, mask)
    grad_down = spread_call(down_near, down_far, where, 5, 1)
    grad_up = spread_call(up_near, up_far, where, 6, 4)
    (
        grad_qkv, grad_out, grad_proj, grad_bqkv, grad_bout, grad_g1, grad_s1, grad_bup,
        grad_bdown, grad_g2, grad_s2,
    ) = call(
        spread_rest,
        (where, rest_near, rest_far),
        [SMEM, VMEM, VMEM],
        [
            shape_of((D, 3 * D)), shape_of((D, D)), shape_of((D, PROJ)), shape_of((1, 3 * D)),
            shape_of((1, D)), shape_of((1, D)), shape_of((1, D)), shape_of((1, FF)),
            shape_of((1, D)), shape_of((1, D)), shape_of((1, D)),
        ],
        [pltpu.VMEM((REST, D), BF16)],
    )
    return (
        loss[0, 0],
        tokens_grad[None],
        grad_qkv[None],
        grad_bqkv,
        grad_out[None],
        grad_bout,
        grad_g1,
        grad_s1,
        grad_up[None],
        grad_bup,
        grad_down[None],
        grad_bdown,
        grad_g2,
        grad_s2,
        grad_proj[None],
        loss[1, 0],
    )


def solution(mesh):
    return jax.shard_map(
        per_device,
        mesh=mesh,
        in_specs=(
            P("stream", "dp", None),
            P("stream", None, None),
            P("stream", None),
            P("stream", None, None),
            P("stream", None),
            P("stream", None),
            P("stream", None),
            P("stream", None, None),
            P("stream", None),
            P("stream", None, None),
            P("stream", None),
            P("stream", None),
            P("stream", None),
            P("stream", None, None),
            P(),
            P(),
            P("dp"),
        ),
        out_specs=(
            P(),
            P("stream", "dp", None),
            P("stream", None, None),
            P("stream", None),
            P("stream", None, None),
            P("stream", None),
            P("stream", None),
            P("stream", None),
            P("stream", None, None),
            P("stream", None),
            P("stream", None, None),
            P("stream", None),
            P("stream", None),
            P("stream", None),
            P("stream", None, None),
            P(),
        ),
        check_vma=False,
    )
```

```python
from functools import partial
import math

import jax
import jax.numpy as jnp
import numpy as np
from jax import lax
from jax.experimental import pallas as pl
from jax.experimental.pallas import tpu as pltpu
from jax.sharding import PartitionSpec as P

D = 512
HEADS = 8
HD = 64
FF = 2048
PROJ = 128
QLEN = 32
DOCS_ROW = 4
ROW = 256
EXT = 16
RANGES = (64, 96, 128)

SHARPNESS = 8.0
EPS_NORM = 1e-06
EPS_LAYER = 1e-05
LOG2E = 1.4426950408889634

F32 = jnp.float32
BF16 = jnp.bfloat16
REST = 2304
FINAL = ((0,), (1,), (2, 3))
ORDER = [4, 2, 3, 0, 1, 2, 3, 2, 4, 3, 0, 2, 1, 3, 0, 2, 1, 3, 4, 2, 0, 3, 1, 2, 0, 2, 1, 3, 0, 3, 12, 1, 0, 1, 0, 10, 1, 11]
MIB = 1024 * 1024

VMEM = pl.BlockSpec(memory_space=pltpu.VMEM)
SMEM = pl.BlockSpec(memory_space=pltpu.SMEM)


def mm(a, b):
    return lax.dot_general(a, b, (((1,), (0,)), ((), ())), preferred_element_type=F32)


def mm_nt(a, b):
    return lax.dot_general(a, b, (((1,), (1,)), ((), ())), preferred_element_type=F32)


def mm_tn(a, b):
    return lax.dot_general(a, b, (((0,), (0,)), ((), ())), preferred_element_type=F32)


def iota(shape, axis):
    return lax.broadcasted_iota(jnp.int32, shape, axis)


def rope_table():
    half = HD // 2
    freqs = (10000.0 ** (-np.arange(half, dtype=np.float32) / np.float32(half))).astype(np.float32)
    turned = np.arange(ROW, dtype=np.float32)[:, None] * freqs[None, :]
    cosine = np.cos(turned.astype(np.float64))
    sine = np.sin(turned.astype(np.float64))
    cosine = np.concatenate([cosine, cosine, cosine, cosine], axis=1).astype(np.float32)
    sine = np.concatenate([-sine, sine, -sine, sine], axis=1).astype(np.float32)
    parts = []
    for table in (cosine, sine):
        high = table.astype(jnp.bfloat16)
        low = (table - high.astype(np.float32)).astype(jnp.bfloat16)
        parts += [high, low]
    return np.concatenate(parts, axis=1)


def swap_halves(block):
    lane = iota(block.shape, 1)
    return jnp.where(lane % HD < HD // 2, pltpu.roll(block, 96, 1), pltpu.roll(block, 32, 1))


def bounds_of(lens_ref, row):
    ends, total = [], jnp.int32(0)
    for k in range(DOCS_ROW):
        total = total + lens_ref[row, k]
        ends.append(total)
    return ends


def segment_of(spot, ends):
    seg = jnp.zeros_like(spot)
    for end in ends:
        seg = seg + (spot >= end).astype(jnp.int32)
    return seg


def norm_rows(values):
    mean = jnp.mean(values, axis=1, keepdims=True)
    centred = values - mean
    spread = jnp.mean(centred * centred, axis=1, keepdims=True)
    rstd = lax.rsqrt(spread + EPS_LAYER)
    return centred * rstd, rstd


def norm_back(d_out, xhat, rstd, gain):
    scaled = d_out * gain
    first = jnp.mean(scaled, axis=1, keepdims=True)
    second = jnp.mean(scaled * xhat, axis=1, keepdims=True)
    return rstd * (scaled - first - xhat * second)


def col_sum(values):
    return jnp.sum(values, axis=0, keepdims=True)


def encoder_forward(
    where_ref, lens_ref, labels_ref, table_ref, x_ref, wqkv_ref, bqkv_ref, wout_ref, bout_ref,
    g1_ref, s1_ref, wup_ref, bup_ref, wdown_ref, bdown_ref, g2_ref, s2_ref, wproj_ref,
    vec_ref, qkv_ref, rope_ref, probs_ref, mixed_ref, xh1_ref, rs1_ref, act_ref, slope_ref,
    xh2_ref, rs2_ref,
):
    me, is_query = where_ref[0], where_ref[1] == 0
    ends = bounds_of(lens_ref, me)

    def layout(spot):
        seg_doc = segment_of(spot, ends)
        start_doc = jnp.zeros_like(spot)
        for k in range(DOCS_ROW):
            start_doc = jnp.where(seg_doc == k + 1, ends[k], start_doc)
        seg_query = spot // QLEN
        seg = jnp.where(is_query, seg_query, seg_doc)
        start = jnp.where(is_query, seg_query * QLEN, start_doc)
        return seg, start

    shape = (ROW, ROW)
    seg_q, start_q = layout(iota(shape, 0))
    seg_k, _ = layout(iota(shape, 1))
    same = seg_q == seg_k
    onehot = (iota(shape, 1) == iota(shape, 0) - start_q).astype(F32).astype(BF16)
    turned = mm(onehot, table_ref[...])
    cosine = turned[:, :128] + turned[:, 128:256]
    sine = turned[:, 256:384] + turned[:, 384:]
    rope_ref[:, :128] = cosine
    rope_ref[:, 128:] = sine

    x = x_ref[...]
    joined = mm(x, wqkv_ref[...]) + bqkv_ref[...].astype(F32)
    for g in range(2 * D // 128):
        block = joined[:, g * 128 : (g + 1) * 128]
        qkv_ref[:, g * 128 : (g + 1) * 128] = (
            block * cosine + swap_halves(block) * sine
        ).astype(BF16)
    qkv_ref[:, 2 * D :] = joined[:, 2 * D :].astype(BF16)

    low_half = iota((ROW, 128), 1) < HD
    for g in range(HEADS // 2):
        q_g = qkv_ref[:, g * 128 : (g + 1) * 128]
        k_g = qkv_ref[:, D + g * 128 : D + (g + 1) * 128]
        v_g = qkv_ref[:, 2 * D + g * 128 : 2 * D + (g + 1) * 128]
        outs = []
        for h in range(2):
            pick = low_half if h == 0 else jnp.logical_not(low_half)
            scores = mm_nt(jnp.where(pick, q_g, jnp.zeros_like(q_g)), k_g) * (1.0 / math.sqrt(HD))
            scores = jnp.where(same, scores, -1e30)
            top = jnp.max(scores, axis=1, keepdims=True)
            exps = jnp.exp(scores - top)
            probs = (exps / jnp.sum(exps, axis=1, keepdims=True)).astype(BF16)
            probs_ref[2 * g + h] = probs
            outs.append(mm(probs, v_g))
        mixed_ref[:, g * 128 : (g + 1) * 128] = jnp.where(low_half, outs[0], outs[1]).astype(BF16)

    attended = mm(mixed_ref[...], wout_ref[...]) + bout_ref[...].astype(F32)
    xhat, rstd = norm_rows(x.astype(F32) + attended)
    xh1_ref[...] = xhat
    rs1_ref[...] = jnp.broadcast_to(rstd, (ROW, 128))
    first = xhat * g1_ref[...].astype(F32) + s1_ref[...].astype(F32)
    first_low = first.astype(BF16)
    branch = bdown_ref[...].astype(F32) + first
    step = 512
    for c in range(FF // step):
        cols = slice(c * step, (c + 1) * step)
        inner = mm(first_low, wup_ref[:, cols]) + bup_ref[:, cols].astype(F32)
        gate = 0.5 + 0.5 * lax.erf(inner * math.sqrt(0.5))
        bell = jnp.exp(inner * inner * -0.5) * (1.0 / math.sqrt(2.0 * math.pi))
        act = (inner * gate).astype(BF16)
        act_ref[:, cols] = act
        slope_ref[:, cols] = (gate + inner * bell).astype(BF16)
        branch = branch + mm(act, wdown_ref[cols, :])
    xhat, rstd = norm_rows(branch)
    xh2_ref[...] = xhat
    rs2_ref[...] = jnp.broadcast_to(rstd, (ROW, 128))
    second = xhat * g2_ref[...].astype(F32) + s2_ref[...].astype(F32)
    vec_ref[:ROW, :] = mm(second.astype(BF16), wproj_ref[...]).astype(BF16)
    line = iota((EXT, PROJ), 0)
    tag = jnp.zeros((EXT, PROJ), jnp.int32)
    for k in range(labels_ref.shape[0]):
        label = labels_ref[k]
        tag = jnp.where(line == k, label >> 6, tag)
        tag = jnp.where(line == k + 8, label & 63, tag)
    vec_ref[ROW:, :] = tag.astype(F32).astype(BF16)


def prefix_norms(values, axis):
    place = iota(values.shape, axis)
    squared = values * values
    sums = [
        jnp.sum(jnp.where(place < cut, squared, 0.0), axis=axis, keepdims=True) for cut in RANGES
    ]
    return [lax.rsqrt(s + EPS_NORM) for s in sums]


def load_queries(near_ref, far_ref):
    span = ROW + EXT
    rows = []
    for ref in (near_ref, far_ref):
        for k in range(ref.shape[0] // span):
            rows.append(ref[k * span : k * span + ROW, :])
    return jnp.concatenate(rows, axis=0).astype(F32)


def unit_queries(queries, scale):
    lane = iota(queries.shape, 1)
    inverse = prefix_norms(queries, 1)
    unit = [
        jnp.where(lane < cut, queries * (inv * scale), 0.0) for cut, inv in zip(RANGES, inverse)
    ]
    return unit, inverse


def unit_docs(doc_refs, scratch_ref):
    at = 0
    for ref in doc_refs:
        for k in range(ref.shape[0] // ROW):
            scratch_ref[:, at * ROW : (at + 1) * ROW] = ref[
                k * ROW : (k + 1) * ROW, :
            ].astype(F32).T
            at += 1
    turned = scratch_ref[...]
    inverse = prefix_norms(turned, 0)
    place = iota(turned.shape, 0)
    unit = [jnp.where(place < cut, turned * inv, 0.0) for cut, inv in zip(RANGES, inverse)]
    return unit, inverse


def row_ids(base, masks, doc_rows):
    ids = []
    for p in range(doc_rows):
        offset = 0
        for k, mask in enumerate(masks):
            if (p >> k) & 1:
                offset ^= mask
        ids.append(base ^ offset)
    return ids


def doc_marks(lens_ref, ids, lanes, transposed):
    docs = len(ids) * DOCS_ROW
    shape = (lanes, ROW) if transposed else (ROW, lanes)
    spot, lane = (iota(shape, 1), iota(shape, 0)) if transposed else (iota(shape, 0), iota(shape, 1))
    marks = []
    for p, row in enumerate(ids):
        seg = segment_of(spot, bounds_of(lens_ref, row))
        local = jnp.where(seg < DOCS_ROW, seg + p * DOCS_ROW, -1 - lanes)
        marks.append(
            [(lane == local + m * docs).astype(F32).astype(BF16) for m in range(len(RANGES))]
        )
    return marks


def matching_stats(
    masks, lanes, where_ref, scale_ref, lens_ref, near_ref, far_ref, *refs
):
    doc_refs = refs[:-6]
    totals_ref, el_ref, hot_ref, stats_ref, turn_ref, unit_ref = refs[-6:]
    base, near_at = where_ref[2], where_ref[3]
    span = ROW + EXT
    queries = load_queries(near_ref, far_ref)
    count = queries.shape[0]
    unit_q, _ = unit_queries(queries, SHARPNESS * LOG2E)
    unit_q = [u.astype(BF16) for u in unit_q]
    unit_d, _ = unit_docs(doc_refs, turn_ref)
    for m in range(len(RANGES)):
        unit_ref[m] = unit_d[m].astype(BF16)
    doc_rows = turn_ref.shape[1] // ROW
    docs = doc_rows * DOCS_ROW
    ids = row_ids(base, masks, doc_rows)
    marks = doc_marks(lens_ref, ids, lanes, False)
    totals = jnp.zeros((count, lanes), F32)
    for p in range(doc_rows):
        for m in range(len(RANGES)):
            sims = mm(unit_q[m], unit_ref[m, :, p * ROW : (p + 1) * ROW])
            totals = totals + mm(jnp.exp2(sims).astype(BF16), marks[p][m])
    lane_t = iota((count, lanes), 1)
    totals = jnp.where(lane_t < len(RANGES) * docs, totals, 1.0)
    totals_ref[...] = totals
    shape = (8, lanes)
    lane = iota(shape, 1)
    length = jnp.ones(shape, jnp.int32)
    name = jnp.full(shape, -1, jnp.int32)
    for p in range(doc_rows):
        for k in range(DOCS_ROW):
            own = jnp.zeros(shape, jnp.bool_)
            for m in range(len(RANGES)):
                own = jnp.logical_or(own, lane == m * docs + p * DOCS_ROW + k)
            length = jnp.where(own, lens_ref[ids[p], k], length)
            name = jnp.where(own, ids[p] * DOCS_ROW + k, name)
    log_length = jnp.log(length.astype(F32))
    matched = (jnp.log(totals) - log_length[:1]) * (1.0 / SHARPNESS)
    per_query = jnp.sum(matched.reshape(count // QLEN, QLEN, lanes), axis=1)
    scale = jnp.exp(jnp.full(shape, scale_ref[0], F32))[:1]
    logits = per_query * (scale * (1.0 / QLEN))
    groups = count // ROW
    tags = []
    for ref in (near_ref, far_ref):
        for k in range(ref.shape[0] // span):
            high = ref[k * span + ROW : k * span + ROW + 8, :].astype(F32).astype(jnp.int32)
            low = ref[k * span + ROW + 8 : k * span + ROW + 16, :].astype(F32).astype(jnp.int32)
            tag = high * 64 + low
            tags.append(jnp.concatenate([tag] * (lanes // 128), axis=1))
    tag = jnp.concatenate(tags, axis=0)
    lane_q = iota(logits.shape, 1)
    valid = lane_q < len(RANGES) * docs
    el = jnp.where(valid, jnp.exp(logits), 0.0)
    hot = jnp.where(jnp.logical_and(valid, jnp.concatenate([name] * groups, axis=0) == tag), 1.0, 0.0)
    el_ref[...] = el
    hot_ref[...] = hot
    place = iota((groups * 8, 128), 1)
    stats = jnp.zeros((groups * 8, 128), F32)
    for k, values in enumerate((el, el * logits, hot * logits)):
        for m in range(len(RANGES)):
            inside = jnp.logical_and(lane_q >= m * docs, lane_q < (m + 1) * docs)
            one = jnp.sum(jnp.where(inside, values, 0.0), axis=1, keepdims=True)
            stats = jnp.where(place == k * 3 + m, one, stats)
    for a in range(groups):
        at = pl.multiple_of((near_at ^ a) * 8, 8)
        stats_ref[pl.ds(at, 8), :] = stats[a * 8 : (a + 1) * 8, :]


def matching_back(
    masks, lanes, total_queries, where_ref, scale_ref, lens_ref, near_ref, far_ref, totals_ref,
    el_ref, hot_ref, stats_ref, *refs
):
    doc_refs = refs[:-8]
    dq_ref, dd_ref, loss_ref, turn_ref, unit_ref, qt_ref, dot_ref, dt_ref = refs[-8:]
    base, near_at = where_ref[2], where_ref[3]
    temper = SHARPNESS * LOG2E
    queries = load_queries(near_ref, far_ref)
    count = queries.shape[0]
    unit_q, inv_q = unit_queries(queries, temper)
    unit_q = [u.astype(BF16) for u in unit_q]
    unit_d, inv_d = unit_docs(doc_refs, turn_ref)
    for m in range(len(RANGES)):
        unit_ref[m] = unit_d[m].astype(BF16)
        qt_ref[m] = unit_q[m].astype(F32).T.astype(BF16)
    doc_rows = turn_ref.shape[1] // ROW
    docs = doc_rows * DOCS_ROW
    ids = row_ids(base, masks, doc_rows)
    marks = doc_marks(lens_ref, ids, lanes, True)
    groups = count // ROW
    rows = []
    for a in range(groups):
        at = pl.multiple_of((near_at ^ a) * 8, 8)
        rows.append(stats_ref[pl.ds(at, 8), :])
    stats = jnp.concatenate(rows, axis=0)
    place = iota(stats.shape, 1)

    def column(k):
        return jnp.sum(jnp.where(place == k, stats, 0.0), axis=1, keepdims=True)

    shape = (groups * 8, lanes)
    lane_q = iota(shape, 1)
    sums = jnp.ones(shape, F32)
    loss = jnp.zeros((groups * 8, 1), F32)
    moved = jnp.zeros((groups * 8, 1), F32)
    for m in range(len(RANGES)):
        whole, weighted, picked = column(m), column(3 + m), column(6 + m)
        inside = jnp.logical_and(lane_q >= m * docs, lane_q < (m + 1) * docs)
        sums = jnp.where(inside, whole, sums)
        loss = loss + (jnp.log(whole) - picked)
        moved = moved + (weighted / whole - picked)
    line = iota((8, 128), 0)
    loss_ref[...] = jnp.where(
        line == 0,
        jnp.sum(loss, axis=0, keepdims=True) * (1.0 / total_queries),
        jnp.where(line == 1, jnp.sum(moved, axis=0, keepdims=True) * (1.0 / total_queries), 0.0),
    )
    scale = jnp.exp(jnp.full((8, lanes), scale_ref[0], F32))[:1]
    coeff = (el_ref[...] / sums - hot_ref[...]) * (scale * (1.0 / (QLEN * total_queries)))
    coeff = jnp.broadcast_to(coeff[:, None, :], (groups * 8, QLEN, lanes)).reshape(count, lanes)
    ratio = coeff / totals_ref[...]
    ratio_high = ratio.astype(BF16)
    ratio_low = (ratio - ratio_high.astype(F32)).astype(BF16)
    ratio = jnp.concatenate([ratio_high, ratio_low], axis=1)
    for m in range(len(RANGES)):
        grad = jnp.zeros((count, PROJ), F32)
        for p in range(doc_rows):
            block = unit_ref[m, :, p * ROW : (p + 1) * ROW]
            mark = marks[p][m]
            exps = jnp.exp2(mm(unit_q[m], block))
            d_sims = (exps * mm(ratio, jnp.concatenate([mark, mark], axis=0))).astype(BF16)
            grad = grad + mm_nt(d_sims, block)
            dt_ref[m, :, p * ROW : (p + 1) * ROW] = mm(qt_ref[m], d_sims)
        unit = unit_q[m].astype(F32) * (1.0 / temper)
        along = jnp.sum(grad * unit, axis=1, keepdims=True)
        part = inv_q[m] * (grad - unit * along)
        if m == 0:
            dot_ref[...] = part
        else:
            dot_ref[...] += part
    dq_ref[...] = dot_ref[...].astype(BF16)
    total = jnp.zeros(turn_ref.shape, F32)
    for m in range(len(RANGES)):
        grad = dt_ref[m] * (1.0 / temper)
        unit = unit_ref[m].astype(F32)
        along = jnp.sum(grad * unit, axis=0, keepdims=True)
        total = total + inv_d[m] * (grad - unit * along)
    for p in range(doc_rows):
        dd_ref[p * ROW : (p + 1) * ROW, :] = total[:, p * ROW : (p + 1) * ROW].T.astype(BF16)


def store_block(refs, block, places, value):
    keep_ref, send_ref = refs
    core, near_place, far_place = places
    half = keep_ref.shape[0]
    mine = core == block // half

    @pl.when(mine)
    def _():
        keep_ref[(block % half) ^ near_place] = value

    @pl.when(jnp.logical_not(mine))
    def _():
        send_ref[(block % half) ^ far_place] = value


def feed_back(
    where_ref, dq_ref, dd_ref, got_ref, xh2_ref, rs2_ref, g2_ref, s2_ref, xh1_ref, g1_ref, s1_ref,
    act_ref, slope_ref, wproj_ref, wdown_ref, wup_ref,
    down_keep, down_send, up_keep, up_send, dfirst_ref, gproj_ref, small_ref, dinner_ref,
):
    is_query, docs_there = where_ref[1] == 0, where_ref[4] == 0
    places = (where_ref[5], where_ref[6], where_ref[7])
    got = got_ref[...].astype(F32)
    d_vec = jnp.where(
        is_query,
        dq_ref[...].astype(F32) + got,
        jnp.where(docs_there, got, dd_ref[...].astype(F32)),
    )
    d_proj = d_vec.astype(BF16)
    xhat = xh2_ref[...]
    gain = g2_ref[...].astype(F32)
    second = (xhat * gain + s2_ref[...].astype(F32)).astype(BF16)
    gproj_ref[...] = mm_tn(second, d_proj)
    d_second = mm_nt(d_proj, wproj_ref[...])
    small_ref[...] = jnp.zeros_like(small_ref)
    small_ref[5:6, :] = col_sum(d_second * xhat)
    small_ref[6:7, :] = col_sum(d_second)
    d_sum = norm_back(d_second, xhat, rs2_ref[:, :1], gain)
    d_branch = d_sum.astype(BF16)
    small_ref[4:5, :] = col_sum(d_branch.astype(F32))
    step = 512
    blocks = 2 * down_keep.shape[0]
    size = down_keep.shape[1]
    d_first = d_sum
    for c in range(FF // step):
        cols = slice(c * step, (c + 1) * step)
        d_act = mm_nt(d_branch, wdown_ref[cols, :])
        d_inner = (d_act * slope_ref[:, cols].astype(F32)).astype(BF16)
        dinner_ref[:, cols] = d_inner
        small_ref[c : c + 1, :] = col_sum(d_inner.astype(F32))
        grad = mm_tn(act_ref[:, cols], d_branch).astype(BF16)
        for k in range(step // size):
            store_block(
                (down_keep, down_send),
                c * (step // size) + k,
                places,
                grad[k * size : (k + 1) * size, :],
            )
        d_first = d_first + mm_nt(d_inner, wup_ref[:, cols])
    dfirst_ref[...] = d_first
    first = (xh1_ref[...] * g1_ref[...].astype(F32) + s1_ref[...].astype(F32)).astype(BF16)
    for c in range(FF // step):
        cols = slice(c * step, (c + 1) * step)
        grad = mm_tn(first, dinner_ref[:, cols]).astype(BF16)
        for k in range(D // size):
            store_block(
                (up_keep, up_send),
                c * (D // size) + k,
                places,
                grad[k * size : (k + 1) * size, :],
            )


def attend_back(
    where_ref, dfirst_ref, xh1_ref, rs1_ref, g1_ref, mixed_ref, wout_ref, qkv_ref, probs_ref,
    rope_ref, x_ref, wqkv_ref, gproj_ref, small_ref,
    keep_one, send_one, keep_two, send_two, tokens_ref, djoined_ref, rest_ref,
):
    core, near_place, far_place = where_ref[5], where_ref[6], where_ref[7]
    d_first = dfirst_ref[...]
    xhat = xh1_ref[...]
    gain = g1_ref[...].astype(F32)
    gain_grad = col_sum(d_first * xhat)
    shift_grad = col_sum(d_first)
    d_sum = norm_back(d_first, xhat, rs1_ref[:, :1], gain)
    d_att = d_sum.astype(BF16)
    bias_out = col_sum(d_att.astype(F32))
    rest_ref[3 * D : 4 * D, :] = mm_tn(mixed_ref[...], d_att)
    d_mixed = mm_nt(d_att, wout_ref[...]).astype(BF16)
    cosine, sine = rope_ref[:, :128], rope_ref[:, 128:]
    low_half = iota((ROW, 128), 1) < HD

    def unrotate(values):
        values = values * (1.0 / math.sqrt(HD))
        return (values * cosine - swap_halves(values) * sine).astype(BF16)

    for g in range(HEADS // 2):
        span = slice(g * 128, (g + 1) * 128)
        q_g = qkv_ref[:, g * 128 : (g + 1) * 128]
        k_g = qkv_ref[:, D + g * 128 : D + (g + 1) * 128]
        v_g = qkv_ref[:, 2 * D + g * 128 : 2 * D + (g + 1) * 128]
        m_g = d_mixed[:, span]
        d_q = jnp.zeros((ROW, 128), F32)
        d_k = jnp.zeros((ROW, 128), F32)
        d_v = jnp.zeros((ROW, 128), F32)
        zero = jnp.zeros((ROW, 128), BF16)
        for h in range(2):
            pick = low_half if h == 0 else jnp.logical_not(low_half)
            probs_low = probs_ref[2 * g + h]
            probs = probs_low.astype(F32)
            m_h = jnp.where(pick, m_g, zero)
            d_probs = mm_nt(m_h, v_g)
            d_v = d_v + mm_tn(probs_low, m_h)
            inner = jnp.sum(d_probs * probs, axis=1, keepdims=True)
            d_scores = (probs * (d_probs - inner)).astype(BF16)
            d_q = d_q + mm(d_scores, jnp.where(pick, k_g, zero))
            d_k = d_k + mm_tn(d_scores, jnp.where(pick, q_g, zero))
        djoined_ref[:, g * 128 : (g + 1) * 128] = unrotate(d_q)
        djoined_ref[:, D + g * 128 : D + (g + 1) * 128] = unrotate(d_k)
        djoined_ref[:, 2 * D + g * 128 : 2 * D + (g + 1) * 128] = d_v.astype(BF16)
    x = x_ref[...]
    tokens = d_sum
    rest_ref[4 * D + 128 :, :] = jnp.zeros((REST - 4 * D - 128, D), F32)
    smalls = []
    for c in range(3):
        cols = slice(c * D, (c + 1) * D)
        d_part = djoined_ref[:, cols]
        rest_ref[c * D : (c + 1) * D, :] = mm_tn(x, d_part)
        smalls.append(col_sum(d_part.astype(F32)))
        tokens = tokens + mm_nt(d_part, wqkv_ref[:, cols])
    tokens_ref[...] = tokens
    for k in range(4):
        rest_ref[4 * D : 4 * D + 128, k * 128 : (k + 1) * 128] = gproj_ref[
            k * 128 : (k + 1) * 128, :
        ]
    smalls += [bias_out, gain_grad, shift_grad] + [small_ref[k : k + 1, :] for k in range(7)]
    smalls += [jnp.zeros((EXT - len(smalls), D), F32)]
    rest_ref[4 * D + 128 : 4 * D + 128 + EXT, :] = jnp.concatenate(smalls, axis=0)
    first = 0
    for keep_ref, send_ref in ((keep_one, send_one), (keep_two, send_two)):
        half, size = keep_ref.shape[0], keep_ref.shape[1]
        for p in range(half):
            for ref, owner, place in ((keep_ref, core, near_place), (send_ref, 1 - core, far_place)):
                block = owner * half + (p ^ place)
                start = pl.multiple_of(first + block * size, 8)
                ref[p] = rest_ref[pl.ds(start, size), :].astype(BF16)
        first += 2 * half * size


def spread_out(columns, where_ref, near_ref, far_ref, out_ref):
    core, near_place, far_place = where_ref[5], where_ref[6], where_ref[7]
    half, size, width = near_ref.shape
    per_column = 2 * half // columns
    for p in range(half):
        for ref, owner, place in ((near_ref, core, near_place), (far_ref, 1 - core, far_place)):
            block = owner * half + (p ^ place)
            start = pl.multiple_of((block % per_column) * size, 8)
            left = pl.multiple_of((block // per_column) * width, 128)
            out_ref[pl.ds(start, size), pl.ds(left, width)] = ref[p].astype(F32)


def spread_rest(
    where_ref, near_one, far_one, near_two, far_two, qkv_ref, out_ref, proj_ref, bqkv_ref, bout_ref,
    g1_ref, s1_ref, bup_ref, bdown_ref, g2_ref, s2_ref, rest_ref,
):
    core, near_place, far_place = where_ref[5], where_ref[6], where_ref[7]
    first = 0
    for near_ref, far_ref in ((near_one, far_one), (near_two, far_two)):
        half, size = near_ref.shape[0], near_ref.shape[1]
        for p in range(half):
            for ref, owner, place in ((near_ref, core, near_place), (far_ref, 1 - core, far_place)):
                block = owner * half + (p ^ place)
                start = pl.multiple_of(first + block * size, 8)
                rest_ref[pl.ds(start, size), :] = ref[p].astype(F32)
        first += 2 * half * size
    for c in range(3):
        qkv_ref[:, c * D : (c + 1) * D] = rest_ref[c * D : (c + 1) * D, :]
    out_ref[...] = rest_ref[3 * D : 4 * D, :]
    for k in range(4):
        proj_ref[k * 128 : (k + 1) * 128, :] = rest_ref[
            4 * D : 4 * D + 128, k * 128 : (k + 1) * 128
        ]
    small = rest_ref[4 * D + 128 : 4 * D + 128 + EXT, :]
    row = [small[k : k + 1, :] for k in range(13)]
    for c in range(3):
        bqkv_ref[:, c * D : (c + 1) * D] = row[c]
    bout_ref[...] = row[3]
    g1_ref[...] = row[4]
    s1_ref[...] = row[5]
    for c in range(4):
        bup_ref[:, c * D : (c + 1) * D] = row[6 + c]
    bdown_ref[...] = row[10]
    g2_ref[...] = row[11]
    s2_ref[...] = row[12]


def shape_of(shape, dtype=F32):
    return jax.ShapeDtypeStruct(tuple(shape), dtype)


def call(kernel, args, specs, outs, scratch=(), room=24):
    return pl.pallas_call(
        kernel,
        out_shape=outs,
        in_specs=specs,
        out_specs=[VMEM] * len(outs),
        scratch_shapes=list(scratch),
        compiler_params=pltpu.CompilerParams(vmem_limit_bytes=room * MIB),
        cost_estimate=pl.CostEstimate(flops=10**9, bytes_accessed=10**7, transcendentals=0),
    )(*args)


def spread_call(kind, where, halves):
    if kind < 2:
        columns = (1, 4)[kind]
        kernel, outs, scratch = (
            partial(spread_out, columns), [shape_of((FF // columns, D * columns))], []
        )
    else:
        kernel, scratch = spread_rest, [pltpu.VMEM((REST, D), F32)]
        outs = [
            shape_of((D, 3 * D)), shape_of((D, D)), shape_of((D, PROJ)), shape_of((1, 3 * D)),
            shape_of((1, D)), shape_of((1, D)), shape_of((1, D)), shape_of((1, FF)),
            shape_of((1, D)), shape_of((1, D)), shape_of((1, D)),
        ]
    return call(kernel, (where, *halves), [SMEM] + [VMEM] * len(halves), outs, scratch)


def swapped(value, mask, axis="dp"):
    size = lax.axis_size(axis)
    return lax.ppermute(value, axis, [(k, k ^ mask) for k in range(size)])


def added(a, b):
    return (a.astype(F32) + b.astype(F32)).astype(BF16)


def block_place(me, order):
    place = jnp.int32(0)
    for k, mask in enumerate(order):
        place = place | jnp.where((me & mask) != 0, 1 << (len(order) - 1 - k), 0)
    return place


def swapped_by_core(value, masks):
    size = lax.axis_size("dp")
    return lax.ppermute(value, "dp", [(k, k ^ masks[k & 1]) for k in range(size)])


class Summed:
    def __init__(self, keep, send, masks, others):
        self.keep, self.masks, self.others, self.at = keep, masks, others, 0
        self.got = swapped_by_core(send, masks[0])

    def step(self, after):
        keep, got = self.keep, self.got
        if after is not None:
            keep, got, _ = lax.optimization_barrier((keep, got, after))
        self.at += 1
        last = len(self.masks)
        if self.at < last:
            half = keep.shape[0] // 2
            send = added(keep[half:], got[half:])
            self.keep = added(keep[:half], got[:half])
            self.got = swapped_by_core(send, self.masks[self.at])
            return send
        if self.at == last:
            keep = added(keep, got)
            for mask in self.others:
                keep = added(keep, swapped(keep, mask))
        elif self.at < 2 * last:
            keep = jnp.concatenate([keep, got], axis=0)
        else:
            self.keep, self.got = keep, got
            return got
        self.keep = keep
        self.got = swapped_by_core(keep, self.masks[2 * last - 1 - self.at])
        return keep


class Doubled:
    def __init__(self, value, masks):
        self.value, self.masks, self.got = value, list(masks), None

    def step(self, after):
        value, got = self.value, self.got
        if after is not None:
            value, _ = lax.optimization_barrier((value, after))
        if got is not None:
            value = value + got
        self.value, self.got = value, None
        if self.masks:
            self.got = swapped(value, self.masks.pop(0))
        return value


def per_device(
    tokens, qkv_weight, qkv_bias, out_weight, out_bias, first_gain, first_shift, up_weight,
    up_bias, down_weight, down_bias, second_gain, second_shift, proj_weight, log_scale,
    doc_lengths, labels,
):
    size = lax.axis_size("dp")
    bits = [1 << k for k in range(size.bit_length() - 1)]
    near_masks, doc_masks = bits[:2], bits[2:]
    top_mask, doc_masks = doc_masks[-1], doc_masks[:-1]
    masks = [(bits[0], bits[0]), (bits[1], bits[2]), (bits[2], bits[1]), (bits[3], bits[3])]
    others = bits[4:]
    blocks = 16
    me = lax.axis_index("dp")
    stream = lax.axis_index("stream")
    is_query = stream == 0
    has_top = (me & top_mask) != 0
    base = jnp.where(is_query, me & ~top_mask, me | top_mask)
    near_at = jnp.where((me & near_masks[1]) != 0, 1, 0) + jnp.where((me & near_masks[0]) != 0, 2, 0)
    core = me & 1
    places = [block_place(me, [pair[k] for pair in masks[1:]]) for k in range(2)]
    where = jnp.stack(
        [me, stream, base, near_at, has_top.astype(jnp.int32), core]
        + [jnp.where(core == 0, *places), jnp.where(core == 0, *places[::-1])]
    ).astype(jnp.int32)
    scale = log_scale.reshape(1)

    vec, qkv, rope, probs, mixed, xh1, rs1, act, slope, xh2, rs2 = call(
        encoder_forward,
        (
            where, doc_lengths, labels, jnp.asarray(rope_table()), tokens[0], qkv_weight[0], qkv_bias,
            out_weight[0], out_bias, first_gain, first_shift, up_weight[0], up_bias,
            down_weight[0], down_bias, second_gain, second_shift, proj_weight[0],
        ),
        [SMEM] * 3 + [VMEM] * 15,
        [
            shape_of((ROW + EXT, PROJ), BF16),
            shape_of((ROW, 3 * D), BF16),
            shape_of((ROW, 256)),
            shape_of((HEADS, ROW, ROW), BF16),
            shape_of((ROW, D), BF16),
            shape_of((ROW, D)),
            shape_of((ROW, 128)),
            shape_of((ROW, FF), BF16),
            shape_of((ROW, FF), BF16),
            shape_of((ROW, D)),
            shape_of((ROW, 128)),
        ],
    )

    other = swapped(vec, 1, "stream")
    near = jnp.where(is_query, vec, other)
    rows = jnp.where(is_query, other, vec)[:ROW]
    moved = swapped(rows, top_mask)
    near = jnp.concatenate([near, swapped(near, near_masks[1])], axis=0)
    rows = jnp.where(has_top == is_query, moved, rows)
    far = swapped(near, near_masks[0])
    pieces = []
    for k, mask in enumerate(doc_masks):
        pieces.append(rows)
        got = swapped(rows, mask)
        if k + 1 < len(doc_masks):
            rows = jnp.concatenate([rows, got], axis=0)
        else:
            pieces = [rows, got]
    doc_rows = sum(p.shape[0] for p in pieces) // ROW
    tokens_d = doc_rows * ROW
    tokens_q = 4 * ROW
    lanes = -(-3 * doc_rows * DOCS_ROW // 128) * 128
    total_queries = size * (ROW // QLEN)
    room = 20 if doc_rows <= 4 else 56
    totals, el, hot, stats = call(
        partial(matching_stats, doc_masks, lanes),
        (where, scale, doc_lengths, near, far, *pieces),
        [SMEM] * 3 + [VMEM] * (2 + len(pieces)),
        [
            shape_of((tokens_q, lanes)),
            shape_of((tokens_q // QLEN, lanes)),
            shape_of((tokens_q // QLEN, lanes)),
            shape_of((tokens_q // QLEN, 128)),
        ],
        [pltpu.VMEM((PROJ, tokens_d), F32), pltpu.VMEM((3, PROJ, tokens_d), BF16)],
        room=room,
    )
    stats = stats + swapped(stats, near_masks[0])
    stats = stats + swapped(stats, near_masks[1])
    stats = stats + swapped(stats, 1, "stream")
    dq, dd, loss = call(
        partial(matching_back, doc_masks, lanes, total_queries),
        (where, scale, doc_lengths, near, far, totals, el, hot, stats, *pieces),
        [SMEM] * 3 + [VMEM] * (6 + len(pieces)),
        [shape_of((tokens_q, PROJ), BF16), shape_of((tokens_d, PROJ), BF16), shape_of((8, 128))],
        [
            pltpu.VMEM((PROJ, tokens_d), F32),
            pltpu.VMEM((3, PROJ, tokens_d), BF16),
            pltpu.VMEM((3, PROJ, tokens_q), BF16),
            pltpu.VMEM((tokens_q, PROJ), F32),
            pltpu.VMEM((3, PROJ, tokens_d), F32),
        ],
        room=room,
    )
    for mask in reversed(doc_masks):
        half = dd.shape[0] // 2
        dd = added(dd[:half], swapped(dd[half:], mask))
    for mask in near_masks:
        half = dq.shape[0] // 2
        dq = added(dq[:half], swapped(dq[half:], mask))
    dd = added(dd, swapped(dd, top_mask))
    got = swapped(jnp.where(is_query, dd, dq), 1, "stream")

    down_keep, down_send, up_keep, up_send, d_first, gproj, small = call(
        feed_back,
        (
            where, dq, dd, got, xh2, rs2, second_gain, second_shift, xh1, first_gain, first_shift,
            act, slope, proj_weight[0], down_weight[0], up_weight[0],
        ),
        [SMEM] + [VMEM] * 15,
        [shape_of((blocks // 2, FF // blocks, D), BF16)] * 4
        + [shape_of((ROW, D)), shape_of((D, PROJ)), shape_of((8, D))],
        [pltpu.VMEM((ROW, FF), BF16)],
    )
    keep_one, send_one, keep_two, send_two, tokens_grad = call(
        attend_back,
        (
            where, d_first, xh1, rs1, first_gain, mixed, out_weight[0], qkv, probs, rope,
            tokens[0], qkv_weight[0], gproj, small,
        ),
        [SMEM] + [VMEM] * 13,
        [shape_of((blocks // 2, 3 * D // blocks, D), BF16)] * 2
        + [shape_of((blocks // 2, (REST - 3 * D) // blocks, D), BF16)] * 2
        + [shape_of((ROW, D))],
        [pltpu.VMEM((ROW, 3 * D), BF16), pltpu.VMEM((REST, D), F32)],
    )
    pieces = [
        Summed(keep, send, masks, others)
        for keep, send in (
            (down_keep, down_send), (up_keep, up_send), (keep_one, send_one), (keep_two, send_two)
        )
    ] + [Doubled(loss, doc_masks + [top_mask])]
    token, spread = None, {}
    for k in ORDER:
        if k >= 10:
            ready = [pieces[j] for j in FINAL[k - 10]]
            halves = [half for piece in ready for half in (piece.keep, piece.got)]
            *halves, _ = lax.optimization_barrier((*halves, token))
            spread[k - 10] = spread_call(k - 10, where, halves)
            token = spread[k - 10][0]
        else:
            token = pieces[k].step(token)
    grad_down, grad_up = spread[0][0], spread[1][0]
    (
        grad_qkv, grad_out, grad_proj, grad_bqkv, grad_bout, grad_g1, grad_s1, grad_bup,
        grad_bdown, grad_g2, grad_s2,
    ) = spread[2]
    while pieces[-1].got is not None:
        pieces[-1].step(None)
    loss = pieces[-1].value
    return (
        loss[0, 0],
        tokens_grad[None],
        grad_qkv[None],
        grad_bqkv,
        grad_out[None],
        grad_bout,
        grad_g1,
        grad_s1,
        grad_up[None],
        grad_bup,
        grad_down[None],
        grad_bdown,
        grad_g2,
        grad_s2,
        grad_proj[None],
        loss[1, 0],
    )


def solution(mesh):
    return jax.shard_map(
        per_device,
        mesh=mesh,
        in_specs=(
            P("stream", "dp", None),
            P("stream", None, None),
            P("stream", None),
            P("stream", None, None),
            P("stream", None),
            P("stream", None),
            P("stream", None),
            P("stream", None, None),
            P("stream", None),
            P("stream", None, None),
            P("stream", None),
            P("stream", None),
            P("stream", None),
            P("stream", None, None),
            P(),
            P(),
            P("dp"),
        ),
        out_specs=(
            P(),
            P("stream", "dp", None),
            P("stream", None, None),
            P("stream", None),
            P("stream", None, None),
            P("stream", None),
            P("stream", None),
            P("stream", None),
            P("stream", None, None),
            P("stream", None),
            P("stream", None, None),
            P("stream", None),
            P("stream", None),
            P("stream", None),
            P("stream", None, None),
            P(),
        ),
        check_vma=False,
    )
```

```python
from functools import partial
import math

import jax
import jax.numpy as jnp
import numpy as np
from jax import lax
from jax.experimental import pallas as pl
from jax.experimental.pallas import tpu as pltpu
from jax.sharding import PartitionSpec as P

D = 512
HEADS = 8
HD = 64
FF = 2048
PROJ = 128
QLEN = 32
DOCS_ROW = 4
ROW = 256
EXT = 16
RANGES = (64, 96, 128)

SHARPNESS = 8.0
EPS_NORM = 1e-06
EPS_LAYER = 1e-05
LOG2E = 1.4426950408889634

F32 = jnp.float32
BF16 = jnp.bfloat16
REST = 2304
FINAL = ((0,), (1,), (2, 3))
ORDER = [4, 2, 3, 0, 1, 2, 3, 2, 4, 3, 0, 2, 1, 3, 0, 2, 1, 3, 4, 2, 0, 3, 1, 2, 0, 2, 1, 3, 0, 3, 12, 1, 0, 1, 0, 10, 1, 11]
MIB = 1024 * 1024

VMEM = pl.BlockSpec(memory_space=pltpu.VMEM)
SMEM = pl.BlockSpec(memory_space=pltpu.SMEM)
HBM = pl.BlockSpec(memory_space=pltpu.HBM)
HELD = pl.BlockSpec(memory_space=pltpu.VMEM)


def mm(a, b):
    return lax.dot_general(a, b, (((1,), (0,)), ((), ())), preferred_element_type=F32)


def mm_nt(a, b):
    return lax.dot_general(a, b, (((1,), (1,)), ((), ())), preferred_element_type=F32)


def mm_tn(a, b):
    return lax.dot_general(a, b, (((0,), (0,)), ((), ())), preferred_element_type=F32)


def iota(shape, axis):
    return lax.broadcasted_iota(jnp.int32, shape, axis)


def rope_table():
    half = HD // 2
    freqs = (10000.0 ** (-np.arange(half, dtype=np.float32) / np.float32(half))).astype(np.float32)
    turned = np.arange(ROW, dtype=np.float32)[:, None] * freqs[None, :]
    cosine = np.cos(turned.astype(np.float64))
    sine = np.sin(turned.astype(np.float64))
    cosine = np.concatenate([cosine, cosine, cosine, cosine], axis=1).astype(np.float32)
    sine = np.concatenate([-sine, sine, -sine, sine], axis=1).astype(np.float32)
    parts = []
    for table in (cosine, sine):
        high = table.astype(jnp.bfloat16)
        low = (table - high.astype(np.float32)).astype(jnp.bfloat16)
        parts += [high, low]
    return np.concatenate(parts, axis=1)


def swap_halves(block):
    lane = iota(block.shape, 1)
    return jnp.where(lane % HD < HD // 2, pltpu.roll(block, 96, 1), pltpu.roll(block, 32, 1))


def bounds_of(lens_ref, row):
    ends, total = [], jnp.int32(0)
    for k in range(DOCS_ROW):
        total = total + lens_ref[row, k]
        ends.append(total)
    return ends


def segment_of(spot, ends):
    seg = jnp.zeros_like(spot)
    for end in ends:
        seg = seg + (spot >= end).astype(jnp.int32)
    return seg


def norm_rows(values):
    mean = jnp.mean(values, axis=1, keepdims=True)
    centred = values - mean
    spread = jnp.mean(centred * centred, axis=1, keepdims=True)
    rstd = lax.rsqrt(spread + EPS_LAYER)
    return centred * rstd, rstd


def norm_back(d_out, xhat, rstd, gain):
    scaled = d_out * gain
    first = jnp.mean(scaled, axis=1, keepdims=True)
    second = jnp.mean(scaled * xhat, axis=1, keepdims=True)
    return rstd * (scaled - first - xhat * second)


def col_sum(values):
    return jnp.sum(values, axis=0, keepdims=True)


def fetch(pairs, sems):
    copies = [pltpu.make_async_copy(src, dst, sems.at[k]) for k, (src, dst) in enumerate(pairs)]
    for copy in copies:
        copy.start()
    return copies


KEPT = (
    ((ROW, 3 * D), BF16),
    ((ROW, 256), F32),
    ((HEADS, ROW, ROW), BF16),
    ((ROW, D), BF16),
    ((ROW, D), F32),
    ((ROW, 128), F32),
    ((ROW, FF), BF16),
    ((ROW, FF), BF16),
    ((ROW, D), F32),
    ((ROW, 128), F32),
    ((8, D), F32),
)


def encoder_forward(
    where_ref, lens_ref, labels_ref, table_hbm, x_hbm, wqkv_hbm, bqkv_hbm, wout_hbm, bout_hbm,
    g1_hbm, s1_hbm, wup_hbm, bup_hbm, wdown_hbm, bdown_hbm, g2_hbm, s2_hbm, wproj_hbm,
    vec_ref, qkv_hbm, rope_hbm, probs_hbm, mixed_hbm, xh1_hbm, rs1_hbm, act_hbm, slope_hbm,
    xh2_hbm, rs2_hbm, affine_hbm,
    qkv_ref, rope_ref, probs_ref, mixed_ref, xh1_ref, rs1_ref, act_ref, slope_ref,
    xh2_ref, rs2_ref, affine_ref, out_sems,
    table_ref, x_ref, wqkv_ref, bqkv_ref, wout_ref, bout_ref, g1_ref, s1_ref, wup_ref, bup_ref,
    wdown_ref, bdown_ref, g2_ref, s2_ref, wproj_ref, sems,
):
    copies = fetch(
        (
            (table_hbm, table_ref), (x_hbm, x_ref), (wqkv_hbm, wqkv_ref), (bqkv_hbm, bqkv_ref),
            (wout_hbm, wout_ref), (bout_hbm, bout_ref), (g1_hbm, g1_ref), (s1_hbm, s1_ref),
            (bup_hbm, bup_ref), (bdown_hbm, bdown_ref), (g2_hbm, g2_ref), (s2_hbm, s2_ref),
            (wup_hbm, wup_ref), (wdown_hbm, wdown_ref), (wproj_hbm, wproj_ref),
        ),
        sems,
    )
    kept = []

    def keep(src, dst):
        copy = pltpu.make_async_copy(src, dst, out_sems.at[len(kept)])
        copy.start()
        kept.append(copy)

    me, is_query = where_ref[0], where_ref[1] == 0
    ends = bounds_of(lens_ref, me)

    def layout(spot):
        seg_doc = segment_of(spot, ends)
        start_doc = jnp.zeros_like(spot)
        for k in range(DOCS_ROW):
            start_doc = jnp.where(seg_doc == k + 1, ends[k], start_doc)
        seg_query = spot // QLEN
        seg = jnp.where(is_query, seg_query, seg_doc)
        start = jnp.where(is_query, seg_query * QLEN, start_doc)
        return seg, start

    shape = (ROW, ROW)
    seg_q, start_q = layout(iota(shape, 0))
    seg_k, _ = layout(iota(shape, 1))
    same = seg_q == seg_k
    onehot = (iota(shape, 1) == iota(shape, 0) - start_q).astype(F32).astype(BF16)
    for copy in copies[:4]:
        copy.wait()
    turned = mm(onehot, table_ref[...])
    cosine = turned[:, :128] + turned[:, 128:256]
    sine = turned[:, 256:384] + turned[:, 384:]
    rope_ref[:, :128] = cosine
    rope_ref[:, 128:] = sine
    keep(rope_ref, rope_hbm)

    x = x_ref[...]
    joined = mm(x, wqkv_ref[...]) + bqkv_ref[...].astype(F32)
    for g in range(2 * D // 128):
        block = joined[:, g * 128 : (g + 1) * 128]
        qkv_ref[:, g * 128 : (g + 1) * 128] = (
            block * cosine + swap_halves(block) * sine
        ).astype(BF16)
    qkv_ref[:, 2 * D :] = joined[:, 2 * D :].astype(BF16)
    keep(qkv_ref, qkv_hbm)

    low_half = iota((ROW, 128), 1) < HD
    for g in range(HEADS // 2):
        q_g = qkv_ref[:, g * 128 : (g + 1) * 128]
        k_g = qkv_ref[:, D + g * 128 : D + (g + 1) * 128]
        v_g = qkv_ref[:, 2 * D + g * 128 : 2 * D + (g + 1) * 128]
        outs = []
        for h in range(2):
            pick = low_half if h == 0 else jnp.logical_not(low_half)
            scores = mm_nt(jnp.where(pick, q_g, jnp.zeros_like(q_g)), k_g) * (1.0 / math.sqrt(HD))
            scores = jnp.where(same, scores, -1e30)
            top = jnp.max(scores, axis=1, keepdims=True)
            exps = jnp.exp(scores - top)
            probs = (exps / jnp.sum(exps, axis=1, keepdims=True)).astype(BF16)
            probs_ref[2 * g + h] = probs
            outs.append(mm(probs, v_g))
        mixed_ref[:, g * 128 : (g + 1) * 128] = jnp.where(low_half, outs[0], outs[1]).astype(BF16)

    keep(probs_ref, probs_hbm)
    keep(mixed_ref, mixed_hbm)
    for copy in copies[4:12]:
        copy.wait()
    for k, ref in enumerate((g1_ref, s1_ref, g2_ref, s2_ref)):
        affine_ref[k : k + 1, :] = ref[...].astype(F32)
    affine_ref[4:, :] = jnp.zeros((4, D), F32)
    keep(affine_ref, affine_hbm)
    attended = mm(mixed_ref[...], wout_ref[...]) + bout_ref[...].astype(F32)
    xhat, rstd = norm_rows(x.astype(F32) + attended)
    xh1_ref[...] = xhat
    rs1_ref[...] = jnp.broadcast_to(rstd, (ROW, 128))
    keep(xh1_ref, xh1_hbm)
    keep(rs1_ref, rs1_hbm)
    first = xhat * g1_ref[...].astype(F32) + s1_ref[...].astype(F32)
    first_low = first.astype(BF16)
    branch = bdown_ref[...].astype(F32) + first
    step = 512
    for copy in copies[12:]:
        copy.wait()
    for c in range(FF // step):
        cols = slice(c * step, (c + 1) * step)
        inner = mm(first_low, wup_ref[:, cols]) + bup_ref[:, cols].astype(F32)
        gate = 0.5 + 0.5 * lax.erf(inner * math.sqrt(0.5))
        bell = jnp.exp(inner * inner * -0.5) * (1.0 / math.sqrt(2.0 * math.pi))
        act = (inner * gate).astype(BF16)
        act_ref[:, cols] = act
        slope_ref[:, cols] = (gate + inner * bell).astype(BF16)
        keep(act_ref.at[:, cols], act_hbm.at[:, cols])
        keep(slope_ref.at[:, cols], slope_hbm.at[:, cols])
        branch = branch + mm(act, wdown_ref[cols, :])
    xhat, rstd = norm_rows(branch)
    xh2_ref[...] = xhat
    rs2_ref[...] = jnp.broadcast_to(rstd, (ROW, 128))
    keep(xh2_ref, xh2_hbm)
    keep(rs2_ref, rs2_hbm)
    second = xhat * g2_ref[...].astype(F32) + s2_ref[...].astype(F32)
    vec_ref[:ROW, :] = mm(second.astype(BF16), wproj_ref[...]).astype(BF16)
    line = iota((EXT, PROJ), 0)
    tag = jnp.zeros((EXT, PROJ), jnp.int32)
    for k in range(labels_ref.shape[0]):
        label = labels_ref[k]
        tag = jnp.where(line == k, label >> 6, tag)
        tag = jnp.where(line == k + 8, label & 63, tag)
    vec_ref[ROW:, :] = tag.astype(F32).astype(BF16)
    for copy in kept:
        copy.wait()


def prefix_norms(values, axis):
    place = iota(values.shape, axis)
    squared = values * values
    sums = [
        jnp.sum(jnp.where(place < cut, squared, 0.0), axis=axis, keepdims=True) for cut in RANGES
    ]
    return [lax.rsqrt(s + EPS_NORM) for s in sums]


def load_queries(near_ref, far_ref):
    span = ROW + EXT
    rows = []
    for ref in (near_ref, far_ref):
        for k in range(ref.shape[0] // span):
            rows.append(ref[k * span : k * span + ROW, :])
    return jnp.concatenate(rows, axis=0).astype(F32)


def unit_queries(queries, scale):
    lane = iota(queries.shape, 1)
    inverse = prefix_norms(queries, 1)
    unit = [
        jnp.where(lane < cut, queries * (inv * scale), 0.0) for cut, inv in zip(RANGES, inverse)
    ]
    return unit, inverse


def unit_docs(doc_refs, scratch_ref):
    at = 0
    for ref in doc_refs:
        for k in range(ref.shape[0] // ROW):
            scratch_ref[:, at * ROW : (at + 1) * ROW] = ref[
                k * ROW : (k + 1) * ROW, :
            ].astype(F32).T
            at += 1
    turned = scratch_ref[...]
    inverse = prefix_norms(turned, 0)
    place = iota(turned.shape, 0)
    unit = [jnp.where(place < cut, turned * inv, 0.0) for cut, inv in zip(RANGES, inverse)]
    return unit, inverse


def row_ids(base, masks, doc_rows):
    ids = []
    for p in range(doc_rows):
        offset = 0
        for k, mask in enumerate(masks):
            if (p >> k) & 1:
                offset ^= mask
        ids.append(base ^ offset)
    return ids


def doc_marks(lens_ref, ids, lanes, transposed):
    docs = len(ids) * DOCS_ROW
    shape = (lanes, ROW) if transposed else (ROW, lanes)
    spot, lane = (iota(shape, 1), iota(shape, 0)) if transposed else (iota(shape, 0), iota(shape, 1))
    marks = []
    for p, row in enumerate(ids):
        seg = segment_of(spot, bounds_of(lens_ref, row))
        local = jnp.where(seg < DOCS_ROW, seg + p * DOCS_ROW, -1 - lanes)
        marks.append(
            [(lane == local + m * docs).astype(F32).astype(BF16) for m in range(len(RANGES))]
        )
    return marks


def matching_stats(
    masks, lanes, where_ref, scale_ref, lens_ref, near_ref, far_ref, *refs
):
    doc_refs = refs[:-6]
    totals_ref, el_ref, hot_ref, stats_ref, turn_ref, unit_ref = refs[-6:]
    base, near_at = where_ref[2], where_ref[3]
    span = ROW + EXT
    queries = load_queries(near_ref, far_ref)
    count = queries.shape[0]
    unit_q, _ = unit_queries(queries, SHARPNESS * LOG2E)
    unit_q = [u.astype(BF16) for u in unit_q]
    unit_d, _ = unit_docs(doc_refs, turn_ref)
    for m in range(len(RANGES)):
        unit_ref[m] = unit_d[m].astype(BF16)
    doc_rows = turn_ref.shape[1] // ROW
    docs = doc_rows * DOCS_ROW
    ids = row_ids(base, masks, doc_rows)
    marks = doc_marks(lens_ref, ids, lanes, False)
    totals = jnp.zeros((count, lanes), F32)
    for p in range(doc_rows):
        for m in range(len(RANGES)):
            sims = mm(unit_q[m], unit_ref[m, :, p * ROW : (p + 1) * ROW])
            totals = totals + mm(jnp.exp2(sims).astype(BF16), marks[p][m])
    lane_t = iota((count, lanes), 1)
    totals = jnp.where(lane_t < len(RANGES) * docs, totals, 1.0)
    totals_ref[...] = totals
    shape = (8, lanes)
    lane = iota(shape, 1)
    length = jnp.ones(shape, jnp.int32)
    name = jnp.full(shape, -1, jnp.int32)
    for p in range(doc_rows):
        for k in range(DOCS_ROW):
            own = jnp.zeros(shape, jnp.bool_)
            for m in range(len(RANGES)):
                own = jnp.logical_or(own, lane == m * docs + p * DOCS_ROW + k)
            length = jnp.where(own, lens_ref[ids[p], k], length)
            name = jnp.where(own, ids[p] * DOCS_ROW + k, name)
    log_length = jnp.log(length.astype(F32))
    matched = (jnp.log(totals) - log_length[:1]) * (1.0 / SHARPNESS)
    per_query = jnp.sum(matched.reshape(count // QLEN, QLEN, lanes), axis=1)
    scale = jnp.exp(jnp.full(shape, scale_ref[0], F32))[:1]
    logits = per_query * (scale * (1.0 / QLEN))
    groups = count // ROW
    tags = []
    for ref in (near_ref, far_ref):
        for k in range(ref.shape[0] // span):
            high = ref[k * span + ROW : k * span + ROW + 8, :].astype(F32).astype(jnp.int32)
            low = ref[k * span + ROW + 8 : k * span + ROW + 16, :].astype(F32).astype(jnp.int32)
            tag = high * 64 + low
            tags.append(jnp.concatenate([tag] * (lanes // 128), axis=1))
    tag = jnp.concatenate(tags, axis=0)
    lane_q = iota(logits.shape, 1)
    valid = lane_q < len(RANGES) * docs
    el = jnp.where(valid, jnp.exp(logits), 0.0)
    hot = jnp.where(jnp.logical_and(valid, jnp.concatenate([name] * groups, axis=0) == tag), 1.0, 0.0)
    el_ref[...] = el
    hot_ref[...] = hot
    place = iota((groups * 8, 128), 1)
    stats = jnp.zeros((groups * 8, 128), F32)
    for k, values in enumerate((el, el * logits, hot * logits)):
        for m in range(len(RANGES)):
            inside = jnp.logical_and(lane_q >= m * docs, lane_q < (m + 1) * docs)
            one = jnp.sum(jnp.where(inside, values, 0.0), axis=1, keepdims=True)
            stats = jnp.where(place == k * 3 + m, one, stats)
    for a in range(groups):
        at = pl.multiple_of((near_at ^ a) * 8, 8)
        stats_ref[pl.ds(at, 8), :] = stats[a * 8 : (a + 1) * 8, :]


def matching_back(
    masks, lanes, total_queries, where_ref, scale_ref, lens_ref, near_ref, far_ref, totals_ref,
    el_ref, hot_ref, stats_ref, *refs
):
    doc_refs = refs[:-8]
    dq_ref, dd_ref, loss_ref, turn_ref, unit_ref, qt_ref, dot_ref, dt_ref = refs[-8:]
    base, near_at = where_ref[2], where_ref[3]
    temper = SHARPNESS * LOG2E
    queries = load_queries(near_ref, far_ref)
    count = queries.shape[0]
    unit_q, inv_q = unit_queries(queries, temper)
    unit_q = [u.astype(BF16) for u in unit_q]
    unit_d, inv_d = unit_docs(doc_refs, turn_ref)
    for m in range(len(RANGES)):
        unit_ref[m] = unit_d[m].astype(BF16)
        qt_ref[m] = unit_q[m].astype(F32).T.astype(BF16)
    doc_rows = turn_ref.shape[1] // ROW
    docs = doc_rows * DOCS_ROW
    ids = row_ids(base, masks, doc_rows)
    marks = doc_marks(lens_ref, ids, lanes, True)
    groups = count // ROW
    rows = []
    for a in range(groups):
        at = pl.multiple_of((near_at ^ a) * 8, 8)
        rows.append(stats_ref[pl.ds(at, 8), :])
    stats = jnp.concatenate(rows, axis=0)
    place = iota(stats.shape, 1)

    def column(k):
        return jnp.sum(jnp.where(place == k, stats, 0.0), axis=1, keepdims=True)

    shape = (groups * 8, lanes)
    lane_q = iota(shape, 1)
    sums = jnp.ones(shape, F32)
    loss = jnp.zeros((groups * 8, 1), F32)
    moved = jnp.zeros((groups * 8, 1), F32)
    for m in range(len(RANGES)):
        whole, weighted, picked = column(m), column(3 + m), column(6 + m)
        inside = jnp.logical_and(lane_q >= m * docs, lane_q < (m + 1) * docs)
        sums = jnp.where(inside, whole, sums)
        loss = loss + (jnp.log(whole) - picked)
        moved = moved + (weighted / whole - picked)
    line = iota((8, 128), 0)
    loss_ref[...] = jnp.where(
        line == 0,
        jnp.sum(loss, axis=0, keepdims=True) * (1.0 / total_queries),
        jnp.where(line == 1, jnp.sum(moved, axis=0, keepdims=True) * (1.0 / total_queries), 0.0),
    )
    scale = jnp.exp(jnp.full((8, lanes), scale_ref[0], F32))[:1]
    coeff = (el_ref[...] / sums - hot_ref[...]) * (scale * (1.0 / (QLEN * total_queries)))
    coeff = jnp.broadcast_to(coeff[:, None, :], (groups * 8, QLEN, lanes)).reshape(count, lanes)
    ratio = coeff / totals_ref[...]
    ratio_high = ratio.astype(BF16)
    ratio_low = (ratio - ratio_high.astype(F32)).astype(BF16)
    ratio = jnp.concatenate([ratio_high, ratio_low], axis=1)
    for m in range(len(RANGES)):
        grad = jnp.zeros((count, PROJ), F32)
        for p in range(doc_rows):
            block = unit_ref[m, :, p * ROW : (p + 1) * ROW]
            mark = marks[p][m]
            exps = jnp.exp2(mm(unit_q[m], block))
            d_sims = (exps * mm(ratio, jnp.concatenate([mark, mark], axis=0))).astype(BF16)
            grad = grad + mm_nt(d_sims, block)
            dt_ref[m, :, p * ROW : (p + 1) * ROW] = mm(qt_ref[m], d_sims)
        unit = unit_q[m].astype(F32) * (1.0 / temper)
        along = jnp.sum(grad * unit, axis=1, keepdims=True)
        part = inv_q[m] * (grad - unit * along)
        if m == 0:
            dot_ref[...] = part
        else:
            dot_ref[...] += part
    dq_ref[...] = dot_ref[...].astype(BF16)
    total = jnp.zeros(turn_ref.shape, F32)
    for m in range(len(RANGES)):
        grad = dt_ref[m] * (1.0 / temper)
        unit = unit_ref[m].astype(F32)
        along = jnp.sum(grad * unit, axis=0, keepdims=True)
        total = total + inv_d[m] * (grad - unit * along)
    for p in range(doc_rows):
        dd_ref[p * ROW : (p + 1) * ROW, :] = total[:, p * ROW : (p + 1) * ROW].T.astype(BF16)


def store_block(refs, block, places, value):
    keep_ref, send_ref = refs
    core, near_place, far_place = places
    half = keep_ref.shape[0]
    mine = core == block // half

    @pl.when(mine)
    def _():
        keep_ref[(block % half) ^ near_place] = value

    @pl.when(jnp.logical_not(mine))
    def _():
        send_ref[(block % half) ^ far_place] = value


def feed_back(
    where_ref, dq_ref, dd_ref, got_ref, xh2_ref, rs2_ref, affine_ref, wproj_ref, wdown_ref,
    slope_ref, act_ref, wup_ref, xh1_ref,
    down_keep, down_send, up_keep, up_send, dfirst_ref, gproj_ref, small_ref, dinner_ref,
):
    g1, s1, g2, s2 = [affine_ref[k : k + 1, :] for k in range(4)]
    is_query, docs_there = where_ref[1] == 0, where_ref[4] == 0
    places = (where_ref[5], where_ref[6], where_ref[7])
    got = got_ref[...].astype(F32)
    d_vec = jnp.where(
        is_query,
        dq_ref[...].astype(F32) + got,
        jnp.where(docs_there, got, dd_ref[...].astype(F32)),
    )
    d_proj = d_vec.astype(BF16)
    xhat = xh2_ref[...]
    gain = g2
    second = (xhat * gain + s2).astype(BF16)
    gproj_ref[...] = mm_tn(second, d_proj)
    d_second = mm_nt(d_proj, wproj_ref[...])
    small_ref[...] = jnp.zeros_like(small_ref)
    small_ref[5:6, :] = col_sum(d_second * xhat)
    small_ref[6:7, :] = col_sum(d_second)
    d_sum = norm_back(d_second, xhat, rs2_ref[:, :1], gain)
    d_branch = d_sum.astype(BF16)
    small_ref[4:5, :] = col_sum(d_branch.astype(F32))
    step = 512
    blocks = 2 * down_keep.shape[0]
    size = down_keep.shape[1]
    d_first = d_sum
    for c in range(FF // step):
        cols = slice(c * step, (c + 1) * step)
        d_act = mm_nt(d_branch, wdown_ref[cols, :])
        d_inner = (d_act * slope_ref[:, cols].astype(F32)).astype(BF16)
        dinner_ref[:, cols] = d_inner
        small_ref[c : c + 1, :] = col_sum(d_inner.astype(F32))
        grad = mm_tn(act_ref[:, cols], d_branch).astype(BF16)
        for k in range(step // size):
            store_block(
                (down_keep, down_send),
                c * (step // size) + k,
                places,
                grad[k * size : (k + 1) * size, :],
            )
        d_first = d_first + mm_nt(d_inner, wup_ref[:, cols])
    dfirst_ref[...] = d_first
    first = (xh1_ref[...] * g1 + s1).astype(BF16)
    for c in range(FF // step):
        cols = slice(c * step, (c + 1) * step)
        grad = mm_tn(first, dinner_ref[:, cols]).astype(BF16)
        for k in range(D // size):
            store_block(
                (up_keep, up_send),
                c * (D // size) + k,
                places,
                grad[k * size : (k + 1) * size, :],
            )


def attend_back(
    where_ref, dfirst_ref, gproj_ref, small_ref, xh1_ref, rs1_ref, affine_ref, mixed_ref, wout_ref,
    qkv_ref, probs_ref, rope_ref, x_ref, wqkv_ref,
    keep_one, send_one, keep_two, send_two, tokens_ref, djoined_ref, rest_ref,
):
    core, near_place, far_place = where_ref[5], where_ref[6], where_ref[7]
    d_first = dfirst_ref[...]
    xhat = xh1_ref[...]
    gain = affine_ref[0:1, :]
    gain_grad = col_sum(d_first * xhat)
    shift_grad = col_sum(d_first)
    d_sum = norm_back(d_first, xhat, rs1_ref[:, :1], gain)
    d_att = d_sum.astype(BF16)
    bias_out = col_sum(d_att.astype(F32))
    rest_ref[3 * D : 4 * D, :] = mm_tn(mixed_ref[...], d_att)
    d_mixed = mm_nt(d_att, wout_ref[...]).astype(BF16)
    cosine, sine = rope_ref[:, :128], rope_ref[:, 128:]
    low_half = iota((ROW, 128), 1) < HD

    def unrotate(values):
        values = values * (1.0 / math.sqrt(HD))
        return (values * cosine - swap_halves(values) * sine).astype(BF16)

    for g in range(HEADS // 2):
        span = slice(g * 128, (g + 1) * 128)
        q_g = qkv_ref[:, g * 128 : (g + 1) * 128]
        k_g = qkv_ref[:, D + g * 128 : D + (g + 1) * 128]
        v_g = qkv_ref[:, 2 * D + g * 128 : 2 * D + (g + 1) * 128]
        m_g = d_mixed[:, span]
        d_q = jnp.zeros((ROW, 128), F32)
        d_k = jnp.zeros((ROW, 128), F32)
        d_v = jnp.zeros((ROW, 128), F32)
        zero = jnp.zeros((ROW, 128), BF16)
        for h in range(2):
            pick = low_half if h == 0 else jnp.logical_not(low_half)
            probs_low = probs_ref[2 * g + h]
            probs = probs_low.astype(F32)
            m_h = jnp.where(pick, m_g, zero)
            d_probs = mm_nt(m_h, v_g)
            d_v = d_v + mm_tn(probs_low, m_h)
            inner = jnp.sum(d_probs * probs, axis=1, keepdims=True)
            d_scores = (probs * (d_probs - inner)).astype(BF16)
            d_q = d_q + mm(d_scores, jnp.where(pick, k_g, zero))
            d_k = d_k + mm_tn(d_scores, jnp.where(pick, q_g, zero))
        djoined_ref[:, g * 128 : (g + 1) * 128] = unrotate(d_q)
        djoined_ref[:, D + g * 128 : D + (g + 1) * 128] = unrotate(d_k)
        djoined_ref[:, 2 * D + g * 128 : 2 * D + (g + 1) * 128] = d_v.astype(BF16)
    x = x_ref[...]
    tokens = d_sum
    rest_ref[4 * D + 128 :, :] = jnp.zeros((REST - 4 * D - 128, D), F32)
    smalls = []
    for c in range(3):
        cols = slice(c * D, (c + 1) * D)
        d_part = djoined_ref[:, cols]
        rest_ref[c * D : (c + 1) * D, :] = mm_tn(x, d_part)
        smalls.append(col_sum(d_part.astype(F32)))
        tokens = tokens + mm_nt(d_part, wqkv_ref[:, cols])
    tokens_ref[...] = tokens
    for k in range(4):
        rest_ref[4 * D : 4 * D + 128, k * 128 : (k + 1) * 128] = gproj_ref[
            k * 128 : (k + 1) * 128, :
        ]
    smalls += [bias_out, gain_grad, shift_grad] + [small_ref[k : k + 1, :] for k in range(7)]
    smalls += [jnp.zeros((EXT - len(smalls), D), F32)]
    rest_ref[4 * D + 128 : 4 * D + 128 + EXT, :] = jnp.concatenate(smalls, axis=0)
    first = 0
    for keep_ref, send_ref in ((keep_one, send_one), (keep_two, send_two)):
        half, size = keep_ref.shape[0], keep_ref.shape[1]
        for p in range(half):
            for ref, owner, place in ((keep_ref, core, near_place), (send_ref, 1 - core, far_place)):
                block = owner * half + (p ^ place)
                start = pl.multiple_of(first + block * size, 8)
                ref[p] = rest_ref[pl.ds(start, size), :].astype(BF16)
        first += 2 * half * size


def spread_out(columns, where_ref, near_ref, far_ref, out_ref):
    core, near_place, far_place = where_ref[5], where_ref[6], where_ref[7]
    half, size, width = near_ref.shape
    per_column = 2 * half // columns
    for p in range(half):
        for ref, owner, place in ((near_ref, core, near_place), (far_ref, 1 - core, far_place)):
            block = owner * half + (p ^ place)
            start = pl.multiple_of((block % per_column) * size, 8)
            left = pl.multiple_of((block // per_column) * width, 128)
            out_ref[pl.ds(start, size), pl.ds(left, width)] = ref[p].astype(F32)


def spread_rest(
    where_ref, near_one, far_one, near_two, far_two, qkv_ref, out_ref, proj_ref, bqkv_ref, bout_ref,
    g1_ref, s1_ref, bup_ref, bdown_ref, g2_ref, s2_ref, rest_ref,
):
    core, near_place, far_place = where_ref[5], where_ref[6], where_ref[7]
    first = 0
    for near_ref, far_ref in ((near_one, far_one), (near_two, far_two)):
        half, size = near_ref.shape[0], near_ref.shape[1]
        for p in range(half):
            for ref, owner, place in ((near_ref, core, near_place), (far_ref, 1 - core, far_place)):
                block = owner * half + (p ^ place)
                start = pl.multiple_of(first + block * size, 8)
                rest_ref[pl.ds(start, size), :] = ref[p].astype(F32)
        first += 2 * half * size
    for c in range(3):
        qkv_ref[:, c * D : (c + 1) * D] = rest_ref[c * D : (c + 1) * D, :]
    out_ref[...] = rest_ref[3 * D : 4 * D, :]
    for k in range(4):
        proj_ref[k * 128 : (k + 1) * 128, :] = rest_ref[
            4 * D : 4 * D + 128, k * 128 : (k + 1) * 128
        ]
    small = rest_ref[4 * D + 128 : 4 * D + 128 + EXT, :]
    row = [small[k : k + 1, :] for k in range(13)]
    for c in range(3):
        bqkv_ref[:, c * D : (c + 1) * D] = row[c]
    bout_ref[...] = row[3]
    g1_ref[...] = row[4]
    s1_ref[...] = row[5]
    for c in range(4):
        bup_ref[:, c * D : (c + 1) * D] = row[6 + c]
    bdown_ref[...] = row[10]
    g2_ref[...] = row[11]
    s2_ref[...] = row[12]


def shape_of(shape, dtype=F32):
    return jax.ShapeDtypeStruct(tuple(shape), dtype)


def call(kernel, args, specs, outs, scratch=(), room=24, out_specs=None):
    spaces = {id(HBM): pltpu.HBM, id(HELD): pltpu.VMEM}
    args = [
        pltpu.with_memory_space_constraint(arg, spaces[id(spec)]) if id(spec) in spaces else arg
        for arg, spec in zip(args, specs)
    ]
    return pl.pallas_call(
        kernel,
        out_shape=outs,
        in_specs=specs,
        out_specs=out_specs or [VMEM] * len(outs),
        scratch_shapes=list(scratch),
        compiler_params=pltpu.CompilerParams(vmem_limit_bytes=room * MIB),
        cost_estimate=pl.CostEstimate(flops=10**9, bytes_accessed=10**7, transcendentals=0),
    )(*args)


def spread_call(kind, where, halves):
    if kind < 2:
        columns = (1, 4)[kind]
        kernel, outs, scratch = (
            partial(spread_out, columns), [shape_of((FF // columns, D * columns))], []
        )
    else:
        kernel, scratch = spread_rest, [pltpu.VMEM((REST, D), F32)]
        outs = [
            shape_of((D, 3 * D)), shape_of((D, D)), shape_of((D, PROJ)), shape_of((1, 3 * D)),
            shape_of((1, D)), shape_of((1, D)), shape_of((1, D)), shape_of((1, FF)),
            shape_of((1, D)), shape_of((1, D)), shape_of((1, D)),
        ]
    return call(kernel, (where, *halves), [SMEM] + [VMEM] * len(halves), outs, scratch)


def swapped(value, mask, axis="dp"):
    size = lax.axis_size(axis)
    return lax.ppermute(value, axis, [(k, k ^ mask) for k in range(size)])


def added(a, b):
    return (a.astype(F32) + b.astype(F32)).astype(BF16)


def block_place(me, order):
    place = jnp.int32(0)
    for k, mask in enumerate(order):
        place = place | jnp.where((me & mask) != 0, 1 << (len(order) - 1 - k), 0)
    return place


def swapped_by_core(value, masks):
    size = lax.axis_size("dp")
    return lax.ppermute(value, "dp", [(k, k ^ masks[k & 1]) for k in range(size)])


class Summed:
    def __init__(self, keep, send, masks, others):
        self.keep, self.masks, self.others, self.at = keep, masks, others, 0
        self.got = swapped_by_core(send, masks[0])

    def step(self, after):
        keep, got = self.keep, self.got
        if after is not None:
            keep, got, _ = lax.optimization_barrier((keep, got, after))
        self.at += 1
        last = len(self.masks)
        if self.at < last:
            half = keep.shape[0] // 2
            send = added(keep[half:], got[half:])
            self.keep = added(keep[:half], got[:half])
            self.got = swapped_by_core(send, self.masks[self.at])
            return send
        if self.at == last:
            keep = added(keep, got)
            for mask in self.others:
                keep = added(keep, swapped(keep, mask))
        elif self.at < 2 * last:
            keep = jnp.concatenate([keep, got], axis=0)
        else:
            self.keep, self.got = keep, got
            return got
        self.keep = keep
        self.got = swapped_by_core(keep, self.masks[2 * last - 1 - self.at])
        return keep


class Doubled:
    def __init__(self, value, masks):
        self.value, self.masks, self.got = value, list(masks), None

    def step(self, after):
        value, got = self.value, self.got
        if after is not None:
            value, _ = lax.optimization_barrier((value, after))
        if got is not None:
            value = value + got
        self.value, self.got = value, None
        if self.masks:
            self.got = swapped(value, self.masks.pop(0))
        return value


def per_device(
    tokens, qkv_weight, qkv_bias, out_weight, out_bias, first_gain, first_shift, up_weight,
    up_bias, down_weight, down_bias, second_gain, second_shift, proj_weight, log_scale,
    doc_lengths, labels,
):
    size = lax.axis_size("dp")
    bits = [1 << k for k in range(size.bit_length() - 1)]
    near_masks, doc_masks = bits[:2], bits[2:]
    top_mask, doc_masks = doc_masks[-1], doc_masks[:-1]
    masks = [(bits[0], bits[0]), (bits[1], bits[2]), (bits[2], bits[1]), (bits[3], bits[3])]
    others = bits[4:]
    blocks = 16
    me = lax.axis_index("dp")
    stream = lax.axis_index("stream")
    is_query = stream == 0
    has_top = (me & top_mask) != 0
    base = jnp.where(is_query, me & ~top_mask, me | top_mask)
    near_at = jnp.where((me & near_masks[1]) != 0, 1, 0) + jnp.where((me & near_masks[0]) != 0, 2, 0)
    core = me & 1
    places = [block_place(me, [pair[k] for pair in masks[1:]]) for k in range(2)]
    where = jnp.stack(
        [me, stream, base, near_at, has_top.astype(jnp.int32), core]
        + [jnp.where(core == 0, *places), jnp.where(core == 0, *places[::-1])]
    ).astype(jnp.int32)
    scale = log_scale.reshape(1)

    vec, qkv, rope, probs, mixed, xh1, rs1, act, slope, xh2, rs2, affine = call(
        encoder_forward,
        (
            where, doc_lengths, labels, jnp.asarray(rope_table()), tokens[0], qkv_weight[0], qkv_bias,
            out_weight[0], out_bias, first_gain, first_shift, up_weight[0], up_bias,
            down_weight[0], down_bias, second_gain, second_shift, proj_weight[0],
        ),
        [SMEM] * 3 + [HBM] * 15,
        [shape_of((ROW + EXT, PROJ), BF16)] + [pltpu.HBM(*kind) for kind in KEPT],
        [pltpu.VMEM(*kind) for kind in KEPT]
        + [pltpu.SemaphoreType.DMA((len(KEPT) + 6,))]
        + [
            pltpu.VMEM(shape, BF16)
            for shape in (
                (ROW, 512), (ROW, D), (D, 3 * D), (1, 3 * D), (D, D), (1, D), (1, D), (1, D), (D, FF),
                (1, FF), (FF, D), (1, D), (1, D), (1, D), (D, PROJ),
            )
        ]
        + [pltpu.SemaphoreType.DMA((15,))],
        room=40,
        out_specs=[VMEM] + [HBM] * len(KEPT),
    )

    other = swapped(vec, 1, "stream")
    near = jnp.where(is_query, vec, other)
    rows = jnp.where(is_query, other, vec)[:ROW]
    moved = swapped(rows, top_mask)
    near = jnp.concatenate([near, swapped(near, near_masks[1])], axis=0)
    rows = jnp.where(has_top == is_query, moved, rows)
    far = swapped(near, near_masks[0])
    pieces = []
    for k, mask in enumerate(doc_masks):
        pieces.append(rows)
        got = swapped(rows, mask)
        if k + 1 < len(doc_masks):
            rows = jnp.concatenate([rows, got], axis=0)
        else:
            pieces = [rows, got]
    doc_rows = sum(p.shape[0] for p in pieces) // ROW
    tokens_d = doc_rows * ROW
    tokens_q = 4 * ROW
    lanes = -(-3 * doc_rows * DOCS_ROW // 128) * 128
    total_queries = size * (ROW // QLEN)
    room = 20 if doc_rows <= 4 else 56
    totals, el, hot, stats = call(
        partial(matching_stats, doc_masks, lanes),
        (where, scale, doc_lengths, near, far, *pieces),
        [SMEM] * 3 + [VMEM] * (2 + len(pieces)),
        [
            shape_of((tokens_q, lanes)),
            shape_of((tokens_q // QLEN, lanes)),
            shape_of((tokens_q // QLEN, lanes)),
            shape_of((tokens_q // QLEN, 128)),
        ],
        [pltpu.VMEM((PROJ, tokens_d), F32), pltpu.VMEM((3, PROJ, tokens_d), BF16)],
        room=room,
    )
    stats = stats + swapped(stats, near_masks[0])
    stats = stats + swapped(stats, near_masks[1])
    stats = stats + swapped(stats, 1, "stream")
    dq, dd, loss = call(
        partial(matching_back, doc_masks, lanes, total_queries),
        (where, scale, doc_lengths, near, far, totals, el, hot, stats, *pieces),
        [SMEM] * 3 + [VMEM] * (6 + len(pieces)),
        [shape_of((tokens_q, PROJ), BF16), shape_of((tokens_d, PROJ), BF16), shape_of((8, 128))],
        [
            pltpu.VMEM((PROJ, tokens_d), F32),
            pltpu.VMEM((3, PROJ, tokens_d), BF16),
            pltpu.VMEM((3, PROJ, tokens_q), BF16),
            pltpu.VMEM((tokens_q, PROJ), F32),
            pltpu.VMEM((3, PROJ, tokens_d), F32),
        ],
        room=room,
    )
    for mask in reversed(doc_masks):
        half = dd.shape[0] // 2
        dd = added(dd[:half], swapped(dd[half:], mask))
    for mask in near_masks:
        half = dq.shape[0] // 2
        dq = added(dq[:half], swapped(dq[half:], mask))
    dd = added(dd, swapped(dd, top_mask))
    got = swapped(jnp.where(is_query, dd, dq), 1, "stream")

    down_keep, down_send, up_keep, up_send, d_first, gproj, small = call(
        feed_back,
        (
            where, dq, dd, got, xh2, rs2, affine, proj_weight[0], down_weight[0], slope, act,
            up_weight[0], xh1,
        ),
        [SMEM] + [VMEM] * 3 + [HELD] * 9,
        [shape_of((blocks // 2, FF // blocks, D), BF16)] * 4
        + [shape_of((ROW, D)), shape_of((D, PROJ)), shape_of((8, D))],
        [
            pltpu.VMEM((ROW, FF), BF16),
        ],
    )
    keep_one, send_one, keep_two, send_two, tokens_grad = call(
        attend_back,
        (
            where, d_first, gproj, small, xh1, rs1, affine, mixed, out_weight[0], qkv, probs, rope,
            tokens[0], qkv_weight[0],
        ),
        [SMEM] + [VMEM] * 3 + [HELD] * 10,
        [shape_of((blocks // 2, 3 * D // blocks, D), BF16)] * 2
        + [shape_of((blocks // 2, (REST - 3 * D) // blocks, D), BF16)] * 2
        + [shape_of((ROW, D))],
        [
            pltpu.VMEM((ROW, 3 * D), BF16),
            pltpu.VMEM((REST, D), F32),
        ],
    )
    pieces = [
        Summed(keep, send, masks, others)
        for keep, send in (
            (down_keep, down_send), (up_keep, up_send), (keep_one, send_one), (keep_two, send_two)
        )
    ] + [Doubled(loss, doc_masks + [top_mask])]
    token, spread = None, {}
    for k in ORDER:
        if k >= 10:
            ready = [pieces[j] for j in FINAL[k - 10]]
            halves = [half for piece in ready for half in (piece.keep, piece.got)]
            *halves, _ = lax.optimization_barrier((*halves, token))
            spread[k - 10] = spread_call(k - 10, where, halves)
            token = spread[k - 10][0]
        else:
            token = pieces[k].step(token)
    grad_down, grad_up = spread[0][0], spread[1][0]
    (
        grad_qkv, grad_out, grad_proj, grad_bqkv, grad_bout, grad_g1, grad_s1, grad_bup,
        grad_bdown, grad_g2, grad_s2,
    ) = spread[2]
    while pieces[-1].got is not None:
        pieces[-1].step(None)
    loss = pieces[-1].value
    return (
        loss[0, 0],
        tokens_grad[None],
        grad_qkv[None],
        grad_bqkv,
        grad_out[None],
        grad_bout,
        grad_g1,
        grad_s1,
        grad_up[None],
        grad_bup,
        grad_down[None],
        grad_bdown,
        grad_g2,
        grad_s2,
        grad_proj[None],
        loss[1, 0],
    )


def solution(mesh):
    return jax.shard_map(
        per_device,
        mesh=mesh,
        in_specs=(
            P("stream", "dp", None),
            P("stream", None, None),
            P("stream", None),
            P("stream", None, None),
            P("stream", None),
            P("stream", None),
            P("stream", None),
            P("stream", None, None),
            P("stream", None),
            P("stream", None, None),
            P("stream", None),
            P("stream", None),
            P("stream", None),
            P("stream", None, None),
            P(),
            P(),
            P("dp"),
        ),
        out_specs=(
            P(),
            P("stream", "dp", None),
            P("stream", None, None),
            P("stream", None),
            P("stream", None, None),
            P("stream", None),
            P("stream", None),
            P("stream", None),
            P("stream", None, None),
            P("stream", None),
            P("stream", None, None),
            P("stream", None),
            P("stream", None),
            P("stream", None),
            P("stream", None, None),
            P(),
        ),
        check_vma=False,
    )
```

```python
from functools import partial
import math

import jax
import jax.numpy as jnp
import numpy as np
from jax import lax
from jax.experimental import pallas as pl
from jax.experimental.pallas import tpu as pltpu
from jax.sharding import PartitionSpec as P

D = 512
HEADS = 8
HD = 64
FF = 2048
PROJ = 128
QLEN = 32
DOCS_ROW = 4
ROW = 256
EXT = 16
RANGES = (64, 96, 128)

SHARPNESS = 8.0
EPS_NORM = 1e-06
EPS_LAYER = 1e-05
LOG2E = 1.4426950408889634

F32 = jnp.float32
BF16 = jnp.bfloat16
REST = 2304
SHARE = 32
DOWN = FF // 16
HEAD = 80
TAIL = DOWN - HEAD
FIRST = DOWN + HEAD
SECOND = REST // 16 + TAIL
CIRCLE = (0, 2, 4, 6, 7, 5, 3, 1)
RING = len(CIRCLE)
GROUPS = ((0, 1, 2, 6, 7), (3, 4, 5))
STEP_COST = 3 * 10**7
ROUND = (("step", 0), ("step", 1))
ORDER = (
    (("open", 0), ("open", 1), ("total", 0), ("total", 1)) + ROUND * 6
    + (("share0", 0), ("share0", 1), ("near", 0)) + ROUND + (("far", 0),) + ROUND
    + (("share1", 0), ("share1", 1), ("near", 1), ("far", 1))
)
MIB = 1024 * 1024

VMEM = pl.BlockSpec(memory_space=pltpu.VMEM)
SMEM = pl.BlockSpec(memory_space=pltpu.SMEM)
HBM = pl.BlockSpec(memory_space=pltpu.HBM)
HELD = pl.BlockSpec(memory_space=pltpu.VMEM)


def mm(a, b):
    return lax.dot_general(a, b, (((1,), (0,)), ((), ())), preferred_element_type=F32)


def mm_nt(a, b):
    return lax.dot_general(a, b, (((1,), (1,)), ((), ())), preferred_element_type=F32)


def mm_tn(a, b):
    return lax.dot_general(a, b, (((0,), (0,)), ((), ())), preferred_element_type=F32)


def iota(shape, axis):
    return lax.broadcasted_iota(jnp.int32, shape, axis)


def rope_table():
    half = HD // 2
    freqs = (10000.0 ** (-np.arange(half, dtype=np.float32) / np.float32(half))).astype(np.float32)
    turned = np.arange(ROW, dtype=np.float32)[:, None] * freqs[None, :]
    cosine = np.cos(turned.astype(np.float64))
    sine = np.sin(turned.astype(np.float64))
    cosine = np.concatenate([cosine, cosine, cosine, cosine], axis=1).astype(np.float32)
    sine = np.concatenate([-sine, sine, -sine, sine], axis=1).astype(np.float32)
    parts = []
    for table in (cosine, sine):
        high = table.astype(jnp.bfloat16)
        low = (table - high.astype(np.float32)).astype(jnp.bfloat16)
        parts += [high, low]
    return np.concatenate(parts, axis=1)


def swap_halves(block):
    lane = iota(block.shape, 1)
    return jnp.where(lane % HD < HD // 2, pltpu.roll(block, 96, 1), pltpu.roll(block, 32, 1))


def bounds_of(lens_ref, row):
    ends, total = [], jnp.int32(0)
    for k in range(DOCS_ROW):
        total = total + lens_ref[row, k]
        ends.append(total)
    return ends


def segment_of(spot, ends):
    seg = jnp.zeros_like(spot)
    for end in ends:
        seg = seg + (spot >= end).astype(jnp.int32)
    return seg


def norm_rows(values):
    mean = jnp.mean(values, axis=1, keepdims=True)
    centred = values - mean
    spread = jnp.mean(centred * centred, axis=1, keepdims=True)
    rstd = lax.rsqrt(spread + EPS_LAYER)
    return centred * rstd, rstd


def norm_back(d_out, xhat, rstd, gain):
    scaled = d_out * gain
    first = jnp.mean(scaled, axis=1, keepdims=True)
    second = jnp.mean(scaled * xhat, axis=1, keepdims=True)
    return rstd * (scaled - first - xhat * second)


def col_sum(values):
    return jnp.sum(values, axis=0, keepdims=True)


def fetch(pairs, sems):
    copies = [pltpu.make_async_copy(src, dst, sems.at[k]) for k, (src, dst) in enumerate(pairs)]
    for copy in copies:
        copy.start()
    return copies


KEPT = (
    ((ROW, 3 * D), BF16),
    ((ROW, 256), F32),
    ((HEADS, ROW, ROW), BF16),
    ((ROW, D), BF16),
    ((ROW, D), F32),
    ((ROW, 128), F32),
    ((ROW, FF), BF16),
    ((ROW, FF), BF16),
    ((ROW, D), F32),
    ((ROW, 128), F32),
    ((8, D), F32),
)


def encoder_forward(
    where_ref, lens_ref, labels_ref, table_hbm, x_hbm, wqkv_hbm, bqkv_hbm, wout_hbm, bout_hbm,
    g1_hbm, s1_hbm, wup_hbm, bup_hbm, wdown_hbm, bdown_hbm, g2_hbm, s2_hbm, wproj_hbm,
    vec_ref, qkv_hbm, rope_hbm, probs_hbm, mixed_hbm, xh1_hbm, rs1_hbm, act_hbm, slope_hbm,
    xh2_hbm, rs2_hbm, affine_hbm,
    qkv_ref, rope_ref, probs_ref, mixed_ref, xh1_ref, rs1_ref, act_ref, slope_ref,
    xh2_ref, rs2_ref, affine_ref, out_sems,
    table_ref, x_ref, wqkv_ref, bqkv_ref, wout_ref, bout_ref, g1_ref, s1_ref, wup_ref, bup_ref,
    wdown_ref, bdown_ref, g2_ref, s2_ref, wproj_ref, sems,
):
    copies = fetch(
        (
            (table_hbm, table_ref), (x_hbm, x_ref), (wqkv_hbm, wqkv_ref), (bqkv_hbm, bqkv_ref),
            (wout_hbm, wout_ref), (bout_hbm, bout_ref), (g1_hbm, g1_ref), (s1_hbm, s1_ref),
            (bup_hbm, bup_ref), (bdown_hbm, bdown_ref), (g2_hbm, g2_ref), (s2_hbm, s2_ref),
            (wup_hbm, wup_ref), (wdown_hbm, wdown_ref), (wproj_hbm, wproj_ref),
        ),
        sems,
    )
    kept = []

    def keep(src, dst):
        copy = pltpu.make_async_copy(src, dst, out_sems.at[len(kept)])
        copy.start()
        kept.append(copy)

    me, is_query = where_ref[0], where_ref[1] == 0
    ends = bounds_of(lens_ref, me)

    def layout(spot):
        seg_doc = segment_of(spot, ends)
        start_doc = jnp.zeros_like(spot)
        for k in range(DOCS_ROW):
            start_doc = jnp.where(seg_doc == k + 1, ends[k], start_doc)
        seg_query = spot // QLEN
        seg = jnp.where(is_query, seg_query, seg_doc)
        start = jnp.where(is_query, seg_query * QLEN, start_doc)
        return seg, start

    shape = (ROW, ROW)
    seg_q, start_q = layout(iota(shape, 0))
    seg_k, _ = layout(iota(shape, 1))
    same = seg_q == seg_k
    onehot = (iota(shape, 1) == iota(shape, 0) - start_q).astype(F32).astype(BF16)
    for copy in copies[:4]:
        copy.wait()
    turned = mm(onehot, table_ref[...])
    cosine = turned[:, :128] + turned[:, 128:256]
    sine = turned[:, 256:384] + turned[:, 384:]
    rope_ref[:, :128] = cosine
    rope_ref[:, 128:] = sine
    keep(rope_ref, rope_hbm)

    x = x_ref[...]
    joined = mm(x, wqkv_ref[...]) + bqkv_ref[...].astype(F32)
    for g in range(2 * D // 128):
        block = joined[:, g * 128 : (g + 1) * 128]
        qkv_ref[:, g * 128 : (g + 1) * 128] = (
            block * cosine + swap_halves(block) * sine
        ).astype(BF16)
    qkv_ref[:, 2 * D :] = joined[:, 2 * D :].astype(BF16)
    keep(qkv_ref, qkv_hbm)

    low_half = iota((ROW, 128), 1) < HD
    for g in range(HEADS // 2):
        q_g = qkv_ref[:, g * 128 : (g + 1) * 128]
        k_g = qkv_ref[:, D + g * 128 : D + (g + 1) * 128]
        v_g = qkv_ref[:, 2 * D + g * 128 : 2 * D + (g + 1) * 128]
        outs = []
        for h in range(2):
            pick = low_half if h == 0 else jnp.logical_not(low_half)
            scores = mm_nt(jnp.where(pick, q_g, jnp.zeros_like(q_g)), k_g) * (1.0 / math.sqrt(HD))
            scores = jnp.where(same, scores, -1e30)
            top = jnp.max(scores, axis=1, keepdims=True)
            exps = jnp.exp(scores - top)
            probs = (exps / jnp.sum(exps, axis=1, keepdims=True)).astype(BF16)
            probs_ref[2 * g + h] = probs
            outs.append(mm(probs, v_g))
        mixed_ref[:, g * 128 : (g + 1) * 128] = jnp.where(low_half, outs[0], outs[1]).astype(BF16)

    keep(probs_ref, probs_hbm)
    keep(mixed_ref, mixed_hbm)
    for copy in copies[4:12]:
        copy.wait()
    for k, ref in enumerate((g1_ref, s1_ref, g2_ref, s2_ref)):
        affine_ref[k : k + 1, :] = ref[...].astype(F32)
    affine_ref[4:, :] = jnp.zeros((4, D), F32)
    keep(affine_ref, affine_hbm)
    attended = mm(mixed_ref[...], wout_ref[...]) + bout_ref[...].astype(F32)
    xhat, rstd = norm_rows(x.astype(F32) + attended)
    xh1_ref[...] = xhat
    rs1_ref[...] = jnp.broadcast_to(rstd, (ROW, 128))
    keep(xh1_ref, xh1_hbm)
    keep(rs1_ref, rs1_hbm)
    first = xhat * g1_ref[...].astype(F32) + s1_ref[...].astype(F32)
    first_low = first.astype(BF16)
    branch = bdown_ref[...].astype(F32) + first
    step = 512
    for copy in copies[12:]:
        copy.wait()
    for c in range(FF // step):
        cols = slice(c * step, (c + 1) * step)
        inner = mm(first_low, wup_ref[:, cols]) + bup_ref[:, cols].astype(F32)
        gate = 0.5 + 0.5 * lax.erf(inner * math.sqrt(0.5))
        bell = jnp.exp(inner * inner * -0.5) * (1.0 / math.sqrt(2.0 * math.pi))
        act = (inner * gate).astype(BF16)
        act_ref[:, cols] = act
        slope_ref[:, cols] = (gate + inner * bell).astype(BF16)
        keep(act_ref.at[:, cols], act_hbm.at[:, cols])
        keep(slope_ref.at[:, cols], slope_hbm.at[:, cols])
        branch = branch + mm(act, wdown_ref[cols, :])
    xhat, rstd = norm_rows(branch)
    xh2_ref[...] = xhat
    rs2_ref[...] = jnp.broadcast_to(rstd, (ROW, 128))
    keep(xh2_ref, xh2_hbm)
    keep(rs2_ref, rs2_hbm)
    second = xhat * g2_ref[...].astype(F32) + s2_ref[...].astype(F32)
    vec_ref[:ROW, :] = mm(second.astype(BF16), wproj_ref[...]).astype(BF16)
    line = iota((EXT, PROJ), 0)
    tag = jnp.zeros((EXT, PROJ), jnp.int32)
    for k in range(labels_ref.shape[0]):
        label = labels_ref[k]
        tag = jnp.where(line == k, label >> 6, tag)
        tag = jnp.where(line == k + 8, label & 63, tag)
    vec_ref[ROW:, :] = tag.astype(F32).astype(BF16)
    for copy in kept:
        copy.wait()


def prefix_norms(values, axis):
    place = iota(values.shape, axis)
    squared = values * values
    sums = [
        jnp.sum(jnp.where(place < cut, squared, 0.0), axis=axis, keepdims=True) for cut in RANGES
    ]
    return [lax.rsqrt(s + EPS_NORM) for s in sums]


def load_queries(near_ref, far_ref):
    span = ROW + EXT
    rows = []
    for ref in (near_ref, far_ref):
        for k in range(ref.shape[0] // span):
            rows.append(ref[k * span : k * span + ROW, :])
    return jnp.concatenate(rows, axis=0).astype(F32)


def unit_queries(queries, scale):
    lane = iota(queries.shape, 1)
    inverse = prefix_norms(queries, 1)
    unit = [
        jnp.where(lane < cut, queries * (inv * scale), 0.0) for cut, inv in zip(RANGES, inverse)
    ]
    return unit, inverse


def unit_docs(doc_refs, scratch_ref):
    at = 0
    for ref in doc_refs:
        for k in range(ref.shape[0] // ROW):
            scratch_ref[:, at * ROW : (at + 1) * ROW] = ref[
                k * ROW : (k + 1) * ROW, :
            ].astype(F32).T
            at += 1
    turned = scratch_ref[...]
    inverse = prefix_norms(turned, 0)
    place = iota(turned.shape, 0)
    unit = [jnp.where(place < cut, turned * inv, 0.0) for cut, inv in zip(RANGES, inverse)]
    return unit, inverse


def row_ids(base, masks, doc_rows):
    ids = []
    for p in range(doc_rows):
        offset = 0
        for k, mask in enumerate(masks):
            if (p >> k) & 1:
                offset ^= mask
        ids.append(base ^ offset)
    return ids


def doc_marks(lens_ref, ids, lanes, transposed):
    docs = len(ids) * DOCS_ROW
    shape = (lanes, ROW) if transposed else (ROW, lanes)
    spot, lane = (iota(shape, 1), iota(shape, 0)) if transposed else (iota(shape, 0), iota(shape, 1))
    marks = []
    for p, row in enumerate(ids):
        seg = segment_of(spot, bounds_of(lens_ref, row))
        local = jnp.where(seg < DOCS_ROW, seg + p * DOCS_ROW, -1 - lanes)
        marks.append(
            [(lane == local + m * docs).astype(F32).astype(BF16) for m in range(len(RANGES))]
        )
    return marks


def matching_stats(
    masks, lanes, where_ref, scale_ref, lens_ref, near_ref, far_ref, *refs
):
    doc_refs = refs[:-6]
    totals_ref, el_ref, hot_ref, stats_ref, turn_ref, unit_ref = refs[-6:]
    base, near_at = where_ref[2], where_ref[3]
    span = ROW + EXT
    queries = load_queries(near_ref, far_ref)
    count = queries.shape[0]
    unit_q, _ = unit_queries(queries, SHARPNESS * LOG2E)
    unit_q = [u.astype(BF16) for u in unit_q]
    unit_d, _ = unit_docs(doc_refs, turn_ref)
    for m in range(len(RANGES)):
        unit_ref[m] = unit_d[m].astype(BF16)
    doc_rows = turn_ref.shape[1] // ROW
    docs = doc_rows * DOCS_ROW
    ids = row_ids(base, masks, doc_rows)
    marks = doc_marks(lens_ref, ids, lanes, False)
    totals = jnp.zeros((count, lanes), F32)
    for p in range(doc_rows):
        for m in range(len(RANGES)):
            sims = mm(unit_q[m], unit_ref[m, :, p * ROW : (p + 1) * ROW])
            totals = totals + mm(jnp.exp2(sims).astype(BF16), marks[p][m])
    lane_t = iota((count, lanes), 1)
    totals = jnp.where(lane_t < len(RANGES) * docs, totals, 1.0)
    totals_ref[...] = totals
    shape = (8, lanes)
    lane = iota(shape, 1)
    length = jnp.ones(shape, jnp.int32)
    name = jnp.full(shape, -1, jnp.int32)
    for p in range(doc_rows):
        for k in range(DOCS_ROW):
            own = jnp.zeros(shape, jnp.bool_)
            for m in range(len(RANGES)):
                own = jnp.logical_or(own, lane == m * docs + p * DOCS_ROW + k)
            length = jnp.where(own, lens_ref[ids[p], k], length)
            name = jnp.where(own, ids[p] * DOCS_ROW + k, name)
    log_length = jnp.log(length.astype(F32))
    matched = (jnp.log(totals) - log_length[:1]) * (1.0 / SHARPNESS)
    per_query = jnp.sum(matched.reshape(count // QLEN, QLEN, lanes), axis=1)
    scale = jnp.exp(jnp.full(shape, scale_ref[0], F32))[:1]
    logits = per_query * (scale * (1.0 / QLEN))
    groups = count // ROW
    tags = []
    for ref in (near_ref, far_ref):
        for k in range(ref.shape[0] // span):
            high = ref[k * span + ROW : k * span + ROW + 8, :].astype(F32).astype(jnp.int32)
            low = ref[k * span + ROW + 8 : k * span + ROW + 16, :].astype(F32).astype(jnp.int32)
            tag = high * 64 + low
            tags.append(jnp.concatenate([tag] * (lanes // 128), axis=1))
    tag = jnp.concatenate(tags, axis=0)
    lane_q = iota(logits.shape, 1)
    valid = lane_q < len(RANGES) * docs
    el = jnp.where(valid, jnp.exp(logits), 0.0)
    hot = jnp.where(jnp.logical_and(valid, jnp.concatenate([name] * groups, axis=0) == tag), 1.0, 0.0)
    el_ref[...] = el
    hot_ref[...] = hot
    place = iota((groups * 8, 128), 1)
    stats = jnp.zeros((groups * 8, 128), F32)
    for k, values in enumerate((el, el * logits, hot * logits)):
        for m in range(len(RANGES)):
            inside = jnp.logical_and(lane_q >= m * docs, lane_q < (m + 1) * docs)
            one = jnp.sum(jnp.where(inside, values, 0.0), axis=1, keepdims=True)
            stats = jnp.where(place == k * 3 + m, one, stats)
    for a in range(groups):
        at = pl.multiple_of((near_at ^ a) * 8, 8)
        stats_ref[pl.ds(at, 8), :] = stats[a * 8 : (a + 1) * 8, :]


def matching_back(
    masks, lanes, total_queries, where_ref, scale_ref, lens_ref, near_ref, far_ref, totals_ref,
    el_ref, hot_ref, stats_ref, *refs
):
    doc_refs = refs[:-9]
    dq_ref, send_ref, keep_ref, loss_ref, turn_ref, unit_ref, qt_ref, dot_ref, dt_ref = refs[-9:]
    base, near_at = where_ref[2], where_ref[3]
    temper = SHARPNESS * LOG2E
    queries = load_queries(near_ref, far_ref)
    count = queries.shape[0]
    unit_q, inv_q = unit_queries(queries, temper)
    unit_q = [u.astype(BF16) for u in unit_q]
    unit_d, inv_d = unit_docs(doc_refs, turn_ref)
    for m in range(len(RANGES)):
        unit_ref[m] = unit_d[m].astype(BF16)
        qt_ref[m] = unit_q[m].astype(F32).T.astype(BF16)
    doc_rows = turn_ref.shape[1] // ROW
    docs = doc_rows * DOCS_ROW
    ids = row_ids(base, masks, doc_rows)
    marks = doc_marks(lens_ref, ids, lanes, True)
    groups = count // ROW
    rows = []
    for a in range(groups):
        at = pl.multiple_of((near_at ^ a) * 8, 8)
        rows.append(stats_ref[pl.ds(at, 8), :])
    stats = jnp.concatenate(rows, axis=0)
    place = iota(stats.shape, 1)

    def column(k):
        return jnp.sum(jnp.where(place == k, stats, 0.0), axis=1, keepdims=True)

    shape = (groups * 8, lanes)
    lane_q = iota(shape, 1)
    sums = jnp.ones(shape, F32)
    loss = jnp.zeros((groups * 8, 1), F32)
    moved = jnp.zeros((groups * 8, 1), F32)
    for m in range(len(RANGES)):
        whole, weighted, picked = column(m), column(3 + m), column(6 + m)
        inside = jnp.logical_and(lane_q >= m * docs, lane_q < (m + 1) * docs)
        sums = jnp.where(inside, whole, sums)
        loss = loss + (jnp.log(whole) - picked)
        moved = moved + (weighted / whole - picked)
    line = iota((8, 128), 0)
    loss = jnp.where(
        line == 0,
        jnp.sum(loss, axis=0, keepdims=True) * (1.0 / total_queries),
        jnp.where(line == 1, jnp.sum(moved, axis=0, keepdims=True) * (1.0 / total_queries), 0.0),
    )
    loss_ref[...] = loss
    scale = jnp.exp(jnp.full((8, lanes), scale_ref[0], F32))[:1]
    coeff = (el_ref[...] / sums - hot_ref[...]) * (scale * (1.0 / (QLEN * total_queries)))
    coeff = jnp.broadcast_to(coeff[:, None, :], (groups * 8, QLEN, lanes)).reshape(count, lanes)
    ratio = coeff / totals_ref[...]
    ratio_high = ratio.astype(BF16)
    ratio_low = (ratio - ratio_high.astype(F32)).astype(BF16)
    ratio = jnp.concatenate([ratio_high, ratio_low], axis=1)
    for m in range(len(RANGES)):
        grad = jnp.zeros((count, PROJ), F32)
        for p in range(doc_rows):
            block = unit_ref[m, :, p * ROW : (p + 1) * ROW]
            mark = marks[p][m]
            exps = jnp.exp2(mm(unit_q[m], block))
            d_sims = (exps * mm(ratio, jnp.concatenate([mark, mark], axis=0))).astype(BF16)
            grad = grad + mm_nt(d_sims, block)
            dt_ref[m, :, p * ROW : (p + 1) * ROW] = mm(qt_ref[m], d_sims)
        unit = unit_q[m].astype(F32) * (1.0 / temper)
        along = jnp.sum(grad * unit, axis=1, keepdims=True)
        part = inv_q[m] * (grad - unit * along)
        if m == 0:
            dot_ref[...] = part
        else:
            dot_ref[...] += part
    dq_ref[...] = dot_ref[...].astype(BF16)
    total = jnp.zeros(turn_ref.shape, F32)
    for m in range(len(RANGES)):
        grad = dt_ref[m] * (1.0 / temper)
        unit = unit_ref[m].astype(F32)
        along = jnp.sum(grad * unit, axis=0, keepdims=True)
        total = total + inv_d[m] * (grad - unit * along)
    for p in range(doc_rows):
        ref, at = (keep_ref, p) if p < doc_rows // 2 else (send_ref, p - doc_rows // 2)
        ref[at * ROW : (at + 1) * ROW, :] = total[:, p * ROW : (p + 1) * ROW].T.astype(BF16)
    send_ref[doc_rows // 2 * ROW :, :] = packed_loss(loss)


def packed_loss(loss):
    high = loss.astype(BF16)
    rest = loss - high.astype(F32)
    middle = rest.astype(BF16)
    low = rest - middle.astype(F32)
    lane = iota(loss.shape, 1)
    packed = jnp.where(lane == 0, high.astype(F32), jnp.where(lane == 1, middle.astype(F32), low))
    return jnp.concatenate([packed, jnp.zeros_like(packed)], axis=0).astype(BF16)


def loss_of(packed):
    lines = packed.astype(F32)[:8, :]
    return jnp.sum(jnp.where(iota(lines.shape, 1) < 3, lines, 0.0), axis=1, keepdims=True)


def fold_docs(keep_ref, got_ref, loss_ref, *outs):
    rows = keep_ref.shape[0]
    loss = loss_ref[...] + loss_of(got_ref[rows:, :])
    total = (keep_ref[...].astype(F32) + got_ref[:rows, :].astype(F32)).astype(BF16)
    outs[-1][...] = loss
    if rows > ROW:
        outs[0][: rows // 2, :] = total[rows // 2 :, :]
        outs[0][rows // 2 :, :] = packed_loss(loss)
        outs[1][...] = total[: rows // 2, :]
    else:
        outs[0][:rows, :] = total
        outs[0][rows:, :] = packed_loss(loss)


def last_docs(where_ref, near_ref, got_ref, loss_ref, dq_ref, dd_ref, send_ref, sum_ref):
    sum_ref[...] = loss_ref[...] + loss_of(got_ref[ROW:, :])
    total = (near_ref[:ROW, :].astype(F32) + got_ref[:ROW, :].astype(F32)).astype(BF16)
    dd_ref[...] = total
    send_ref[...] = jnp.where(where_ref[1] == 0, total, dq_ref[...])


def turn(core, place, block):
    return jnp.where(core == 0, place - block, block - place) & (RING - 1)


def block_at(core, place, distance):
    return jnp.where(core == 0, place - distance, place + distance) & (RING - 1)


def store_block(keep_ref, send_ref, rows, block, places, value):
    core, place = places
    mine = core == block // RING
    at = turn(block // RING, place, block % RING)

    @pl.when(mine)
    def _():
        keep_ref[at, rows, :] = value

    @pl.when(jnp.logical_not(mine))
    def _():
        send_ref[at, rows, :] = value


def feed_back(
    where_ref, dq_ref, dd_ref, got_ref, xh2_ref, rs2_ref, affine_ref, wproj_ref, wdown_ref,
    slope_ref, act_ref, wup_ref, xh1_ref,
    keep_ref, send_ref, tail_keep, tail_send, dfirst_ref, gproj_ref, small_ref, dinner_ref,
):
    g1, s1, g2, s2 = [affine_ref[k : k + 1, :] for k in range(4)]
    is_query, docs_there = where_ref[1] == 0, where_ref[4] == 0
    places = (where_ref[5], where_ref[6])
    got = got_ref[...].astype(F32)
    d_vec = jnp.where(
        is_query,
        dq_ref[...].astype(F32) + got,
        jnp.where(docs_there, got, dd_ref[...].astype(F32)),
    )
    d_proj = d_vec.astype(BF16)
    xhat = xh2_ref[...]
    gain = g2
    second = (xhat * gain + s2).astype(BF16)
    gproj_ref[...] = mm_tn(second, d_proj)
    d_second = mm_nt(d_proj, wproj_ref[...])
    small_ref[...] = jnp.zeros_like(small_ref)
    small_ref[5:6, :] = col_sum(d_second * xhat)
    small_ref[6:7, :] = col_sum(d_second)
    d_sum = norm_back(d_second, xhat, rs2_ref[:, :1], gain)
    d_branch = d_sum.astype(BF16)
    small_ref[4:5, :] = col_sum(d_branch.astype(F32))
    step = 512
    d_first = d_sum
    for c in range(FF // step):
        cols = slice(c * step, (c + 1) * step)
        d_act = mm_nt(d_branch, wdown_ref[cols, :])
        d_inner = (d_act * slope_ref[:, cols].astype(F32)).astype(BF16)
        dinner_ref[:, cols] = d_inner
        small_ref[c : c + 1, :] = col_sum(d_inner.astype(F32))
        grad = mm_tn(act_ref[:, cols], d_branch).astype(BF16)
        for k in range(step // DOWN):
            store_block(
                keep_ref, send_ref, slice(0, DOWN), c * (step // DOWN) + k, places,
                grad[k * DOWN : (k + 1) * DOWN, :],
            )
        d_first = d_first + mm_nt(d_inner, wup_ref[:, cols])
    dfirst_ref[...] = d_first
    first = (xh1_ref[...] * g1 + s1).astype(BF16)
    for c in range(FF // step):
        cols = slice(c * step, (c + 1) * step)
        grad = mm_tn(first, dinner_ref[:, cols]).astype(BF16)
        for k in range(D // DOWN):
            block = c * (D // DOWN) + k
            start = k * DOWN
            store_block(
                keep_ref, send_ref, slice(DOWN, FIRST), block, places, grad[start : start + HEAD, :]
            )
            store_block(
                tail_keep, tail_send, slice(0, TAIL), block, places,
                grad[start + HEAD : start + DOWN, :],
            )


def attend_back(
    where_ref, dfirst_ref, gproj_ref, small_ref, tail_keep, tail_send, xh1_ref, rs1_ref, affine_ref, mixed_ref, wout_ref,
    qkv_ref, probs_ref, rope_ref, x_ref, wqkv_ref,
    keep_ref, send_ref, tokens_ref, djoined_ref, rest_ref,
):
    core, place = where_ref[5], where_ref[6]
    d_first = dfirst_ref[...]
    xhat = xh1_ref[...]
    gain = affine_ref[0:1, :]
    gain_grad = col_sum(d_first * xhat)
    shift_grad = col_sum(d_first)
    d_sum = norm_back(d_first, xhat, rs1_ref[:, :1], gain)
    d_att = d_sum.astype(BF16)
    bias_out = col_sum(d_att.astype(F32))
    rest_ref[3 * D : 4 * D, :] = mm_tn(mixed_ref[...], d_att)
    d_mixed = mm_nt(d_att, wout_ref[...]).astype(BF16)
    cosine, sine = rope_ref[:, :128], rope_ref[:, 128:]
    low_half = iota((ROW, 128), 1) < HD

    def unrotate(values):
        values = values * (1.0 / math.sqrt(HD))
        return (values * cosine - swap_halves(values) * sine).astype(BF16)

    for g in range(HEADS // 2):
        span = slice(g * 128, (g + 1) * 128)
        q_g = qkv_ref[:, g * 128 : (g + 1) * 128]
        k_g = qkv_ref[:, D + g * 128 : D + (g + 1) * 128]
        v_g = qkv_ref[:, 2 * D + g * 128 : 2 * D + (g + 1) * 128]
        m_g = d_mixed[:, span]
        d_q = jnp.zeros((ROW, 128), F32)
        d_k = jnp.zeros((ROW, 128), F32)
        d_v = jnp.zeros((ROW, 128), F32)
        zero = jnp.zeros((ROW, 128), BF16)
        for h in range(2):
            pick = low_half if h == 0 else jnp.logical_not(low_half)
            probs_low = probs_ref[2 * g + h]
            probs = probs_low.astype(F32)
            m_h = jnp.where(pick, m_g, zero)
            d_probs = mm_nt(m_h, v_g)
            d_v = d_v + mm_tn(probs_low, m_h)
            inner = jnp.sum(d_probs * probs, axis=1, keepdims=True)
            d_scores = (probs * (d_probs - inner)).astype(BF16)
            d_q = d_q + mm(d_scores, jnp.where(pick, k_g, zero))
            d_k = d_k + mm_tn(d_scores, jnp.where(pick, q_g, zero))
        djoined_ref[:, g * 128 : (g + 1) * 128] = unrotate(d_q)
        djoined_ref[:, D + g * 128 : D + (g + 1) * 128] = unrotate(d_k)
        djoined_ref[:, 2 * D + g * 128 : 2 * D + (g + 1) * 128] = d_v.astype(BF16)
    x = x_ref[...]
    tokens = d_sum
    rest_ref[4 * D :, :] = jnp.zeros((8 * 2 * RING, D), F32)
    smalls = []
    for c in range(3):
        cols = slice(c * D, (c + 1) * D)
        d_part = djoined_ref[:, cols]
        rest_ref[c * D : (c + 1) * D, :] = mm_tn(x, d_part)
        smalls.append(col_sum(d_part.astype(F32)))
        tokens = tokens + mm_nt(d_part, wqkv_ref[:, cols])
    tokens_ref[...] = tokens
    smalls += [bias_out, gain_grad, shift_grad] + [small_ref[k : k + 1, :] for k in range(7)]
    for k, row in enumerate(smalls):
        rest_ref[4 * D + 8 * k : 4 * D + 8 * k + 1, :] = row
    for k in range(RING):
        for ref, tail_ref, owner in (
            (keep_ref, tail_keep, core), (send_ref, tail_send, 1 - core)
        ):
            block = owner * RING + block_at(owner, place, k)
            parts = []
            for c in range(4):
                start = pl.multiple_of(c * D + block * SHARE, SHARE)
                parts.append(rest_ref[pl.ds(start, SHARE), :])
            row = pl.multiple_of(block * SHARE, SHARE)
            parts.append(
                jnp.concatenate(
                    [gproj_ref[pl.ds(row + 8 * j, 8), :] for j in range(SHARE // 8)], axis=1
                )
            )
            parts.append(rest_ref[pl.ds(pl.multiple_of(4 * D + block * 8, 8), 8), :])
            ref[k, : REST // 16, :] = jnp.concatenate(parts, axis=0).astype(BF16)
            ref[k, REST // 16 :, :] = tail_ref[k]


def spread(mine, group, last, where_ref, *refs):
    core, place = where_ref[5], where_ref[6]
    owner = core if mine else 1 - core
    one_ref, two_ref = refs[:2]
    wide_one, wide_two, wide_proj, small_ref, sems = refs[-5:]
    outs = refs[-18:-5] if last else refs[-10:-5]
    down_hbm, up_hbm, qkv_hbm, out_hbm, proj_hbm = outs[:5]
    copies = []

    def move(src, dst):
        copy = pltpu.make_async_copy(src, dst, sems.at[len(copies)])
        copy.start()
        copies.append(copy)

    for p, distance in enumerate(GROUPS[group]):
        block = owner * RING + block_at(owner, place, distance)
        wide_one[p] = one_ref[p].astype(F32)
        rows = pl.ds(pl.multiple_of(block * DOWN, DOWN), DOWN)
        move(wide_one.at[p, :DOWN, :], down_hbm.at[rows, :])
        wide = two_ref[p].astype(F32)
        wide_two[p, : 4 * SHARE, :] = wide[: 4 * SHARE, :]
        wide_two[p, 4 * SHARE :, :] = wide[REST // 16 :, :]
        start = (block % (D // DOWN)) * DOWN
        columns = pl.ds(pl.multiple_of((block // (D // DOWN)) * D, D), D)
        rows = pl.ds(pl.multiple_of(start, DOWN), HEAD)
        move(wide_one.at[p, DOWN:, :], up_hbm.at[rows, columns])
        rows = pl.ds(pl.multiple_of(start + HEAD, 16), TAIL)
        move(wide_two.at[p, 4 * SHARE :, :], up_hbm.at[rows, columns])
        rows = pl.ds(pl.multiple_of(block * SHARE, SHARE), SHARE)
        for c in range(3):
            move(
                wide_two.at[p, c * SHARE : (c + 1) * SHARE, :],
                qkv_hbm.at[rows, c * D : (c + 1) * D],
            )
        move(wide_two.at[p, 3 * SHARE : 4 * SHARE, :], out_hbm.at[rows, :])
        for j in range(SHARE // 8):
            wide_proj[p, 8 * j : 8 * j + 8, :] = wide[
                4 * SHARE : 4 * SHARE + 8, j * PROJ : (j + 1) * PROJ
            ]
        move(wide_proj.at[p], proj_hbm.at[rows, :])
    if last:
        sources = ((refs[2], core, 0), (refs[3], core, 1), (refs[4], 1 - core, 0), (two_ref, 1 - core, 1))
        for ref, at, one_group in sources:
            for p, distance in enumerate(GROUPS[one_group]):
                block = at * RING + block_at(at, place, distance)
                line = ref[p, 4 * SHARE : 4 * SHARE + 16, :].astype(F32)[8:, :]
                small_ref[pl.ds(pl.multiple_of(block * 8, 8), 8), :] = line
        rows = [small_ref[8 * k : 8 * k + 1, :] for k in range(13)]
        bqkv_ref, bout_ref, g1_ref, s1_ref, bup_ref, bdown_ref, g2_ref, s2_ref = outs[5:]
        for c in range(3):
            bqkv_ref[:, c * D : (c + 1) * D] = rows[c]
        bout_ref[...] = rows[3]
        g1_ref[...] = rows[4]
        s1_ref[...] = rows[5]
        for c in range(4):
            bup_ref[:, c * D : (c + 1) * D] = rows[6 + c]
        bdown_ref[...] = rows[10]
        g2_ref[...] = rows[11]
        s2_ref[...] = rows[12]
    for copy in copies:
        copy.wait()


def spread_call(mine, group, where, one, two, outs, others):
    last = len(others) > 0
    shapes = ((FF, D), (D, FF), (D, 3 * D), (D, D), (D, PROJ))
    widths = (3 * D, D, D, D, FF, D, D, D) if last else ()
    args = [where, one, two, *others, *outs]
    half = len(GROUPS[group])
    return call(
        partial(spread, mine, group, last),
        args,
        [SMEM] + [VMEM] * (2 + len(others)) + [HBM] * len(outs),
        [pltpu.HBM(shape, F32) for shape in shapes] + [shape_of((1, width)) for width in widths],
        [
            pltpu.VMEM((half, FIRST, D), F32),
            pltpu.VMEM((half, 4 * SHARE + TAIL, D), F32),
            pltpu.VMEM((half, SHARE, PROJ), F32),
            pltpu.VMEM((16 * RING, D), F32),
            pltpu.SemaphoreType.DMA((8 * half,)),
        ],
        out_specs=[HBM] * 5 + [VMEM] * len(widths),
        aliases={3 + len(others) + k: k for k in range(len(outs))},
        room=14,
    )


def shape_of(shape, dtype=F32):
    return jax.ShapeDtypeStruct(tuple(shape), dtype)


def call(kernel, args, specs, outs, scratch=(), room=24, out_specs=None, aliases={}, cost=10**7):
    spaces = {id(HBM): pltpu.HBM, id(HELD): pltpu.VMEM}
    args = [
        pltpu.with_memory_space_constraint(arg, spaces[id(spec)]) if id(spec) in spaces else arg
        for arg, spec in zip(args, specs)
    ]
    return pl.pallas_call(
        kernel,
        out_shape=outs,
        in_specs=specs,
        out_specs=out_specs or [VMEM] * len(outs),
        scratch_shapes=list(scratch),
        input_output_aliases=aliases,
        compiler_params=pltpu.CompilerParams(vmem_limit_bytes=room * MIB),
        cost_estimate=pl.CostEstimate(
            flops=10**8, bytes_accessed=cost, transcendentals=0
        ),
    )(*args)


def spread_half_call(where, halves, near=None, outs=()):
    mine = near is None
    args = [where, *halves] + ([] if mine else [near, *outs])
    specs = [SMEM] + [VMEM] * (3 if mine else 4) + [HBM] * len(outs)
    shapes = ((FF, D), (D, FF), (D, 3 * D), (D, D), (D, PROJ))
    widths = () if mine else (3 * D, D, D, D, FF, D, D, D)
    return call(
        partial(spread_half, mine),
        args,
        specs,
        [pltpu.HBM(shape, F32) for shape in shapes] + [shape_of((1, width)) for width in widths],
        [
            pltpu.VMEM((RING, FF // (2 * RING), D), F32),
            pltpu.VMEM((RING, FF // (2 * RING), D), F32),
            pltpu.VMEM((RING, 4 * SHARE, D), F32),
            pltpu.VMEM((RING, SHARE, PROJ), F32),
            pltpu.SemaphoreType.DMA((7 * RING,)),
        ],
        out_specs=[HBM] * 5 + [VMEM] * len(widths),
        aliases={} if mine else {5 + k: k for k in range(5)},
        room=14,
    )


def swapped(value, mask, axis="dp"):
    size = lax.axis_size(axis)
    return lax.ppermute(value, axis, [(k, k ^ mask) for k in range(size)])


def added(a, b):
    return (a.astype(F32) + b.astype(F32)).astype(BF16)


def join_blocks(*refs):
    for k, ref in enumerate(refs[:-1]):
        refs[-1][k] = ref[0]


def ring_swap(value, onward):
    size = lax.axis_size("dp")
    pairs = []
    for k in range(size):
        at = CIRCLE.index((k >> 1) % RING)
        to = CIRCLE[(at + (1 if (k % 2 == 0) == onward else -1)) % RING]
        pairs.append((k, (k & ~(2 * RING - 1)) | (to << 1) | (k & 1)))
    return lax.ppermute(value, "dp", pairs)


def add_blocks(places, *refs):
    count = len(places)
    held_ref = refs[count] if any(place is not None for place in places) else None
    for k, place in enumerate(places):
        value = refs[k][...]
        if place is not None:
            value = (value.astype(F32) + held_ref[place : place + 1].astype(F32)).astype(BF16)
        refs[-count + k][...] = value


class Summed:
    def __init__(self, keep, send, others):
        self.keep, self.others, self.hop = keep, others, 0
        self.pair = swapped(send, 1)
        self.got, self.blocks, self.near, self.far = [], {}, [], []

    def blocks_call(self, blocks, places, held):
        return call(
            partial(add_blocks, places),
            (*blocks, *held),
            [VMEM] * (len(blocks) + len(held)),
            [shape_of(block.shape, BF16) for block in blocks],
            room=8,
            cost=STEP_COST,
        )

    def open(self, after):
        keep, pair, _ = lax.optimization_barrier((self.keep, self.pair, after))
        half = RING // 2
        first = added(keep[half : half + 1], pair[half : half + 1])
        second = added(keep[half - 1 : half], pair[half - 1 : half])
        self.got = [ring_swap(first, True), ring_swap(second, False)]
        return second

    def total(self, after):
        keep, _ = lax.optimization_barrier((self.keep, after))
        self.keep = added(keep, self.pair)
        return self.keep

    def step(self, after):
        half = RING // 2
        self.hop += 1
        hop = self.hop
        *got, _ = lax.optimization_barrier((*self.got, after))
        if hop < half:
            out = self.blocks_call(got, (half + hop, half - 1 - hop), [self.keep])
            self.part = out[1]
        elif hop == half:
            (own,) = self.blocks_call(got, (0,), [self.part])
            for mask in self.others:
                own = added(own, swapped(own, mask))
            self.blocks[0] = own
            out = [own, own]
        else:
            out = self.blocks_call(got, (None,) * len(got), [])
            hop -= half
            self.blocks[hop] = out[0]
            if hop < half:
                self.blocks[RING - hop] = out[1]
        if hop == half - 1:
            self.got = [ring_swap(out[0], True)]
        elif self.hop < 2 * half:
            self.got = [ring_swap(out[0], True), ring_swap(out[1], False)]
        return out[0]

    def share(self, group, after):
        *blocks, _ = lax.optimization_barrier((*[self.blocks[k] for k in GROUPS[group]], after))
        shape = (len(blocks), *blocks[0].shape[1:])
        self.near += call(
            join_blocks, blocks, [VMEM] * len(blocks), [shape_of(shape, BF16)], room=8, cost=STEP_COST
        )
        self.far.append(swapped(self.near[-1], 1))
        return self.near[-1]


def per_device(
    tokens, qkv_weight, qkv_bias, out_weight, out_bias, first_gain, first_shift, up_weight,
    up_bias, down_weight, down_bias, second_gain, second_shift, proj_weight, log_scale,
    doc_lengths, labels,
):
    size = lax.axis_size("dp")
    bits = [1 << k for k in range(size.bit_length() - 1)]
    near_masks, doc_masks = bits[:2], bits[2:]
    top_mask, doc_masks = doc_masks[-1], doc_masks[:-1]
    others = bits[4:]
    me = lax.axis_index("dp")
    stream = lax.axis_index("stream")
    is_query = stream == 0
    has_top = (me & top_mask) != 0
    base = jnp.where(is_query, me & ~top_mask, me | top_mask)
    near_at = jnp.where((me & near_masks[1]) != 0, 1, 0) + jnp.where((me & near_masks[0]) != 0, 2, 0)
    core = me & 1
    chip = (me >> 1) % RING
    place = jnp.int32(0)
    for k, one in enumerate(CIRCLE):
        place = jnp.where(chip == one, k, place)
    where = jnp.stack(
        [me, stream, base, near_at, has_top.astype(jnp.int32), core, place, place]
    ).astype(jnp.int32)
    scale = log_scale.reshape(1)

    vec, qkv, rope, probs, mixed, xh1, rs1, act, slope, xh2, rs2, affine = call(
        encoder_forward,
        (
            where, doc_lengths, labels, jnp.asarray(rope_table()), tokens[0], qkv_weight[0], qkv_bias,
            out_weight[0], out_bias, first_gain, first_shift, up_weight[0], up_bias,
            down_weight[0], down_bias, second_gain, second_shift, proj_weight[0],
        ),
        [SMEM] * 3 + [HBM] * 15,
        [shape_of((ROW + EXT, PROJ), BF16)] + [pltpu.HBM(*kind) for kind in KEPT],
        [pltpu.VMEM(*kind) for kind in KEPT]
        + [pltpu.SemaphoreType.DMA((len(KEPT) + 6,))]
        + [
            pltpu.VMEM(shape, BF16)
            for shape in (
                (ROW, 512), (ROW, D), (D, 3 * D), (1, 3 * D), (D, D), (1, D), (1, D), (1, D), (D, FF),
                (1, FF), (FF, D), (1, D), (1, D), (1, D), (D, PROJ),
            )
        ]
        + [pltpu.SemaphoreType.DMA((15,))],
        room=40,
        out_specs=[VMEM] + [HBM] * len(KEPT),
    )

    other = swapped(vec, 1, "stream")
    near = jnp.where(is_query, vec, other)
    rows = jnp.where(is_query, other, vec)[:ROW]
    moved = swapped(rows, top_mask)
    near = jnp.concatenate([near, swapped(near, near_masks[1])], axis=0)
    rows = jnp.where(has_top == is_query, moved, rows)
    far = swapped(near, near_masks[0])
    pieces = []
    for k, mask in enumerate(doc_masks):
        pieces.append(rows)
        got = swapped(rows, mask)
        if k + 1 < len(doc_masks):
            rows = jnp.concatenate([rows, got], axis=0)
        else:
            pieces = [rows, got]
    doc_rows = sum(p.shape[0] for p in pieces) // ROW
    tokens_d = doc_rows * ROW
    tokens_q = 4 * ROW
    lanes = -(-3 * doc_rows * DOCS_ROW // 128) * 128
    total_queries = size * (ROW // QLEN)
    room = 20 if doc_rows <= 4 else 56
    totals, el, hot, stats = call(
        partial(matching_stats, doc_masks, lanes),
        (where, scale, doc_lengths, near, far, *pieces),
        [SMEM] * 3 + [VMEM] * (2 + len(pieces)),
        [
            shape_of((tokens_q, lanes)),
            shape_of((tokens_q // QLEN, lanes)),
            shape_of((tokens_q // QLEN, lanes)),
            shape_of((tokens_q // QLEN, 128)),
        ],
        [pltpu.VMEM((PROJ, tokens_d), F32), pltpu.VMEM((3, PROJ, tokens_d), BF16)],
        room=room,
    )
    stats = stats + swapped(stats, near_masks[0])
    stats = stats + swapped(stats, near_masks[1])
    stats = stats + swapped(stats, 1, "stream")
    dq, send, keep, loss = call(
        partial(matching_back, doc_masks, lanes, total_queries),
        (where, scale, doc_lengths, near, far, totals, el, hot, stats, *pieces),
        [SMEM] * 3 + [VMEM] * (6 + len(pieces)),
        [
            shape_of((tokens_q, PROJ), BF16), shape_of((tokens_d // 2 + EXT, PROJ), BF16),
            shape_of((tokens_d // 2, PROJ), BF16), shape_of((8, 128)),
        ],
        [
            pltpu.VMEM((PROJ, tokens_d), F32),
            pltpu.VMEM((3, PROJ, tokens_d), BF16),
            pltpu.VMEM((3, PROJ, tokens_q), BF16),
            pltpu.VMEM((tokens_q, PROJ), F32),
            pltpu.VMEM((3, PROJ, tokens_d), F32),
        ],
        room=room,
    )
    for mask in reversed(doc_masks):
        got, rows = swapped(send, mask), keep.shape[0]
        outs = [shape_of((rows // 2 + EXT, PROJ), BF16), shape_of((rows // 2, PROJ), BF16)]
        if rows == ROW:
            outs = [shape_of((ROW + EXT, PROJ), BF16)]
        send, *keep, loss = call(
            fold_docs, (keep, got, loss), [VMEM] * 3, outs + [shape_of((8, 128))], room=8
        )
        keep = keep[0] if keep else None
    for mask in near_masks:
        half = dq.shape[0] // 2
        dq = added(dq[:half], swapped(dq[half:], mask))
    dd, send, loss = call(
        last_docs,
        (where, send, swapped(send, top_mask), loss, dq),
        [SMEM] + [VMEM] * 4,
        [shape_of((ROW, PROJ), BF16), shape_of((ROW, PROJ), BF16), shape_of((8, 128))],
        room=8,
    )
    got = swapped(send, 1, "stream")

    one_keep, one_send, tail_keep, tail_send, d_first, gproj, small = call(
        feed_back,
        (
            where, dq, dd, got, xh2, rs2, affine, proj_weight[0], down_weight[0], slope, act,
            up_weight[0], xh1,
        ),
        [SMEM] + [VMEM] * 3 + [HELD] * 9,
        [shape_of((RING, FIRST, D), BF16)] * 2
        + [shape_of((RING, TAIL, D), BF16)] * 2
        + [shape_of((ROW, D)), shape_of((D, PROJ)), shape_of((8, D))],
        [pltpu.VMEM((ROW, FF), BF16)],
        room=24,
    )
    two_keep, two_send, tokens_grad = call(
        attend_back,
        (
            where, d_first, gproj, small, tail_keep, tail_send, xh1, rs1, affine, mixed, out_weight[0], qkv, probs, rope,
            tokens[0], qkv_weight[0],
        ),
        [SMEM] + [VMEM] * 5 + [HELD] * 10,
        [shape_of((RING, SECOND, D), BF16)] * 2 + [shape_of((ROW, D))],
        [
            pltpu.VMEM((ROW, 3 * D), BF16),
            pltpu.VMEM((4 * D + 16 * RING, D), F32),
        ],
        room=24,
    )
    one, two = [
        Summed(keep, send, others) for keep, send in ((one_keep, one_send), (two_keep, two_send))
    ]
    token, outs = tokens_grad, ()
    for event in ORDER:
        kind, k = event
        if kind in ("near", "far"):
            mine = kind == "near"
            halves = [piece.near[k] if mine else piece.far[k] for piece in (one, two)]
            *halves, _ = lax.optimization_barrier((*halves, token))
            rest = [*two.near, two.far[0]] if (kind, k) == ("far", 1) else []
            outs = spread_call(mine, k, where, *halves, outs[:5], rest)
            token = outs[0]
            continue
        piece = (one, two)[k]
        if kind in ("share0", "share1"):
            token = piece.share(int(kind[-1]), token)
        else:
            token = getattr(piece, kind)(token)
    grad_down, grad_up, grad_qkv, grad_out, grad_proj = outs[:5]
    (
        grad_bqkv, grad_bout, grad_g1, grad_s1, grad_bup, grad_bdown, grad_g2, grad_s2,
    ) = outs[5:]
    return (
        loss[0, 0],
        tokens_grad[None],
        grad_qkv[None],
        grad_bqkv,
        grad_out[None],
        grad_bout,
        grad_g1,
        grad_s1,
        grad_up[None],
        grad_bup,
        grad_down[None],
        grad_bdown,
        grad_g2,
        grad_s2,
        grad_proj[None],
        loss[1, 0],
    )


def solution(mesh):
    return jax.shard_map(
        per_device,
        mesh=mesh,
        in_specs=(
            P("stream", "dp", None),
            P("stream", None, None),
            P("stream", None),
            P("stream", None, None),
            P("stream", None),
            P("stream", None),
            P("stream", None),
            P("stream", None, None),
            P("stream", None),
            P("stream", None, None),
            P("stream", None),
            P("stream", None),
            P("stream", None),
            P("stream", None, None),
            P(),
            P(),
            P("dp"),
        ),
        out_specs=(
            P(),
            P("stream", "dp", None),
            P("stream", None, None),
            P("stream", None),
            P("stream", None, None),
            P("stream", None),
            P("stream", None),
            P("stream", None),
            P("stream", None, None),
            P("stream", None),
            P("stream", None, None),
            P("stream", None),
            P("stream", None),
            P("stream", None),
            P("stream", None, None),
            P(),
        ),
        check_vma=False,
    )
```

```python
from functools import partial
import math

import jax
import jax.numpy as jnp
import numpy as np
from jax import lax
from jax.experimental import pallas as pl
from jax.experimental.pallas import tpu as pltpu
from jax.sharding import PartitionSpec as P

D = 512
HEADS = 8
HD = 64
FF = 2048
PROJ = 128
QLEN = 32
DOCS_ROW = 4
ROW = 256
EXT = 16
RANGES = (64, 96, 128)

SHARPNESS = 8.0
EPS_NORM = 1e-06
EPS_LAYER = 1e-05
LOG2E = 1.4426950408889634

F32 = jnp.float32
BF16 = jnp.bfloat16
REST = 2304
SHARE = 32
DOWN = FF // 16
HEAD = 80
TAIL = DOWN - HEAD
FIRST = DOWN + HEAD
SECOND = REST // 16 + TAIL
CIRCLE = (0, 2, 4, 6, 7, 5, 3, 1)
RING = len(CIRCLE)
GROUPS = ((0, 1, 2, 3, 5, 6, 7), (4,))
STEP_COST = 3 * 10**7
SPREAD_COST = 0
ROUND = (("step", 0), ("step", 1))
ORDER = (
    (("open", 0), ("open", 1), ("total", 0), ("total", 1)) + ROUND * 7
    + (("share", 0, 0), ("share", 1, 0), ("spread", ((True, 0),))) + ROUND
    + (("share", 0, 1), ("share", 1, 1), ("spread", ((False, 0),)), ("spread", ((True, 1), (False, 1))))
)
MIB = 1024 * 1024

VMEM = pl.BlockSpec(memory_space=pltpu.VMEM)
SMEM = pl.BlockSpec(memory_space=pltpu.SMEM)
HBM = pl.BlockSpec(memory_space=pltpu.HBM)
HELD = pl.BlockSpec(memory_space=pltpu.VMEM)


def mm(a, b):
    return lax.dot_general(a, b, (((1,), (0,)), ((), ())), preferred_element_type=F32)


def mm_nt(a, b):
    return lax.dot_general(a, b, (((1,), (1,)), ((), ())), preferred_element_type=F32)


def mm_tn(a, b):
    return lax.dot_general(a, b, (((0,), (0,)), ((), ())), preferred_element_type=F32)


def iota(shape, axis):
    return lax.broadcasted_iota(jnp.int32, shape, axis)


def rope_table():
    half = HD // 2
    freqs = (10000.0 ** (-np.arange(half, dtype=np.float32) / np.float32(half))).astype(np.float32)
    turned = np.arange(ROW, dtype=np.float32)[:, None] * freqs[None, :]
    cosine = np.cos(turned.astype(np.float64))
    sine = np.sin(turned.astype(np.float64))
    cosine = np.concatenate([cosine, cosine, cosine, cosine], axis=1).astype(np.float32)
    sine = np.concatenate([-sine, sine, -sine, sine], axis=1).astype(np.float32)
    parts = []
    for table in (cosine, sine):
        high = table.astype(jnp.bfloat16)
        low = (table - high.astype(np.float32)).astype(jnp.bfloat16)
        parts += [high, low]
    return np.concatenate(parts, axis=1)


def swap_halves(block):
    lane = iota(block.shape, 1)
    return jnp.where(lane % HD < HD // 2, pltpu.roll(block, 96, 1), pltpu.roll(block, 32, 1))


def bounds_of(lens_ref, row):
    ends, total = [], jnp.int32(0)
    for k in range(DOCS_ROW):
        total = total + lens_ref[row, k]
        ends.append(total)
    return ends


def segment_of(spot, ends):
    seg = jnp.zeros_like(spot)
    for end in ends:
        seg = seg + (spot >= end).astype(jnp.int32)
    return seg


def norm_rows(values):
    mean = jnp.mean(values, axis=1, keepdims=True)
    centred = values - mean
    spread = jnp.mean(centred * centred, axis=1, keepdims=True)
    rstd = lax.rsqrt(spread + EPS_LAYER)
    return centred * rstd, rstd


def norm_back(d_out, xhat, rstd, gain):
    scaled = d_out * gain
    first = jnp.mean(scaled, axis=1, keepdims=True)
    second = jnp.mean(scaled * xhat, axis=1, keepdims=True)
    return rstd * (scaled - first - xhat * second)


def col_sum(values):
    return jnp.sum(values, axis=0, keepdims=True)


def fetch(pairs, sems):
    copies = [pltpu.make_async_copy(src, dst, sems.at[k]) for k, (src, dst) in enumerate(pairs)]
    for copy in copies:
        copy.start()
    return copies


KEPT = (
    ((ROW, 3 * D), BF16),
    ((ROW, 256), F32),
    ((HEADS, ROW, ROW), BF16),
    ((ROW, D), BF16),
    ((ROW, D), F32),
    ((ROW, 128), F32),
    ((ROW, FF), BF16),
    ((ROW, FF), BF16),
    ((ROW, D), F32),
    ((ROW, 128), F32),
    ((8, D), F32),
)


def encoder_forward(
    where_ref, lens_ref, labels_ref, table_hbm, x_hbm, wqkv_hbm, bqkv_hbm, wout_hbm, bout_hbm,
    g1_hbm, s1_hbm, wup_hbm, bup_hbm, wdown_hbm, bdown_hbm, g2_hbm, s2_hbm, wproj_hbm,
    vec_ref, qkv_hbm, rope_hbm, probs_hbm, mixed_hbm, xh1_hbm, rs1_hbm, act_hbm, slope_hbm,
    xh2_hbm, rs2_hbm, affine_hbm,
    qkv_ref, rope_ref, probs_ref, mixed_ref, xh1_ref, rs1_ref, act_ref, slope_ref,
    xh2_ref, rs2_ref, affine_ref, out_sems,
    table_ref, x_ref, wqkv_ref, bqkv_ref, wout_ref, bout_ref, g1_ref, s1_ref, wup_ref, bup_ref,
    wdown_ref, bdown_ref, g2_ref, s2_ref, wproj_ref, sems,
):
    copies = fetch(
        (
            (table_hbm, table_ref), (x_hbm, x_ref), (wqkv_hbm, wqkv_ref), (bqkv_hbm, bqkv_ref),
            (wout_hbm, wout_ref), (bout_hbm, bout_ref), (g1_hbm, g1_ref), (s1_hbm, s1_ref),
            (bup_hbm, bup_ref), (bdown_hbm, bdown_ref), (g2_hbm, g2_ref), (s2_hbm, s2_ref),
            (wup_hbm, wup_ref), (wdown_hbm, wdown_ref), (wproj_hbm, wproj_ref),
        ),
        sems,
    )
    kept = []

    def keep(src, dst):
        copy = pltpu.make_async_copy(src, dst, out_sems.at[len(kept)])
        copy.start()
        kept.append(copy)

    me, is_query = where_ref[0], where_ref[1] == 0
    ends = bounds_of(lens_ref, me)

    def layout(spot):
        seg_doc = segment_of(spot, ends)
        start_doc = jnp.zeros_like(spot)
        for k in range(DOCS_ROW):
            start_doc = jnp.where(seg_doc == k + 1, ends[k], start_doc)
        seg_query = spot // QLEN
        seg = jnp.where(is_query, seg_query, seg_doc)
        start = jnp.where(is_query, seg_query * QLEN, start_doc)
        return seg, start

    shape = (ROW, ROW)
    seg_q, start_q = layout(iota(shape, 0))
    seg_k, _ = layout(iota(shape, 1))
    same = seg_q == seg_k
    onehot = (iota(shape, 1) == iota(shape, 0) - start_q).astype(F32).astype(BF16)
    for copy in copies[:4]:
        copy.wait()
    turned = mm(onehot, table_ref[...])
    cosine = turned[:, :128] + turned[:, 128:256]
    sine = turned[:, 256:384] + turned[:, 384:]
    rope_ref[:, :128] = cosine
    rope_ref[:, 128:] = sine
    keep(rope_ref, rope_hbm)

    x = x_ref[...]
    joined = mm(x, wqkv_ref[...]) + bqkv_ref[...].astype(F32)
    for g in range(2 * D // 128):
        block = joined[:, g * 128 : (g + 1) * 128]
        qkv_ref[:, g * 128 : (g + 1) * 128] = (
            block * cosine + swap_halves(block) * sine
        ).astype(BF16)
    qkv_ref[:, 2 * D :] = joined[:, 2 * D :].astype(BF16)
    keep(qkv_ref, qkv_hbm)

    low_half = iota((ROW, 128), 1) < HD
    for g in range(HEADS // 2):
        q_g = qkv_ref[:, g * 128 : (g + 1) * 128]
        k_g = qkv_ref[:, D + g * 128 : D + (g + 1) * 128]
        v_g = qkv_ref[:, 2 * D + g * 128 : 2 * D + (g + 1) * 128]
        outs = []
        for h in range(2):
            pick = low_half if h == 0 else jnp.logical_not(low_half)
            scores = mm_nt(jnp.where(pick, q_g, jnp.zeros_like(q_g)), k_g) * (1.0 / math.sqrt(HD))
            scores = jnp.where(same, scores, -1e30)
            top = jnp.max(scores, axis=1, keepdims=True)
            exps = jnp.exp(scores - top)
            probs = (exps / jnp.sum(exps, axis=1, keepdims=True)).astype(BF16)
            probs_ref[2 * g + h] = probs
            outs.append(mm(probs, v_g))
        mixed_ref[:, g * 128 : (g + 1) * 128] = jnp.where(low_half, outs[0], outs[1]).astype(BF16)

    keep(probs_ref, probs_hbm)
    keep(mixed_ref, mixed_hbm)
    for copy in copies[4:12]:
        copy.wait()
    for k, ref in enumerate((g1_ref, s1_ref, g2_ref, s2_ref)):
        affine_ref[k : k + 1, :] = ref[...].astype(F32)
    affine_ref[4:, :] = jnp.zeros((4, D), F32)
    keep(affine_ref, affine_hbm)
    attended = mm(mixed_ref[...], wout_ref[...]) + bout_ref[...].astype(F32)
    xhat, rstd = norm_rows(x.astype(F32) + attended)
    xh1_ref[...] = xhat
    rs1_ref[...] = jnp.broadcast_to(rstd, (ROW, 128))
    keep(xh1_ref, xh1_hbm)
    keep(rs1_ref, rs1_hbm)
    first = xhat * g1_ref[...].astype(F32) + s1_ref[...].astype(F32)
    first_low = first.astype(BF16)
    branch = bdown_ref[...].astype(F32) + first
    step = 512
    for copy in copies[12:]:
        copy.wait()
    for c in range(FF // step):
        cols = slice(c * step, (c + 1) * step)
        inner = mm(first_low, wup_ref[:, cols]) + bup_ref[:, cols].astype(F32)
        gate = 0.5 + 0.5 * lax.erf(inner * math.sqrt(0.5))
        bell = jnp.exp2(inner * inner * (-0.5 * LOG2E)) * (1.0 / math.sqrt(2.0 * math.pi))
        act = (inner * gate).astype(BF16)
        act_ref[:, cols] = act
        slope_ref[:, cols] = (gate + inner * bell).astype(BF16)
        keep(act_ref.at[:, cols], act_hbm.at[:, cols])
        keep(slope_ref.at[:, cols], slope_hbm.at[:, cols])
        branch = branch + mm(act, wdown_ref[cols, :])
    xhat, rstd = norm_rows(branch)
    xh2_ref[...] = xhat
    rs2_ref[...] = jnp.broadcast_to(rstd, (ROW, 128))
    keep(xh2_ref, xh2_hbm)
    keep(rs2_ref, rs2_hbm)
    second = xhat * g2_ref[...].astype(F32) + s2_ref[...].astype(F32)
    vec_ref[:ROW, :] = mm(second.astype(BF16), wproj_ref[...]).astype(BF16)
    line = iota((EXT, PROJ), 0)
    tag = jnp.zeros((EXT, PROJ), jnp.int32)
    for k in range(labels_ref.shape[0]):
        label = labels_ref[k]
        tag = jnp.where(line == k, label >> 6, tag)
        tag = jnp.where(line == k + 8, label & 63, tag)
    vec_ref[ROW:, :] = tag.astype(F32).astype(BF16)
    for copy in kept:
        copy.wait()


def prefix_norms(values, axis):
    place = iota(values.shape, axis)
    squared = values * values
    sums = [
        jnp.sum(jnp.where(place < cut, squared, 0.0), axis=axis, keepdims=True) for cut in RANGES
    ]
    return [lax.rsqrt(s + EPS_NORM) for s in sums]


def load_queries(near_ref, far_ref):
    span = ROW + EXT
    rows = []
    for ref in (near_ref, far_ref):
        for k in range(ref.shape[0] // span):
            rows.append(ref[k * span : k * span + ROW, :])
    return jnp.concatenate(rows, axis=0).astype(F32)


def unit_queries(queries, scale):
    lane = iota(queries.shape, 1)
    inverse = prefix_norms(queries, 1)
    unit = [
        jnp.where(lane < cut, queries * (inv * scale), 0.0) for cut, inv in zip(RANGES, inverse)
    ]
    return unit, inverse


def unit_docs(doc_refs, scratch_ref):
    at = 0
    for ref in doc_refs:
        for k in range(ref.shape[0] // ROW):
            scratch_ref[:, at * ROW : (at + 1) * ROW] = ref[
                k * ROW : (k + 1) * ROW, :
            ].astype(F32).T
            at += 1
    turned = scratch_ref[...]
    inverse = prefix_norms(turned, 0)
    place = iota(turned.shape, 0)
    unit = [jnp.where(place < cut, turned * inv, 0.0) for cut, inv in zip(RANGES, inverse)]
    return unit, inverse


def row_ids(base, masks, doc_rows):
    ids = []
    for p in range(doc_rows):
        offset = 0
        for k, mask in enumerate(masks):
            if (p >> k) & 1:
                offset ^= mask
        ids.append(base ^ offset)
    return ids


def doc_marks(lens_ref, ids, lanes, transposed):
    docs = len(ids) * DOCS_ROW
    shape = (lanes, ROW) if transposed else (ROW, lanes)
    spot, lane = (iota(shape, 1), iota(shape, 0)) if transposed else (iota(shape, 0), iota(shape, 1))
    marks = []
    for p, row in enumerate(ids):
        seg = segment_of(spot, bounds_of(lens_ref, row))
        local = jnp.where(seg < DOCS_ROW, seg + p * DOCS_ROW, -1 - lanes)
        marks.append(
            [(lane == local + m * docs).astype(F32).astype(BF16) for m in range(len(RANGES))]
        )
    return marks


def matching_stats(
    masks, lanes, where_ref, scale_ref, lens_ref, near_ref, far_ref, *refs
):
    doc_refs = refs[:-6]
    totals_ref, el_ref, hot_ref, stats_ref, turn_ref, unit_ref = refs[-6:]
    base, near_at = where_ref[2], where_ref[3]
    span = ROW + EXT
    queries = load_queries(near_ref, far_ref)
    count = queries.shape[0]
    unit_q, _ = unit_queries(queries, SHARPNESS * LOG2E)
    unit_q = [u.astype(BF16) for u in unit_q]
    unit_d, _ = unit_docs(doc_refs, turn_ref)
    for m in range(len(RANGES)):
        unit_ref[m] = unit_d[m].astype(BF16)
    doc_rows = turn_ref.shape[1] // ROW
    docs = doc_rows * DOCS_ROW
    ids = row_ids(base, masks, doc_rows)
    marks = doc_marks(lens_ref, ids, lanes, False)
    totals = jnp.zeros((count, lanes), F32)
    for p in range(doc_rows):
        for m in range(len(RANGES)):
            sims = mm(unit_q[m], unit_ref[m, :, p * ROW : (p + 1) * ROW])
            totals = totals + mm(jnp.exp2(sims).astype(BF16), marks[p][m])
    lane_t = iota((count, lanes), 1)
    totals = jnp.where(lane_t < len(RANGES) * docs, totals, 1.0)
    totals_ref[...] = totals
    shape = (8, lanes)
    lane = iota(shape, 1)
    length = jnp.ones(shape, jnp.int32)
    name = jnp.full(shape, -1, jnp.int32)
    for p in range(doc_rows):
        for k in range(DOCS_ROW):
            own = jnp.zeros(shape, jnp.bool_)
            for m in range(len(RANGES)):
                own = jnp.logical_or(own, lane == m * docs + p * DOCS_ROW + k)
            length = jnp.where(own, lens_ref[ids[p], k], length)
            name = jnp.where(own, ids[p] * DOCS_ROW + k, name)
    log_length = jnp.log(length.astype(F32))
    matched = (jnp.log(totals) - log_length[:1]) * (1.0 / SHARPNESS)
    per_query = jnp.sum(matched.reshape(count // QLEN, QLEN, lanes), axis=1)
    scale = jnp.exp(jnp.full(shape, scale_ref[0], F32))[:1]
    logits = per_query * (scale * (1.0 / QLEN))
    groups = count // ROW
    tags = []
    for ref in (near_ref, far_ref):
        for k in range(ref.shape[0] // span):
            high = ref[k * span + ROW : k * span + ROW + 8, :].astype(F32).astype(jnp.int32)
            low = ref[k * span + ROW + 8 : k * span + ROW + 16, :].astype(F32).astype(jnp.int32)
            tag = high * 64 + low
            tags.append(jnp.concatenate([tag] * (lanes // 128), axis=1))
    tag = jnp.concatenate(tags, axis=0)
    lane_q = iota(logits.shape, 1)
    valid = lane_q < len(RANGES) * docs
    el = jnp.where(valid, jnp.exp(logits), 0.0)
    hot = jnp.where(jnp.logical_and(valid, jnp.concatenate([name] * groups, axis=0) == tag), 1.0, 0.0)
    el_ref[...] = el
    hot_ref[...] = hot
    place = iota((groups * 8, 128), 1)
    stats = jnp.zeros((groups * 8, 128), F32)
    for k, values in enumerate((el, el * logits, hot * logits)):
        for m in range(len(RANGES)):
            inside = jnp.logical_and(lane_q >= m * docs, lane_q < (m + 1) * docs)
            one = jnp.sum(jnp.where(inside, values, 0.0), axis=1, keepdims=True)
            stats = jnp.where(place == k * 3 + m, one, stats)
    for a in range(groups):
        at = pl.multiple_of((near_at ^ a) * 8, 8)
        stats_ref[pl.ds(at, 8), :] = stats[a * 8 : (a + 1) * 8, :]


def matching_back(
    masks, lanes, total_queries, where_ref, scale_ref, lens_ref, totals_ref, el_ref, hot_ref,
    own_ref, over_y, over_x, over_both, unitq_ref, qt_ref, invq_ref, unit_ref, invd_ref, *refs
):
    dq_ref, far_ref, keep_ref, send_ref, loss_ref, dot_ref, dt_ref, stats_ref = refs[-8:]
    base, near_at = where_ref[2], where_ref[3]
    temper = SHARPNESS * LOG2E
    count = unitq_ref.shape[1]
    inv_q = [invq_ref[:, m : m + 1] for m in range(len(RANGES))]
    inv_d = [invd_ref[m : m + 1, :] for m in range(len(RANGES))]
    unit_q = [unitq_ref[m] for m in range(len(RANGES))]
    doc_rows = unit_ref.shape[2] // ROW
    docs = doc_rows * DOCS_ROW
    ids = row_ids(base, masks, doc_rows)
    marks = doc_marks(lens_ref, ids, lanes, True)
    groups = count // ROW
    odd_y, odd_x = (near_at & 1) == 1, where_ref[1] == 1
    parts = [own_ref[...], over_y[...], over_x[...], over_both[...]]
    parts = [jnp.where(odd_y, a, b) for a, b in ((parts[1], parts[0]), (parts[0], parts[1]),
                                                  (parts[3], parts[2]), (parts[2], parts[3]))]
    parts = [jnp.where(odd_x, parts[(k + 2) % 4], parts[k]) for k in range(4)]
    stats_ref[...] = (parts[0] + parts[1]) + (parts[2] + parts[3])
    rows = []
    for a in range(groups):
        at = pl.multiple_of((near_at ^ a) * 8, 8)
        rows.append(stats_ref[pl.ds(at, 8), :])
    stats = jnp.concatenate(rows, axis=0)
    place = iota(stats.shape, 1)

    def column(k):
        return jnp.sum(jnp.where(place == k, stats, 0.0), axis=1, keepdims=True)

    shape = (groups * 8, lanes)
    lane_q = iota(shape, 1)
    sums = jnp.ones(shape, F32)
    loss = jnp.zeros((groups * 8, 1), F32)
    moved = jnp.zeros((groups * 8, 1), F32)
    for m in range(len(RANGES)):
        whole, weighted, picked = column(m), column(3 + m), column(6 + m)
        inside = jnp.logical_and(lane_q >= m * docs, lane_q < (m + 1) * docs)
        sums = jnp.where(inside, whole, sums)
        loss = loss + (jnp.log(whole) - picked)
        moved = moved + (weighted / whole - picked)
    line = iota((8, 128), 0)
    loss = jnp.where(
        line == 0,
        jnp.sum(loss, axis=0, keepdims=True) * (1.0 / total_queries),
        jnp.where(line == 1, jnp.sum(moved, axis=0, keepdims=True) * (1.0 / total_queries), 0.0),
    )
    loss_ref[...] = loss
    scale = jnp.exp(jnp.full((8, lanes), scale_ref[0], F32))[:1]
    coeff = (el_ref[...] / sums - hot_ref[...]) * (scale * (1.0 / (QLEN * total_queries)))
    coeff = jnp.broadcast_to(coeff[:, None, :], (groups * 8, QLEN, lanes)).reshape(count, lanes)
    ratio = coeff / totals_ref[...]
    ratio_high = ratio.astype(BF16)
    ratio_low = (ratio - ratio_high.astype(F32)).astype(BF16)
    ratio = jnp.concatenate([ratio_high, ratio_low], axis=1)
    for m in range(len(RANGES)):
        grad = jnp.zeros((count, PROJ), F32)
        for p in range(doc_rows):
            block = unit_ref[m, :, p * ROW : (p + 1) * ROW]
            mark = marks[p][m]
            if len(refs) > 8:
                exps = refs[0][m, :, p * ROW : (p + 1) * ROW].astype(F32)
            else:
                exps = jnp.exp2(mm(unit_q[m], block))
            d_sims = (exps * mm(ratio, jnp.concatenate([mark, mark], axis=0))).astype(BF16)
            grad = grad + mm_nt(d_sims, block)
            dt_ref[m, :, p * ROW : (p + 1) * ROW] = mm(qt_ref[m], d_sims)
        unit = unit_q[m].astype(F32) * (1.0 / temper)
        along = jnp.sum(grad * unit, axis=1, keepdims=True)
        part = inv_q[m] * (grad - unit * along)
        if m == 0:
            dot_ref[...] = part
        else:
            dot_ref[...] += part
    dq_ref[...] = dot_ref[: count // 2, :].astype(BF16)
    far_ref[...] = dot_ref[count // 2 :, :].astype(BF16)
    total = jnp.zeros(unit_ref.shape[1:], F32)
    for m in range(len(RANGES)):
        grad = dt_ref[m] * (1.0 / temper)
        unit = unit_ref[m].astype(F32)
        along = jnp.sum(grad * unit, axis=0, keepdims=True)
        total = total + inv_d[m] * (grad - unit * along)
    for p in range(doc_rows):
        ref, at = (keep_ref, p) if p < doc_rows // 2 else (send_ref, p - doc_rows // 2)
        ref[at * ROW : (at + 1) * ROW, :] = total[:, p * ROW : (p + 1) * ROW].T.astype(BF16)


def matching_ready(near_ref, far_ref, *refs):
    doc_refs = refs[:-6] if refs[-2].shape[0] != len(RANGES) else refs[:-7]
    unitq_ref, qt_ref, invq_ref, unit_ref, invd_ref = refs[len(doc_refs) : len(doc_refs) + 5]
    turn_ref = refs[-1]
    queries = load_queries(near_ref, far_ref)
    unit_q, inv_q = unit_queries(queries, SHARPNESS * LOG2E)
    unit_d, inv_d = unit_docs(doc_refs, turn_ref)
    lane = iota(invq_ref.shape, 1)
    columns = jnp.zeros(invq_ref.shape, F32)
    invd_ref[...] = jnp.zeros_like(invd_ref)
    for m in range(len(RANGES)):
        unitq_ref[m] = unit_q[m].astype(BF16)
        unit_ref[m] = unit_d[m].astype(BF16)
        qt_ref[m] = unit_q[m].T.astype(BF16)
        columns = jnp.where(lane == m, inv_q[m], columns)
        invd_ref[m : m + 1, :] = inv_d[m]
        if len(refs) - len(doc_refs) > 6:
            refs[-2][m] = jnp.exp2(mm(unitq_ref[m], unit_ref[m])).astype(BF16)
    invq_ref[...] = columns


def two_sums(dq_ref, got_ref, dd_ref, got_dd_ref, sum_dq, sum_dd):
    sum_dq[...] = (dq_ref[...].astype(F32) + got_ref[...].astype(F32)).astype(BF16)
    sum_dd[...] = (dd_ref[...].astype(F32) + got_dd_ref[...].astype(F32)).astype(BF16)


DIGITS = 10
POINT = 20


def digits_of(value):
    fixed = (value * float(1 << POINT)).astype(jnp.int32)
    size = jnp.abs(fixed)
    lane = iota(value.shape, 1)
    digits = jnp.zeros(value.shape, jnp.int32)
    for k in range(DIGITS):
        digits = jnp.where(lane == k, (size >> (3 * k)) & 7, digits)
    return jnp.where(fixed < 0, -digits, digits).astype(F32)


def value_of(digits):
    lane = iota(digits.shape, 1)
    half = DIGITS // 2
    weight = jnp.zeros(digits.shape, F32)
    for k in range(half):
        weight = jnp.where(jnp.logical_or(lane == k, lane == k + half), float(8**k), weight)
    low = jnp.sum(jnp.where(lane < half, digits * weight, 0.0))
    high = jnp.sum(jnp.where(jnp.logical_and(lane >= half, lane < DIGITS), digits * weight, 0.0))
    return (high * float(8**half) + low) * (1.0 / (1 << POINT))


def turn(core, place, block):
    return jnp.where(core == 0, place - block, block - place) & (RING - 1)


def block_at(core, place, distance):
    return jnp.where(core == 0, place - distance, place + distance) & (RING - 1)


def store_block(keep_ref, send_ref, rows, block, places, value):
    core, place = places
    mine = core == block // RING
    at = turn(block // RING, place, block % RING)

    @pl.when(mine)
    def _():
        keep_ref[at, rows, :] = value

    @pl.when(jnp.logical_not(mine))
    def _():
        send_ref[at, rows, :] = value


def feed_back(
    where_ref, dq_ref, dd_ref, got_ref, xh2_ref, rs2_ref, affine_ref, wproj_ref, wup_ref, xh1_ref,
    wdown_hbm, slope_hbm, act_hbm,
    keep_ref, send_ref, tail_keep, tail_send, dfirst_ref, gproj_ref, small_ref,
    dinner_ref, wdown_ref, slope_ref, act_ref, sems,
):
    step = 512
    spans = [slice(c * step, (c + 1) * step) for c in range(FF // step)]
    copies = fetch(
        [
            pair
            for span in spans
            for pair in (
                (wdown_hbm.at[span, :], wdown_ref.at[span, :]),
                (slope_hbm.at[:, span], slope_ref.at[:, span]),
                (act_hbm.at[:, span], act_ref.at[:, span]),
            )
        ],
        sems,
    )
    g1, s1, g2, s2 = [affine_ref[k : k + 1, :] for k in range(4)]
    is_query, docs_there = where_ref[1] == 0, where_ref[4] == 0
    places = (where_ref[5], where_ref[6])
    got = got_ref[...].astype(F32)
    d_vec = jnp.where(
        is_query,
        dq_ref[...].astype(F32) + got,
        jnp.where(docs_there, got, dd_ref[...].astype(F32)),
    )
    d_proj = d_vec.astype(BF16)
    xhat = xh2_ref[...]
    gain = g2
    second = (xhat * gain + s2).astype(BF16)
    gproj_ref[...] = mm_tn(second, d_proj)
    d_second = mm_nt(d_proj, wproj_ref[...])
    small_ref[...] = jnp.zeros_like(small_ref)
    small_ref[5:6, :] = col_sum(d_second * xhat)
    small_ref[6:7, :] = col_sum(d_second)
    d_sum = norm_back(d_second, xhat, rs2_ref[:, :1], gain)
    d_branch = d_sum.astype(BF16)
    small_ref[4:5, :] = col_sum(d_branch.astype(F32))
    d_first = d_sum
    for c in range(FF // step):
        cols = spans[c]
        for copy in copies[3 * c : 3 * c + 3]:
            copy.wait()
        d_act = mm_nt(d_branch, wdown_ref[cols, :])
        d_inner = (d_act * slope_ref[:, cols].astype(F32)).astype(BF16)
        dinner_ref[:, cols] = d_inner
        small_ref[c : c + 1, :] = col_sum(d_inner.astype(F32))
        grad = mm_tn(act_ref[:, cols], d_branch).astype(BF16)
        for k in range(step // DOWN):
            store_block(
                keep_ref, send_ref, slice(0, DOWN), c * (step // DOWN) + k, places,
                grad[k * DOWN : (k + 1) * DOWN, :],
            )
        d_first = d_first + mm_nt(d_inner, wup_ref[:, cols])
    dfirst_ref[...] = d_first
    first = (xh1_ref[...] * g1 + s1).astype(BF16)
    for c in range(FF // step):
        cols = slice(c * step, (c + 1) * step)
        grad = mm_tn(first, dinner_ref[:, cols]).astype(BF16)
        for k in range(D // DOWN):
            block = c * (D // DOWN) + k
            start = k * DOWN
            store_block(
                keep_ref, send_ref, slice(DOWN, FIRST), block, places, grad[start : start + HEAD, :]
            )
            store_block(
                tail_keep, tail_send, slice(0, TAIL), block, places,
                grad[start + HEAD : start + DOWN, :],
            )


def attend_back(
    where_ref, dfirst_ref, gproj_ref, small_ref, loss_ref, tail_keep, tail_send, xh1_ref, rs1_ref, affine_ref, mixed_ref, wout_ref,
    qkv_ref, probs_ref, rope_ref, x_ref, wqkv_ref,
    keep_ref, send_ref, tokens_ref, djoined_ref, rest_ref,
):
    core, place = where_ref[5], where_ref[6]
    d_first = dfirst_ref[...]
    xhat = xh1_ref[...]
    gain = affine_ref[0:1, :]
    gain_grad = col_sum(d_first * xhat)
    shift_grad = col_sum(d_first)
    d_sum = norm_back(d_first, xhat, rs1_ref[:, :1], gain)
    d_att = d_sum.astype(BF16)
    bias_out = col_sum(d_att.astype(F32))
    rest_ref[3 * D : 4 * D, :] = mm_tn(mixed_ref[...], d_att)
    d_mixed = mm_nt(d_att, wout_ref[...]).astype(BF16)
    cosine, sine = rope_ref[:, :128], rope_ref[:, 128:]
    low_half = iota((ROW, 128), 1) < HD

    def unrotate(values):
        values = values * (1.0 / math.sqrt(HD))
        return (values * cosine - swap_halves(values) * sine).astype(BF16)

    for g in range(HEADS // 2):
        span = slice(g * 128, (g + 1) * 128)
        q_g = qkv_ref[:, g * 128 : (g + 1) * 128]
        k_g = qkv_ref[:, D + g * 128 : D + (g + 1) * 128]
        v_g = qkv_ref[:, 2 * D + g * 128 : 2 * D + (g + 1) * 128]
        m_g = d_mixed[:, span]
        d_q = jnp.zeros((ROW, 128), F32)
        d_k = jnp.zeros((ROW, 128), F32)
        d_v = jnp.zeros((ROW, 128), F32)
        zero = jnp.zeros((ROW, 128), BF16)
        for h in range(2):
            pick = low_half if h == 0 else jnp.logical_not(low_half)
            probs_low = probs_ref[2 * g + h]
            probs = probs_low.astype(F32)
            m_h = jnp.where(pick, m_g, zero)
            d_probs = mm_nt(m_h, v_g)
            d_v = d_v + mm_tn(probs_low, m_h)
            inner = jnp.sum(d_probs * probs, axis=1, keepdims=True)
            d_scores = (probs * (d_probs - inner)).astype(BF16)
            d_q = d_q + mm(d_scores, jnp.where(pick, k_g, zero))
            d_k = d_k + mm_tn(d_scores, jnp.where(pick, q_g, zero))
        djoined_ref[:, g * 128 : (g + 1) * 128] = unrotate(d_q)
        djoined_ref[:, D + g * 128 : D + (g + 1) * 128] = unrotate(d_k)
        djoined_ref[:, 2 * D + g * 128 : 2 * D + (g + 1) * 128] = d_v.astype(BF16)
    x = x_ref[...]
    tokens = d_sum
    rest_ref[4 * D :, :] = jnp.zeros((8 * 2 * RING, D), F32)
    smalls = []
    for c in range(3):
        cols = slice(c * D, (c + 1) * D)
        d_part = djoined_ref[:, cols]
        rest_ref[c * D : (c + 1) * D, :] = mm_tn(x, d_part)
        smalls.append(col_sum(d_part.astype(F32)))
        tokens = tokens + mm_nt(d_part, wqkv_ref[:, cols])
    tokens_ref[...] = tokens
    smalls += [bias_out, gain_grad, shift_grad] + [small_ref[k : k + 1, :] for k in range(7)]
    counted = jnp.where((where_ref[0] & 3) == 0, 1.0, 0.0)
    lines = [digits_of(loss_ref[k : k + 1, :]) * counted for k in range(2)]
    smalls.append(jnp.concatenate(lines + [jnp.zeros((1, D - 256), F32)], axis=1))
    for k, row in enumerate(smalls):
        rest_ref[4 * D + 8 * k : 4 * D + 8 * k + 1, :] = row
    for k in range(RING):
        for ref, tail_ref, owner in (
            (keep_ref, tail_keep, core), (send_ref, tail_send, 1 - core)
        ):
            block = owner * RING + block_at(owner, place, k)
            parts = []
            for c in range(4):
                start = pl.multiple_of(c * D + block * SHARE, SHARE)
                parts.append(rest_ref[pl.ds(start, SHARE), :])
            row = pl.multiple_of(block * SHARE, SHARE)
            parts.append(
                jnp.concatenate(
                    [gproj_ref[pl.ds(row + 8 * j, 8), :] for j in range(SHARE // 8)], axis=1
                )
            )
            parts.append(rest_ref[pl.ds(pl.multiple_of(4 * D + block * 8, 8), 8), :])
            ref[k, : REST // 16, :] = jnp.concatenate(parts, axis=0).astype(BF16)
            ref[k, REST // 16 :, :] = tail_ref[k]


def spread(jobs, last, where_ref, *refs):
    core, place = where_ref[5], where_ref[6]
    halves = refs[: 2 * len(jobs)]
    wide_one, wide_two, wide_qkv, wide_proj, small_ref, sems = refs[-6:]
    outs = refs[-21:-6] if last else refs[-11:-6]
    down_hbm, up_hbm, qkv_hbm, out_hbm, proj_hbm = outs[:5]
    copies = []

    def move(src, dst):
        copy = pltpu.make_async_copy(src, dst, sems.at[len(copies)])
        copy.start()
        copies.append(copy)

    at = 0
    for job, (mine, group) in enumerate(jobs):
        owner = core if mine else 1 - core
        one_ref, two_ref = halves[2 * job : 2 * job + 2]
        for p, distance in enumerate(GROUPS[group]):
            block = owner * RING + block_at(owner, place, distance)
            wide_one[at] = one_ref[p].astype(F32)
            rows = pl.ds(pl.multiple_of(block * DOWN, DOWN), DOWN)
            move(wide_one.at[at, :DOWN, :], down_hbm.at[rows, :])
            start = (block % (D // DOWN)) * DOWN
            columns = pl.ds(pl.multiple_of((block // (D // DOWN)) * D, D), D)
            rows = pl.ds(pl.multiple_of(start, DOWN), HEAD)
            move(wide_one.at[at, DOWN:, :], up_hbm.at[rows, columns])
            wide = two_ref[p].astype(F32)
            wide_two[at, :SHARE, :] = wide[3 * SHARE : 4 * SHARE, :]
            wide_two[at, SHARE:, :] = wide[REST // 16 :, :]
            rows = pl.ds(pl.multiple_of(start + HEAD, 16), TAIL)
            move(wide_two.at[at, SHARE:, :], up_hbm.at[rows, columns])
            rows = pl.ds(pl.multiple_of(block * SHARE, SHARE), SHARE)
            for c in range(3):
                wide_qkv[at, :, c * D : (c + 1) * D] = wide[c * SHARE : (c + 1) * SHARE, :]
            move(wide_qkv.at[at], qkv_hbm.at[rows, :])
            move(wide_two.at[at, :SHARE, :], out_hbm.at[rows, :])
            for j in range(SHARE // 8):
                wide_proj[at, 8 * j : 8 * j + 8, :] = wide[
                    4 * SHARE : 4 * SHARE + 8, j * PROJ : (j + 1) * PROJ
                ]
            move(wide_proj.at[at], proj_hbm.at[rows, :])
            at += 1
    if last:
        sources = refs[2 * len(jobs) : 2 * len(jobs) + 2 * len(GROUPS)]
        for k, ref in enumerate(sources):
            owner = core if k < len(GROUPS) else 1 - core
            for p, distance in enumerate(GROUPS[k % len(GROUPS)]):
                block = owner * RING + block_at(owner, place, distance)
                line = ref[p, 4 * SHARE : 4 * SHARE + 16, :].astype(F32)[8:, :]
                small_ref[pl.ds(pl.multiple_of(block * 8, 8), 8), :] = line
        rows = [small_ref[8 * k : 8 * k + 1, :] for k in range(14)]
        bqkv_ref, bout_ref, g1_ref, s1_ref, bup_ref, bdown_ref, g2_ref, s2_ref = outs[5:13]
        for k, ref in enumerate(outs[13:]):
            ref[0] = value_of(rows[13][:, k * 128 : (k + 1) * 128])
        for c in range(3):
            bqkv_ref[:, c * D : (c + 1) * D] = rows[c]
        bout_ref[...] = rows[3]
        g1_ref[...] = rows[4]
        s1_ref[...] = rows[5]
        for c in range(4):
            bup_ref[:, c * D : (c + 1) * D] = rows[6 + c]
        bdown_ref[...] = rows[10]
        g2_ref[...] = rows[11]
        s2_ref[...] = rows[12]
    for copy in copies:
        copy.wait()


def spread_call(jobs, where, halves, outs, others):
    last = len(others) > 0
    shapes = ((FF, D), (D, FF), (D, 3 * D), (D, D), (D, PROJ))
    widths = (3 * D, D, D, D, FF, D, D, D) if last else ()
    args = [where, *halves, *others, *outs]
    count = sum(len(GROUPS[group]) for _, group in jobs)
    before = 1 + len(halves) + len(others)
    return call(
        partial(spread, jobs, last),
        args,
        [SMEM] + [VMEM] * (before - 1) + [HBM] * len(outs),
        [pltpu.HBM(shape, F32) for shape in shapes]
        + [shape_of((1, width)) for width in widths]
        + [shape_of((1,))] * (2 * last),
        [
            pltpu.VMEM((count, FIRST, D), F32),
            pltpu.VMEM((count, SHARE + TAIL, D), F32),
            pltpu.VMEM((count, SHARE, 3 * D), F32),
            pltpu.VMEM((count, SHARE, PROJ), F32),
            pltpu.VMEM((16 * RING, D), F32),
            pltpu.SemaphoreType.DMA((6 * count,)),
        ],
        out_specs=[HBM] * 5 + [VMEM] * len(widths) + [SMEM] * (2 * last),
        aliases={before + k: k for k in range(len(outs))},
        cost=SPREAD_COST,
        room=14,
    )


def shape_of(shape, dtype=F32):
    return jax.ShapeDtypeStruct(tuple(shape), dtype)


def call(kernel, args, specs, outs, scratch=(), room=24, out_specs=None, aliases={}, cost=10**7):
    spaces = {id(HBM): pltpu.HBM, id(HELD): pltpu.VMEM}
    args = [
        pltpu.with_memory_space_constraint(arg, spaces[id(spec)]) if id(spec) in spaces else arg
        for arg, spec in zip(args, specs)
    ]
    return pl.pallas_call(
        kernel,
        out_shape=outs,
        in_specs=specs,
        out_specs=out_specs or [VMEM] * len(outs),
        scratch_shapes=list(scratch),
        input_output_aliases=aliases,
        compiler_params=pltpu.CompilerParams(vmem_limit_bytes=room * MIB),
        cost_estimate=pl.CostEstimate(
            flops=10 * cost, bytes_accessed=cost, transcendentals=0
        ),
    )(*args)


def spread_half_call(where, halves, near=None, outs=()):
    mine = near is None
    args = [where, *halves] + ([] if mine else [near, *outs])
    specs = [SMEM] + [VMEM] * (3 if mine else 4) + [HBM] * len(outs)
    shapes = ((FF, D), (D, FF), (D, 3 * D), (D, D), (D, PROJ))
    widths = () if mine else (3 * D, D, D, D, FF, D, D, D)
    return call(
        partial(spread_half, mine),
        args,
        specs,
        [pltpu.HBM(shape, F32) for shape in shapes] + [shape_of((1, width)) for width in widths],
        [
            pltpu.VMEM((RING, FF // (2 * RING), D), F32),
            pltpu.VMEM((RING, FF // (2 * RING), D), F32),
            pltpu.VMEM((RING, 4 * SHARE, D), F32),
            pltpu.VMEM((RING, SHARE, PROJ), F32),
            pltpu.SemaphoreType.DMA((7 * RING,)),
        ],
        out_specs=[HBM] * 5 + [VMEM] * len(widths) + [SMEM] * (2 * last),
        aliases={} if mine else {5 + k: k for k in range(5)},
        room=14,
    )


def swapped(value, mask, axis="dp"):
    size = lax.axis_size(axis)
    return lax.ppermute(value, axis, [(k, k ^ mask) for k in range(size)])


def added(a, b):
    return (a.astype(F32) + b.astype(F32)).astype(BF16)


def join_blocks(*refs):
    for k, ref in enumerate(refs[:-1]):
        refs[-1][k] = ref[0]


def ring_swap(value, onward):
    size = lax.axis_size("dp")
    pairs = []
    for k in range(size):
        at = CIRCLE.index((k >> 1) % RING)
        to = CIRCLE[(at + (1 if (k % 2 == 0) == onward else -1)) % RING]
        pairs.append((k, (k & ~(2 * RING - 1)) | (to << 1) | (k & 1)))
    return lax.ppermute(value, "dp", pairs)


def add_blocks(places, *refs):
    count = len(places)
    held_ref = refs[count] if any(place is not None for place in places) else None
    for k, place in enumerate(places):
        value = refs[k][...]
        if place is not None:
            value = (value.astype(F32) + held_ref[place : place + 1].astype(F32)).astype(BF16)
        refs[-count + k][...] = value


def first_blocks(places, keep_ref, pair_ref, *outs):
    for ref, k in zip(outs, places):
        ref[0] = (keep_ref[k].astype(F32) + pair_ref[k].astype(F32)).astype(BF16)


class Summed:
    def __init__(self, keep, send, others):
        self.keep, self.others, self.hop = keep, others, 0
        self.pair = swapped(send, 1)
        self.sent, self.blocks, self.near, self.far = [], {}, [], []

    def blocks_call(self, blocks, places, held):
        return call(
            partial(add_blocks, places),
            (*blocks, *held),
            [VMEM] * (len(blocks) + len(held)),
            [shape_of(block.shape, BF16) for block in blocks],
            room=8,
            cost=STEP_COST,
        )

    def open(self, after):
        keep, pair, _ = lax.optimization_barrier((self.keep, self.pair, after))
        half = RING // 2
        shape = (1, *keep.shape[1:])
        first, second = call(
            partial(first_blocks, (half, half - 1)),
            (keep, pair),
            [VMEM] * 2,
            [shape_of(shape, BF16)] * 2,
            room=8,
            cost=STEP_COST,
        )
        self.sent = [(first, True), (second, False)]
        return second

    def total(self, after):
        keep, _ = lax.optimization_barrier((self.keep, after))
        self.keep = added(keep, self.pair)
        return self.keep

    def step(self, after):
        half = RING // 2
        self.hop += 1
        hop = self.hop
        *got, _ = lax.optimization_barrier((*[ring_swap(*one) for one in self.sent], after))
        if hop < half:
            out = self.blocks_call(got, (half + hop, half - 1 - hop), [self.keep])
            self.part = out[1]
        elif hop == half:
            (own,) = self.blocks_call(got, (0,), [self.part])
            for mask in self.others:
                own = added(own, swapped(own, mask))
            self.blocks[0] = own
            out = [own, own]
        else:
            out = self.blocks_call(got, (None,) * len(got), [])
            hop -= half
            self.blocks[hop] = out[0]
            if hop < half:
                self.blocks[RING - hop] = out[1]
        if hop == half - 1:
            self.sent = [(out[0], True)]
        elif self.hop < 2 * half:
            self.sent = [(out[0], True), (out[1], False)]
        return out[0]

    def share(self, group, after):
        *blocks, _ = lax.optimization_barrier((*[self.blocks[k] for k in GROUPS[group]], after))
        shape = (len(blocks), *blocks[0].shape[1:])
        self.near += call(
            join_blocks, blocks, [VMEM] * len(blocks), [shape_of(shape, BF16)], room=8, cost=0
        )
        self.far.append(swapped(self.near[-1], 1))
        return self.near[-1]


def per_device(
    tokens, qkv_weight, qkv_bias, out_weight, out_bias, first_gain, first_shift, up_weight,
    up_bias, down_weight, down_bias, second_gain, second_shift, proj_weight, log_scale,
    doc_lengths, labels,
):
    size = lax.axis_size("dp")
    bits = [1 << k for k in range(size.bit_length() - 1)]
    near_masks, doc_masks = bits[:2], bits[2:]
    top_mask, doc_masks = doc_masks[-1], doc_masks[:-1]
    others = bits[4:]
    me = lax.axis_index("dp")
    stream = lax.axis_index("stream")
    is_query = stream == 0
    has_top = (me & top_mask) != 0
    base = jnp.where(is_query, me & ~top_mask, me | top_mask)
    near_at = jnp.where((me & near_masks[1]) != 0, 1, 0) + jnp.where((me & near_masks[0]) != 0, 2, 0)
    core = me & 1
    chip = (me >> 1) % RING
    place = jnp.int32(0)
    for k, one in enumerate(CIRCLE):
        place = jnp.where(chip == one, k, place)
    where = jnp.stack(
        [me, stream, base, near_at, has_top.astype(jnp.int32), core, place, place]
    ).astype(jnp.int32)
    scale = log_scale.reshape(1)

    vec, qkv, rope, probs, mixed, xh1, rs1, act, slope, xh2, rs2, affine = call(
        encoder_forward,
        (
            where, doc_lengths, labels, jnp.asarray(rope_table()), tokens[0], qkv_weight[0], qkv_bias,
            out_weight[0], out_bias, first_gain, first_shift, up_weight[0], up_bias,
            down_weight[0], down_bias, second_gain, second_shift, proj_weight[0],
        ),
        [SMEM] * 3 + [HBM] * 15,
        [shape_of((ROW + EXT, PROJ), BF16)] + [pltpu.HBM(*kind) for kind in KEPT],
        [pltpu.VMEM(*kind) for kind in KEPT]
        + [pltpu.SemaphoreType.DMA((len(KEPT) + 6,))]
        + [
            pltpu.VMEM(shape, BF16)
            for shape in (
                (ROW, 512), (ROW, D), (D, 3 * D), (1, 3 * D), (D, D), (1, D), (1, D), (1, D), (D, FF),
                (1, FF), (FF, D), (1, D), (1, D), (1, D), (D, PROJ),
            )
        ]
        + [pltpu.SemaphoreType.DMA((15,))],
        room=40,
        out_specs=[VMEM] + [HBM] * len(KEPT),
    )

    every, other_y = range(size), near_masks[1]
    other = swapped(vec, 1, "stream")
    near = jnp.where(is_query, vec, other)
    rows = jnp.where(is_query, other, vec)[:ROW]
    moved = swapped(rows, top_mask)
    near = jnp.concatenate([near, swapped(near, other_y)], axis=0)
    rows = jnp.where(has_top == is_query, moved, rows)
    far = swapped(near, near_masks[0])
    pieces = []
    for k, mask in enumerate(doc_masks):
        pieces.append(rows)
        got = swapped(rows, mask)
        if k + 1 < len(doc_masks):
            rows = jnp.concatenate([rows, got], axis=0)
        else:
            pieces = [rows, got]
    doc_rows = sum(p.shape[0] for p in pieces) // ROW
    tokens_d = doc_rows * ROW
    tokens_q = 4 * ROW
    lanes = -(-3 * doc_rows * DOCS_ROW // 128) * 128
    total_queries = size * (ROW // QLEN)
    room = 20 if doc_rows <= 4 else 56
    totals, el, hot, stats = call(
        partial(matching_stats, doc_masks, lanes),
        (where, scale, doc_lengths, near, far, *pieces),
        [SMEM] * 3 + [VMEM] * (2 + len(pieces)),
        [
            shape_of((tokens_q, lanes)),
            shape_of((tokens_q // QLEN, lanes)),
            shape_of((tokens_q // QLEN, lanes)),
            shape_of((tokens_q // QLEN, 128)),
        ],
        [pltpu.VMEM((PROJ, tokens_d), F32), pltpu.VMEM((3, PROJ, tokens_d), BF16)],
        room=room,
    )
    small_enough = doc_rows <= 4
    ready = call(
        matching_ready,
        (near, far, *pieces),
        [VMEM] * (2 + len(pieces)),
        [
            shape_of((3, tokens_q, PROJ), BF16),
            shape_of((3, PROJ, tokens_q), BF16),
            shape_of((tokens_q, 128)),
            shape_of((3, PROJ, tokens_d), BF16),
            shape_of((8, tokens_d)),
        ]
        + [shape_of((3, tokens_q, tokens_d), BF16)] * small_enough,
        [pltpu.VMEM((PROJ, tokens_d), F32)],
        room=room,
    )
    stats = stats + swapped(stats, near_masks[0])
    over_y = swapped(stats, other_y)
    over_x = swapped(stats, 1, "stream")
    pairs = [(k * size + r, (1 - k) * size + (r ^ other_y)) for k in range(2) for r in every]
    over_both = lax.ppermute(stats, ("stream", "dp"), pairs)
    dq, dq_send, keep, send, loss = call(
        partial(matching_back, doc_masks, lanes, total_queries),
        (where, scale, doc_lengths, totals, el, hot, stats, over_y, over_x, over_both, *ready),
        [SMEM] * 3 + [VMEM] * (7 + len(ready)),
        [shape_of((tokens_q // 2, PROJ), BF16)] * 2
        + [shape_of((tokens_d // 2, PROJ), BF16)] * 2
        + [shape_of((8, 128))],
        [
            pltpu.VMEM((tokens_q, PROJ), F32),
            pltpu.VMEM((3, PROJ, tokens_d), F32),
            pltpu.VMEM((tokens_q // QLEN, 128), F32),
        ],
        room=room,
    )
    got_dq = swapped(dq_send, near_masks[0])
    for mask in reversed(doc_masks[1:]):
        total, half = added(keep, swapped(send, mask)), keep.shape[0] // 2
        keep, send = total[:half], total[half:]
    got_dd = swapped(send, doc_masks[0])
    dq, dd = call(
        two_sums,
        (dq, got_dq, keep, got_dd),
        [VMEM] * 4,
        [shape_of((2 * ROW, PROJ), BF16), shape_of((ROW, PROJ), BF16)],
        room=8,
    )
    dq = added(dq[:ROW], swapped(dq[ROW:], other_y))
    dd = added(dd, swapped(dd, top_mask))
    got = swapped(jnp.where(is_query, dd, dq), 1, "stream")

    one_keep, one_send, tail_keep, tail_send, d_first, gproj, small = call(
        feed_back,
        (
            where, dq, dd, got, xh2, rs2, affine, proj_weight[0], up_weight[0], xh1,
            down_weight[0], slope, act,
        ),
        [SMEM] + [VMEM] * 3 + [HELD] * 6 + [HBM] * 3,
        [shape_of((RING, FIRST, D), BF16)] * 2
        + [shape_of((RING, TAIL, D), BF16)] * 2
        + [shape_of((ROW, D)), shape_of((D, PROJ)), shape_of((8, D))],
        [
            pltpu.VMEM((ROW, FF), BF16),
            pltpu.VMEM((FF, D), BF16),
            pltpu.VMEM((ROW, FF), BF16),
            pltpu.VMEM((ROW, FF), BF16),
            pltpu.SemaphoreType.DMA((12,)),
        ],
        room=24,
    )
    two_keep, two_send, tokens_grad = call(
        attend_back,
        (
            where, d_first, gproj, small, loss, tail_keep, tail_send, xh1, rs1, affine, mixed, out_weight[0], qkv, probs, rope,
            tokens[0], qkv_weight[0],
        ),
        [SMEM] + [VMEM] * 6 + [HELD] * 10,
        [shape_of((RING, SECOND, D), BF16)] * 2 + [shape_of((ROW, D))],
        [
            pltpu.VMEM((ROW, 3 * D), BF16),
            pltpu.VMEM((4 * D + 16 * RING, D), F32),
        ],
        room=24,
    )
    one, two = [
        Summed(keep, send, others) for keep, send in ((one_keep, one_send), (two_keep, two_send))
    ]
    token, outs = tokens_grad, ()
    for event in ORDER:
        kind, k, *group = event
        if kind == "spread":
            jobs = event[1]
            halves = [
                (piece.near if mine else piece.far)[group] for mine, group in jobs for piece in (one, two)
            ]
            *halves, _ = lax.optimization_barrier((*halves, token))
            others = [*two.near, *two.far] if event == ORDER[-1] else []
            outs = spread_call(jobs, where, halves, outs[:5], others)
            token = outs[0]
            continue
        piece = (one, two)[k]
        token = getattr(piece, kind)(*group, token)
    grad_down, grad_up, grad_qkv, grad_out, grad_proj = outs[:5]
    (
        grad_bqkv, grad_bout, grad_g1, grad_s1, grad_bup, grad_bdown, grad_g2, grad_s2, loss,
        scale_grad,
    ) = outs[5:]
    return (
        loss.reshape(()),
        tokens_grad[None],
        grad_qkv[None],
        grad_bqkv,
        grad_out[None],
        grad_bout,
        grad_g1,
        grad_s1,
        grad_up[None],
        grad_bup,
        grad_down[None],
        grad_bdown,
        grad_g2,
        grad_s2,
        grad_proj[None],
        scale_grad.reshape(()),
    )


def solution(mesh):
    return jax.shard_map(
        per_device,
        mesh=mesh,
        in_specs=(
            P("stream", "dp", None),
            P("stream", None, None),
            P("stream", None),
            P("stream", None, None),
            P("stream", None),
            P("stream", None),
            P("stream", None),
            P("stream", None, None),
            P("stream", None),
            P("stream", None, None),
            P("stream", None),
            P("stream", None),
            P("stream", None),
            P("stream", None, None),
            P(),
            P(),
            P("dp"),
        ),
        out_specs=(
            P(),
            P("stream", "dp", None),
            P("stream", None, None),
            P("stream", None),
            P("stream", None, None),
            P("stream", None),
            P("stream", None),
            P("stream", None),
            P("stream", None, None),
            P("stream", None),
            P("stream", None, None),
            P("stream", None),
            P("stream", None),
            P("stream", None),
            P("stream", None, None),
            P(),
        ),
        check_vma=False,
    )
```

```python
from functools import partial
import math

import jax
import jax.numpy as jnp
import numpy as np
from jax import lax
from jax.experimental import pallas as pl
from jax.experimental.pallas import tpu as pltpu
from jax.sharding import PartitionSpec as P

D = 512
HEADS = 8
HD = 64
FF = 2048
PROJ = 128
QLEN = 32
DOCS_ROW = 4
ROW = 256
EXT = 16
RANGES = (64, 96, 128)

SHARPNESS = 8.0
EPS_NORM = 1e-06
EPS_LAYER = 1e-05
LOG2E = 1.4426950408889634

F32 = jnp.float32
BF16 = jnp.bfloat16
REST = 2304
SHARE = 32
DOWN = FF // 16
HEAD = 80
TAIL = DOWN - HEAD
FIRST = DOWN + HEAD
SECOND = REST // 16 + TAIL
CIRCLE = (0, 2, 4, 6, 7, 5, 3, 1)
RING = len(CIRCLE)
AHEAD = (RING // 2, RING // 2 - 1)
LATER = tuple(k for k in range(RING) if k not in AHEAD)
GROUPS = ((0, 1, 2, 3, 5, 6, 7), (4,))
STEP_COST = 3 * 10**7
SPREAD_COST = 0
ROUND = (("step", 0), ("step", 1))
ORDER = (
    (("open", 0), ("open", 1), ("total", 0), ("total", 1)) + ROUND * 7
    + (("share", 0, 0), ("share", 1, 0), ("spread", ((True, 0),)), ("spread", ((False, 0),))) + ROUND
    + (("share", 0, 1), ("share", 1, 1), ("spread", ((True, 1), (False, 1))))
)
MIB = 1024 * 1024

VMEM = pl.BlockSpec(memory_space=pltpu.VMEM)
SMEM = pl.BlockSpec(memory_space=pltpu.SMEM)
HBM = pl.BlockSpec(memory_space=pltpu.HBM)
HELD = pl.BlockSpec(memory_space=pltpu.VMEM)


def mm(a, b):
    return lax.dot_general(a, b, (((1,), (0,)), ((), ())), preferred_element_type=F32)


def mm_nt(a, b):
    return lax.dot_general(a, b, (((1,), (1,)), ((), ())), preferred_element_type=F32)


def mm_tn(a, b):
    return lax.dot_general(a, b, (((0,), (0,)), ((), ())), preferred_element_type=F32)


def iota(shape, axis):
    return lax.broadcasted_iota(jnp.int32, shape, axis)


def rope_table():
    half = HD // 2
    freqs = (10000.0 ** (-np.arange(half, dtype=np.float32) / np.float32(half))).astype(np.float32)
    turned = np.arange(ROW, dtype=np.float32)[:, None] * freqs[None, :]
    cosine = np.cos(turned.astype(np.float64))
    sine = np.sin(turned.astype(np.float64))
    cosine = np.concatenate([cosine, cosine, cosine, cosine], axis=1).astype(np.float32)
    sine = np.concatenate([-sine, sine, -sine, sine], axis=1).astype(np.float32)
    parts = []
    for table in (cosine, sine):
        high = table.astype(jnp.bfloat16)
        low = (table - high.astype(np.float32)).astype(jnp.bfloat16)
        parts += [high, low]
    return np.concatenate(parts, axis=1)


def swap_halves(block):
    lane = iota(block.shape, 1)
    return jnp.where(lane % HD < HD // 2, pltpu.roll(block, 96, 1), pltpu.roll(block, 32, 1))


def bounds_of(lens_ref, row):
    ends, total = [], jnp.int32(0)
    for k in range(DOCS_ROW):
        total = total + lens_ref[k, row]
        ends.append(total)
    return ends


def segment_of(spot, ends):
    seg = jnp.zeros_like(spot)
    for end in ends:
        seg = seg + (spot >= end).astype(jnp.int32)
    return seg


def norm_rows(values):
    mean = jnp.mean(values, axis=1, keepdims=True)
    centred = values - mean
    spread = jnp.mean(centred * centred, axis=1, keepdims=True)
    rstd = lax.rsqrt(spread + EPS_LAYER)
    return centred * rstd, rstd


def norm_back(d_out, xhat, rstd, gain):
    scaled = d_out * gain
    first = jnp.mean(scaled, axis=1, keepdims=True)
    second = jnp.mean(scaled * xhat, axis=1, keepdims=True)
    return rstd * (scaled - first - xhat * second)


def col_sum(values):
    return jnp.sum(values, axis=0, keepdims=True)


def here(size):
    me, stream = lax.axis_index("dp"), lax.axis_index("stream")
    top = size // 2
    has_top = jnp.where((me & top) != 0, 1, 0)
    base = jnp.where(stream == 0, me & ~top, me | top)
    near_at = jnp.where((me & 2) != 0, 1, 0) + jnp.where((me & 1) != 0, 2, 0)
    chip = (me >> 1) % RING
    place = jnp.int32(0)
    for k, one in enumerate(CIRCLE):
        place = jnp.where(chip == one, k, place)
    return me, stream, base, near_at, has_top, me & 1, place


def fetch(pairs, sems):
    copies = [pltpu.make_async_copy(src, dst, sems.at[k]) for k, (src, dst) in enumerate(pairs)]
    for copy in copies:
        copy.start()
    return copies


KEPT = (
    ((ROW, 3 * D), BF16),
    ((ROW, 256), F32),
    ((HEADS, ROW, ROW), BF16),
    ((ROW, D), BF16),
    ((ROW, D), F32),
    ((ROW, 128), F32),
    ((ROW, FF), BF16),
    ((ROW, FF), BF16),
    ((ROW, D), F32),
    ((ROW, 128), F32),
    ((8, D), F32),
)


def encoder_forward(
    size, lens_hbm, labels_hbm, table_hbm, x_hbm, wqkv_hbm, bqkv_hbm, wout_hbm, bout_hbm,
    g1_hbm, s1_hbm, wup_hbm, bup_hbm, wdown_hbm, bdown_hbm, g2_hbm, s2_hbm, wproj_hbm,
    vec_ref, qkv_hbm, rope_hbm, probs_hbm, mixed_hbm, xh1_hbm, rs1_hbm, act_hbm, slope_hbm,
    xh2_hbm, rs2_hbm, affine_hbm,
    qkv_ref, rope_ref, probs_ref, mixed_ref, xh1_ref, rs1_ref, act_ref, slope_ref,
    xh2_ref, rs2_ref, affine_ref, out_sems,
    table_ref, x_ref, wqkv_ref, bqkv_ref, wout_ref, bout_ref, g1_ref, s1_ref, wup_ref, bup_ref,
    wdown_ref, bdown_ref, g2_ref, s2_ref, wproj_ref, lens_ref, labels_ref, sems,
):
    me, stream = here(size)[:2]
    is_query = stream == 0
    scalars = fetch(((lens_hbm, lens_ref), (labels_hbm, labels_ref)), sems.at[pl.ds(15, 2)])
    copies = fetch(
        (
            (table_hbm, table_ref), (x_hbm, x_ref), (wqkv_hbm, wqkv_ref), (bqkv_hbm, bqkv_ref),
            (wout_hbm, wout_ref), (bout_hbm, bout_ref), (g1_hbm, g1_ref), (s1_hbm, s1_ref),
            (bup_hbm, bup_ref), (bdown_hbm, bdown_ref), (g2_hbm, g2_ref), (s2_hbm, s2_ref),
            (wup_hbm, wup_ref), (wdown_hbm, wdown_ref), (wproj_hbm, wproj_ref),
        ),
        sems,
    )
    kept = []

    def keep(src, dst):
        copy = pltpu.make_async_copy(src, dst, out_sems.at[len(kept)])
        copy.start()
        kept.append(copy)

    for copy in scalars:
        copy.wait()
    ends = bounds_of(lens_ref, me)

    def layout(spot):
        seg_doc = segment_of(spot, ends)
        start_doc = jnp.zeros_like(spot)
        for k in range(DOCS_ROW):
            start_doc = jnp.where(seg_doc == k + 1, ends[k], start_doc)
        seg_query = spot // QLEN
        seg = jnp.where(is_query, seg_query, seg_doc)
        start = jnp.where(is_query, seg_query * QLEN, start_doc)
        return seg, start

    shape = (ROW, ROW)
    seg_q, start_q = layout(iota(shape, 0))
    seg_k, _ = layout(iota(shape, 1))
    same = seg_q == seg_k
    onehot = (iota(shape, 1) == iota(shape, 0) - start_q).astype(F32).astype(BF16)
    for copy in copies[:4]:
        copy.wait()
    turned = mm(onehot, table_ref[...])
    cosine = turned[:, :128] + turned[:, 128:256]
    sine = turned[:, 256:384] + turned[:, 384:]
    rope_ref[:, :128] = cosine
    rope_ref[:, 128:] = sine
    keep(rope_ref, rope_hbm)

    x = x_ref[...]
    joined = mm(x, wqkv_ref[...]) + bqkv_ref[...].astype(F32)
    for g in range(2 * D // 128):
        block = joined[:, g * 128 : (g + 1) * 128]
        qkv_ref[:, g * 128 : (g + 1) * 128] = (
            block * cosine + swap_halves(block) * sine
        ).astype(BF16)
    qkv_ref[:, 2 * D :] = joined[:, 2 * D :].astype(BF16)
    keep(qkv_ref, qkv_hbm)

    low_half = iota((ROW, 128), 1) < HD
    for g in range(HEADS // 2):
        q_g = qkv_ref[:, g * 128 : (g + 1) * 128]
        k_g = qkv_ref[:, D + g * 128 : D + (g + 1) * 128]
        v_g = qkv_ref[:, 2 * D + g * 128 : 2 * D + (g + 1) * 128]
        outs = []
        for h in range(2):
            pick = low_half if h == 0 else jnp.logical_not(low_half)
            scores = mm_nt(jnp.where(pick, q_g, jnp.zeros_like(q_g)), k_g) * (1.0 / math.sqrt(HD))
            scores = jnp.where(same, scores, -1e30)
            top = jnp.max(scores, axis=1, keepdims=True)
            exps = jnp.exp(scores - top)
            probs = (exps / jnp.sum(exps, axis=1, keepdims=True)).astype(BF16)
            probs_ref[2 * g + h] = probs
            outs.append(mm(probs, v_g))
        mixed_ref[:, g * 128 : (g + 1) * 128] = jnp.where(low_half, outs[0], outs[1]).astype(BF16)

    keep(probs_ref, probs_hbm)
    keep(mixed_ref, mixed_hbm)
    for copy in copies[4:12]:
        copy.wait()
    for k, ref in enumerate((g1_ref, s1_ref, g2_ref, s2_ref)):
        affine_ref[k : k + 1, :] = ref[...].astype(F32)
    affine_ref[4:, :] = jnp.zeros((4, D), F32)
    keep(affine_ref, affine_hbm)
    attended = mm(mixed_ref[...], wout_ref[...]) + bout_ref[...].astype(F32)
    xhat, rstd = norm_rows(x.astype(F32) + attended)
    xh1_ref[...] = xhat
    rs1_ref[...] = jnp.broadcast_to(rstd, (ROW, 128))
    keep(xh1_ref, xh1_hbm)
    keep(rs1_ref, rs1_hbm)
    first = xhat * g1_ref[...].astype(F32) + s1_ref[...].astype(F32)
    first_low = first.astype(BF16)
    branch = bdown_ref[...].astype(F32) + first
    step = 512
    for copy in copies[12:]:
        copy.wait()
    for c in range(FF // step):
        cols = slice(c * step, (c + 1) * step)
        inner = mm(first_low, wup_ref[:, cols]) + bup_ref[:, cols].astype(F32)
        gate = 0.5 + 0.5 * lax.erf(inner * math.sqrt(0.5))
        bell = jnp.exp2(inner * inner * (-0.5 * LOG2E)) * (1.0 / math.sqrt(2.0 * math.pi))
        act = (inner * gate).astype(BF16)
        act_ref[:, cols] = act
        slope_ref[:, cols] = (gate + inner * bell).astype(BF16)
        keep(act_ref.at[:, cols], act_hbm.at[:, cols])
        keep(slope_ref.at[:, cols], slope_hbm.at[:, cols])
        branch = branch + mm(act, wdown_ref[cols, :])
    xhat, rstd = norm_rows(branch)
    xh2_ref[...] = xhat
    rs2_ref[...] = jnp.broadcast_to(rstd, (ROW, 128))
    keep(xh2_ref, xh2_hbm)
    keep(rs2_ref, rs2_hbm)
    second = xhat * g2_ref[...].astype(F32) + s2_ref[...].astype(F32)
    vec_ref[:ROW, :] = mm(second.astype(BF16), wproj_ref[...]).astype(BF16)
    line = iota((EXT, PROJ), 0)
    tag = jnp.zeros((EXT, PROJ), jnp.int32)
    for k in range(labels_ref.shape[0]):
        label = labels_ref[k]
        tag = jnp.where(line == k, label >> 6, tag)
        tag = jnp.where(line == k + 8, label & 63, tag)
    vec_ref[ROW:, :] = tag.astype(F32).astype(BF16)
    for copy in kept:
        copy.wait()


def prefix_norms(values, axis):
    place = iota(values.shape, axis)
    squared = values * values
    sums = [
        jnp.sum(jnp.where(place < cut, squared, 0.0), axis=axis, keepdims=True) for cut in RANGES
    ]
    return [lax.rsqrt(s + EPS_NORM) for s in sums]


def load_queries(near_ref, far_ref):
    span = ROW + EXT
    rows = []
    for ref in (near_ref, far_ref):
        for k in range(ref.shape[0] // span):
            rows.append(ref[k * span : k * span + ROW, :])
    return jnp.concatenate(rows, axis=0).astype(F32)


def unit_queries(queries, scale):
    lane = iota(queries.shape, 1)
    inverse = prefix_norms(queries, 1)
    unit = [
        jnp.where(lane < cut, queries * (inv * scale), 0.0) for cut, inv in zip(RANGES, inverse)
    ]
    return unit, inverse


def unit_docs(doc_refs, scratch_ref):
    at = 0
    for ref in doc_refs:
        for k in range(ref.shape[0] // ROW):
            scratch_ref[:, at * ROW : (at + 1) * ROW] = ref[
                k * ROW : (k + 1) * ROW, :
            ].astype(F32).T
            at += 1
    turned = scratch_ref[...]
    inverse = prefix_norms(turned, 0)
    place = iota(turned.shape, 0)
    unit = [jnp.where(place < cut, turned * inv, 0.0) for cut, inv in zip(RANGES, inverse)]
    return unit, inverse


def row_ids(base, masks, doc_rows):
    ids = []
    for p in range(doc_rows):
        offset = 0
        for k, mask in enumerate(masks):
            if (p >> k) & 1:
                offset ^= mask
        ids.append(base ^ offset)
    return ids


def doc_marks(lens_ref, ids, lanes, transposed):
    docs = len(ids) * DOCS_ROW
    shape = (lanes, ROW) if transposed else (ROW, lanes)
    spot, lane = (iota(shape, 1), iota(shape, 0)) if transposed else (iota(shape, 0), iota(shape, 1))
    marks = []
    for p, row in enumerate(ids):
        seg = segment_of(spot, bounds_of(lens_ref, row))
        local = jnp.where(seg < DOCS_ROW, seg + p * DOCS_ROW, -1 - lanes)
        marks.append(
            [(lane == local + m * docs).astype(F32).astype(BF16) for m in range(len(RANGES))]
        )
    return marks


def matching_stats(
    size, masks, lanes, scale_ref, lens_hbm, near_ref, far_ref, *refs
):
    doc_refs = refs[:-8]
    totals_ref, el_ref, hot_ref, stats_ref, turn_ref, unit_ref, lens_ref, sems = refs[-8:]
    scalars = fetch(((lens_hbm, lens_ref),), sems)
    base, near_at = here(size)[2:4]
    span = ROW + EXT
    queries = load_queries(near_ref, far_ref)
    count = queries.shape[0]
    unit_q, _ = unit_queries(queries, SHARPNESS * LOG2E)
    unit_q = [u.astype(BF16) for u in unit_q]
    unit_d, _ = unit_docs(doc_refs, turn_ref)
    for m in range(len(RANGES)):
        unit_ref[m] = unit_d[m].astype(BF16)
    doc_rows = turn_ref.shape[1] // ROW
    docs = doc_rows * DOCS_ROW
    ids = row_ids(base, masks, doc_rows)
    for copy in scalars:
        copy.wait()
    marks = doc_marks(lens_ref, ids, lanes, False)
    totals = jnp.zeros((count, lanes), F32)
    for p in range(doc_rows):
        for m in range(len(RANGES)):
            sims = mm(unit_q[m], unit_ref[m, :, p * ROW : (p + 1) * ROW])
            totals = totals + mm(jnp.exp2(sims).astype(BF16), marks[p][m])
    lane_t = iota((count, lanes), 1)
    totals = jnp.where(lane_t < len(RANGES) * docs, totals, 1.0)
    totals_ref[...] = totals
    shape = (8, lanes)
    lane = iota(shape, 1)
    length = jnp.ones(shape, jnp.int32)
    name = jnp.full(shape, -1, jnp.int32)
    for p in range(doc_rows):
        for k in range(DOCS_ROW):
            own = jnp.zeros(shape, jnp.bool_)
            for m in range(len(RANGES)):
                own = jnp.logical_or(own, lane == m * docs + p * DOCS_ROW + k)
            length = jnp.where(own, lens_ref[k, ids[p]], length)
            name = jnp.where(own, ids[p] * DOCS_ROW + k, name)
    log_length = jnp.log(length.astype(F32))
    matched = (jnp.log(totals) - log_length[:1]) * (1.0 / SHARPNESS)
    per_query = jnp.sum(matched.reshape(count // QLEN, QLEN, lanes), axis=1)
    scale = jnp.exp(jnp.full(shape, scale_ref[0], F32))[:1]
    logits = per_query * (scale * (1.0 / QLEN))
    groups = count // ROW
    tags = []
    for ref in (near_ref, far_ref):
        for k in range(ref.shape[0] // span):
            high = ref[k * span + ROW : k * span + ROW + 8, :].astype(F32).astype(jnp.int32)
            low = ref[k * span + ROW + 8 : k * span + ROW + 16, :].astype(F32).astype(jnp.int32)
            tag = high * 64 + low
            tags.append(jnp.concatenate([tag] * (lanes // 128), axis=1))
    tag = jnp.concatenate(tags, axis=0)
    lane_q = iota(logits.shape, 1)
    valid = lane_q < len(RANGES) * docs
    el = jnp.where(valid, jnp.exp(logits), 0.0)
    hot = jnp.where(jnp.logical_and(valid, jnp.concatenate([name] * groups, axis=0) == tag), 1.0, 0.0)
    el_ref[...] = el
    hot_ref[...] = hot
    place = iota((groups * 8, 128), 1)
    stats = jnp.zeros((groups * 8, 128), F32)
    for k, values in enumerate((el, el * logits, hot * logits)):
        for m in range(len(RANGES)):
            inside = jnp.logical_and(lane_q >= m * docs, lane_q < (m + 1) * docs)
            one = jnp.sum(jnp.where(inside, values, 0.0), axis=1, keepdims=True)
            stats = jnp.where(place == k * 3 + m, one, stats)
    for a in range(groups):
        at = pl.multiple_of((near_at ^ a) * 8, 8)
        stats_ref[pl.ds(at, 8), :] = stats[a * 8 : (a + 1) * 8, :]


def matching_back(
    size, masks, lanes, scale_ref, lens_hbm, totals_ref, el_ref, hot_ref, own_ref, over_y, over_x, over_both, unitq_ref, qt_ref, invq_ref, unit_ref, invd_ref, *refs
):
    dq_ref, far_ref, keep_ref, send_ref, loss_ref = refs[-10:-5]
    dot_ref, dt_ref, stats_ref, lens_ref, sems = refs[-5:]
    scalars = fetch(((lens_hbm, lens_ref),), sems)
    _, stream, base, near_at = here(size)[:4]
    total_queries = size * (ROW // QLEN)
    temper = SHARPNESS * LOG2E
    count = unitq_ref.shape[1]
    inv_q = [invq_ref[:, m : m + 1] for m in range(len(RANGES))]
    inv_d = [invd_ref[m : m + 1, :] for m in range(len(RANGES))]
    unit_q = [unitq_ref[m] for m in range(len(RANGES))]
    doc_rows = unit_ref.shape[2] // ROW
    docs = doc_rows * DOCS_ROW
    ids = row_ids(base, masks, doc_rows)
    groups = count // ROW
    odd_y, odd_x = (near_at & 1) == 1, stream == 1
    parts = [own_ref[...], over_y[...], over_x[...], over_both[...]]
    parts = [jnp.where(odd_y, a, b) for a, b in ((parts[1], parts[0]), (parts[0], parts[1]),
                                                  (parts[3], parts[2]), (parts[2], parts[3]))]
    parts = [jnp.where(odd_x, parts[(k + 2) % 4], parts[k]) for k in range(4)]
    stats_ref[...] = (parts[0] + parts[1]) + (parts[2] + parts[3])
    rows = []
    for a in range(groups):
        at = pl.multiple_of((near_at ^ a) * 8, 8)
        rows.append(stats_ref[pl.ds(at, 8), :])
    stats = jnp.concatenate(rows, axis=0)
    place = iota(stats.shape, 1)

    def column(k):
        return jnp.sum(jnp.where(place == k, stats, 0.0), axis=1, keepdims=True)

    shape = (groups * 8, lanes)
    lane_q = iota(shape, 1)
    sums = jnp.ones(shape, F32)
    loss = jnp.zeros((groups * 8, 1), F32)
    moved = jnp.zeros((groups * 8, 1), F32)
    for m in range(len(RANGES)):
        whole, weighted, picked = column(m), column(3 + m), column(6 + m)
        inside = jnp.logical_and(lane_q >= m * docs, lane_q < (m + 1) * docs)
        sums = jnp.where(inside, whole, sums)
        loss = loss + (jnp.log(whole) - picked)
        moved = moved + (weighted / whole - picked)
    line = iota((8, 128), 0)
    loss = jnp.where(
        line == 0,
        jnp.sum(loss, axis=0, keepdims=True) * (1.0 / total_queries),
        jnp.where(line == 1, jnp.sum(moved, axis=0, keepdims=True) * (1.0 / total_queries), 0.0),
    )
    loss_ref[...] = loss
    for copy in scalars:
        copy.wait()
    marks = doc_marks(lens_ref, ids, lanes, True)
    scale = jnp.exp(jnp.full((8, lanes), scale_ref[0], F32))[:1]
    coeff = (el_ref[...] / sums - hot_ref[...]) * (scale * (1.0 / (QLEN * total_queries)))
    coeff = jnp.broadcast_to(coeff[:, None, :], (groups * 8, QLEN, lanes)).reshape(count, lanes)
    ratio = coeff / totals_ref[...]
    ratio_high = ratio.astype(BF16)
    ratio_low = (ratio - ratio_high.astype(F32)).astype(BF16)
    ratio = jnp.concatenate([ratio_high, ratio_low], axis=1)
    for m in range(len(RANGES)):
        grad = jnp.zeros((count, PROJ), F32)
        for p in range(doc_rows):
            block = unit_ref[m, :, p * ROW : (p + 1) * ROW]
            mark = marks[p][m]
            if len(refs) > 10:
                exps = refs[0][m, :, p * ROW : (p + 1) * ROW].astype(F32)
            else:
                exps = jnp.exp2(mm(unit_q[m], block))
            d_sims = (exps * mm(ratio, jnp.concatenate([mark, mark], axis=0))).astype(BF16)
            grad = grad + mm_nt(d_sims, block)
            dt_ref[m, :, p * ROW : (p + 1) * ROW] = mm(qt_ref[m], d_sims)
        unit = unit_q[m].astype(F32) * (1.0 / temper)
        along = jnp.sum(grad * unit, axis=1, keepdims=True)
        part = inv_q[m] * (grad - unit * along)
        if m == 0:
            dot_ref[...] = part
        else:
            dot_ref[...] += part
    dq_ref[...] = dot_ref[: count // 2, :].astype(BF16)
    far_ref[...] = dot_ref[count // 2 :, :].astype(BF16)
    total = jnp.zeros(unit_ref.shape[1:], F32)
    for m in range(len(RANGES)):
        grad = dt_ref[m] * (1.0 / temper)
        unit = unit_ref[m].astype(F32)
        along = jnp.sum(grad * unit, axis=0, keepdims=True)
        total = total + inv_d[m] * (grad - unit * along)
    for p in range(doc_rows):
        ref, at = (keep_ref, p) if p < doc_rows // 2 else (send_ref, p - doc_rows // 2)
        ref[at * ROW : (at + 1) * ROW, :] = total[:, p * ROW : (p + 1) * ROW].T.astype(BF16)


def matching_ready(near_ref, far_ref, *refs):
    doc_refs = refs[:-6] if refs[-2].shape[0] != len(RANGES) else refs[:-7]
    unitq_ref, qt_ref, invq_ref, unit_ref, invd_ref = refs[len(doc_refs) : len(doc_refs) + 5]
    turn_ref = refs[-1]
    queries = load_queries(near_ref, far_ref)
    unit_q, inv_q = unit_queries(queries, SHARPNESS * LOG2E)
    unit_d, inv_d = unit_docs(doc_refs, turn_ref)
    lane = iota(invq_ref.shape, 1)
    columns = jnp.zeros(invq_ref.shape, F32)
    invd_ref[...] = jnp.zeros_like(invd_ref)
    for m in range(len(RANGES)):
        unitq_ref[m] = unit_q[m].astype(BF16)
        unit_ref[m] = unit_d[m].astype(BF16)
        qt_ref[m] = unit_q[m].T.astype(BF16)
        columns = jnp.where(lane == m, inv_q[m], columns)
        invd_ref[m : m + 1, :] = inv_d[m]
        if len(refs) - len(doc_refs) > 6:
            refs[-2][m] = jnp.exp2(mm(unitq_ref[m], unit_ref[m])).astype(BF16)
    invq_ref[...] = columns


def two_sums(dq_ref, got_ref, dd_ref, got_dd_ref, sum_dq, sum_dd):
    sum_dq[...] = (dq_ref[...].astype(F32) + got_ref[...].astype(F32)).astype(BF16)
    sum_dd[...] = (dd_ref[...].astype(F32) + got_dd_ref[...].astype(F32)).astype(BF16)


DIGITS = 10
POINT = 20


def digits_of(value):
    fixed = (value * float(1 << POINT)).astype(jnp.int32)
    size = jnp.abs(fixed)
    lane = iota(value.shape, 1)
    digits = jnp.zeros(value.shape, jnp.int32)
    for k in range(DIGITS):
        digits = jnp.where(lane == k, (size >> (3 * k)) & 7, digits)
    return jnp.where(fixed < 0, -digits, digits).astype(F32)


def value_of(digits):
    lane = iota(digits.shape, 1)
    half = DIGITS // 2
    weight = jnp.zeros(digits.shape, F32)
    for k in range(half):
        weight = jnp.where(jnp.logical_or(lane == k, lane == k + half), float(8**k), weight)
    low = jnp.sum(jnp.where(lane < half, digits * weight, 0.0))
    high = jnp.sum(jnp.where(jnp.logical_and(lane >= half, lane < DIGITS), digits * weight, 0.0))
    return (high * float(8**half) + low) * (1.0 / (1 << POINT))


def turn(core, place, block):
    return jnp.where(core == 0, place - block, block - place) & (RING - 1)


def block_at(core, place, distance):
    return jnp.where(core == 0, place - distance, place + distance) & (RING - 1)


def store_block(keep_ref, send_ref, rows, block, places, value):
    core, place = places
    mine = core == block // RING
    at = turn(block // RING, place, block % RING)

    @pl.when(mine)
    def _():
        keep_ref[at, rows, :] = value

    @pl.when(jnp.logical_not(mine))
    def _():
        send_ref[at, rows, :] = value


def feed_back(
    size, dq_ref, dd_ref, got_ref, xh2_ref, rs2_ref, affine_ref, wproj_ref, slope_ref, act_ref,
    xh1_ref, wup_ref, wdown_hbm,
    keep_ref, send_ref, tail_keep, tail_send, dfirst_ref, gproj_ref, small_ref,
    dinner_ref, wdown_ref, sems,
):
    step = 512
    spans = [slice(c * step, (c + 1) * step) for c in range(FF // step)]
    copies = fetch([(wdown_hbm.at[span, :], wdown_ref.at[span, :]) for span in spans], sems)
    g1, s1, g2, s2 = [affine_ref[k : k + 1, :] for k in range(4)]
    _, stream, _, _, has_top, *places = here(size)
    is_query, docs_there = stream == 0, has_top == 0
    got = got_ref[...].astype(F32)
    d_vec = jnp.where(
        is_query,
        dq_ref[...].astype(F32) + got,
        jnp.where(docs_there, got, dd_ref[...].astype(F32)),
    )
    d_proj = d_vec.astype(BF16)
    xhat = xh2_ref[...]
    gain = g2
    second = (xhat * gain + s2).astype(BF16)
    gproj_ref[...] = mm_tn(second, d_proj)
    d_second = mm_nt(d_proj, wproj_ref[...])
    small_ref[...] = jnp.zeros_like(small_ref)
    small_ref[5:6, :] = col_sum(d_second * xhat)
    small_ref[6:7, :] = col_sum(d_second)
    d_sum = norm_back(d_second, xhat, rs2_ref[:, :1], gain)
    d_branch = d_sum.astype(BF16)
    small_ref[4:5, :] = col_sum(d_branch.astype(F32))
    d_first = d_sum
    for c in range(FF // step):
        cols = spans[c]
        copies[c].wait()
        d_act = mm_nt(d_branch, wdown_ref[cols, :])
        d_inner = (d_act * slope_ref[:, cols].astype(F32)).astype(BF16)
        dinner_ref[:, cols] = d_inner
        small_ref[c : c + 1, :] = col_sum(d_inner.astype(F32))
        grad = mm_tn(act_ref[:, cols], d_branch).astype(BF16)
        for k in range(step // DOWN):
            store_block(
                keep_ref, send_ref, slice(0, DOWN), c * (step // DOWN) + k, places,
                grad[k * DOWN : (k + 1) * DOWN, :],
            )
        d_first = d_first + mm_nt(d_inner, wup_ref[:, cols])
    dfirst_ref[...] = d_first
    first = (xh1_ref[...] * g1 + s1).astype(BF16)
    for c in range(FF // step):
        cols = slice(c * step, (c + 1) * step)
        grad = mm_tn(first, dinner_ref[:, cols]).astype(BF16)
        for k in range(D // DOWN):
            block = c * (D // DOWN) + k
            start = k * DOWN
            store_block(
                keep_ref, send_ref, slice(DOWN, FIRST), block, places, grad[start : start + HEAD, :]
            )
            store_block(
                tail_keep, tail_send, slice(0, TAIL), block, places,
                grad[start + HEAD : start + DOWN, :],
            )


def attend_back(
    size, dfirst_ref, gproj_ref, small_ref, loss_ref, tail_keep, tail_send, xh1_ref, rs1_ref, affine_ref, mixed_ref, wout_ref,
    qkv_ref, probs_ref, rope_ref, x_ref, wqkv_ref,
    keep_ref, ahead_ref, send_ref, tokens_ref, djoined_ref, rest_ref,
):
    me, *_, core, place = here(size)
    d_first = dfirst_ref[...]
    xhat = xh1_ref[...]
    gain = affine_ref[0:1, :]
    gain_grad = col_sum(d_first * xhat)
    shift_grad = col_sum(d_first)
    d_sum = norm_back(d_first, xhat, rs1_ref[:, :1], gain)
    d_att = d_sum.astype(BF16)
    bias_out = col_sum(d_att.astype(F32))
    rest_ref[3 * D : 4 * D, :] = mm_tn(mixed_ref[...], d_att)
    d_mixed = mm_nt(d_att, wout_ref[...]).astype(BF16)
    cosine, sine = rope_ref[:, :128], rope_ref[:, 128:]
    low_half = iota((ROW, 128), 1) < HD

    def unrotate(values):
        values = values * (1.0 / math.sqrt(HD))
        return (values * cosine - swap_halves(values) * sine).astype(BF16)

    for g in range(HEADS // 2):
        span = slice(g * 128, (g + 1) * 128)
        q_g = qkv_ref[:, g * 128 : (g + 1) * 128]
        k_g = qkv_ref[:, D + g * 128 : D + (g + 1) * 128]
        v_g = qkv_ref[:, 2 * D + g * 128 : 2 * D + (g + 1) * 128]
        m_g = d_mixed[:, span]
        d_q = jnp.zeros((ROW, 128), F32)
        d_k = jnp.zeros((ROW, 128), F32)
        d_v = jnp.zeros((ROW, 128), F32)
        zero = jnp.zeros((ROW, 128), BF16)
        for h in range(2):
            pick = low_half if h == 0 else jnp.logical_not(low_half)
            probs_low = probs_ref[2 * g + h]
            probs = probs_low.astype(F32)
            m_h = jnp.where(pick, m_g, zero)
            d_probs = mm_nt(m_h, v_g)
            d_v = d_v + mm_tn(probs_low, m_h)
            inner = jnp.sum(d_probs * probs, axis=1, keepdims=True)
            d_scores = (probs * (d_probs - inner)).astype(BF16)
            d_q = d_q + mm(d_scores, jnp.where(pick, k_g, zero))
            d_k = d_k + mm_tn(d_scores, jnp.where(pick, q_g, zero))
        djoined_ref[:, g * 128 : (g + 1) * 128] = unrotate(d_q)
        djoined_ref[:, D + g * 128 : D + (g + 1) * 128] = unrotate(d_k)
        djoined_ref[:, 2 * D + g * 128 : 2 * D + (g + 1) * 128] = d_v.astype(BF16)
    x = x_ref[...]
    tokens = d_sum
    rest_ref[4 * D :, :] = jnp.zeros((8 * 2 * RING, D), F32)
    smalls = []
    for c in range(3):
        cols = slice(c * D, (c + 1) * D)
        d_part = djoined_ref[:, cols]
        rest_ref[c * D : (c + 1) * D, :] = mm_tn(x, d_part)
        smalls.append(col_sum(d_part.astype(F32)))
        tokens = tokens + mm_nt(d_part, wqkv_ref[:, cols])
    tokens_ref[...] = tokens
    smalls += [bias_out, gain_grad, shift_grad] + [small_ref[k : k + 1, :] for k in range(7)]
    counted = jnp.where((me & 3) == 0, 1.0, 0.0)
    lines = [digits_of(loss_ref[k : k + 1, :]) * counted for k in range(2)]
    smalls.append(jnp.concatenate(lines + [jnp.zeros((1, D - 256), F32)], axis=1))
    for k, row in enumerate(smalls):
        rest_ref[4 * D + 8 * k : 4 * D + 8 * k + 1, :] = row
    for k in range(RING):
        sent, at = (ahead_ref, AHEAD.index(k)) if k in AHEAD else (send_ref, LATER.index(k))
        for ref, index, tail_ref, owner in (
            (keep_ref, k, tail_keep, core), (sent, at, tail_send, 1 - core)
        ):
            block = owner * RING + block_at(owner, place, k)
            parts = []
            for c in range(4):
                start = pl.multiple_of(c * D + block * SHARE, SHARE)
                parts.append(rest_ref[pl.ds(start, SHARE), :])
            row = pl.multiple_of(block * SHARE, SHARE)
            parts.append(
                jnp.concatenate(
                    [gproj_ref[pl.ds(row + 8 * j, 8), :] for j in range(SHARE // 8)], axis=1
                )
            )
            parts.append(rest_ref[pl.ds(pl.multiple_of(4 * D + block * 8, 8), 8), :])
            ref[index, : REST // 16, :] = jnp.concatenate(parts, axis=0).astype(BF16)
            ref[index, REST // 16 :, :] = tail_ref[k]


def spread(size, jobs, last, *refs):
    core, place = here(size)[-2:]
    halves = refs[: 2 * len(jobs)]
    wide_one, wide_two, wide_qkv, wide_proj, small_ref, sems = refs[-6:]
    outs = refs[-21:-6] if last else refs[-11:-6]
    down_hbm, up_hbm, qkv_hbm, out_hbm, proj_hbm = outs[:5]
    copies = []

    def move(src, dst):
        copy = pltpu.make_async_copy(src, dst, sems.at[len(copies)])
        copy.start()
        copies.append(copy)

    at = 0
    for job, (mine, group) in enumerate(jobs):
        owner = core if mine else 1 - core
        one_ref, two_ref = halves[2 * job : 2 * job + 2]
        for p, distance in enumerate(GROUPS[group]):
            block = owner * RING + block_at(owner, place, distance)
            wide_one[at] = one_ref[p].astype(F32)
            rows = pl.ds(pl.multiple_of(block * DOWN, DOWN), DOWN)
            move(wide_one.at[at, :DOWN, :], down_hbm.at[rows, :])
            start = (block % (D // DOWN)) * DOWN
            columns = pl.ds(pl.multiple_of((block // (D // DOWN)) * D, D), D)
            rows = pl.ds(pl.multiple_of(start, DOWN), HEAD)
            move(wide_one.at[at, DOWN:, :], up_hbm.at[rows, columns])
            wide = two_ref[p].astype(F32)
            wide_two[at, :SHARE, :] = wide[3 * SHARE : 4 * SHARE, :]
            wide_two[at, SHARE:, :] = wide[REST // 16 :, :]
            rows = pl.ds(pl.multiple_of(start + HEAD, 16), TAIL)
            move(wide_two.at[at, SHARE:, :], up_hbm.at[rows, columns])
            rows = pl.ds(pl.multiple_of(block * SHARE, SHARE), SHARE)
            for c in range(3):
                wide_qkv[at, :, c * D : (c + 1) * D] = wide[c * SHARE : (c + 1) * SHARE, :]
            move(wide_qkv.at[at], qkv_hbm.at[rows, :])
            move(wide_two.at[at, :SHARE, :], out_hbm.at[rows, :])
            for j in range(SHARE // 8):
                wide_proj[at, 8 * j : 8 * j + 8, :] = wide[
                    4 * SHARE : 4 * SHARE + 8, j * PROJ : (j + 1) * PROJ
                ]
            move(wide_proj.at[at], proj_hbm.at[rows, :])
            at += 1
    if last:
        sources = refs[2 * len(jobs) : 2 * len(jobs) + 2 * len(GROUPS)]
        for k, ref in enumerate(sources):
            owner = core if k < len(GROUPS) else 1 - core
            for p, distance in enumerate(GROUPS[k % len(GROUPS)]):
                block = owner * RING + block_at(owner, place, distance)
                line = ref[p, 4 * SHARE : 4 * SHARE + 16, :].astype(F32)[8:, :]
                small_ref[pl.ds(pl.multiple_of(block * 8, 8), 8), :] = line
        rows = [small_ref[8 * k : 8 * k + 1, :] for k in range(14)]
        bqkv_ref, bout_ref, g1_ref, s1_ref, bup_ref, bdown_ref, g2_ref, s2_ref = outs[5:13]
        for k, ref in enumerate(outs[13:]):
            ref[0] = value_of(rows[13][:, k * 128 : (k + 1) * 128])
        for c in range(3):
            bqkv_ref[:, c * D : (c + 1) * D] = rows[c]
        bout_ref[...] = rows[3]
        g1_ref[...] = rows[4]
        s1_ref[...] = rows[5]
        for c in range(4):
            bup_ref[:, c * D : (c + 1) * D] = rows[6 + c]
        bdown_ref[...] = rows[10]
        g2_ref[...] = rows[11]
        s2_ref[...] = rows[12]
    for copy in copies:
        copy.wait()


def spread_call(size, jobs, halves, outs, others):
    last = len(others) > 0
    shapes = ((FF, D), (D, FF), (D, 3 * D), (D, D), (D, PROJ))
    widths = (3 * D, D, D, D, FF, D, D, D) if last else ()
    args = [*halves, *others, *outs]
    count = sum(len(GROUPS[group]) for _, group in jobs)
    before = len(halves) + len(others)
    return call(
        partial(spread, size, jobs, last),
        args,
        [VMEM] * before + [HBM] * len(outs),
        [pltpu.HBM(shape, F32) for shape in shapes]
        + [shape_of((1, width)) for width in widths]
        + [shape_of((1,))] * (2 * last),
        [
            pltpu.VMEM((count, FIRST, D), F32),
            pltpu.VMEM((count, SHARE + TAIL, D), F32),
            pltpu.VMEM((count, SHARE, 3 * D), F32),
            pltpu.VMEM((count, SHARE, PROJ), F32),
            pltpu.VMEM((16 * RING, D), F32),
            pltpu.SemaphoreType.DMA((6 * count,)),
        ],
        out_specs=[HBM] * 5 + [VMEM] * len(widths) + [SMEM] * (2 * last),
        aliases={before + k: k for k in range(len(outs))},
        cost=SPREAD_COST,
        room=14,
    )


def shape_of(shape, dtype=F32):
    return jax.ShapeDtypeStruct(tuple(shape), dtype)


def call(kernel, args, specs, outs, scratch=(), room=24, out_specs=None, aliases={}, cost=10**7):
    spaces = {id(HBM): pltpu.HBM, id(HELD): pltpu.VMEM}
    args = [
        pltpu.with_memory_space_constraint(arg, spaces[id(spec)]) if id(spec) in spaces else arg
        for arg, spec in zip(args, specs)
    ]
    return pl.pallas_call(
        kernel,
        out_shape=outs,
        in_specs=specs,
        out_specs=out_specs or [VMEM] * len(outs),
        scratch_shapes=list(scratch),
        input_output_aliases=aliases,
        compiler_params=pltpu.CompilerParams(vmem_limit_bytes=room * MIB),
        cost_estimate=pl.CostEstimate(
            flops=10 * cost, bytes_accessed=cost, transcendentals=0
        ),
    )(*args)


def swapped(value, mask, axis="dp"):
    size = lax.axis_size(axis)
    return lax.ppermute(value, axis, [(k, k ^ mask) for k in range(size)])


def added(a, b):
    return (a.astype(F32) + b.astype(F32)).astype(BF16)


def join_blocks(*refs):
    for k, ref in enumerate(refs[:-1]):
        refs[-1][k] = ref[0]


def ring_swap(value, onward):
    size = lax.axis_size("dp")
    pairs = []
    for k in range(size):
        at = CIRCLE.index((k >> 1) % RING)
        to = CIRCLE[(at + (1 if (k % 2 == 0) == onward else -1)) % RING]
        pairs.append((k, (k & ~(2 * RING - 1)) | (to << 1) | (k & 1)))
    return lax.ppermute(value, "dp", pairs)


def add_blocks(places, *refs):
    count = len(places)
    held_ref = refs[count] if any(place is not None for place in places) else None
    for k, place in enumerate(places):
        value = refs[k][...]
        if place is not None:
            value = (value.astype(F32) + held_ref[place : place + 1].astype(F32)).astype(BF16)
        refs[-count + k][...] = value


def first_blocks(places, keep_ref, pair_ref, *outs):
    for ref, (k, j) in zip(outs, places):
        ref[0] = (keep_ref[k].astype(F32) + pair_ref[j].astype(F32)).astype(BF16)


def later_blocks(places, keep_ref, pair_ref, out_ref):
    for k in AHEAD:
        out_ref[k] = jnp.zeros(out_ref.shape[1:], BF16)
    for k, j in places:
        out_ref[k] = (keep_ref[k].astype(F32) + pair_ref[j].astype(F32)).astype(BF16)


class Summed:
    def __init__(self, keep, sends, others):
        self.keep, self.others, self.hop = keep, others, 0
        self.pairs = [swapped(send, 1) for send in sends]
        self.sent, self.blocks, self.near, self.far = [], {}, [], []

    def blocks_call(self, blocks, places, held):
        return call(
            partial(add_blocks, places),
            (*blocks, *held),
            [VMEM] * (len(blocks) + len(held)),
            [shape_of(block.shape, BF16) for block in blocks],
            room=8,
            cost=STEP_COST,
        )

    def open(self, after):
        keep, pair, _ = lax.optimization_barrier((self.keep, self.pairs[0], after))
        shape = (1, *keep.shape[1:])
        places = [(k, AHEAD.index(k) if len(self.pairs) > 1 else k) for k in AHEAD]
        first, second = call(
            partial(first_blocks, places),
            (keep, pair),
            [VMEM] * 2,
            [shape_of(shape, BF16)] * 2,
            room=8,
            cost=STEP_COST,
        )
        self.sent = [(first, True), (second, False)]
        return second

    def total(self, after):
        keep, _ = lax.optimization_barrier((self.keep, after))
        later = [(k, LATER.index(k) if len(self.pairs) > 1 else k) for k in LATER]
        (self.keep,) = call(
            partial(later_blocks, later),
            (keep, self.pairs[-1]),
            [VMEM] * 2,
            [shape_of(keep.shape, BF16)],
            room=8,
            cost=STEP_COST,
        )
        return self.keep

    def step(self, after):
        half = RING // 2
        self.hop += 1
        hop = self.hop
        *got, _ = lax.optimization_barrier((*[ring_swap(*one) for one in self.sent], after))
        if hop < half:
            out = self.blocks_call(got, (half + hop, half - 1 - hop), [self.keep])
            self.part = out[1]
        elif hop == half:
            (own,) = self.blocks_call(got, (0,), [self.part])
            for mask in self.others:
                own = added(own, swapped(own, mask))
            self.blocks[0] = own
            out = [own, own]
        else:
            out = self.blocks_call(got, (None,) * len(got), [])
            hop -= half
            self.blocks[hop] = out[0]
            if hop < half:
                self.blocks[RING - hop] = out[1]
        if hop == half - 1:
            self.sent = [(out[0], True)]
        elif self.hop < 2 * half:
            self.sent = [(out[0], True), (out[1], False)]
        return out[0]

    def share(self, group, after):
        *blocks, _ = lax.optimization_barrier((*[self.blocks[k] for k in GROUPS[group]], after))
        shape = (len(blocks), *blocks[0].shape[1:])
        self.near += call(
            join_blocks, blocks, [VMEM] * len(blocks), [shape_of(shape, BF16)], room=8, cost=0
        )
        self.far.append(swapped(self.near[-1], 1))
        return self.near[-1]


def per_device(
    tokens, qkv_weight, qkv_bias, out_weight, out_bias, first_gain, first_shift, up_weight,
    up_bias, down_weight, down_bias, second_gain, second_shift, proj_weight, log_scale,
    doc_lengths, labels,
):
    size = lax.axis_size("dp")
    bits = [1 << k for k in range(size.bit_length() - 1)]
    near_masks, doc_masks = bits[:2], bits[2:]
    top_mask, doc_masks = doc_masks[-1], doc_masks[:-1]
    others = bits[4:]
    me = lax.axis_index("dp")
    stream = lax.axis_index("stream")
    is_query = stream == 0
    has_top = (me & top_mask) != 0
    lens = doc_lengths.T
    scale = log_scale.reshape(1)

    vec, qkv, rope, probs, mixed, xh1, rs1, act, slope, xh2, rs2, affine = call(
        partial(encoder_forward, size),
        (
            lens, labels, jnp.asarray(rope_table()), tokens[0], qkv_weight[0], qkv_bias,
            out_weight[0], out_bias, first_gain, first_shift, up_weight[0], up_bias,
            down_weight[0], down_bias, second_gain, second_shift, proj_weight[0],
        ),
        [HBM] * 17,
        [shape_of((ROW + EXT, PROJ), BF16)] + [pltpu.HBM(*kind) for kind in KEPT],
        [pltpu.VMEM(*kind) for kind in KEPT]
        + [pltpu.SemaphoreType.DMA((len(KEPT) + 6,))]
        + [
            pltpu.VMEM(shape, BF16)
            for shape in (
                (ROW, 512), (ROW, D), (D, 3 * D), (1, 3 * D), (D, D), (1, D), (1, D), (1, D), (D, FF),
                (1, FF), (FF, D), (1, D), (1, D), (1, D), (D, PROJ),
            )
        ]
        + [
            pltpu.SMEM(lens.shape, jnp.int32),
            pltpu.SMEM(labels.shape, jnp.int32),
            pltpu.SemaphoreType.DMA((17,)),
        ],
        room=40,
        out_specs=[VMEM] + [HBM] * len(KEPT),
    )

    every, other_y = range(size), near_masks[1]
    other = swapped(vec, 1, "stream")
    near = jnp.where(is_query, vec, other)
    rows = jnp.where(is_query, other, vec)[:ROW]
    moved = swapped(rows, top_mask)
    near = jnp.concatenate([near, swapped(near, other_y)], axis=0)
    rows = jnp.where(has_top == is_query, moved, rows)
    far = swapped(near, near_masks[0])
    pieces = []
    for k, mask in enumerate(doc_masks):
        pieces.append(rows)
        got = swapped(rows, mask)
        if k + 1 < len(doc_masks):
            rows = jnp.concatenate([rows, got], axis=0)
        else:
            pieces = [rows, got]
    doc_rows = sum(p.shape[0] for p in pieces) // ROW
    tokens_d = doc_rows * ROW
    tokens_q = 4 * ROW
    lanes = -(-3 * doc_rows * DOCS_ROW // 128) * 128
    room = 20 if doc_rows <= 4 else 56
    scalars = [pltpu.SMEM(lens.shape, jnp.int32), pltpu.SemaphoreType.DMA((1,))]
    totals, el, hot, stats = call(
        partial(matching_stats, size, doc_masks, lanes),
        (scale, lens, near, far, *pieces),
        [SMEM, HBM] + [VMEM] * (2 + len(pieces)),
        [
            shape_of((tokens_q, lanes)),
            shape_of((tokens_q // QLEN, lanes)),
            shape_of((tokens_q // QLEN, lanes)),
            shape_of((tokens_q // QLEN, 128)),
        ],
        [pltpu.VMEM((PROJ, tokens_d), F32), pltpu.VMEM((3, PROJ, tokens_d), BF16), *scalars],
        room=room,
    )
    small_enough = doc_rows <= 4
    ready = call(
        matching_ready,
        (near, far, *pieces),
        [VMEM] * (2 + len(pieces)),
        [
            shape_of((3, tokens_q, PROJ), BF16),
            shape_of((3, PROJ, tokens_q), BF16),
            shape_of((tokens_q, 128)),
            shape_of((3, PROJ, tokens_d), BF16),
            shape_of((8, tokens_d)),
        ]
        + [shape_of((3, tokens_q, tokens_d), BF16)] * small_enough,
        [pltpu.VMEM((PROJ, tokens_d), F32)],
        room=room,
    )
    stats = stats + swapped(stats, near_masks[0])
    over_y = swapped(stats, other_y)
    over_x = swapped(stats, 1, "stream")
    pairs = [(k * size + r, (1 - k) * size + (r ^ other_y)) for k in range(2) for r in every]
    over_both = lax.ppermute(stats, ("stream", "dp"), pairs)
    dq, dq_send, keep, send, loss = call(
        partial(matching_back, size, doc_masks, lanes),
        (scale, lens, totals, el, hot, stats, over_y, over_x, over_both, *ready),
        [SMEM, HBM] + [VMEM] * (7 + len(ready)),
        [shape_of((tokens_q // 2, PROJ), BF16)] * 2
        + [shape_of((tokens_d // 2, PROJ), BF16)] * 2
        + [shape_of((8, 128))],
        [
            pltpu.VMEM((tokens_q, PROJ), F32),
            pltpu.VMEM((3, PROJ, tokens_d), F32),
            pltpu.VMEM((tokens_q // QLEN, 128), F32),
            *scalars,
        ],
        room=room,
    )
    got_dq = swapped(dq_send, near_masks[0])
    for mask in reversed(doc_masks[1:]):
        total, half = added(keep, swapped(send, mask)), keep.shape[0] // 2
        keep, send = total[:half], total[half:]
    got_dd = swapped(send, doc_masks[0])
    dq, dd = call(
        two_sums,
        (dq, got_dq, keep, got_dd),
        [VMEM] * 4,
        [shape_of((2 * ROW, PROJ), BF16), shape_of((ROW, PROJ), BF16)],
        room=8,
    )
    dq = added(dq[:ROW], swapped(dq[ROW:], other_y))
    dd = added(dd, swapped(dd, top_mask))
    got = swapped(jnp.where(is_query, dd, dq), 1, "stream")

    one_keep, one_send, tail_keep, tail_send, d_first, gproj, small = call(
        partial(feed_back, size),
        (
            dq, dd, got, xh2, rs2, affine, proj_weight[0], slope, act, xh1, up_weight[0],
            down_weight[0],
        ),
        [VMEM] * 3 + [HELD] * 8 + [HBM],
        [shape_of((RING, FIRST, D), BF16)] * 2
        + [shape_of((RING, TAIL, D), BF16)] * 2
        + [shape_of((ROW, D)), shape_of((D, PROJ)), shape_of((8, D))],
        [
            pltpu.VMEM((ROW, FF), BF16),
            pltpu.VMEM((FF, D), BF16),
            pltpu.SemaphoreType.DMA((4,)),
        ],
        room=24,
    )
    two_keep, two_ahead, two_send, tokens_grad = call(
        partial(attend_back, size),
        (
            d_first, gproj, small, loss, tail_keep, tail_send, xh1, rs1, affine, mixed, out_weight[0], qkv, probs, rope,
            tokens[0], qkv_weight[0],
        ),
        [VMEM] * 6 + [HELD] * 10,
        [shape_of((count, SECOND, D), BF16) for count in (RING, len(AHEAD), len(LATER))]
        + [shape_of((ROW, D))],
        [
            pltpu.VMEM((ROW, 3 * D), BF16),
            pltpu.VMEM((4 * D + 16 * RING, D), F32),
        ],
        room=24,
    )
    one, two = [
        Summed(keep, sends, others)
        for keep, *sends in ((one_keep, one_send), (two_keep, two_ahead, two_send))
    ]
    token, outs = tokens_grad, ()
    for event in ORDER:
        kind, k, *group = event
        if kind == "spread":
            jobs = event[1]
            halves = [
                (piece.near if mine else piece.far)[group] for mine, group in jobs for piece in (one, two)
            ]
            *halves, _ = lax.optimization_barrier((*halves, token))
            others = [*two.near, *two.far] if event == ORDER[-1] else []
            outs = spread_call(size, jobs, halves, outs[:5], others)
            token = outs[0]
            continue
        piece = (one, two)[k]
        token = getattr(piece, kind)(*group, token)
    grad_down, grad_up, grad_qkv, grad_out, grad_proj = outs[:5]
    (
        grad_bqkv, grad_bout, grad_g1, grad_s1, grad_bup, grad_bdown, grad_g2, grad_s2, loss,
        scale_grad,
    ) = outs[5:]
    return (
        loss.reshape(()),
        tokens_grad[None],
        grad_qkv[None],
        grad_bqkv,
        grad_out[None],
        grad_bout,
        grad_g1,
        grad_s1,
        grad_up[None],
        grad_bup,
        grad_down[None],
        grad_bdown,
        grad_g2,
        grad_s2,
        grad_proj[None],
        scale_grad.reshape(()),
    )


def solution(mesh):
    return jax.shard_map(
        per_device,
        mesh=mesh,
        in_specs=(
            P("stream", "dp", None),
            P("stream", None, None),
            P("stream", None),
            P("stream", None, None),
            P("stream", None),
            P("stream", None),
            P("stream", None),
            P("stream", None, None),
            P("stream", None),
            P("stream", None, None),
            P("stream", None),
            P("stream", None),
            P("stream", None),
            P("stream", None, None),
            P(),
            P(),
            P("dp"),
        ),
        out_specs=(
            P(),
            P("stream", "dp", None),
            P("stream", None, None),
            P("stream", None),
            P("stream", None, None),
            P("stream", None),
            P("stream", None),
            P("stream", None),
            P("stream", None, None),
            P("stream", None),
            P("stream", None, None),
            P("stream", None),
            P("stream", None),
            P("stream", None),
            P("stream", None, None),
            P(),
        ),
        check_vma=False,
    )
```

```python
from functools import partial
import math

import jax
import jax.numpy as jnp
import numpy as np
from jax import lax
from jax.experimental import pallas as pl
from jax.experimental.pallas import tpu as pltpu
from jax.sharding import PartitionSpec as P

D = 512
HEADS = 8
HD = 64
FF = 2048
PROJ = 128
QLEN = 32
DOCS_ROW = 4
ROW = 256
EXT = 16
RANGES = (64, 96, 128)

SHARPNESS = 8.0
EPS_NORM = 1e-06
EPS_LAYER = 1e-05
LOG2E = 1.4426950408889634

F32 = jnp.float32
BF16 = jnp.bfloat16
REST = 2304
SHARE = 32
DOWN = FF // 16
HEAD = 80
TAIL = DOWN - HEAD
FIRST = DOWN + HEAD
SECOND = REST // 16 + TAIL
CIRCLE = (0, 2, 4, 6, 7, 5, 3, 1)
RING = len(CIRCLE)
AHEAD = (RING // 2, RING // 2 - 1)
LATER = tuple(k for k in range(RING) if k not in AHEAD)
GROUPS = ((0, 1, 2, 3, 5, 6, 7), (4,))
STEP_COST = 3 * 10**7
SPREAD_COST = 0
ROUND = (("step", 0), ("step", 1))
ORDER = (
    (("open", 0), ("open", 1), ("total", 0), ("total", 1), ("tokens", 0)) + ROUND * 7
    + (("share", 0, 0), ("share", 1, 0), ("spread", ((True, 0),)), ("spread", ((False, 0),))) + ROUND
    + (("share", 0, 1), ("share", 1, 1), ("spread", ((True, 1), (False, 1))))
)
MIB = 1024 * 1024

VMEM = pl.BlockSpec(memory_space=pltpu.VMEM)
SMEM = pl.BlockSpec(memory_space=pltpu.SMEM)
HBM = pl.BlockSpec(memory_space=pltpu.HBM)
HELD = pl.BlockSpec(memory_space=pltpu.VMEM)


def mm(a, b):
    return lax.dot_general(a, b, (((1,), (0,)), ((), ())), preferred_element_type=F32)


def mm_nt(a, b):
    return lax.dot_general(a, b, (((1,), (1,)), ((), ())), preferred_element_type=F32)


def mm_tn(a, b):
    return lax.dot_general(a, b, (((0,), (0,)), ((), ())), preferred_element_type=F32)


def iota(shape, axis):
    return lax.broadcasted_iota(jnp.int32, shape, axis)


def rope_table():
    half = HD // 2
    freqs = (10000.0 ** (-np.arange(half, dtype=np.float32) / np.float32(half))).astype(np.float32)
    turned = np.arange(ROW, dtype=np.float32)[:, None] * freqs[None, :]
    cosine = np.cos(turned.astype(np.float64))
    sine = np.sin(turned.astype(np.float64))
    cosine = np.concatenate([cosine, cosine, cosine, cosine], axis=1).astype(np.float32)
    sine = np.concatenate([-sine, sine, -sine, sine], axis=1).astype(np.float32)
    parts = []
    for table in (cosine, sine):
        high = table.astype(jnp.bfloat16)
        low = (table - high.astype(np.float32)).astype(jnp.bfloat16)
        parts += [high, low]
    return np.concatenate(parts, axis=1)


def swap_halves(block):
    lane = iota(block.shape, 1)
    return jnp.where(lane % HD < HD // 2, pltpu.roll(block, 96, 1), pltpu.roll(block, 32, 1))


def bounds_of(lens_ref, row):
    ends, total = [], jnp.int32(0)
    for k in range(DOCS_ROW):
        total = total + lens_ref[k, row]
        ends.append(total)
    return ends


def segment_of(spot, ends):
    seg = jnp.zeros_like(spot)
    for end in ends:
        seg = seg + (spot >= end).astype(jnp.int32)
    return seg


def norm_rows(values):
    mean = jnp.mean(values, axis=1, keepdims=True)
    centred = values - mean
    spread = jnp.mean(centred * centred, axis=1, keepdims=True)
    rstd = lax.rsqrt(spread + EPS_LAYER)
    return centred * rstd, rstd


def norm_back(d_out, xhat, rstd, gain):
    scaled = d_out * gain
    first = jnp.mean(scaled, axis=1, keepdims=True)
    second = jnp.mean(scaled * xhat, axis=1, keepdims=True)
    return rstd * (scaled - first - xhat * second)


def col_sum(values):
    return jnp.sum(values, axis=0, keepdims=True)


def here(size):
    me, stream = lax.axis_index("dp"), lax.axis_index("stream")
    top = size // 2
    has_top = jnp.where((me & top) != 0, 1, 0)
    base = jnp.where(stream == 0, me & ~top, me | top)
    near_at = jnp.where((me & 2) != 0, 1, 0) + jnp.where((me & 1) != 0, 2, 0)
    chip = (me >> 1) % RING
    place = jnp.int32(0)
    for k, one in enumerate(CIRCLE):
        place = jnp.where(chip == one, k, place)
    return me, stream, base, near_at, has_top, me & 1, place


def fetch(pairs, sems):
    copies = [pltpu.make_async_copy(src, dst, sems.at[k]) for k, (src, dst) in enumerate(pairs)]
    for copy in copies:
        copy.start()
    return copies


KEPT = (
    ((ROW, 3 * D), BF16),
    ((ROW, 256), F32),
    ((HEADS, ROW, ROW), BF16),
    ((ROW, D), BF16),
    ((ROW, D), F32),
    ((ROW, 128), F32),
    ((8, D), F32),
)
MOVED = (((ROW, FF), BF16), ((ROW, FF), BF16), ((ROW, D), F32), ((ROW, 128), F32))


def move_kept(*refs):
    count = len(MOVED)
    for copy in fetch([*zip(refs[:count], refs[count:-1])], refs[-1]):
        copy.wait()


def encoder_forward(
    size, lens_hbm, labels_hbm, table_hbm, x_hbm, wqkv_hbm, bqkv_hbm, wout_hbm, bout_hbm,
    g1_hbm, s1_hbm, wup_hbm, bup_hbm, wdown_hbm, bdown_hbm, g2_hbm, s2_hbm, wproj_hbm,
    vec_ref, act_ref, slope_ref, xh2_ref, rs2_ref, qkv_hbm, rope_hbm, probs_hbm, mixed_hbm, xh1_hbm,
    rs1_hbm, affine_hbm,
    qkv_ref, rope_ref, probs_ref, mixed_ref, xh1_ref, rs1_ref, affine_ref, out_sems,
    table_ref, x_ref, wqkv_ref, bqkv_ref, wout_ref, bout_ref, g1_ref, s1_ref, wup_ref, bup_ref,
    wdown_ref, bdown_ref, g2_ref, s2_ref, wproj_ref, lens_ref, labels_ref, sems,
):
    me, stream = here(size)[:2]
    is_query = stream == 0
    scalars = fetch(((lens_hbm, lens_ref), (labels_hbm, labels_ref)), sems.at[pl.ds(15, 2)])
    copies = fetch(
        (
            (table_hbm, table_ref), (x_hbm, x_ref), (wqkv_hbm, wqkv_ref), (bqkv_hbm, bqkv_ref),
            (wout_hbm, wout_ref), (bout_hbm, bout_ref), (g1_hbm, g1_ref), (s1_hbm, s1_ref),
            (bup_hbm, bup_ref), (bdown_hbm, bdown_ref), (g2_hbm, g2_ref), (s2_hbm, s2_ref),
            (wup_hbm, wup_ref), (wdown_hbm, wdown_ref), (wproj_hbm, wproj_ref),
        ),
        sems,
    )
    kept = []

    def keep(src, dst):
        copy = pltpu.make_async_copy(src, dst, out_sems.at[len(kept)])
        copy.start()
        kept.append(copy)

    for copy in scalars:
        copy.wait()
    ends = bounds_of(lens_ref, me)

    def layout(spot):
        seg_doc = segment_of(spot, ends)
        start_doc = jnp.zeros_like(spot)
        for k in range(DOCS_ROW):
            start_doc = jnp.where(seg_doc == k + 1, ends[k], start_doc)
        seg_query = spot // QLEN
        seg = jnp.where(is_query, seg_query, seg_doc)
        start = jnp.where(is_query, seg_query * QLEN, start_doc)
        return seg, start

    shape = (ROW, ROW)
    seg_q, start_q = layout(iota(shape, 0))
    seg_k, _ = layout(iota(shape, 1))
    same = seg_q == seg_k
    onehot = (iota(shape, 1) == iota(shape, 0) - start_q).astype(F32).astype(BF16)
    for copy in copies[:4]:
        copy.wait()
    turned = mm(onehot, table_ref[...])
    cosine = turned[:, :128] + turned[:, 128:256]
    sine = turned[:, 256:384] + turned[:, 384:]
    rope_ref[:, :128] = cosine
    rope_ref[:, 128:] = sine
    keep(rope_ref, rope_hbm)

    x = x_ref[...]
    joined = mm(x, wqkv_ref[...]) + bqkv_ref[...].astype(F32)
    for g in range(2 * D // 128):
        block = joined[:, g * 128 : (g + 1) * 128]
        qkv_ref[:, g * 128 : (g + 1) * 128] = (
            block * cosine + swap_halves(block) * sine
        ).astype(BF16)
    qkv_ref[:, 2 * D :] = joined[:, 2 * D :].astype(BF16)
    keep(qkv_ref, qkv_hbm)

    low_half = iota((ROW, 128), 1) < HD
    for g in range(HEADS // 2):
        q_g = qkv_ref[:, g * 128 : (g + 1) * 128]
        k_g = qkv_ref[:, D + g * 128 : D + (g + 1) * 128]
        v_g = qkv_ref[:, 2 * D + g * 128 : 2 * D + (g + 1) * 128]
        outs = []
        for h in range(2):
            pick = low_half if h == 0 else jnp.logical_not(low_half)
            scores = mm_nt(jnp.where(pick, q_g, jnp.zeros_like(q_g)), k_g) * (1.0 / math.sqrt(HD))
            scores = jnp.where(same, scores, -1e30)
            top = jnp.max(scores, axis=1, keepdims=True)
            exps = jnp.exp(scores - top)
            probs = (exps / jnp.sum(exps, axis=1, keepdims=True)).astype(BF16)
            probs_ref[2 * g + h] = probs
            outs.append(mm(probs, v_g))
        mixed_ref[:, g * 128 : (g + 1) * 128] = jnp.where(low_half, outs[0], outs[1]).astype(BF16)

    keep(probs_ref, probs_hbm)
    keep(mixed_ref, mixed_hbm)
    for copy in copies[4:12]:
        copy.wait()
    for k, ref in enumerate((g1_ref, s1_ref, g2_ref, s2_ref)):
        affine_ref[k : k + 1, :] = ref[...].astype(F32)
    affine_ref[4:, :] = jnp.zeros((4, D), F32)
    keep(affine_ref, affine_hbm)
    attended = mm(mixed_ref[...], wout_ref[...]) + bout_ref[...].astype(F32)
    xhat, rstd = norm_rows(x.astype(F32) + attended)
    xh1_ref[...] = xhat
    rs1_ref[...] = jnp.broadcast_to(rstd, (ROW, 128))
    keep(xh1_ref, xh1_hbm)
    keep(rs1_ref, rs1_hbm)
    first = xhat * g1_ref[...].astype(F32) + s1_ref[...].astype(F32)
    first_low = first.astype(BF16)
    branch = bdown_ref[...].astype(F32) + first
    step = 512
    for copy in copies[12:]:
        copy.wait()
    for c in range(FF // step):
        cols = slice(c * step, (c + 1) * step)
        inner = mm(first_low, wup_ref[:, cols]) + bup_ref[:, cols].astype(F32)
        gate = 0.5 + 0.5 * lax.erf(inner * math.sqrt(0.5))
        bell = jnp.exp2(inner * inner * (-0.5 * LOG2E)) * (1.0 / math.sqrt(2.0 * math.pi))
        act = (inner * gate).astype(BF16)
        act_ref[:, cols] = act
        slope_ref[:, cols] = (gate + inner * bell).astype(BF16)
        branch = branch + mm(act, wdown_ref[cols, :])
    xhat, rstd = norm_rows(branch)
    xh2_ref[...] = xhat
    rs2_ref[...] = jnp.broadcast_to(rstd, (ROW, 128))
    second = xhat * g2_ref[...].astype(F32) + s2_ref[...].astype(F32)
    vec_ref[:ROW, :] = mm(second.astype(BF16), wproj_ref[...]).astype(BF16)
    line = iota((EXT, PROJ), 0)
    tag = jnp.zeros((EXT, PROJ), jnp.int32)
    for k in range(labels_ref.shape[0]):
        label = labels_ref[k]
        tag = jnp.where(line == k, label >> 6, tag)
        tag = jnp.where(line == k + 8, label & 63, tag)
    vec_ref[ROW:, :] = tag.astype(F32).astype(BF16)
    for copy in kept:
        copy.wait()


def prefix_norms(values, axis):
    place = iota(values.shape, axis)
    squared = values * values
    sums = [
        jnp.sum(jnp.where(place < cut, squared, 0.0), axis=axis, keepdims=True) for cut in RANGES
    ]
    return [lax.rsqrt(s + EPS_NORM) for s in sums]


def load_queries(near_ref, far_ref):
    span = ROW + EXT
    rows = []
    for ref in (near_ref, far_ref):
        for k in range(ref.shape[0] // span):
            rows.append(ref[k * span : k * span + ROW, :])
    return jnp.concatenate(rows, axis=0).astype(F32)


def unit_queries(queries, scale):
    lane = iota(queries.shape, 1)
    inverse = prefix_norms(queries, 1)
    unit = [
        jnp.where(lane < cut, queries * (inv * scale), 0.0) for cut, inv in zip(RANGES, inverse)
    ]
    return unit, inverse


def unit_docs(doc_refs, scratch_ref):
    at = 0
    for ref in doc_refs:
        for k in range(ref.shape[0] // ROW):
            scratch_ref[:, at * ROW : (at + 1) * ROW] = ref[
                k * ROW : (k + 1) * ROW, :
            ].astype(F32).T
            at += 1
    turned = scratch_ref[...]
    inverse = prefix_norms(turned, 0)
    place = iota(turned.shape, 0)
    unit = [jnp.where(place < cut, turned * inv, 0.0) for cut, inv in zip(RANGES, inverse)]
    return unit, inverse


def row_ids(base, masks, doc_rows):
    ids = []
    for p in range(doc_rows):
        offset = 0
        for k, mask in enumerate(masks):
            if (p >> k) & 1:
                offset ^= mask
        ids.append(base ^ offset)
    return ids


def doc_marks(lens_ref, ids, lanes, transposed):
    docs = len(ids) * DOCS_ROW
    shape = (lanes, ROW) if transposed else (ROW, lanes)
    spot, lane = (iota(shape, 1), iota(shape, 0)) if transposed else (iota(shape, 0), iota(shape, 1))
    marks = []
    for p, row in enumerate(ids):
        seg = segment_of(spot, bounds_of(lens_ref, row))
        local = jnp.where(seg < DOCS_ROW, seg + p * DOCS_ROW, -1 - lanes)
        marks.append(
            [(lane == local + m * docs).astype(F32).astype(BF16) for m in range(len(RANGES))]
        )
    return marks


def matching_stats(
    size, masks, lanes, scale_ref, lens_ref, near_ref, far_ref, *refs
):
    doc_refs = refs[:-6]
    totals_ref, el_ref, hot_ref, stats_ref, turn_ref, unit_ref = refs[-6:]
    base, near_at = here(size)[2:4]
    span = ROW + EXT
    queries = load_queries(near_ref, far_ref)
    count = queries.shape[0]
    unit_q, _ = unit_queries(queries, SHARPNESS * LOG2E)
    unit_q = [u.astype(BF16) for u in unit_q]
    unit_d, _ = unit_docs(doc_refs, turn_ref)
    for m in range(len(RANGES)):
        unit_ref[m] = unit_d[m].astype(BF16)
    doc_rows = turn_ref.shape[1] // ROW
    docs = doc_rows * DOCS_ROW
    ids = row_ids(base, masks, doc_rows)
    marks = doc_marks(lens_ref, ids, lanes, False)
    totals = jnp.zeros((count, lanes), F32)
    for p in range(doc_rows):
        for m in range(len(RANGES)):
            sims = mm(unit_q[m], unit_ref[m, :, p * ROW : (p + 1) * ROW])
            totals = totals + mm(jnp.exp2(sims).astype(BF16), marks[p][m])
    lane_t = iota((count, lanes), 1)
    totals = jnp.where(lane_t < len(RANGES) * docs, totals, 1.0)
    totals_ref[...] = totals
    shape = (8, lanes)
    lane = iota(shape, 1)
    length = jnp.ones(shape, jnp.int32)
    name = jnp.full(shape, -1, jnp.int32)
    for p in range(doc_rows):
        for k in range(DOCS_ROW):
            own = jnp.zeros(shape, jnp.bool_)
            for m in range(len(RANGES)):
                own = jnp.logical_or(own, lane == m * docs + p * DOCS_ROW + k)
            length = jnp.where(own, lens_ref[k, ids[p]], length)
            name = jnp.where(own, ids[p] * DOCS_ROW + k, name)
    log_length = jnp.log(length.astype(F32))
    matched = (jnp.log(totals) - log_length[:1]) * (1.0 / SHARPNESS)
    per_query = jnp.sum(matched.reshape(count // QLEN, QLEN, lanes), axis=1)
    scale = jnp.exp(jnp.full(shape, scale_ref[0], F32))[:1]
    logits = per_query * (scale * (1.0 / QLEN))
    groups = count // ROW
    tags = []
    for ref in (near_ref, far_ref):
        for k in range(ref.shape[0] // span):
            high = ref[k * span + ROW : k * span + ROW + 8, :].astype(F32).astype(jnp.int32)
            low = ref[k * span + ROW + 8 : k * span + ROW + 16, :].astype(F32).astype(jnp.int32)
            tag = high * 64 + low
            tags.append(jnp.concatenate([tag] * (lanes // 128), axis=1))
    tag = jnp.concatenate(tags, axis=0)
    lane_q = iota(logits.shape, 1)
    valid = lane_q < len(RANGES) * docs
    el = jnp.where(valid, jnp.exp(logits), 0.0)
    hot = jnp.where(jnp.logical_and(valid, jnp.concatenate([name] * groups, axis=0) == tag), 1.0, 0.0)
    el_ref[...] = el
    hot_ref[...] = hot
    place = iota((groups * 8, 128), 1)
    stats = jnp.zeros((groups * 8, 128), F32)
    for k, values in enumerate((el, el * logits, hot * logits)):
        for m in range(len(RANGES)):
            inside = jnp.logical_and(lane_q >= m * docs, lane_q < (m + 1) * docs)
            one = jnp.sum(jnp.where(inside, values, 0.0), axis=1, keepdims=True)
            stats = jnp.where(place == k * 3 + m, one, stats)
    for a in range(groups):
        at = pl.multiple_of((near_at ^ a) * 8, 8)
        stats_ref[pl.ds(at, 8), :] = stats[a * 8 : (a + 1) * 8, :]


def matching_back(
    size, masks, lanes, scale_ref, lens_ref, totals_ref, el_ref, hot_ref, own_ref, over_y, over_x, over_both, unitq_ref, qt_ref, invq_ref, unit_ref, invd_ref, *refs
):
    dq_ref, far_ref, keep_ref, send_ref, loss_ref, dot_ref, dt_ref, stats_ref = refs[-8:]
    _, stream, base, near_at = here(size)[:4]
    total_queries = size * (ROW // QLEN)
    temper = SHARPNESS * LOG2E
    count = unitq_ref.shape[1]
    inv_q = [invq_ref[:, m : m + 1] for m in range(len(RANGES))]
    inv_d = [invd_ref[m : m + 1, :] for m in range(len(RANGES))]
    unit_q = [unitq_ref[m] for m in range(len(RANGES))]
    doc_rows = unit_ref.shape[2] // ROW
    docs = doc_rows * DOCS_ROW
    ids = row_ids(base, masks, doc_rows)
    groups = count // ROW
    odd_y, odd_x = (near_at & 1) == 1, stream == 1
    parts = [own_ref[...], over_y[...], over_x[...], over_both[...]]
    parts = [jnp.where(odd_y, a, b) for a, b in ((parts[1], parts[0]), (parts[0], parts[1]),
                                                  (parts[3], parts[2]), (parts[2], parts[3]))]
    parts = [jnp.where(odd_x, parts[(k + 2) % 4], parts[k]) for k in range(4)]
    stats_ref[...] = (parts[0] + parts[1]) + (parts[2] + parts[3])
    rows = []
    for a in range(groups):
        at = pl.multiple_of((near_at ^ a) * 8, 8)
        rows.append(stats_ref[pl.ds(at, 8), :])
    stats = jnp.concatenate(rows, axis=0)
    place = iota(stats.shape, 1)

    def column(k):
        return jnp.sum(jnp.where(place == k, stats, 0.0), axis=1, keepdims=True)

    shape = (groups * 8, lanes)
    lane_q = iota(shape, 1)
    sums = jnp.ones(shape, F32)
    loss = jnp.zeros((groups * 8, 1), F32)
    moved = jnp.zeros((groups * 8, 1), F32)
    for m in range(len(RANGES)):
        whole, weighted, picked = column(m), column(3 + m), column(6 + m)
        inside = jnp.logical_and(lane_q >= m * docs, lane_q < (m + 1) * docs)
        sums = jnp.where(inside, whole, sums)
        loss = loss + (jnp.log(whole) - picked)
        moved = moved + (weighted / whole - picked)
    line = iota((8, 128), 0)
    loss = jnp.where(
        line == 0,
        jnp.sum(loss, axis=0, keepdims=True) * (1.0 / total_queries),
        jnp.where(line == 1, jnp.sum(moved, axis=0, keepdims=True) * (1.0 / total_queries), 0.0),
    )
    loss_ref[...] = loss
    marks = doc_marks(lens_ref, ids, lanes, True)
    scale = jnp.exp(jnp.full((8, lanes), scale_ref[0], F32))[:1]
    coeff = (el_ref[...] / sums - hot_ref[...]) * (scale * (1.0 / (QLEN * total_queries)))
    coeff = jnp.broadcast_to(coeff[:, None, :], (groups * 8, QLEN, lanes)).reshape(count, lanes)
    ratio = coeff / totals_ref[...]
    ratio_high = ratio.astype(BF16)
    ratio_low = (ratio - ratio_high.astype(F32)).astype(BF16)
    ratio = jnp.concatenate([ratio_high, ratio_low], axis=1)
    for m in range(len(RANGES)):
        grad = jnp.zeros((count, PROJ), F32)
        for p in range(doc_rows):
            block = unit_ref[m, :, p * ROW : (p + 1) * ROW]
            mark = marks[p][m]
            if len(refs) > 8:
                exps = refs[0][m, :, p * ROW : (p + 1) * ROW].astype(F32)
            else:
                exps = jnp.exp2(mm(unit_q[m], block))
            d_sims = (exps * mm(ratio, jnp.concatenate([mark, mark], axis=0))).astype(BF16)
            grad = grad + mm_nt(d_sims, block)
            dt_ref[m, :, p * ROW : (p + 1) * ROW] = mm(qt_ref[m], d_sims)
        unit = unit_q[m].astype(F32) * (1.0 / temper)
        along = jnp.sum(grad * unit, axis=1, keepdims=True)
        part = inv_q[m] * (grad - unit * along)
        if m == 0:
            dot_ref[...] = part
        else:
            dot_ref[...] += part
    dq_ref[...] = dot_ref[: count // 2, :].astype(BF16)
    far_ref[...] = dot_ref[count // 2 :, :].astype(BF16)
    total = jnp.zeros(unit_ref.shape[1:], F32)
    for m in range(len(RANGES)):
        grad = dt_ref[m] * (1.0 / temper)
        unit = unit_ref[m].astype(F32)
        along = jnp.sum(grad * unit, axis=0, keepdims=True)
        total = total + inv_d[m] * (grad - unit * along)
    for p in range(doc_rows):
        ref, at = (keep_ref, p) if p < doc_rows // 2 else (send_ref, p - doc_rows // 2)
        ref[at * ROW : (at + 1) * ROW, :] = total[:, p * ROW : (p + 1) * ROW].T.astype(BF16)


def matching_ready(near_ref, far_ref, *refs):
    doc_refs = refs[:-6] if refs[-2].shape[0] != len(RANGES) else refs[:-7]
    unitq_ref, qt_ref, invq_ref, unit_ref, invd_ref = refs[len(doc_refs) : len(doc_refs) + 5]
    turn_ref = refs[-1]
    queries = load_queries(near_ref, far_ref)
    unit_q, inv_q = unit_queries(queries, SHARPNESS * LOG2E)
    unit_d, inv_d = unit_docs(doc_refs, turn_ref)
    lane = iota(invq_ref.shape, 1)
    columns = jnp.zeros(invq_ref.shape, F32)
    invd_ref[...] = jnp.zeros_like(invd_ref)
    for m in range(len(RANGES)):
        unitq_ref[m] = unit_q[m].astype(BF16)
        unit_ref[m] = unit_d[m].astype(BF16)
        qt_ref[m] = unit_q[m].T.astype(BF16)
        columns = jnp.where(lane == m, inv_q[m], columns)
        invd_ref[m : m + 1, :] = inv_d[m]
        if len(refs) - len(doc_refs) > 6:
            refs[-2][m] = jnp.exp2(mm(unitq_ref[m], unit_ref[m])).astype(BF16)
    invq_ref[...] = columns


def pick_rows(size, here_ref, there_ref, rows_ref):
    _, stream, _, _, has_top = here(size)[:5]
    rows_ref[...] = jnp.where(has_top == stream, here_ref[...], there_ref[...])


def add_rows(rows_ref, got_ref, sum_ref):
    sum_ref[...] = (rows_ref[...].astype(F32) + got_ref[...].astype(F32)).astype(BF16)


DIGITS = 10
POINT = 20


def digits_of(value):
    fixed = (value * float(1 << POINT)).astype(jnp.int32)
    size = jnp.abs(fixed)
    lane = iota(value.shape, 1)
    digits = jnp.zeros(value.shape, jnp.int32)
    for k in range(DIGITS):
        digits = jnp.where(lane == k, (size >> (3 * k)) & 7, digits)
    return jnp.where(fixed < 0, -digits, digits).astype(F32)


def value_of(digits):
    lane = iota(digits.shape, 1)
    half = DIGITS // 2
    weight = jnp.zeros(digits.shape, F32)
    for k in range(half):
        weight = jnp.where(jnp.logical_or(lane == k, lane == k + half), float(8**k), weight)
    low = jnp.sum(jnp.where(lane < half, digits * weight, 0.0))
    high = jnp.sum(jnp.where(jnp.logical_and(lane >= half, lane < DIGITS), digits * weight, 0.0))
    return (high * float(8**half) + low) * (1.0 / (1 << POINT))


def turn(core, place, block):
    return jnp.where(core == 0, place - block, block - place) & (RING - 1)


def block_at(core, place, distance):
    return jnp.where(core == 0, place - distance, place + distance) & (RING - 1)


def store_block(keep_ref, send_ref, rows, block, places, value):
    core, place = places
    mine = core == block // RING
    at = turn(block // RING, place, block % RING)

    @pl.when(mine)
    def _():
        keep_ref[at, rows, :] = value

    @pl.when(jnp.logical_not(mine))
    def _():
        send_ref[at, rows, :] = value


def feed_back(
    size, dq_ref, dd_ref, got_ref, xh2_ref, rs2_ref, affine_ref, wproj_ref, slope_ref, act_ref,
    xh1_ref, wup_ref, wdown_hbm,
    keep_ref, send_ref, tail_keep, tail_send, dfirst_ref, gproj_ref, small_ref,
    dinner_ref, wdown_ref, sems,
):
    step = 512
    spans = [slice(c * step, (c + 1) * step) for c in range(FF // step)]
    copies = fetch([(wdown_hbm.at[span, :], wdown_ref.at[span, :]) for span in spans], sems)
    g1, s1, g2, s2 = [affine_ref[k : k + 1, :] for k in range(4)]
    _, stream, _, _, has_top, *places = here(size)
    is_query, docs_there = stream == 0, has_top == 0
    got = got_ref[...].astype(F32)
    d_vec = jnp.where(
        is_query,
        dq_ref[...].astype(F32) + got,
        jnp.where(docs_there, got, dd_ref[...].astype(F32)),
    )
    d_proj = d_vec.astype(BF16)
    xhat = xh2_ref[...]
    gain = g2
    second = (xhat * gain + s2).astype(BF16)
    gproj_ref[...] = mm_tn(second, d_proj)
    d_second = mm_nt(d_proj, wproj_ref[...])
    small_ref[...] = jnp.zeros_like(small_ref)
    small_ref[5:6, :] = col_sum(d_second * xhat)
    small_ref[6:7, :] = col_sum(d_second)
    d_sum = norm_back(d_second, xhat, rs2_ref[:, :1], gain)
    d_branch = d_sum.astype(BF16)
    small_ref[4:5, :] = col_sum(d_branch.astype(F32))
    d_first = d_sum
    for c in range(FF // step):
        cols = spans[c]
        copies[c].wait()
        d_act = mm_nt(d_branch, wdown_ref[cols, :])
        d_inner = (d_act * slope_ref[:, cols].astype(F32)).astype(BF16)
        dinner_ref[:, cols] = d_inner
        small_ref[c : c + 1, :] = col_sum(d_inner.astype(F32))
        grad = mm_tn(act_ref[:, cols], d_branch).astype(BF16)
        for k in range(step // DOWN):
            store_block(
                keep_ref, send_ref, slice(0, DOWN), c * (step // DOWN) + k, places,
                grad[k * DOWN : (k + 1) * DOWN, :],
            )
        d_first = d_first + mm_nt(d_inner, wup_ref[:, cols])
    dfirst_ref[...] = d_first
    first = (xh1_ref[...] * g1 + s1).astype(BF16)
    for c in range(FF // step):
        cols = slice(c * step, (c + 1) * step)
        grad = mm_tn(first, dinner_ref[:, cols]).astype(BF16)
        for k in range(D // DOWN):
            block = c * (D // DOWN) + k
            start = k * DOWN
            store_block(
                keep_ref, send_ref, slice(DOWN, FIRST), block, places, grad[start : start + HEAD, :]
            )
            store_block(
                tail_keep, tail_send, slice(0, TAIL), block, places,
                grad[start + HEAD : start + DOWN, :],
            )


def attend_back(
    size, dfirst_ref, gproj_ref, small_ref, loss_ref, tail_keep, tail_send, xh1_ref, rs1_ref, affine_ref, mixed_ref, wout_ref,
    qkv_ref, probs_ref, rope_ref, x_ref,
    keep_ref, ahead_ref, send_ref, dsum_ref, djoined_ref, rest_ref,
):
    me, *_, core, place = here(size)
    d_first = dfirst_ref[...]
    xhat = xh1_ref[...]
    gain = affine_ref[0:1, :]
    gain_grad = col_sum(d_first * xhat)
    shift_grad = col_sum(d_first)
    d_sum = norm_back(d_first, xhat, rs1_ref[:, :1], gain)
    d_att = d_sum.astype(BF16)
    bias_out = col_sum(d_att.astype(F32))
    rest_ref[3 * D : 4 * D, :] = mm_tn(mixed_ref[...], d_att)
    d_mixed = mm_nt(d_att, wout_ref[...]).astype(BF16)
    cosine, sine = rope_ref[:, :128], rope_ref[:, 128:]
    low_half = iota((ROW, 128), 1) < HD

    def unrotate(values):
        values = values * (1.0 / math.sqrt(HD))
        return (values * cosine - swap_halves(values) * sine).astype(BF16)

    for g in range(HEADS // 2):
        span = slice(g * 128, (g + 1) * 128)
        q_g = qkv_ref[:, g * 128 : (g + 1) * 128]
        k_g = qkv_ref[:, D + g * 128 : D + (g + 1) * 128]
        v_g = qkv_ref[:, 2 * D + g * 128 : 2 * D + (g + 1) * 128]
        m_g = d_mixed[:, span]
        d_q = jnp.zeros((ROW, 128), F32)
        d_k = jnp.zeros((ROW, 128), F32)
        d_v = jnp.zeros((ROW, 128), F32)
        zero = jnp.zeros((ROW, 128), BF16)
        for h in range(2):
            pick = low_half if h == 0 else jnp.logical_not(low_half)
            probs_low = probs_ref[2 * g + h]
            probs = probs_low.astype(F32)
            m_h = jnp.where(pick, m_g, zero)
            d_probs = mm_nt(m_h, v_g)
            d_v = d_v + mm_tn(probs_low, m_h)
            inner = jnp.sum(d_probs * probs, axis=1, keepdims=True)
            d_scores = (probs * (d_probs - inner)).astype(BF16)
            d_q = d_q + mm(d_scores, jnp.where(pick, k_g, zero))
            d_k = d_k + mm_tn(d_scores, jnp.where(pick, q_g, zero))
        djoined_ref[:, g * 128 : (g + 1) * 128] = unrotate(d_q)
        djoined_ref[:, D + g * 128 : D + (g + 1) * 128] = unrotate(d_k)
        djoined_ref[:, 2 * D + g * 128 : 2 * D + (g + 1) * 128] = d_v.astype(BF16)
    x = x_ref[...]
    dsum_ref[...] = d_sum
    rest_ref[4 * D :, :] = jnp.zeros((8 * 2 * RING, D), F32)
    smalls = []
    for c in range(3):
        cols = slice(c * D, (c + 1) * D)
        d_part = djoined_ref[:, cols]
        rest_ref[c * D : (c + 1) * D, :] = mm_tn(x, d_part)
        smalls.append(col_sum(d_part.astype(F32)))
    smalls += [bias_out, gain_grad, shift_grad] + [small_ref[k : k + 1, :] for k in range(7)]
    counted = jnp.where((me & 3) == 0, 1.0, 0.0)
    lines = [digits_of(loss_ref[k : k + 1, :]) * counted for k in range(2)]
    smalls.append(jnp.concatenate(lines + [jnp.zeros((1, D - 256), F32)], axis=1))
    for k, row in enumerate(smalls):
        rest_ref[4 * D + 8 * k : 4 * D + 8 * k + 1, :] = row
    for k in range(RING):
        sent, at = (ahead_ref, AHEAD.index(k)) if k in AHEAD else (send_ref, LATER.index(k))
        for ref, index, tail_ref, owner in (
            (keep_ref, k, tail_keep, core), (sent, at, tail_send, 1 - core)
        ):
            block = owner * RING + block_at(owner, place, k)
            parts = []
            for c in range(4):
                start = pl.multiple_of(c * D + block * SHARE, SHARE)
                parts.append(rest_ref[pl.ds(start, SHARE), :])
            row = pl.multiple_of(block * SHARE, SHARE)
            parts.append(
                jnp.concatenate(
                    [gproj_ref[pl.ds(row + 8 * j, 8), :] for j in range(SHARE // 8)], axis=1
                )
            )
            parts.append(rest_ref[pl.ds(pl.multiple_of(4 * D + block * 8, 8), 8), :])
            ref[index, : REST // 16, :] = jnp.concatenate(parts, axis=0).astype(BF16)
            ref[index, REST // 16 :, :] = tail_ref[k]


def tokens_back(dsum_ref, djoined_ref, wqkv_ref, tokens_ref):
    tokens = dsum_ref[...]
    for c in range(3):
        cols = slice(c * D, (c + 1) * D)
        tokens = tokens + mm_nt(djoined_ref[:, cols], wqkv_ref[:, cols])
    tokens_ref[...] = tokens


def spread(size, jobs, last, *refs):
    core, place = here(size)[-2:]
    halves = refs[: 2 * len(jobs)]
    wide_one, wide_two, wide_qkv, wide_proj, small_ref, sems = refs[-6:]
    outs = refs[-21:-6] if last else refs[-11:-6]
    down_hbm, up_hbm, qkv_hbm, out_hbm, proj_hbm = outs[:5]
    copies = []

    def move(src, dst):
        copy = pltpu.make_async_copy(src, dst, sems.at[len(copies)])
        copy.start()
        copies.append(copy)

    at = 0
    for job, (mine, group) in enumerate(jobs):
        owner = core if mine else 1 - core
        one_ref, two_ref = halves[2 * job : 2 * job + 2]
        for p, distance in enumerate(GROUPS[group]):
            block = owner * RING + block_at(owner, place, distance)
            wide_one[at] = one_ref[p].astype(F32)
            rows = pl.ds(pl.multiple_of(block * DOWN, DOWN), DOWN)
            move(wide_one.at[at, :DOWN, :], down_hbm.at[rows, :])
            start = (block % (D // DOWN)) * DOWN
            columns = pl.ds(pl.multiple_of((block // (D // DOWN)) * D, D), D)
            rows = pl.ds(pl.multiple_of(start, DOWN), HEAD)
            move(wide_one.at[at, DOWN:, :], up_hbm.at[rows, columns])
            wide = two_ref[p].astype(F32)
            wide_two[at, :SHARE, :] = wide[3 * SHARE : 4 * SHARE, :]
            wide_two[at, SHARE:, :] = wide[REST // 16 :, :]
            rows = pl.ds(pl.multiple_of(start + HEAD, 16), TAIL)
            move(wide_two.at[at, SHARE:, :], up_hbm.at[rows, columns])
            rows = pl.ds(pl.multiple_of(block * SHARE, SHARE), SHARE)
            for c in range(3):
                wide_qkv[at, :, c * D : (c + 1) * D] = wide[c * SHARE : (c + 1) * SHARE, :]
            move(wide_qkv.at[at], qkv_hbm.at[rows, :])
            move(wide_two.at[at, :SHARE, :], out_hbm.at[rows, :])
            for j in range(SHARE // 8):
                wide_proj[at, 8 * j : 8 * j + 8, :] = wide[
                    4 * SHARE : 4 * SHARE + 8, j * PROJ : (j + 1) * PROJ
                ]
            move(wide_proj.at[at], proj_hbm.at[rows, :])
            at += 1
    if last:
        sources = refs[2 * len(jobs) : 2 * len(jobs) + 2 * len(GROUPS)]
        for k, ref in enumerate(sources):
            owner = core if k < len(GROUPS) else 1 - core
            for p, distance in enumerate(GROUPS[k % len(GROUPS)]):
                block = owner * RING + block_at(owner, place, distance)
                line = ref[p, 4 * SHARE : 4 * SHARE + 16, :].astype(F32)[8:, :]
                small_ref[pl.ds(pl.multiple_of(block * 8, 8), 8), :] = line
        rows = [small_ref[8 * k : 8 * k + 1, :] for k in range(14)]
        bqkv_ref, bout_ref, g1_ref, s1_ref, bup_ref, bdown_ref, g2_ref, s2_ref = outs[5:13]
        for k, ref in enumerate(outs[13:]):
            ref[0] = value_of(rows[13][:, k * 128 : (k + 1) * 128])
        for c in range(3):
            bqkv_ref[:, c * D : (c + 1) * D] = rows[c]
        bout_ref[...] = rows[3]
        g1_ref[...] = rows[4]
        s1_ref[...] = rows[5]
        for c in range(4):
            bup_ref[:, c * D : (c + 1) * D] = rows[6 + c]
        bdown_ref[...] = rows[10]
        g2_ref[...] = rows[11]
        s2_ref[...] = rows[12]
    for copy in copies:
        copy.wait()


def spread_call(size, jobs, halves, outs, others):
    last = len(others) > 0
    shapes = ((FF, D), (D, FF), (D, 3 * D), (D, D), (D, PROJ))
    widths = (3 * D, D, D, D, FF, D, D, D) if last else ()
    args = [*halves, *others, *outs]
    count = sum(len(GROUPS[group]) for _, group in jobs)
    before = len(halves) + len(others)
    return call(
        partial(spread, size, jobs, last),
        args,
        [VMEM] * before + [HBM] * len(outs),
        [pltpu.HBM(shape, F32) for shape in shapes]
        + [shape_of((1, width)) for width in widths]
        + [shape_of((1,))] * (2 * last),
        [
            pltpu.VMEM((count, FIRST, D), F32),
            pltpu.VMEM((count, SHARE + TAIL, D), F32),
            pltpu.VMEM((count, SHARE, 3 * D), F32),
            pltpu.VMEM((count, SHARE, PROJ), F32),
            pltpu.VMEM((16 * RING, D), F32),
            pltpu.SemaphoreType.DMA((6 * count,)),
        ],
        out_specs=[HBM] * 5 + [VMEM] * len(widths) + [SMEM] * (2 * last),
        aliases={before + k: k for k in range(len(outs))},
        cost=SPREAD_COST,
        room=14,
    )


def shape_of(shape, dtype=F32):
    return jax.ShapeDtypeStruct(tuple(shape), dtype)


def call(kernel, args, specs, outs, scratch=(), room=24, out_specs=None, aliases={}, cost=10**7):
    spaces = {id(HBM): pltpu.HBM, id(HELD): pltpu.VMEM}
    args = [
        pltpu.with_memory_space_constraint(arg, spaces[id(spec)]) if id(spec) in spaces else arg
        for arg, spec in zip(args, specs)
    ]
    return pl.pallas_call(
        kernel,
        out_shape=outs,
        in_specs=specs,
        out_specs=out_specs or [VMEM] * len(outs),
        scratch_shapes=list(scratch),
        input_output_aliases=aliases,
        compiler_params=pltpu.CompilerParams(vmem_limit_bytes=room * MIB),
        cost_estimate=pl.CostEstimate(
            flops=10 * cost, bytes_accessed=cost, transcendentals=0
        ),
    )(*args)


def swapped(value, mask, axis="dp"):
    size = lax.axis_size(axis)
    return lax.ppermute(value, axis, [(k, k ^ mask) for k in range(size)])


def added(a, b):
    return (a.astype(F32) + b.astype(F32)).astype(BF16)


def join_blocks(*refs):
    for k, ref in enumerate(refs[:-1]):
        refs[-1][k] = ref[0]


def ring_swap(value, onward):
    size = lax.axis_size("dp")
    pairs = []
    for k in range(size):
        at = CIRCLE.index((k >> 1) % RING)
        to = CIRCLE[(at + (1 if (k % 2 == 0) == onward else -1)) % RING]
        pairs.append((k, (k & ~(2 * RING - 1)) | (to << 1) | (k & 1)))
    return lax.ppermute(value, "dp", pairs)


def add_blocks(places, *refs):
    count = len(places)
    held_ref = refs[count] if any(place is not None for place in places) else None
    for k, place in enumerate(places):
        value = refs[k][...]
        if place is not None:
            value = (value.astype(F32) + held_ref[place : place + 1].astype(F32)).astype(BF16)
        refs[-count + k][...] = value


def first_blocks(places, keep_ref, pair_ref, *outs):
    for ref, (k, j) in zip(outs, places):
        ref[0] = (keep_ref[k].astype(F32) + pair_ref[j].astype(F32)).astype(BF16)


def later_blocks(places, keep_ref, pair_ref, out_ref):
    for k in AHEAD:
        out_ref[k] = jnp.zeros(out_ref.shape[1:], BF16)
    for k, j in places:
        out_ref[k] = (keep_ref[k].astype(F32) + pair_ref[j].astype(F32)).astype(BF16)


class Summed:
    def __init__(self, keep, sends, others):
        self.keep, self.others, self.hop = keep, others, 0
        self.pairs = [swapped(send, 1) for send in sends]
        self.sent, self.blocks, self.near, self.far = [], {}, [], []

    def blocks_call(self, blocks, places, held):
        return call(
            partial(add_blocks, places),
            (*blocks, *held),
            [VMEM] * (len(blocks) + len(held)),
            [shape_of(block.shape, BF16) for block in blocks],
            room=8,
            cost=STEP_COST,
        )

    def open(self, after):
        keep, pair, _ = lax.optimization_barrier((self.keep, self.pairs[0], after))
        shape = (1, *keep.shape[1:])
        places = [(k, AHEAD.index(k) if len(self.pairs) > 1 else k) for k in AHEAD]
        first, second = call(
            partial(first_blocks, places),
            (keep, pair),
            [VMEM] * 2,
            [shape_of(shape, BF16)] * 2,
            room=8,
            cost=STEP_COST,
        )
        self.sent = [(first, True), (second, False)]
        return second

    def total(self, after):
        keep, _ = lax.optimization_barrier((self.keep, after))
        later = [(k, LATER.index(k) if len(self.pairs) > 1 else k) for k in LATER]
        (self.keep,) = call(
            partial(later_blocks, later),
            (keep, self.pairs[-1]),
            [VMEM] * 2,
            [shape_of(keep.shape, BF16)],
            room=8,
            cost=STEP_COST,
        )
        return self.keep

    def step(self, after):
        half = RING // 2
        self.hop += 1
        hop = self.hop
        *got, _ = lax.optimization_barrier((*[ring_swap(*one) for one in self.sent], after))
        if hop < half:
            out = self.blocks_call(got, (half + hop, half - 1 - hop), [self.keep])
            self.part = out[1]
        elif hop == half:
            (own,) = self.blocks_call(got, (0,), [self.part])
            for mask in self.others:
                own = added(own, swapped(own, mask))
            self.blocks[0] = own
            out = [own, own]
        else:
            out = self.blocks_call(got, (None,) * len(got), [])
            hop -= half
            self.blocks[hop] = out[0]
            if hop < half:
                self.blocks[RING - hop] = out[1]
        if hop == half - 1:
            self.sent = [(out[0], True)]
        elif self.hop < 2 * half:
            self.sent = [(out[0], True), (out[1], False)]
        return out[0]

    def share(self, group, after):
        *blocks, _ = lax.optimization_barrier((*[self.blocks[k] for k in GROUPS[group]], after))
        shape = (len(blocks), *blocks[0].shape[1:])
        self.near += call(
            join_blocks, blocks, [VMEM] * len(blocks), [shape_of(shape, BF16)], room=8, cost=0
        )
        self.far.append(swapped(self.near[-1], 1))
        return self.near[-1]


def per_device(
    tokens, qkv_weight, qkv_bias, out_weight, out_bias, first_gain, first_shift, up_weight,
    up_bias, down_weight, down_bias, second_gain, second_shift, proj_weight, log_scale,
    doc_lengths, labels,
):
    size = lax.axis_size("dp")
    bits = [1 << k for k in range(size.bit_length() - 1)]
    near_masks, doc_masks = bits[:2], bits[2:]
    top_mask, doc_masks = doc_masks[-1], doc_masks[:-1]
    others = bits[4:]
    me = lax.axis_index("dp")
    stream = lax.axis_index("stream")
    is_query = stream == 0
    has_top = (me & top_mask) != 0
    lens = doc_lengths.T
    scale = log_scale.reshape(1)

    vec, *moved, qkv, rope, probs, mixed, xh1, rs1, affine = call(
        partial(encoder_forward, size),
        (
            lens, labels, jnp.asarray(rope_table()), tokens[0], qkv_weight[0], qkv_bias,
            out_weight[0], out_bias, first_gain, first_shift, up_weight[0], up_bias,
            down_weight[0], down_bias, second_gain, second_shift, proj_weight[0],
        ),
        [HBM] * 17,
        [shape_of((ROW + EXT, PROJ), BF16)]
        + [shape_of(*kind) for kind in MOVED]
        + [pltpu.HBM(*kind) for kind in KEPT],
        [pltpu.VMEM(*kind) for kind in KEPT]
        + [pltpu.SemaphoreType.DMA((len(KEPT),))]
        + [
            pltpu.VMEM(shape, BF16)
            for shape in (
                (ROW, 512), (ROW, D), (D, 3 * D), (1, 3 * D), (D, D), (1, D), (1, D), (1, D), (D, FF),
                (1, FF), (FF, D), (1, D), (1, D), (1, D), (D, PROJ),
            )
        ]
        + [
            pltpu.SMEM(lens.shape, jnp.int32),
            pltpu.SMEM(labels.shape, jnp.int32),
            pltpu.SemaphoreType.DMA((17,)),
        ],
        room=40,
        out_specs=[VMEM] * (1 + len(MOVED)) + [HBM] * len(KEPT),
    )
    act, slope, xh2, rs2 = call(
        move_kept,
        moved,
        [VMEM] * len(MOVED),
        [pltpu.HBM(*kind) for kind in MOVED],
        [pltpu.SemaphoreType.DMA((len(MOVED),))],
        room=8,
        out_specs=[HBM] * len(MOVED),
        cost=STEP_COST,
    )

    every, other_y = range(size), near_masks[1]
    other, _ = lax.optimization_barrier((swapped(vec, 1, "stream"), rs2))
    near = jnp.where(is_query, vec, other)
    rows = jnp.where(is_query, other, vec)[:ROW]
    moved = swapped(rows, top_mask)
    (rows,) = call(
        partial(pick_rows, size),
        (rows, moved),
        [VMEM] * 2,
        [shape_of((ROW, PROJ), BF16)],
        room=8,
        cost=STEP_COST,
    )
    got_y, _ = lax.optimization_barrier((swapped(near, other_y), rows))
    near = jnp.concatenate([near, got_y], axis=0)
    far = swapped(near, near_masks[0])
    pieces = []
    for k, mask in enumerate(doc_masks):
        pieces.append(rows)
        got = swapped(rows, mask)
        if k + 1 < len(doc_masks):
            rows = jnp.concatenate([rows, got], axis=0)
        else:
            pieces = [rows, got]
    doc_rows = sum(p.shape[0] for p in pieces) // ROW
    tokens_d = doc_rows * ROW
    tokens_q = 4 * ROW
    lanes = -(-3 * doc_rows * DOCS_ROW // 128) * 128
    room = 20 if doc_rows <= 4 else 56
    totals, el, hot, stats = call(
        partial(matching_stats, size, doc_masks, lanes),
        (scale, lens, near, far, *pieces),
        [SMEM] * 2 + [VMEM] * (2 + len(pieces)),
        [
            shape_of((tokens_q, lanes)),
            shape_of((tokens_q // QLEN, lanes)),
            shape_of((tokens_q // QLEN, lanes)),
            shape_of((tokens_q // QLEN, 128)),
        ],
        [pltpu.VMEM((PROJ, tokens_d), F32), pltpu.VMEM((3, PROJ, tokens_d), BF16)],
        room=room,
    )
    small_enough = doc_rows <= 4
    ready = call(
        matching_ready,
        (near, far, *pieces),
        [VMEM] * (2 + len(pieces)),
        [
            shape_of((3, tokens_q, PROJ), BF16),
            shape_of((3, PROJ, tokens_q), BF16),
            shape_of((tokens_q, 128)),
            shape_of((3, PROJ, tokens_d), BF16),
            shape_of((8, tokens_d)),
        ]
        + [shape_of((3, tokens_q, tokens_d), BF16)] * small_enough,
        [pltpu.VMEM((PROJ, tokens_d), F32)],
        room=room,
    )
    stats = stats + swapped(stats, near_masks[0])
    over_y = swapped(stats, other_y)
    over_x = swapped(stats, 1, "stream")
    pairs = [(k * size + r, (1 - k) * size + (r ^ other_y)) for k in range(2) for r in every]
    over_both = lax.ppermute(stats, ("stream", "dp"), pairs)
    dq, dq_send, keep, send, loss = call(
        partial(matching_back, size, doc_masks, lanes),
        (scale, lens, totals, el, hot, stats, over_y, over_x, over_both, *ready),
        [SMEM] * 2 + [VMEM] * (7 + len(ready)),
        [shape_of((tokens_q // 2, PROJ), BF16)] * 2
        + [shape_of((tokens_d // 2, PROJ), BF16)] * 2
        + [shape_of((8, 128))],
        [
            pltpu.VMEM((tokens_q, PROJ), F32),
            pltpu.VMEM((3, PROJ, tokens_d), F32),
            pltpu.VMEM((tokens_q // QLEN, 128), F32),
        ],
        room=room,
    )
    got_dq = swapped(dq_send, near_masks[0])
    for mask in reversed(doc_masks[1:]):
        total, half = added(keep, swapped(send, mask)), keep.shape[0] // 2
        keep, send = total[:half], total[half:]
    got_dd = swapped(send, doc_masks[0])
    def summed(rows, got, after=None):
        if after is not None:
            got, _ = lax.optimization_barrier((got, after))
        return call(
            add_rows, (rows, got), [VMEM] * 2, [shape_of(rows.shape, BF16)], room=8, cost=STEP_COST
        )[0]

    dq = summed(dq, got_dq)
    dd = summed(keep, got_dd, dq)
    dd = summed(dd, swapped(dd, top_mask))
    dq = summed(dq[:ROW], swapped(dq[ROW:], other_y), dd)
    got = swapped(jnp.where(is_query, dd, dq), 1, "stream")

    one_keep, one_send, tail_keep, tail_send, d_first, gproj, small = call(
        partial(feed_back, size),
        (
            dq, dd, got, xh2, rs2, affine, proj_weight[0], slope, act, xh1, up_weight[0],
            down_weight[0],
        ),
        [VMEM] * 3 + [HELD] * 8 + [HBM],
        [shape_of((RING, FIRST, D), BF16)] * 2
        + [shape_of((RING, TAIL, D), BF16)] * 2
        + [shape_of((ROW, D)), shape_of((D, PROJ)), shape_of((8, D))],
        [
            pltpu.VMEM((ROW, FF), BF16),
            pltpu.VMEM((FF, D), BF16),
            pltpu.SemaphoreType.DMA((4,)),
        ],
        room=24,
    )
    two_keep, two_ahead, two_send, d_sum, d_joined = call(
        partial(attend_back, size),
        (
            d_first, gproj, small, loss, tail_keep, tail_send, xh1, rs1, affine, mixed, out_weight[0], qkv, probs, rope,
            tokens[0],
        ),
        [VMEM] * 6 + [HELD] * 9,
        [shape_of((count, SECOND, D), BF16) for count in (RING, len(AHEAD), len(LATER))]
        + [shape_of((ROW, D)), shape_of((ROW, 3 * D), BF16)],
        [pltpu.VMEM((4 * D + 16 * RING, D), F32)],
        room=24,
    )
    one, two = [
        Summed(keep, sends, others)
        for keep, *sends in ((one_keep, one_send), (two_keep, two_ahead, two_send))
    ]
    token, outs = d_sum, ()
    for event in ORDER:
        kind, k, *group = event
        if kind == "tokens":
            d_sum, _ = lax.optimization_barrier((d_sum, token))
            (tokens_grad,) = call(
                tokens_back,
                (d_sum, d_joined, qkv_weight[0]),
                [VMEM] * 3,
                [shape_of((ROW, D))],
                room=8,
                cost=STEP_COST,
            )
            token = tokens_grad
            continue
        if kind == "spread":
            jobs = event[1]
            halves = [
                (piece.near if mine else piece.far)[group] for mine, group in jobs for piece in (one, two)
            ]
            *halves, _ = lax.optimization_barrier((*halves, token))
            others = [*two.near, *two.far] if event == ORDER[-1] else []
            outs = spread_call(size, jobs, halves, outs[:5], others)
            token = outs[0]
            continue
        piece = (one, two)[k]
        token = getattr(piece, kind)(*group, token)
    grad_down, grad_up, grad_qkv, grad_out, grad_proj = outs[:5]
    (
        grad_bqkv, grad_bout, grad_g1, grad_s1, grad_bup, grad_bdown, grad_g2, grad_s2, loss,
        scale_grad,
    ) = outs[5:]
    return (
        loss.reshape(()),
        tokens_grad[None],
        grad_qkv[None],
        grad_bqkv,
        grad_out[None],
        grad_bout,
        grad_g1,
        grad_s1,
        grad_up[None],
        grad_bup,
        grad_down[None],
        grad_bdown,
        grad_g2,
        grad_s2,
        grad_proj[None],
        scale_grad.reshape(()),
    )


def solution(mesh):
    return jax.shard_map(
        per_device,
        mesh=mesh,
        in_specs=(
            P("stream", "dp", None),
            P("stream", None, None),
            P("stream", None),
            P("stream", None, None),
            P("stream", None),
            P("stream", None),
            P("stream", None),
            P("stream", None, None),
            P("stream", None),
            P("stream", None, None),
            P("stream", None),
            P("stream", None),
            P("stream", None),
            P("stream", None, None),
            P(),
            P(),
            P("dp"),
        ),
        out_specs=(
            P(),
            P("stream", "dp", None),
            P("stream", None, None),
            P("stream", None),
            P("stream", None, None),
            P("stream", None),
            P("stream", None),
            P("stream", None),
            P("stream", None, None),
            P("stream", None),
            P("stream", None, None),
            P("stream", None),
            P("stream", None),
            P("stream", None),
            P("stream", None, None),
            P(),
        ),
        check_vma=False,
    )
```

```python
from functools import partial
import math

import jax
import jax.numpy as jnp
import numpy as np
from jax import lax
from jax.experimental import pallas as pl
from jax.experimental.pallas import tpu as pltpu
from jax.sharding import PartitionSpec as P

D = 512
HEADS = 8
HD = 64
FF = 2048
PROJ = 128
QLEN = 32
DOCS_ROW = 4
ROW = 256
EXT = 16
RANGES = (64, 96, 128)

SHARPNESS = 8.0
EPS_NORM = 1e-06
EPS_LAYER = 1e-05
LOG2E = 1.4426950408889634

F32 = jnp.float32
BF16 = jnp.bfloat16
REST = 2304
SHARE = 32
DOWN = FF // 16
HEAD = 80
TAIL = DOWN - HEAD
FIRST = DOWN + HEAD
SECOND = REST // 16 + TAIL
CIRCLE = (0, 2, 4, 6, 7, 5, 3, 1)
RING = len(CIRCLE)
AHEAD = (RING // 2, RING // 2 - 1)
LATER = tuple(k for k in range(RING) if k not in AHEAD)
GROUPS = ((0, 1, 2, 3, 5, 6, 7), (4,))
STEP_COST = 3 * 10**7
SPREAD_COST = 0
ROUND = (("step", 0), ("step", 1))
ORDER = (
    (("open", 0), ("open", 1), ("total", 0), ("total", 1), ("tokens", 0)) + ROUND * 7
    + (("share", 0, 0), ("share", 1, 0), ("spread", ((True, 0),)), ("spread", ((False, 0),))) + ROUND
    + (("share", 0, 1), ("share", 1, 1), ("spread", ((True, 1), (False, 1))))
)
MIB = 1024 * 1024

VMEM = pl.BlockSpec(memory_space=pltpu.VMEM)
SMEM = pl.BlockSpec(memory_space=pltpu.SMEM)
HBM = pl.BlockSpec(memory_space=pltpu.HBM)
HELD = pl.BlockSpec(memory_space=pltpu.VMEM)


def mm(a, b):
    return lax.dot_general(a, b, (((1,), (0,)), ((), ())), preferred_element_type=F32)


def mm_nt(a, b):
    return lax.dot_general(a, b, (((1,), (1,)), ((), ())), preferred_element_type=F32)


def mm_tn(a, b):
    return lax.dot_general(a, b, (((0,), (0,)), ((), ())), preferred_element_type=F32)


def iota(shape, axis):
    return lax.broadcasted_iota(jnp.int32, shape, axis)


def rope_table():
    half = HD // 2
    freqs = (10000.0 ** (-np.arange(half, dtype=np.float32) / np.float32(half))).astype(np.float32)
    turned = np.arange(ROW, dtype=np.float32)[:, None] * freqs[None, :]
    cosine = np.cos(turned.astype(np.float64))
    sine = np.sin(turned.astype(np.float64))
    cosine = np.concatenate([cosine, cosine, cosine, cosine], axis=1).astype(np.float32)
    sine = np.concatenate([-sine, sine, -sine, sine], axis=1).astype(np.float32)
    parts = []
    for table in (cosine, sine):
        high = table.astype(jnp.bfloat16)
        low = (table - high.astype(np.float32)).astype(jnp.bfloat16)
        parts += [high, low]
    return np.concatenate(parts, axis=1)


def swapping():
    shape = (128, 128)
    return (iota(shape, 0) == (iota(shape, 1) ^ (HD // 2))).astype(F32).astype(BF16)


def bounds_of(lens_ref, row):
    ends, total = [], jnp.int32(0)
    for k in range(DOCS_ROW):
        total = total + lens_ref[k, row]
        ends.append(total)
    return ends


def segment_of(spot, ends):
    seg = jnp.zeros_like(spot)
    for end in ends:
        seg = seg + (spot >= end).astype(jnp.int32)
    return seg


def norm_rows(values):
    mean = jnp.mean(values, axis=1, keepdims=True)
    centred = values - mean
    spread = jnp.mean(centred * centred, axis=1, keepdims=True)
    rstd = lax.rsqrt(spread + EPS_LAYER)
    return centred * rstd, rstd


def norm_back(d_out, xhat, rstd, gain):
    scaled = d_out * gain
    first = jnp.mean(scaled, axis=1, keepdims=True)
    second = jnp.mean(scaled * xhat, axis=1, keepdims=True)
    return rstd * (scaled - first - xhat * second)


def col_sum(values):
    return jnp.sum(values, axis=0, keepdims=True)


def here(size):
    me, stream = lax.axis_index("dp"), lax.axis_index("stream")
    top = size // 2
    has_top = jnp.where((me & top) != 0, 1, 0)
    base = jnp.where(stream == 0, me & ~top, me | top)
    near_at = jnp.where((me & 2) != 0, 1, 0) + jnp.where((me & 1) != 0, 2, 0)
    chip = (me >> 1) % RING
    place = jnp.int32(0)
    for k, one in enumerate(CIRCLE):
        place = jnp.where(chip == one, k, place)
    return me, stream, base, near_at, has_top, me & 1, place


def fetch(pairs, sems):
    copies = [pltpu.make_async_copy(src, dst, sems.at[k]) for k, (src, dst) in enumerate(pairs)]
    for copy in copies:
        copy.start()
    return copies


KEPT = (
    ((ROW, 3 * D), BF16),
    ((ROW, 256), F32),
    ((HEADS, ROW, ROW), BF16),
    ((ROW, D), BF16),
    ((ROW, D), F32),
    ((ROW, 128), F32),
    ((8, D), F32),
)
MOVED = (((ROW, FF), BF16), ((ROW, FF), BF16), ((ROW, D), F32), ((ROW, 128), F32))


def move_kept(*refs):
    count = len(MOVED)
    for copy in fetch([*zip(refs[:count], refs[count:-1])], refs[-1]):
        copy.wait()


def encoder_forward(
    size, lens_hbm, labels_hbm, table_hbm, x_hbm, wqkv_hbm, bqkv_hbm, wout_hbm, bout_hbm,
    g1_hbm, s1_hbm, wup_hbm, bup_hbm, wdown_hbm, bdown_hbm, g2_hbm, s2_hbm, wproj_hbm,
    vec_ref, act_ref, slope_ref, xh2_ref, rs2_ref, qkv_hbm, rope_hbm, probs_hbm, mixed_hbm, xh1_hbm,
    rs1_hbm, affine_hbm,
    qkv_ref, rope_ref, probs_ref, mixed_ref, xh1_ref, rs1_ref, affine_ref, out_sems,
    table_ref, x_ref, wqkv_ref, bqkv_ref, wout_ref, bout_ref, g1_ref, s1_ref, wup_ref, bup_ref,
    wdown_ref, bdown_ref, g2_ref, s2_ref, wproj_ref, lens_ref, labels_ref, sems,
):
    me, stream = here(size)[:2]
    is_query = stream == 0
    scalars = fetch(((lens_hbm, lens_ref), (labels_hbm, labels_ref)), sems.at[pl.ds(15, 2)])
    copies = fetch(
        (
            (table_hbm, table_ref), (x_hbm, x_ref), (wqkv_hbm, wqkv_ref), (bqkv_hbm, bqkv_ref),
            (wout_hbm, wout_ref), (bout_hbm, bout_ref), (g1_hbm, g1_ref), (s1_hbm, s1_ref),
            (bup_hbm, bup_ref), (bdown_hbm, bdown_ref), (g2_hbm, g2_ref), (s2_hbm, s2_ref),
            (wup_hbm, wup_ref), (wdown_hbm, wdown_ref), (wproj_hbm, wproj_ref),
        ),
        sems,
    )
    kept = []

    def keep(src, dst):
        copy = pltpu.make_async_copy(src, dst, out_sems.at[len(kept)])
        copy.start()
        kept.append(copy)

    for copy in scalars:
        copy.wait()
    ends = bounds_of(lens_ref, me)

    def layout(spot):
        seg_doc = segment_of(spot, ends)
        start_doc = jnp.zeros_like(spot)
        for k in range(DOCS_ROW):
            start_doc = jnp.where(seg_doc == k + 1, ends[k], start_doc)
        seg_query = spot // QLEN
        seg = jnp.where(is_query, seg_query, seg_doc)
        start = jnp.where(is_query, seg_query * QLEN, start_doc)
        return seg, start

    shape = (ROW, ROW)
    seg_q, start_q = layout(iota(shape, 0))
    seg_k, _ = layout(iota(shape, 1))
    same = seg_q == seg_k
    onehot = (iota(shape, 1) == iota(shape, 0) - start_q).astype(F32).astype(BF16)
    for copy in copies[:4]:
        copy.wait()
    turned = mm(onehot, table_ref[...])
    cosine = turned[:, :128] + turned[:, 128:256]
    sine = turned[:, 256:384] + turned[:, 384:]
    rope_ref[:, :128] = cosine
    rope_ref[:, 128:] = sine
    keep(rope_ref, rope_hbm)

    x = x_ref[...]
    joined = mm(x, wqkv_ref[...]) + bqkv_ref[...].astype(F32)
    swap = swapping()
    swap = jnp.concatenate([swap, swap], axis=0)
    for g in range(2 * D // 128):
        block = joined[:, g * 128 : (g + 1) * 128]
        high = block.astype(BF16)
        low = (block - high.astype(F32)).astype(BF16)
        other = mm(jnp.concatenate([high, low], axis=1), swap)
        qkv_ref[:, g * 128 : (g + 1) * 128] = (block * cosine + other * sine).astype(BF16)
    qkv_ref[:, 2 * D :] = joined[:, 2 * D :].astype(BF16)
    keep(qkv_ref, qkv_hbm)

    low_half = iota((ROW, 128), 1) < HD
    for g in range(HEADS // 2):
        q_g = qkv_ref[:, g * 128 : (g + 1) * 128]
        k_g = qkv_ref[:, D + g * 128 : D + (g + 1) * 128]
        v_g = qkv_ref[:, 2 * D + g * 128 : 2 * D + (g + 1) * 128]
        v_ones = jnp.concatenate([v_g, jnp.ones((ROW, 128), BF16)], axis=1)
        outs = []
        for h in range(2):
            pick = low_half if h == 0 else jnp.logical_not(low_half)
            scores = mm_nt(jnp.where(pick, q_g, jnp.zeros_like(q_g)), k_g)
            scores = jnp.where(same, scores * (LOG2E / math.sqrt(HD)), -1e30)
            top = jnp.max(scores, axis=1, keepdims=True)
            exps = jnp.exp2(scores - top)
            both = mm(exps.astype(BF16), v_ones)
            inverse = 1.0 / both[:, 128:]
            probs_ref[2 * g + h] = (exps * jnp.concatenate([inverse, inverse], axis=1)).astype(BF16)
            outs.append(both[:, :128] * inverse)
        mixed_ref[:, g * 128 : (g + 1) * 128] = jnp.where(low_half, outs[0], outs[1]).astype(BF16)

    keep(probs_ref, probs_hbm)
    keep(mixed_ref, mixed_hbm)
    for copy in copies[4:12]:
        copy.wait()
    for k, ref in enumerate((g1_ref, s1_ref, g2_ref, s2_ref)):
        affine_ref[k : k + 1, :] = ref[...].astype(F32)
    affine_ref[4:, :] = jnp.zeros((4, D), F32)
    keep(affine_ref, affine_hbm)
    attended = mm(mixed_ref[...], wout_ref[...]) + bout_ref[...].astype(F32)
    xhat, rstd = norm_rows(x.astype(F32) + attended)
    xh1_ref[...] = xhat
    rs1_ref[...] = jnp.broadcast_to(rstd, (ROW, 128))
    keep(xh1_ref, xh1_hbm)
    keep(rs1_ref, rs1_hbm)
    first = xhat * g1_ref[...].astype(F32) + s1_ref[...].astype(F32)
    first_low = first.astype(BF16)
    branch = bdown_ref[...].astype(F32) + first
    step = 512
    for copy in copies[12:]:
        copy.wait()
    for c in range(FF // step):
        cols = slice(c * step, (c + 1) * step)
        inner = mm(first_low, wup_ref[:, cols]) + bup_ref[:, cols].astype(F32)
        gate = 0.5 + 0.5 * lax.erf(inner * math.sqrt(0.5))
        bell = jnp.exp2(inner * inner * (-0.5 * LOG2E)) * (1.0 / math.sqrt(2.0 * math.pi))
        act = (inner * gate).astype(BF16)
        act_ref[:, cols] = act
        slope_ref[:, cols] = (gate + inner * bell).astype(BF16)
        branch = branch + mm(act, wdown_ref[cols, :])
    xhat, rstd = norm_rows(branch)
    xh2_ref[...] = xhat
    rs2_ref[...] = jnp.broadcast_to(rstd, (ROW, 128))
    second = xhat * g2_ref[...].astype(F32) + s2_ref[...].astype(F32)
    vec_ref[:ROW, :] = mm(second.astype(BF16), wproj_ref[...]).astype(BF16)
    line = iota((EXT, PROJ), 0)
    tag = jnp.zeros((EXT, PROJ), jnp.int32)
    for k in range(labels_ref.shape[0]):
        label = labels_ref[k]
        tag = jnp.where(line == k, label >> 6, tag)
        tag = jnp.where(line == k + 8, label & 63, tag)
    vec_ref[ROW:, :] = tag.astype(F32).astype(BF16)
    for copy in kept:
        copy.wait()


def prefix_norms(values, axis):
    place = iota(values.shape, axis)
    squared = values * values
    sums = [
        jnp.sum(jnp.where(place < cut, squared, 0.0), axis=axis, keepdims=True) for cut in RANGES
    ]
    return [lax.rsqrt(s + EPS_NORM) for s in sums]


def load_queries(near_ref, far_ref):
    span = ROW + EXT
    rows = []
    for ref in (near_ref, far_ref):
        for k in range(ref.shape[0] // span):
            rows.append(ref[k * span : k * span + ROW, :])
    return jnp.concatenate(rows, axis=0).astype(F32)


def unit_queries(queries, scale):
    lane = iota(queries.shape, 1)
    inverse = prefix_norms(queries, 1)
    unit = [
        jnp.where(lane < cut, queries * (inv * scale), 0.0) for cut, inv in zip(RANGES, inverse)
    ]
    return unit, inverse


def unit_docs(doc_refs, scratch_ref):
    at = 0
    for ref in doc_refs:
        for k in range(ref.shape[0] // ROW):
            scratch_ref[:, at * ROW : (at + 1) * ROW] = ref[
                k * ROW : (k + 1) * ROW, :
            ].astype(F32).T
            at += 1
    turned = scratch_ref[...]
    inverse = prefix_norms(turned, 0)
    place = iota(turned.shape, 0)
    unit = [jnp.where(place < cut, turned * inv, 0.0) for cut, inv in zip(RANGES, inverse)]
    return unit, inverse


def row_ids(base, masks, doc_rows):
    ids = []
    for p in range(doc_rows):
        offset = 0
        for k, mask in enumerate(masks):
            if (p >> k) & 1:
                offset ^= mask
        ids.append(base ^ offset)
    return ids


def doc_marks(lens_ref, ids, lanes, transposed):
    docs = len(ids) * DOCS_ROW
    shape = (lanes, ROW) if transposed else (ROW, lanes)
    spot, lane = (iota(shape, 1), iota(shape, 0)) if transposed else (iota(shape, 0), iota(shape, 1))
    marks = []
    for p, row in enumerate(ids):
        seg = segment_of(spot, bounds_of(lens_ref, row))
        local = jnp.where(seg < DOCS_ROW, seg + p * DOCS_ROW, -1 - lanes)
        marks.append(
            [(lane == local + m * docs).astype(F32).astype(BF16) for m in range(len(RANGES))]
        )
    return marks


def matching_stats(
    size, masks, lanes, scale_ref, lens_ref, near_ref, far_ref, *refs
):
    doc_refs = refs[:-6]
    totals_ref, el_ref, hot_ref, stats_ref, turn_ref, unit_ref = refs[-6:]
    base, near_at = here(size)[2:4]
    span = ROW + EXT
    queries = load_queries(near_ref, far_ref)
    count = queries.shape[0]
    unit_q, _ = unit_queries(queries, SHARPNESS * LOG2E)
    unit_q = [u.astype(BF16) for u in unit_q]
    unit_d, _ = unit_docs(doc_refs, turn_ref)
    for m in range(len(RANGES)):
        unit_ref[m] = unit_d[m].astype(BF16)
    doc_rows = turn_ref.shape[1] // ROW
    docs = doc_rows * DOCS_ROW
    ids = row_ids(base, masks, doc_rows)
    marks = doc_marks(lens_ref, ids, lanes, False)
    totals = jnp.zeros((count, lanes), F32)
    for p in range(doc_rows):
        for m in range(len(RANGES)):
            sims = mm(unit_q[m], unit_ref[m, :, p * ROW : (p + 1) * ROW])
            totals = totals + mm(jnp.exp2(sims).astype(BF16), marks[p][m])
    lane_t = iota((count, lanes), 1)
    totals = jnp.where(lane_t < len(RANGES) * docs, totals, 1.0)
    totals_ref[...] = totals
    shape = (8, lanes)
    lane = iota(shape, 1)
    length = jnp.ones(shape, jnp.int32)
    name = jnp.full(shape, -1, jnp.int32)
    for p in range(doc_rows):
        for k in range(DOCS_ROW):
            own = jnp.zeros(shape, jnp.bool_)
            for m in range(len(RANGES)):
                own = jnp.logical_or(own, lane == m * docs + p * DOCS_ROW + k)
            length = jnp.where(own, lens_ref[k, ids[p]], length)
            name = jnp.where(own, ids[p] * DOCS_ROW + k, name)
    log_length = jnp.log(length.astype(F32))
    matched = (jnp.log(totals) - log_length[:1]) * (1.0 / SHARPNESS)
    per_query = jnp.sum(matched.reshape(count // QLEN, QLEN, lanes), axis=1)
    scale = jnp.exp(jnp.full(shape, scale_ref[0], F32))[:1]
    logits = per_query * (scale * (1.0 / QLEN))
    groups = count // ROW
    tags = []
    for ref in (near_ref, far_ref):
        for k in range(ref.shape[0] // span):
            high = ref[k * span + ROW : k * span + ROW + 8, :].astype(F32).astype(jnp.int32)
            low = ref[k * span + ROW + 8 : k * span + ROW + 16, :].astype(F32).astype(jnp.int32)
            tag = high * 64 + low
            tags.append(jnp.concatenate([tag] * (lanes // 128), axis=1))
    tag = jnp.concatenate(tags, axis=0)
    lane_q = iota(logits.shape, 1)
    valid = lane_q < len(RANGES) * docs
    el = jnp.where(valid, jnp.exp(logits), 0.0)
    hot = jnp.where(jnp.logical_and(valid, jnp.concatenate([name] * groups, axis=0) == tag), 1.0, 0.0)
    el_ref[...] = el
    hot_ref[...] = hot
    place = iota((groups * 8, 128), 1)
    stats = jnp.zeros((groups * 8, 128), F32)
    for k, values in enumerate((el, el * logits, hot * logits)):
        for m in range(len(RANGES)):
            inside = jnp.logical_and(lane_q >= m * docs, lane_q < (m + 1) * docs)
            one = jnp.sum(jnp.where(inside, values, 0.0), axis=1, keepdims=True)
            stats = jnp.where(place == k * 3 + m, one, stats)
    for a in range(groups):
        at = pl.multiple_of((near_at ^ a) * 8, 8)
        stats_ref[pl.ds(at, 8), :] = stats[a * 8 : (a + 1) * 8, :]


def matching_back(
    size, masks, lanes, scale_ref, lens_ref, totals_ref, el_ref, hot_ref, own_ref, over_y, over_x, over_both, unitq_ref, qt_ref, invq_ref, unit_ref, invd_ref, *refs
):
    dq_ref, far_ref, keep_ref, send_ref, loss_ref, dot_ref, dt_ref, stats_ref = refs[-8:]
    _, stream, base, near_at = here(size)[:4]
    total_queries = size * (ROW // QLEN)
    temper = SHARPNESS * LOG2E
    count = unitq_ref.shape[1]
    inv_q = [invq_ref[:, m : m + 1] for m in range(len(RANGES))]
    inv_d = [invd_ref[m : m + 1, :] for m in range(len(RANGES))]
    unit_q = [unitq_ref[m] for m in range(len(RANGES))]
    doc_rows = unit_ref.shape[2] // ROW
    docs = doc_rows * DOCS_ROW
    ids = row_ids(base, masks, doc_rows)
    groups = count // ROW
    odd_y, odd_x = (near_at & 1) == 1, stream == 1
    parts = [own_ref[...], over_y[...], over_x[...], over_both[...]]
    parts = [jnp.where(odd_y, a, b) for a, b in ((parts[1], parts[0]), (parts[0], parts[1]),
                                                  (parts[3], parts[2]), (parts[2], parts[3]))]
    parts = [jnp.where(odd_x, parts[(k + 2) % 4], parts[k]) for k in range(4)]
    stats_ref[...] = (parts[0] + parts[1]) + (parts[2] + parts[3])
    rows = []
    for a in range(groups):
        at = pl.multiple_of((near_at ^ a) * 8, 8)
        rows.append(stats_ref[pl.ds(at, 8), :])
    stats = jnp.concatenate(rows, axis=0)
    place = iota(stats.shape, 1)

    def column(k):
        return jnp.sum(jnp.where(place == k, stats, 0.0), axis=1, keepdims=True)

    shape = (groups * 8, lanes)
    lane_q = iota(shape, 1)
    sums = jnp.ones(shape, F32)
    loss = jnp.zeros((groups * 8, 1), F32)
    moved = jnp.zeros((groups * 8, 1), F32)
    for m in range(len(RANGES)):
        whole, weighted, picked = column(m), column(3 + m), column(6 + m)
        inside = jnp.logical_and(lane_q >= m * docs, lane_q < (m + 1) * docs)
        sums = jnp.where(inside, whole, sums)
        loss = loss + (jnp.log(whole) - picked)
        moved = moved + (weighted / whole - picked)
    line = iota((8, 128), 0)
    loss = jnp.where(
        line == 0,
        jnp.sum(loss, axis=0, keepdims=True) * (1.0 / total_queries),
        jnp.where(line == 1, jnp.sum(moved, axis=0, keepdims=True) * (1.0 / total_queries), 0.0),
    )
    loss_ref[...] = loss
    marks = doc_marks(lens_ref, ids, lanes, True)
    scale = jnp.exp(jnp.full((8, lanes), scale_ref[0], F32))[:1]
    coeff = (el_ref[...] / sums - hot_ref[...]) * (scale * (1.0 / (QLEN * total_queries)))
    coeff = jnp.broadcast_to(coeff[:, None, :], (groups * 8, QLEN, lanes)).reshape(count, lanes)
    ratio = coeff / totals_ref[...]
    ratio_high = ratio.astype(BF16)
    ratio_low = (ratio - ratio_high.astype(F32)).astype(BF16)
    ratio = jnp.concatenate([ratio_high, ratio_low], axis=1)
    for m in range(len(RANGES)):
        grad = jnp.zeros((count, PROJ), F32)
        for p in range(doc_rows):
            block = unit_ref[m, :, p * ROW : (p + 1) * ROW]
            mark = marks[p][m]
            if len(refs) > 8:
                exps = refs[0][m, :, p * ROW : (p + 1) * ROW].astype(F32)
            else:
                exps = jnp.exp2(mm(unit_q[m], block))
            d_sims = (exps * mm(ratio, jnp.concatenate([mark, mark], axis=0))).astype(BF16)
            grad = grad + mm_nt(d_sims, block)
            dt_ref[m, :, p * ROW : (p + 1) * ROW] = mm(qt_ref[m], d_sims)
        unit = unit_q[m].astype(F32) * (1.0 / temper)
        along = jnp.sum(grad * unit, axis=1, keepdims=True)
        part = inv_q[m] * (grad - unit * along)
        if m == 0:
            dot_ref[...] = part
        else:
            dot_ref[...] += part
    dq_ref[...] = dot_ref[: count // 2, :].astype(BF16)
    far_ref[...] = dot_ref[count // 2 :, :].astype(BF16)
    total = jnp.zeros(unit_ref.shape[1:], F32)
    for m in range(len(RANGES)):
        grad = dt_ref[m] * (1.0 / temper)
        unit = unit_ref[m].astype(F32)
        along = jnp.sum(grad * unit, axis=0, keepdims=True)
        total = total + inv_d[m] * (grad - unit * along)
    for p in range(doc_rows):
        ref, at = (keep_ref, p) if p < doc_rows // 2 else (send_ref, p - doc_rows // 2)
        ref[at * ROW : (at + 1) * ROW, :] = total[:, p * ROW : (p + 1) * ROW].T.astype(BF16)


def matching_ready(near_ref, far_ref, *refs):
    doc_refs = refs[:-6] if refs[-2].shape[0] != len(RANGES) else refs[:-7]
    unitq_ref, qt_ref, invq_ref, unit_ref, invd_ref = refs[len(doc_refs) : len(doc_refs) + 5]
    turn_ref = refs[-1]
    queries = load_queries(near_ref, far_ref)
    unit_q, inv_q = unit_queries(queries, SHARPNESS * LOG2E)
    unit_d, inv_d = unit_docs(doc_refs, turn_ref)
    lane = iota(invq_ref.shape, 1)
    columns = jnp.zeros(invq_ref.shape, F32)
    invd_ref[...] = jnp.zeros_like(invd_ref)
    for m in range(len(RANGES)):
        unitq_ref[m] = unit_q[m].astype(BF16)
        unit_ref[m] = unit_d[m].astype(BF16)
        qt_ref[m] = unit_q[m].T.astype(BF16)
        columns = jnp.where(lane == m, inv_q[m], columns)
        invd_ref[m : m + 1, :] = inv_d[m]
        if len(refs) - len(doc_refs) > 6:
            refs[-2][m] = jnp.exp2(mm(unitq_ref[m], unit_ref[m])).astype(BF16)
    invq_ref[...] = columns


def pick_rows(size, here_ref, there_ref, rows_ref):
    _, stream, _, _, has_top = here(size)[:5]
    rows_ref[...] = jnp.where(has_top == stream, here_ref[...], there_ref[...])


def add_rows(rows_ref, got_ref, sum_ref):
    sum_ref[...] = (rows_ref[...].astype(F32) + got_ref[...].astype(F32)).astype(BF16)


DIGITS = 10
POINT = 20


def digits_of(value):
    fixed = (value * float(1 << POINT)).astype(jnp.int32)
    size = jnp.abs(fixed)
    lane = iota(value.shape, 1)
    digits = jnp.zeros(value.shape, jnp.int32)
    for k in range(DIGITS):
        digits = jnp.where(lane == k, (size >> (3 * k)) & 7, digits)
    return jnp.where(fixed < 0, -digits, digits).astype(F32)


def value_of(digits):
    lane = iota(digits.shape, 1)
    half = DIGITS // 2
    weight = jnp.zeros(digits.shape, F32)
    for k in range(half):
        weight = jnp.where(jnp.logical_or(lane == k, lane == k + half), float(8**k), weight)
    low = jnp.sum(jnp.where(lane < half, digits * weight, 0.0))
    high = jnp.sum(jnp.where(jnp.logical_and(lane >= half, lane < DIGITS), digits * weight, 0.0))
    return (high * float(8**half) + low) * (1.0 / (1 << POINT))


def turn(core, place, block):
    return jnp.where(core == 0, place - block, block - place) & (RING - 1)


def block_at(core, place, distance):
    return jnp.where(core == 0, place - distance, place + distance) & (RING - 1)


def store_block(keep_ref, send_ref, rows, block, places, value):
    core, place = places
    mine = core == block // RING
    at = turn(block // RING, place, block % RING)

    @pl.when(mine)
    def _():
        keep_ref[at, rows, :] = value

    @pl.when(jnp.logical_not(mine))
    def _():
        send_ref[at, rows, :] = value


def feed_back(
    size, dq_ref, dd_ref, got_ref, xh2_ref, rs2_ref, affine_ref, wproj_ref, slope_ref, act_ref,
    xh1_ref, wdown_ref, wup_hbm,
    keep_ref, send_ref, tail_keep, tail_send, dfirst_ref, gproj_ref, small_ref,
    dinner_ref, wup_ref, sems,
):
    step = 512
    spans = [slice(c * step, (c + 1) * step) for c in range(FF // step)]
    copies = fetch([(wup_hbm, wup_ref)], sems)
    g1, s1, g2, s2 = [affine_ref[k : k + 1, :] for k in range(4)]
    _, stream, _, _, has_top, *places = here(size)
    is_query, docs_there = stream == 0, has_top == 0
    got = got_ref[...].astype(F32)
    d_vec = jnp.where(
        is_query,
        dq_ref[...].astype(F32) + got,
        jnp.where(docs_there, got, dd_ref[...].astype(F32)),
    )
    d_proj = d_vec.astype(BF16)
    xhat = xh2_ref[...]
    gain = g2
    second = (xhat * gain + s2).astype(BF16)
    gproj_ref[...] = mm_tn(second, d_proj)
    d_second = mm_nt(d_proj, wproj_ref[...])
    small_ref[...] = jnp.zeros_like(small_ref)
    small_ref[5:6, :] = col_sum(d_second * xhat)
    small_ref[6:7, :] = col_sum(d_second)
    d_sum = norm_back(d_second, xhat, rs2_ref[:, :1], gain)
    d_branch = d_sum.astype(BF16)
    small_ref[4:5, :] = col_sum(d_branch.astype(F32))
    d_first = d_sum
    for c in range(FF // step):
        cols = spans[c]
        d_act = mm_nt(d_branch, wdown_ref[cols, :])
        d_inner = (d_act * slope_ref[:, cols].astype(F32)).astype(BF16)
        dinner_ref[:, cols] = d_inner
        small_ref[c : c + 1, :] = col_sum(d_inner.astype(F32))
        grad = mm_tn(act_ref[:, cols], d_branch).astype(BF16)
        for k in range(step // DOWN):
            store_block(
                keep_ref, send_ref, slice(0, DOWN), c * (step // DOWN) + k, places,
                grad[k * DOWN : (k + 1) * DOWN, :],
            )
    copies[0].wait()
    first = (xh1_ref[...] * g1 + s1).astype(BF16)
    for c in range(FF // step):
        cols = slice(c * step, (c + 1) * step)
        d_first = d_first + mm_nt(dinner_ref[:, cols], wup_ref[:, cols])
        grad = mm_tn(first, dinner_ref[:, cols]).astype(BF16)
        for k in range(D // DOWN):
            block = c * (D // DOWN) + k
            start = k * DOWN
            store_block(
                keep_ref, send_ref, slice(DOWN, FIRST), block, places, grad[start : start + HEAD, :]
            )
            store_block(
                tail_keep, tail_send, slice(0, TAIL), block, places,
                grad[start + HEAD : start + DOWN, :],
            )
    dfirst_ref[...] = d_first


def attend_back(
    size, dfirst_ref, gproj_ref, small_ref, loss_ref, tail_keep, tail_send, xh1_ref, rs1_ref, affine_ref, mixed_ref, wout_ref,
    qkv_ref, probs_ref, rope_ref, x_ref,
    keep_ref, ahead_ref, send_ref, dsum_ref, djoined_ref, rest_ref,
):
    me, *_, core, place = here(size)
    d_first = dfirst_ref[...]
    xhat = xh1_ref[...]
    gain = affine_ref[0:1, :]
    gain_grad = col_sum(d_first * xhat)
    shift_grad = col_sum(d_first)
    d_sum = norm_back(d_first, xhat, rs1_ref[:, :1], gain)
    d_att = d_sum.astype(BF16)
    bias_out = col_sum(d_att.astype(F32))
    rest_ref[3 * D : 4 * D, :] = mm_tn(mixed_ref[...], d_att)
    d_mixed = mm_nt(d_att, wout_ref[...]).astype(BF16)
    cosine, sine = rope_ref[:, :128], rope_ref[:, 128:]
    low_half = iota((ROW, 128), 1) < HD

    scale = 1.0 / math.sqrt(HD)
    cosine, sine = cosine * scale, sine * scale
    swap = swapping()

    def unrotate(both):
        return (both[:, :128] * cosine - both[:, 128:] * sine).astype(BF16)

    for g in range(HEADS // 2):
        span = slice(g * 128, (g + 1) * 128)
        q_g = qkv_ref[:, g * 128 : (g + 1) * 128]
        k_g = qkv_ref[:, D + g * 128 : D + (g + 1) * 128]
        v_g = qkv_ref[:, 2 * D + g * 128 : 2 * D + (g + 1) * 128]
        m_g = d_mixed[:, span]
        q_both = jnp.concatenate([q_g, mm(q_g, swap).astype(BF16)], axis=1)
        k_both = jnp.concatenate([k_g, mm(k_g, swap).astype(BF16)], axis=1)
        d_q = jnp.zeros((ROW, 256), F32)
        d_k = jnp.zeros((ROW, 256), F32)
        d_v = jnp.zeros((ROW, 128), F32)
        zero = jnp.zeros((ROW, 128), BF16)
        zero_both = jnp.zeros((ROW, 256), BF16)
        for h in range(2):
            pick = low_half if h == 0 else jnp.logical_not(low_half)
            probs_low = probs_ref[2 * g + h]
            probs = probs_low.astype(F32)
            m_h = jnp.where(pick, m_g, zero)
            d_probs = mm_nt(m_h, v_g)
            d_v = d_v + mm_tn(probs_low, m_h)
            inner = jnp.sum(d_probs * probs, axis=1, keepdims=True)
            d_scores = (probs * (d_probs - inner)).astype(BF16)
            pick_both = jnp.concatenate([pick, pick], axis=1)
            d_q = d_q + mm(d_scores, jnp.where(pick_both, k_both, zero_both))
            d_k = d_k + mm_tn(d_scores, jnp.where(pick_both, q_both, zero_both))
        djoined_ref[:, g * 128 : (g + 1) * 128] = unrotate(d_q)
        djoined_ref[:, D + g * 128 : D + (g + 1) * 128] = unrotate(d_k)
        djoined_ref[:, 2 * D + g * 128 : 2 * D + (g + 1) * 128] = d_v.astype(BF16)
    x = x_ref[...]
    dsum_ref[...] = d_sum
    rest_ref[4 * D :, :] = jnp.zeros((8 * 2 * RING, D), F32)
    smalls = []
    for c in range(3):
        cols = slice(c * D, (c + 1) * D)
        d_part = djoined_ref[:, cols]
        rest_ref[c * D : (c + 1) * D, :] = mm_tn(x, d_part)
        smalls.append(col_sum(d_part.astype(F32)))
    smalls += [bias_out, gain_grad, shift_grad] + [small_ref[k : k + 1, :] for k in range(7)]
    counted = jnp.where((me & 3) == 0, 1.0, 0.0)
    lines = [digits_of(loss_ref[k : k + 1, :]) * counted for k in range(2)]
    smalls.append(jnp.concatenate(lines + [jnp.zeros((1, D - 256), F32)], axis=1))
    for k, row in enumerate(smalls):
        rest_ref[4 * D + 8 * k : 4 * D + 8 * k + 1, :] = row
    for k in range(RING):
        sent, at = (ahead_ref, AHEAD.index(k)) if k in AHEAD else (send_ref, LATER.index(k))
        for ref, index, tail_ref, owner in (
            (keep_ref, k, tail_keep, core), (sent, at, tail_send, 1 - core)
        ):
            block = owner * RING + block_at(owner, place, k)
            parts = []
            for c in range(4):
                start = pl.multiple_of(c * D + block * SHARE, SHARE)
                parts.append(rest_ref[pl.ds(start, SHARE), :])
            row = pl.multiple_of(block * SHARE, SHARE)
            parts.append(
                jnp.concatenate(
                    [gproj_ref[pl.ds(row + 8 * j, 8), :] for j in range(SHARE // 8)], axis=1
                )
            )
            parts.append(rest_ref[pl.ds(pl.multiple_of(4 * D + block * 8, 8), 8), :])
            ref[index, : REST // 16, :] = jnp.concatenate(parts, axis=0).astype(BF16)
            ref[index, REST // 16 :, :] = tail_ref[k]


def tokens_back(dsum_ref, djoined_ref, wqkv_ref, tokens_ref):
    tokens = dsum_ref[...]
    for c in range(3):
        cols = slice(c * D, (c + 1) * D)
        tokens = tokens + mm_nt(djoined_ref[:, cols], wqkv_ref[:, cols])
    tokens_ref[...] = tokens


def spread(size, jobs, last, *refs):
    core, place = here(size)[-2:]
    halves = refs[: 2 * len(jobs)]
    wide_one, wide_two, wide_qkv, wide_proj, small_ref, sems = refs[-6:]
    outs = refs[-21:-6] if last else refs[-11:-6]
    down_hbm, up_hbm, qkv_hbm, out_hbm, proj_hbm = outs[:5]
    copies = []

    def move(src, dst):
        copy = pltpu.make_async_copy(src, dst, sems.at[len(copies)])
        copy.start()
        copies.append(copy)

    at = 0
    for job, (mine, group) in enumerate(jobs):
        owner = core if mine else 1 - core
        one_ref, two_ref = halves[2 * job : 2 * job + 2]
        for p, distance in enumerate(GROUPS[group]):
            block = owner * RING + block_at(owner, place, distance)
            wide_one[at] = one_ref[p].astype(F32)
            rows = pl.ds(pl.multiple_of(block * DOWN, DOWN), DOWN)
            move(wide_one.at[at, :DOWN, :], down_hbm.at[rows, :])
            start = (block % (D // DOWN)) * DOWN
            columns = pl.ds(pl.multiple_of((block // (D // DOWN)) * D, D), D)
            rows = pl.ds(pl.multiple_of(start, DOWN), HEAD)
            move(wide_one.at[at, DOWN:, :], up_hbm.at[rows, columns])
            wide = two_ref[p].astype(F32)
            wide_two[at, :SHARE, :] = wide[3 * SHARE : 4 * SHARE, :]
            wide_two[at, SHARE:, :] = wide[REST // 16 :, :]
            rows = pl.ds(pl.multiple_of(start + HEAD, 16), TAIL)
            move(wide_two.at[at, SHARE:, :], up_hbm.at[rows, columns])
            rows = pl.ds(pl.multiple_of(block * SHARE, SHARE), SHARE)
            for c in range(3):
                wide_qkv[at, :, c * D : (c + 1) * D] = wide[c * SHARE : (c + 1) * SHARE, :]
            move(wide_qkv.at[at], qkv_hbm.at[rows, :])
            move(wide_two.at[at, :SHARE, :], out_hbm.at[rows, :])
            for j in range(SHARE // 8):
                wide_proj[at, 8 * j : 8 * j + 8, :] = wide[
                    4 * SHARE : 4 * SHARE + 8, j * PROJ : (j + 1) * PROJ
                ]
            move(wide_proj.at[at], proj_hbm.at[rows, :])
            at += 1
    if last:
        sources = refs[2 * len(jobs) : 2 * len(jobs) + 2 * len(GROUPS)]
        for k, ref in enumerate(sources):
            owner = core if k < len(GROUPS) else 1 - core
            for p, distance in enumerate(GROUPS[k % len(GROUPS)]):
                block = owner * RING + block_at(owner, place, distance)
                line = ref[p, 4 * SHARE : 4 * SHARE + 16, :].astype(F32)[8:, :]
                small_ref[pl.ds(pl.multiple_of(block * 8, 8), 8), :] = line
        rows = [small_ref[8 * k : 8 * k + 1, :] for k in range(14)]
        bqkv_ref, bout_ref, g1_ref, s1_ref, bup_ref, bdown_ref, g2_ref, s2_ref = outs[5:13]
        for k, ref in enumerate(outs[13:]):
            ref[0] = value_of(rows[13][:, k * 128 : (k + 1) * 128])
        for c in range(3):
            bqkv_ref[:, c * D : (c + 1) * D] = rows[c]
        bout_ref[...] = rows[3]
        g1_ref[...] = rows[4]
        s1_ref[...] = rows[5]
        for c in range(4):
            bup_ref[:, c * D : (c + 1) * D] = rows[6 + c]
        bdown_ref[...] = rows[10]
        g2_ref[...] = rows[11]
        s2_ref[...] = rows[12]
    for copy in copies:
        copy.wait()


def spread_call(size, jobs, halves, outs, others):
    last = len(others) > 0
    shapes = ((FF, D), (D, FF), (D, 3 * D), (D, D), (D, PROJ))
    widths = (3 * D, D, D, D, FF, D, D, D) if last else ()
    args = [*halves, *others, *outs]
    count = sum(len(GROUPS[group]) for _, group in jobs)
    before = len(halves) + len(others)
    return call(
        partial(spread, size, jobs, last),
        args,
        [VMEM] * before + [HBM] * len(outs),
        [pltpu.HBM(shape, F32) for shape in shapes]
        + [shape_of((1, width)) for width in widths]
        + [shape_of((1,))] * (2 * last),
        [
            pltpu.VMEM((count, FIRST, D), F32),
            pltpu.VMEM((count, SHARE + TAIL, D), F32),
            pltpu.VMEM((count, SHARE, 3 * D), F32),
            pltpu.VMEM((count, SHARE, PROJ), F32),
            pltpu.VMEM((16 * RING, D), F32),
            pltpu.SemaphoreType.DMA((6 * count,)),
        ],
        out_specs=[HBM] * 5 + [VMEM] * len(widths) + [SMEM] * (2 * last),
        aliases={before + k: k for k in range(len(outs))},
        cost=SPREAD_COST,
        room=14,
    )


def shape_of(shape, dtype=F32):
    return jax.ShapeDtypeStruct(tuple(shape), dtype)


def call(kernel, args, specs, outs, scratch=(), room=24, out_specs=None, aliases={}, cost=10**7):
    spaces = {id(HBM): pltpu.HBM, id(HELD): pltpu.VMEM}
    args = [
        pltpu.with_memory_space_constraint(arg, spaces[id(spec)]) if id(spec) in spaces else arg
        for arg, spec in zip(args, specs)
    ]
    return pl.pallas_call(
        kernel,
        out_shape=outs,
        in_specs=specs,
        out_specs=out_specs or [VMEM] * len(outs),
        scratch_shapes=list(scratch),
        input_output_aliases=aliases,
        compiler_params=pltpu.CompilerParams(vmem_limit_bytes=room * MIB),
        cost_estimate=pl.CostEstimate(
            flops=10 * cost, bytes_accessed=cost, transcendentals=0
        ),
    )(*args)


def swapped(value, mask, axis="dp"):
    size = lax.axis_size(axis)
    return lax.ppermute(value, axis, [(k, k ^ mask) for k in range(size)])


def added(a, b):
    return (a.astype(F32) + b.astype(F32)).astype(BF16)


def join_blocks(*refs):
    for k, ref in enumerate(refs[:-1]):
        refs[-1][k] = ref[0]


def ring_swap(value, onward):
    size = lax.axis_size("dp")
    pairs = []
    for k in range(size):
        at = CIRCLE.index((k >> 1) % RING)
        to = CIRCLE[(at + (1 if (k % 2 == 0) == onward else -1)) % RING]
        pairs.append((k, (k & ~(2 * RING - 1)) | (to << 1) | (k & 1)))
    return lax.ppermute(value, "dp", pairs)


def add_blocks(places, *refs):
    count = len(places)
    held_ref = refs[count] if any(place is not None for place in places) else None
    for k, place in enumerate(places):
        value = refs[k][...]
        if place is not None:
            value = (value.astype(F32) + held_ref[place : place + 1].astype(F32)).astype(BF16)
        refs[-count + k][...] = value


def first_blocks(places, keep_ref, pair_ref, *outs):
    for ref, (k, j) in zip(outs, places):
        ref[0] = (keep_ref[k].astype(F32) + pair_ref[j].astype(F32)).astype(BF16)


def later_blocks(places, keep_ref, pair_ref, out_ref):
    for k in AHEAD:
        out_ref[k] = jnp.zeros(out_ref.shape[1:], BF16)
    for k, j in places:
        out_ref[k] = (keep_ref[k].astype(F32) + pair_ref[j].astype(F32)).astype(BF16)


class Summed:
    def __init__(self, keep, sends, others):
        self.keep, self.others, self.hop = keep, others, 0
        self.pairs = [swapped(send, 1) for send in sends]
        self.sent, self.blocks, self.near, self.far = [], {}, [], []

    def blocks_call(self, blocks, places, held):
        return call(
            partial(add_blocks, places),
            (*blocks, *held),
            [VMEM] * (len(blocks) + len(held)),
            [shape_of(block.shape, BF16) for block in blocks],
            room=8,
            cost=STEP_COST,
        )

    def open(self, after):
        keep, pair, _ = lax.optimization_barrier((self.keep, self.pairs[0], after))
        shape = (1, *keep.shape[1:])
        places = [(k, AHEAD.index(k) if len(self.pairs) > 1 else k) for k in AHEAD]
        first, second = call(
            partial(first_blocks, places),
            (keep, pair),
            [VMEM] * 2,
            [shape_of(shape, BF16)] * 2,
            room=8,
            cost=STEP_COST,
        )
        self.sent = [(first, True), (second, False)]
        return second

    def total(self, after):
        keep, _ = lax.optimization_barrier((self.keep, after))
        later = [(k, LATER.index(k) if len(self.pairs) > 1 else k) for k in LATER]
        (self.keep,) = call(
            partial(later_blocks, later),
            (keep, self.pairs[-1]),
            [VMEM] * 2,
            [shape_of(keep.shape, BF16)],
            room=8,
            cost=STEP_COST,
        )
        return self.keep

    def step(self, after):
        half = RING // 2
        self.hop += 1
        hop = self.hop
        *got, _ = lax.optimization_barrier((*[ring_swap(*one) for one in self.sent], after))
        if hop < half:
            out = self.blocks_call(got, (half + hop, half - 1 - hop), [self.keep])
            self.part = out[1]
        elif hop == half:
            (own,) = self.blocks_call(got, (0,), [self.part])
            for mask in self.others:
                own = added(own, swapped(own, mask))
            self.blocks[0] = own
            out = [own, own]
        else:
            out = self.blocks_call(got, (None,) * len(got), [])
            hop -= half
            self.blocks[hop] = out[0]
            if hop < half:
                self.blocks[RING - hop] = out[1]
        if hop == half - 1:
            self.sent = [(out[0], True)]
        elif self.hop < 2 * half:
            self.sent = [(out[0], True), (out[1], False)]
        return out[0]

    def share(self, group, after):
        *blocks, _ = lax.optimization_barrier((*[self.blocks[k] for k in GROUPS[group]], after))
        shape = (len(blocks), *blocks[0].shape[1:])
        self.near += call(
            join_blocks, blocks, [VMEM] * len(blocks), [shape_of(shape, BF16)], room=8, cost=0
        )
        self.far.append(swapped(self.near[-1], 1))
        return self.near[-1]


def per_device(
    tokens, qkv_weight, qkv_bias, out_weight, out_bias, first_gain, first_shift, up_weight,
    up_bias, down_weight, down_bias, second_gain, second_shift, proj_weight, log_scale,
    doc_lengths, labels,
):
    size = lax.axis_size("dp")
    bits = [1 << k for k in range(size.bit_length() - 1)]
    near_masks, doc_masks = bits[:2], bits[2:]
    top_mask, doc_masks = doc_masks[-1], doc_masks[:-1]
    others = bits[4:]
    me = lax.axis_index("dp")
    stream = lax.axis_index("stream")
    is_query = stream == 0
    has_top = (me & top_mask) != 0
    lens = doc_lengths.T
    scale = log_scale.reshape(1)

    vec, *moved, qkv, rope, probs, mixed, xh1, rs1, affine = call(
        partial(encoder_forward, size),
        (
            lens, labels, jnp.asarray(rope_table()), tokens[0], qkv_weight[0], qkv_bias,
            out_weight[0], out_bias, first_gain, first_shift, up_weight[0], up_bias,
            down_weight[0], down_bias, second_gain, second_shift, proj_weight[0],
        ),
        [HBM] * 17,
        [shape_of((ROW + EXT, PROJ), BF16)]
        + [shape_of(*kind) for kind in MOVED]
        + [pltpu.HBM(*kind) for kind in KEPT],
        [pltpu.VMEM(*kind) for kind in KEPT]
        + [pltpu.SemaphoreType.DMA((len(KEPT),))]
        + [
            pltpu.VMEM(shape, BF16)
            for shape in (
                (ROW, 512), (ROW, D), (D, 3 * D), (1, 3 * D), (D, D), (1, D), (1, D), (1, D), (D, FF),
                (1, FF), (FF, D), (1, D), (1, D), (1, D), (D, PROJ),
            )
        ]
        + [
            pltpu.SMEM(lens.shape, jnp.int32),
            pltpu.SMEM(labels.shape, jnp.int32),
            pltpu.SemaphoreType.DMA((17,)),
        ],
        room=40,
        out_specs=[VMEM] * (1 + len(MOVED)) + [HBM] * len(KEPT),
    )
    act, slope, xh2, rs2 = call(
        move_kept,
        moved,
        [VMEM] * len(MOVED),
        [pltpu.HBM(*kind) for kind in MOVED],
        [pltpu.SemaphoreType.DMA((len(MOVED),))],
        room=8,
        out_specs=[HBM] * len(MOVED),
        cost=STEP_COST,
    )

    every, other_y = range(size), near_masks[1]
    other, _ = lax.optimization_barrier((swapped(vec, 1, "stream"), rs2))
    near = jnp.where(is_query, vec, other)
    rows = jnp.where(is_query, other, vec)[:ROW]
    moved = swapped(rows, top_mask)
    (rows,) = call(
        partial(pick_rows, size),
        (rows, moved),
        [VMEM] * 2,
        [shape_of((ROW, PROJ), BF16)],
        room=8,
        cost=STEP_COST,
    )
    got_y, _ = lax.optimization_barrier((swapped(near, other_y), rows))
    near = jnp.concatenate([near, got_y], axis=0)
    far = swapped(near, near_masks[0])
    pieces = []
    for k, mask in enumerate(doc_masks):
        pieces.append(rows)
        got = swapped(rows, mask)
        if k + 1 < len(doc_masks):
            rows = jnp.concatenate([rows, got], axis=0)
        else:
            pieces = [rows, got]
    doc_rows = sum(p.shape[0] for p in pieces) // ROW
    tokens_d = doc_rows * ROW
    tokens_q = 4 * ROW
    lanes = -(-3 * doc_rows * DOCS_ROW // 128) * 128
    room = 20 if doc_rows <= 4 else 56
    totals, el, hot, stats = call(
        partial(matching_stats, size, doc_masks, lanes),
        (scale, lens, near, far, *pieces),
        [SMEM] * 2 + [VMEM] * (2 + len(pieces)),
        [
            shape_of((tokens_q, lanes)),
            shape_of((tokens_q // QLEN, lanes)),
            shape_of((tokens_q // QLEN, lanes)),
            shape_of((tokens_q // QLEN, 128)),
        ],
        [pltpu.VMEM((PROJ, tokens_d), F32), pltpu.VMEM((3, PROJ, tokens_d), BF16)],
        room=room,
    )
    small_enough = doc_rows <= 4
    ready = call(
        matching_ready,
        (near, far, *pieces),
        [VMEM] * (2 + len(pieces)),
        [
            shape_of((3, tokens_q, PROJ), BF16),
            shape_of((3, PROJ, tokens_q), BF16),
            shape_of((tokens_q, 128)),
            shape_of((3, PROJ, tokens_d), BF16),
            shape_of((8, tokens_d)),
        ]
        + [shape_of((3, tokens_q, tokens_d), BF16)] * small_enough,
        [pltpu.VMEM((PROJ, tokens_d), F32)],
        room=room,
    )
    stats = stats + swapped(stats, near_masks[0])
    over_y = swapped(stats, other_y)
    over_x = swapped(stats, 1, "stream")
    pairs = [(k * size + r, (1 - k) * size + (r ^ other_y)) for k in range(2) for r in every]
    over_both = lax.ppermute(stats, ("stream", "dp"), pairs)
    dq, dq_send, keep, send, loss = call(
        partial(matching_back, size, doc_masks, lanes),
        (scale, lens, totals, el, hot, stats, over_y, over_x, over_both, *ready),
        [SMEM] * 2 + [VMEM] * (7 + len(ready)),
        [shape_of((tokens_q // 2, PROJ), BF16)] * 2
        + [shape_of((tokens_d // 2, PROJ), BF16)] * 2
        + [shape_of((8, 128))],
        [
            pltpu.VMEM((tokens_q, PROJ), F32),
            pltpu.VMEM((3, PROJ, tokens_d), F32),
            pltpu.VMEM((tokens_q // QLEN, 128), F32),
        ],
        room=room,
    )
    got_dq = swapped(dq_send, near_masks[0])
    for mask in reversed(doc_masks[1:]):
        total, half = added(keep, swapped(send, mask)), keep.shape[0] // 2
        keep, send = total[:half], total[half:]
    got_dd = swapped(send, doc_masks[0])
    def summed(rows, got, after=None):
        if after is not None:
            got, _ = lax.optimization_barrier((got, after))
        return call(
            add_rows, (rows, got), [VMEM] * 2, [shape_of(rows.shape, BF16)], room=8, cost=STEP_COST
        )[0]

    dq = summed(dq, got_dq)
    dd = summed(keep, got_dd, dq)
    dd = summed(dd, swapped(dd, top_mask))
    dq = summed(dq[:ROW], swapped(dq[ROW:], other_y), dd)
    got = swapped(jnp.where(is_query, dd, dq), 1, "stream")

    one_keep, one_send, tail_keep, tail_send, d_first, gproj, small = call(
        partial(feed_back, size),
        (
            dq, dd, got, xh2, rs2, affine, proj_weight[0], slope, act, xh1, down_weight[0],
            up_weight[0],
        ),
        [VMEM] * 3 + [HELD] * 8 + [HBM],
        [shape_of((RING, FIRST, D), BF16)] * 2
        + [shape_of((RING, TAIL, D), BF16)] * 2
        + [shape_of((ROW, D)), shape_of((D, PROJ)), shape_of((8, D))],
        [
            pltpu.VMEM((ROW, FF), BF16),
            pltpu.VMEM((D, FF), BF16),
            pltpu.SemaphoreType.DMA((1,)),
        ],
        room=24,
    )
    two_keep, two_ahead, two_send, d_sum, d_joined = call(
        partial(attend_back, size),
        (
            d_first, gproj, small, loss, tail_keep, tail_send, xh1, rs1, affine, mixed, out_weight[0], qkv, probs, rope,
            tokens[0],
        ),
        [VMEM] * 6 + [HELD] * 9,
        [shape_of((count, SECOND, D), BF16) for count in (RING, len(AHEAD), len(LATER))]
        + [shape_of((ROW, D)), shape_of((ROW, 3 * D), BF16)],
        [pltpu.VMEM((4 * D + 16 * RING, D), F32)],
        room=24,
    )
    one, two = [
        Summed(keep, sends, others)
        for keep, *sends in ((one_keep, one_send), (two_keep, two_ahead, two_send))
    ]
    token, outs = d_sum, ()
    for event in ORDER:
        kind, k, *group = event
        if kind == "tokens":
            d_sum, _ = lax.optimization_barrier((d_sum, token))
            (tokens_grad,) = call(
                tokens_back,
                (d_sum, d_joined, qkv_weight[0]),
                [VMEM] * 3,
                [shape_of((ROW, D))],
                room=8,
                cost=STEP_COST,
            )
            token = tokens_grad
            continue
        if kind == "spread":
            jobs = event[1]
            halves = [
                (piece.near if mine else piece.far)[group] for mine, group in jobs for piece in (one, two)
            ]
            *halves, _ = lax.optimization_barrier((*halves, token))
            others = [*two.near, *two.far] if event == ORDER[-1] else []
            outs = spread_call(size, jobs, halves, outs[:5], others)
            token = outs[0]
            continue
        piece = (one, two)[k]
        token = getattr(piece, kind)(*group, token)
    grad_down, grad_up, grad_qkv, grad_out, grad_proj = outs[:5]
    (
        grad_bqkv, grad_bout, grad_g1, grad_s1, grad_bup, grad_bdown, grad_g2, grad_s2, loss,
        scale_grad,
    ) = outs[5:]
    return (
        loss.reshape(()),
        tokens_grad[None],
        grad_qkv[None],
        grad_bqkv,
        grad_out[None],
        grad_bout,
        grad_g1,
        grad_s1,
        grad_up[None],
        grad_bup,
        grad_down[None],
        grad_bdown,
        grad_g2,
        grad_s2,
        grad_proj[None],
        scale_grad.reshape(()),
    )


def solution(mesh):
    return jax.shard_map(
        per_device,
        mesh=mesh,
        in_specs=(
            P("stream", "dp", None),
            P("stream", None, None),
            P("stream", None),
            P("stream", None, None),
            P("stream", None),
            P("stream", None),
            P("stream", None),
            P("stream", None, None),
            P("stream", None),
            P("stream", None, None),
            P("stream", None),
            P("stream", None),
            P("stream", None),
            P("stream", None, None),
            P(),
            P(),
            P("dp"),
        ),
        out_specs=(
            P(),
            P("stream", "dp", None),
            P("stream", None, None),
            P("stream", None),
            P("stream", None, None),
            P("stream", None),
            P("stream", None),
            P("stream", None),
            P("stream", None, None),
            P("stream", None),
            P("stream", None, None),
            P("stream", None),
            P("stream", None),
            P("stream", None),
            P("stream", None, None),
            P(),
        ),
        check_vma=False,
    )
```

```python
from functools import partial
import math

import jax
import jax.numpy as jnp
import numpy as np
from jax import lax
from jax.experimental import pallas as pl
from jax.experimental.pallas import tpu as pltpu
from jax.sharding import PartitionSpec as P

D = 512
HEADS = 8
HD = 64
FF = 2048
PROJ = 128
QLEN = 32
DOCS_ROW = 4
ROW = 256
EXT = 16
RANGES = (64, 96, 128)

SHARPNESS = 8.0
EPS_NORM = 1e-06
EPS_LAYER = 1e-05
LOG2E = 1.4426950408889634

F32 = jnp.float32
BF16 = jnp.bfloat16
REST = 2304
SHARE = 32
DOWN = FF // 16
HEAD = 80
TAIL = DOWN - HEAD
FIRST = DOWN + HEAD
SECOND = REST // 16 + TAIL
CIRCLE = (0, 2, 4, 6, 7, 5, 3, 1)
RING = len(CIRCLE)
AHEAD = (RING // 2, RING // 2 - 1)
LATER = tuple(k for k in range(RING) if k not in AHEAD)
GROUPS = ((0, 1, 2, 3, 5, 6, 7), (4,))
STEP_COST = 3 * 10**7
SPREAD_COST = 0
ROUND = (("step", 0), ("step", 1))
ORDER = (
    (("open", 0), ("open", 1), ("total", 0), ("total", 1), ("tokens", 0)) + ROUND * 7
    + (("share", 0, 0), ("share", 1, 0), ("spread", ((True, 0),)), ("spread", ((False, 0),))) + ROUND
    + (("share", 0, 1), ("share", 1, 1), ("spread", ((True, 1),)), ("spread", ((False, 1),)))
)
MIB = 1024 * 1024

VMEM = pl.BlockSpec(memory_space=pltpu.VMEM)
SMEM = pl.BlockSpec(memory_space=pltpu.SMEM)
HBM = pl.BlockSpec(memory_space=pltpu.HBM)
HELD = pl.BlockSpec(memory_space=pltpu.VMEM)


def mm(a, b):
    return lax.dot_general(a, b, (((1,), (0,)), ((), ())), preferred_element_type=F32)


def mm_nt(a, b):
    return lax.dot_general(a, b, (((1,), (1,)), ((), ())), preferred_element_type=F32)


def mm_tn(a, b):
    return lax.dot_general(a, b, (((0,), (0,)), ((), ())), preferred_element_type=F32)


def iota(shape, axis):
    return lax.broadcasted_iota(jnp.int32, shape, axis)


def rope_table():
    half = HD // 2
    freqs = (10000.0 ** (-np.arange(half, dtype=np.float32) / np.float32(half))).astype(np.float32)
    turned = np.arange(ROW, dtype=np.float32)[:, None] * freqs[None, :]
    cosine = np.cos(turned.astype(np.float64))
    sine = np.sin(turned.astype(np.float64))
    cosine = np.concatenate([cosine, cosine, cosine, cosine], axis=1).astype(np.float32)
    sine = np.concatenate([-sine, sine, -sine, sine], axis=1).astype(np.float32)
    parts = []
    for table in (cosine, sine):
        high = table.astype(jnp.bfloat16)
        low = (table - high.astype(np.float32)).astype(jnp.bfloat16)
        parts += [high, low]
    return np.concatenate(parts, axis=1)


def swapping():
    shape = (128, 128)
    return (iota(shape, 0) == (iota(shape, 1) ^ (HD // 2))).astype(F32).astype(BF16)


def bounds_of(lens_ref, row):
    ends, total = [], jnp.int32(0)
    for k in range(DOCS_ROW):
        total = total + lens_ref[k, row]
        ends.append(total)
    return ends


def segment_of(spot, ends):
    seg = jnp.zeros_like(spot)
    for end in ends:
        seg = seg + (spot >= end).astype(jnp.int32)
    return seg


def norm_rows(values):
    mean = jnp.mean(values, axis=1, keepdims=True)
    centred = values - mean
    spread = jnp.mean(centred * centred, axis=1, keepdims=True)
    rstd = lax.rsqrt(spread + EPS_LAYER)
    return centred * rstd, rstd


def norm_back(d_out, xhat, rstd, gain):
    scaled = d_out * gain
    first = jnp.mean(scaled, axis=1, keepdims=True)
    second = jnp.mean(scaled * xhat, axis=1, keepdims=True)
    return rstd * (scaled - first - xhat * second)


def col_sum(values):
    return jnp.sum(values, axis=0, keepdims=True)


def here(size):
    me, stream = lax.axis_index("dp"), lax.axis_index("stream")
    top = size // 2
    has_top = jnp.where((me & top) != 0, 1, 0)
    base = jnp.where(stream == 0, me & ~top, me | top)
    near_at = jnp.where((me & 2) != 0, 1, 0) + jnp.where((me & 1) != 0, 2, 0)
    chip = (me >> 1) % RING
    place = jnp.int32(0)
    for k, one in enumerate(CIRCLE):
        place = jnp.where(chip == one, k, place)
    return me, stream, base, near_at, has_top, me & 1, place


def fetch(pairs, sems):
    copies = [pltpu.make_async_copy(src, dst, sems.at[k]) for k, (src, dst) in enumerate(pairs)]
    for copy in copies:
        copy.start()
    return copies


KEPT = (
    ((ROW, 3 * D), BF16),
    ((ROW, 256), F32),
    ((HEADS, ROW, ROW), BF16),
    ((ROW, D), BF16),
    ((ROW, D), F32),
    ((ROW, 128), F32),
    ((8, D), F32),
)
MOVED = (((ROW, FF), BF16), ((ROW, FF), BF16), ((ROW, D), F32), ((ROW, 128), F32))


def move_kept(*refs):
    count = len(MOVED)
    for copy in fetch([*zip(refs[:count], refs[count:-1])], refs[-1]):
        copy.wait()


def encoder_forward(
    size, lens_hbm, labels_hbm, table_hbm, x_hbm, wqkv_hbm, bqkv_hbm, wout_hbm, bout_hbm,
    g1_hbm, s1_hbm, wup_hbm, bup_hbm, wdown_hbm, bdown_hbm, g2_hbm, s2_hbm, wproj_hbm,
    vec_ref, act_ref, slope_ref, xh2_ref, rs2_ref, qkv_hbm, rope_hbm, probs_hbm, mixed_hbm, xh1_hbm,
    rs1_hbm, affine_hbm,
    qkv_ref, rope_ref, probs_ref, mixed_ref, xh1_ref, rs1_ref, affine_ref, out_sems,
    table_ref, x_ref, wqkv_ref, bqkv_ref, wout_ref, bout_ref, g1_ref, s1_ref, wup_ref, bup_ref,
    wdown_ref, bdown_ref, g2_ref, s2_ref, wproj_ref, lens_ref, labels_ref, sems,
):
    me, stream = here(size)[:2]
    is_query = stream == 0
    scalars = fetch(((lens_hbm, lens_ref), (labels_hbm, labels_ref)), sems.at[pl.ds(15, 2)])
    copies = fetch(
        (
            (table_hbm, table_ref), (x_hbm, x_ref), (wqkv_hbm, wqkv_ref), (bqkv_hbm, bqkv_ref),
            (wout_hbm, wout_ref), (bout_hbm, bout_ref), (g1_hbm, g1_ref), (s1_hbm, s1_ref),
            (bup_hbm, bup_ref), (bdown_hbm, bdown_ref), (g2_hbm, g2_ref), (s2_hbm, s2_ref),
            (wup_hbm, wup_ref), (wdown_hbm, wdown_ref), (wproj_hbm, wproj_ref),
        ),
        sems,
    )
    kept = []

    def keep(src, dst):
        copy = pltpu.make_async_copy(src, dst, out_sems.at[len(kept)])
        copy.start()
        kept.append(copy)

    for copy in scalars:
        copy.wait()
    ends = bounds_of(lens_ref, me)

    def layout(spot):
        seg_doc = segment_of(spot, ends)
        start_doc = jnp.zeros_like(spot)
        for k in range(DOCS_ROW):
            start_doc = jnp.where(seg_doc == k + 1, ends[k], start_doc)
        seg_query = spot // QLEN
        seg = jnp.where(is_query, seg_query, seg_doc)
        start = jnp.where(is_query, seg_query * QLEN, start_doc)
        return seg, start

    shape = (ROW, ROW)
    seg_q, start_q = layout(iota(shape, 0))
    seg_k, _ = layout(iota(shape, 1))
    same = seg_q == seg_k
    onehot = (iota(shape, 1) == iota(shape, 0) - start_q).astype(F32).astype(BF16)
    for copy in copies[:4]:
        copy.wait()
    turned = mm(onehot, table_ref[...])
    cosine = turned[:, :128] + turned[:, 128:256]
    sine = turned[:, 256:384] + turned[:, 384:]
    rope_ref[:, :128] = cosine
    rope_ref[:, 128:] = sine
    keep(rope_ref, rope_hbm)

    x = x_ref[...]
    joined = mm(x, wqkv_ref[...]) + bqkv_ref[...].astype(F32)
    swap = swapping()
    swap = jnp.concatenate([swap, swap], axis=0)
    for g in range(2 * D // 128):
        block = joined[:, g * 128 : (g + 1) * 128]
        high = block.astype(BF16)
        low = (block - high.astype(F32)).astype(BF16)
        other = mm(jnp.concatenate([high, low], axis=1), swap)
        qkv_ref[:, g * 128 : (g + 1) * 128] = (block * cosine + other * sine).astype(BF16)
    qkv_ref[:, 2 * D :] = joined[:, 2 * D :].astype(BF16)
    keep(qkv_ref, qkv_hbm)

    low_half = iota((ROW, 128), 1) < HD
    for g in range(HEADS // 2):
        q_g = qkv_ref[:, g * 128 : (g + 1) * 128]
        k_g = qkv_ref[:, D + g * 128 : D + (g + 1) * 128]
        v_g = qkv_ref[:, 2 * D + g * 128 : 2 * D + (g + 1) * 128]
        v_ones = jnp.concatenate([v_g, jnp.ones((ROW, 128), BF16)], axis=1)
        outs = []
        for h in range(2):
            pick = low_half if h == 0 else jnp.logical_not(low_half)
            scores = mm_nt(jnp.where(pick, q_g, jnp.zeros_like(q_g)), k_g)
            scores = jnp.where(same, scores * (LOG2E / math.sqrt(HD)), -1e30)
            top = jnp.max(scores, axis=1, keepdims=True)
            exps = jnp.exp2(scores - top)
            both = mm(exps.astype(BF16), v_ones)
            inverse = 1.0 / both[:, 128:]
            probs_ref[2 * g + h] = (exps * jnp.concatenate([inverse, inverse], axis=1)).astype(BF16)
            outs.append(both[:, :128] * inverse)
        mixed_ref[:, g * 128 : (g + 1) * 128] = jnp.where(low_half, outs[0], outs[1]).astype(BF16)

    keep(probs_ref, probs_hbm)
    keep(mixed_ref, mixed_hbm)
    for copy in copies[4:12]:
        copy.wait()
    for k, ref in enumerate((g1_ref, s1_ref, g2_ref, s2_ref)):
        affine_ref[k : k + 1, :] = ref[...].astype(F32)
    affine_ref[4:, :] = jnp.zeros((4, D), F32)
    keep(affine_ref, affine_hbm)
    attended = mm(mixed_ref[...], wout_ref[...]) + bout_ref[...].astype(F32)
    xhat, rstd = norm_rows(x.astype(F32) + attended)
    xh1_ref[...] = xhat
    rs1_ref[...] = jnp.broadcast_to(rstd, (ROW, 128))
    keep(xh1_ref, xh1_hbm)
    keep(rs1_ref, rs1_hbm)
    first = xhat * g1_ref[...].astype(F32) + s1_ref[...].astype(F32)
    first_low = first.astype(BF16)
    branch = bdown_ref[...].astype(F32) + first
    step = 512
    copies[12].wait()
    for c in range(FF // step):
        cols = slice(c * step, (c + 1) * step)
        inner = mm(first_low, wup_ref[:, cols]) + bup_ref[:, cols].astype(F32)
        gate = 0.5 + 0.5 * lax.erf(inner * math.sqrt(0.5))
        bell = jnp.exp2(inner * inner * (-0.5 * LOG2E)) * (1.0 / math.sqrt(2.0 * math.pi))
        act = (inner * gate).astype(BF16)
        act_ref[:, cols] = act
        slope_ref[:, cols] = (gate + inner * bell).astype(BF16)
        if c == 0:
            copies[13].wait()
        branch = branch + mm(act, wdown_ref[cols, :])
    xhat, rstd = norm_rows(branch)
    xh2_ref[...] = xhat
    rs2_ref[...] = jnp.broadcast_to(rstd, (ROW, 128))
    second = xhat * g2_ref[...].astype(F32) + s2_ref[...].astype(F32)
    copies[14].wait()
    vec_ref[:ROW, :] = mm(second.astype(BF16), wproj_ref[...]).astype(BF16)
    line = iota((EXT, PROJ), 0)
    tag = jnp.zeros((EXT, PROJ), jnp.int32)
    for k in range(labels_ref.shape[0]):
        label = labels_ref[k]
        tag = jnp.where(line == k, label >> 6, tag)
        tag = jnp.where(line == k + 8, label & 63, tag)
    vec_ref[ROW:, :] = tag.astype(F32).astype(BF16)
    for copy in kept:
        copy.wait()


def prefix_norms(values, axis):
    place = iota(values.shape, axis)
    squared = values * values
    sums = [
        jnp.sum(jnp.where(place < cut, squared, 0.0), axis=axis, keepdims=True) for cut in RANGES
    ]
    return [lax.rsqrt(s + EPS_NORM) for s in sums]


def load_queries(near_ref, far_ref):
    span = ROW + EXT
    rows = []
    for ref in (near_ref, far_ref):
        for k in range(ref.shape[0] // span):
            rows.append(ref[k * span : k * span + ROW, :])
    return jnp.concatenate(rows, axis=0).astype(F32)


def unit_queries(queries, scale):
    lane = iota(queries.shape, 1)
    inverse = prefix_norms(queries, 1)
    unit = [
        jnp.where(lane < cut, queries * (inv * scale), 0.0) for cut, inv in zip(RANGES, inverse)
    ]
    return unit, inverse


def unit_docs(doc_refs, scratch_ref):
    at = 0
    for ref in doc_refs:
        for k in range(ref.shape[0] // ROW):
            scratch_ref[:, at * ROW : (at + 1) * ROW] = ref[
                k * ROW : (k + 1) * ROW, :
            ].astype(F32).T
            at += 1
    turned = scratch_ref[...]
    inverse = prefix_norms(turned, 0)
    place = iota(turned.shape, 0)
    unit = [jnp.where(place < cut, turned * inv, 0.0) for cut, inv in zip(RANGES, inverse)]
    return unit, inverse


def row_ids(base, masks, doc_rows):
    ids = []
    for p in range(doc_rows):
        offset = 0
        for k, mask in enumerate(masks):
            if (p >> k) & 1:
                offset ^= mask
        ids.append(base ^ offset)
    return ids


def doc_marks(lens_ref, ids, lanes, transposed):
    docs = len(ids) * DOCS_ROW
    shape = (lanes, ROW) if transposed else (ROW, lanes)
    spot, lane = (iota(shape, 1), iota(shape, 0)) if transposed else (iota(shape, 0), iota(shape, 1))
    marks = []
    for p, row in enumerate(ids):
        seg = segment_of(spot, bounds_of(lens_ref, row))
        local = jnp.where(seg < DOCS_ROW, seg + p * DOCS_ROW, -1 - lanes)
        marks.append(
            [(lane == local + m * docs).astype(F32).astype(BF16) for m in range(len(RANGES))]
        )
    return marks


def matching_stats(
    size, masks, lanes, scale_ref, lens_ref, near_ref, far_ref, *refs
):
    doc_refs = refs[:-6]
    totals_ref, el_ref, hot_ref, stats_ref, turn_ref, unit_ref = refs[-6:]
    base, near_at = here(size)[2:4]
    span = ROW + EXT
    queries = load_queries(near_ref, far_ref)
    count = queries.shape[0]
    unit_q, _ = unit_queries(queries, SHARPNESS * LOG2E)
    unit_q = [u.astype(BF16) for u in unit_q]
    unit_d, _ = unit_docs(doc_refs, turn_ref)
    for m in range(len(RANGES)):
        unit_ref[m] = unit_d[m].astype(BF16)
    doc_rows = turn_ref.shape[1] // ROW
    docs = doc_rows * DOCS_ROW
    ids = row_ids(base, masks, doc_rows)
    marks = doc_marks(lens_ref, ids, lanes, False)
    totals = jnp.zeros((count, lanes), F32)
    for p in range(doc_rows):
        for m in range(len(RANGES)):
            sims = mm(unit_q[m], unit_ref[m, :, p * ROW : (p + 1) * ROW])
            totals = totals + mm(jnp.exp2(sims).astype(BF16), marks[p][m])
    lane_t = iota((count, lanes), 1)
    totals = jnp.where(lane_t < len(RANGES) * docs, totals, 1.0)
    totals_ref[...] = totals
    shape = (8, lanes)
    lane = iota(shape, 1)
    length = jnp.ones(shape, jnp.int32)
    name = jnp.full(shape, -1, jnp.int32)
    for p in range(doc_rows):
        for k in range(DOCS_ROW):
            own = jnp.zeros(shape, jnp.bool_)
            for m in range(len(RANGES)):
                own = jnp.logical_or(own, lane == m * docs + p * DOCS_ROW + k)
            length = jnp.where(own, lens_ref[k, ids[p]], length)
            name = jnp.where(own, ids[p] * DOCS_ROW + k, name)
    log_length = jnp.log(length.astype(F32))
    matched = (jnp.log(totals) - log_length[:1]) * (1.0 / SHARPNESS)
    per_query = jnp.sum(matched.reshape(count // QLEN, QLEN, lanes), axis=1)
    scale = jnp.exp(jnp.full(shape, scale_ref[0], F32))[:1]
    logits = per_query * (scale * (1.0 / QLEN))
    groups = count // ROW
    tags = []
    for ref in (near_ref, far_ref):
        for k in range(ref.shape[0] // span):
            high = ref[k * span + ROW : k * span + ROW + 8, :].astype(F32).astype(jnp.int32)
            low = ref[k * span + ROW + 8 : k * span + ROW + 16, :].astype(F32).astype(jnp.int32)
            tag = high * 64 + low
            tags.append(jnp.concatenate([tag] * (lanes // 128), axis=1))
    tag = jnp.concatenate(tags, axis=0)
    lane_q = iota(logits.shape, 1)
    valid = lane_q < len(RANGES) * docs
    el = jnp.where(valid, jnp.exp(logits), 0.0)
    hot = jnp.where(jnp.logical_and(valid, jnp.concatenate([name] * groups, axis=0) == tag), 1.0, 0.0)
    el_ref[...] = el
    hot_ref[...] = hot
    place = iota((groups * 8, 128), 1)
    stats = jnp.zeros((groups * 8, 128), F32)
    for k, values in enumerate((el, el * logits, hot * logits)):
        for m in range(len(RANGES)):
            inside = jnp.logical_and(lane_q >= m * docs, lane_q < (m + 1) * docs)
            one = jnp.sum(jnp.where(inside, values, 0.0), axis=1, keepdims=True)
            stats = jnp.where(place == k * 3 + m, one, stats)
    for a in range(groups):
        at = pl.multiple_of((near_at ^ a) * 8, 8)
        stats_ref[pl.ds(at, 8), :] = stats[a * 8 : (a + 1) * 8, :]


def matching_back(
    size, masks, lanes, scale_ref, lens_ref, totals_ref, el_ref, hot_ref, own_ref, over_y, over_x, over_both, unitq_ref, qt_ref, invq_ref, unit_ref, invd_ref, *refs
):
    dq_ref, far_ref, keep_ref, send_ref, loss_ref, dot_ref, dt_ref, stats_ref = refs[-8:]
    _, stream, base, near_at = here(size)[:4]
    total_queries = size * (ROW // QLEN)
    temper = SHARPNESS * LOG2E
    count = unitq_ref.shape[1]
    inv_q = [invq_ref[:, m : m + 1] for m in range(len(RANGES))]
    inv_d = [invd_ref[m : m + 1, :] for m in range(len(RANGES))]
    unit_q = [unitq_ref[m] for m in range(len(RANGES))]
    doc_rows = unit_ref.shape[2] // ROW
    docs = doc_rows * DOCS_ROW
    ids = row_ids(base, masks, doc_rows)
    groups = count // ROW
    odd_y, odd_x = (near_at & 1) == 1, stream == 1
    parts = [own_ref[...], over_y[...], over_x[...], over_both[...]]
    parts = [jnp.where(odd_y, a, b) for a, b in ((parts[1], parts[0]), (parts[0], parts[1]),
                                                  (parts[3], parts[2]), (parts[2], parts[3]))]
    parts = [jnp.where(odd_x, parts[(k + 2) % 4], parts[k]) for k in range(4)]
    stats_ref[...] = (parts[0] + parts[1]) + (parts[2] + parts[3])
    rows = []
    for a in range(groups):
        at = pl.multiple_of((near_at ^ a) * 8, 8)
        rows.append(stats_ref[pl.ds(at, 8), :])
    stats = jnp.concatenate(rows, axis=0)
    place = iota(stats.shape, 1)

    def column(k):
        return jnp.sum(jnp.where(place == k, stats, 0.0), axis=1, keepdims=True)

    shape = (groups * 8, lanes)
    lane_q = iota(shape, 1)
    sums = jnp.ones(shape, F32)
    loss = jnp.zeros((groups * 8, 1), F32)
    moved = jnp.zeros((groups * 8, 1), F32)
    for m in range(len(RANGES)):
        whole, weighted, picked = column(m), column(3 + m), column(6 + m)
        inside = jnp.logical_and(lane_q >= m * docs, lane_q < (m + 1) * docs)
        sums = jnp.where(inside, whole, sums)
        loss = loss + (jnp.log(whole) - picked)
        moved = moved + (weighted / whole - picked)
    line = iota((8, 128), 0)
    loss = jnp.where(
        line == 0,
        jnp.sum(loss, axis=0, keepdims=True) * (1.0 / total_queries),
        jnp.where(line == 1, jnp.sum(moved, axis=0, keepdims=True) * (1.0 / total_queries), 0.0),
    )
    loss_ref[...] = loss
    marks = doc_marks(lens_ref, ids, lanes, True)
    scale = jnp.exp(jnp.full((8, lanes), scale_ref[0], F32))[:1]
    coeff = (el_ref[...] / sums - hot_ref[...]) * (scale * (1.0 / (QLEN * total_queries)))
    coeff = jnp.broadcast_to(coeff[:, None, :], (groups * 8, QLEN, lanes)).reshape(count, lanes)
    ratio = coeff / totals_ref[...]
    ratio_high = ratio.astype(BF16)
    ratio_low = (ratio - ratio_high.astype(F32)).astype(BF16)
    ratio = jnp.concatenate([ratio_high, ratio_low], axis=1)
    for m in range(len(RANGES)):
        grad = jnp.zeros((count, PROJ), F32)
        for p in range(doc_rows):
            block = unit_ref[m, :, p * ROW : (p + 1) * ROW]
            mark = marks[p][m]
            if len(refs) > 8:
                exps = refs[0][m, :, p * ROW : (p + 1) * ROW].astype(F32)
            else:
                exps = jnp.exp2(mm(unit_q[m], block))
            d_sims = (exps * mm(ratio, jnp.concatenate([mark, mark], axis=0))).astype(BF16)
            grad = grad + mm_nt(d_sims, block)
            dt_ref[m, :, p * ROW : (p + 1) * ROW] = mm(qt_ref[m], d_sims)
        unit = unit_q[m].astype(F32) * (1.0 / temper)
        along = jnp.sum(grad * unit, axis=1, keepdims=True)
        part = inv_q[m] * (grad - unit * along)
        if m == 0:
            dot_ref[...] = part
        else:
            dot_ref[...] += part
    dq_ref[...] = dot_ref[: count // 2, :].astype(BF16)
    far_ref[...] = dot_ref[count // 2 :, :].astype(BF16)
    total = jnp.zeros(unit_ref.shape[1:], F32)
    for m in range(len(RANGES)):
        grad = dt_ref[m] * (1.0 / temper)
        unit = unit_ref[m].astype(F32)
        along = jnp.sum(grad * unit, axis=0, keepdims=True)
        total = total + inv_d[m] * (grad - unit * along)
    for p in range(doc_rows):
        ref, at = (keep_ref, p) if p < doc_rows // 2 else (send_ref, p - doc_rows // 2)
        ref[at * ROW : (at + 1) * ROW, :] = total[:, p * ROW : (p + 1) * ROW].T.astype(BF16)


def matching_ready(near_ref, far_ref, *refs):
    doc_refs = refs[:-6] if refs[-2].shape[0] != len(RANGES) else refs[:-7]
    unitq_ref, qt_ref, invq_ref, unit_ref, invd_ref = refs[len(doc_refs) : len(doc_refs) + 5]
    turn_ref = refs[-1]
    queries = load_queries(near_ref, far_ref)
    unit_q, inv_q = unit_queries(queries, SHARPNESS * LOG2E)
    unit_d, inv_d = unit_docs(doc_refs, turn_ref)
    lane = iota(invq_ref.shape, 1)
    columns = jnp.zeros(invq_ref.shape, F32)
    invd_ref[...] = jnp.zeros_like(invd_ref)
    for m in range(len(RANGES)):
        unitq_ref[m] = unit_q[m].astype(BF16)
        unit_ref[m] = unit_d[m].astype(BF16)
        qt_ref[m] = unit_q[m].T.astype(BF16)
        columns = jnp.where(lane == m, inv_q[m], columns)
        invd_ref[m : m + 1, :] = inv_d[m]
        if len(refs) - len(doc_refs) > 6:
            refs[-2][m] = jnp.exp2(mm(unitq_ref[m], unit_ref[m])).astype(BF16)
    invq_ref[...] = columns


def pick_rows(size, here_ref, there_ref, rows_ref):
    _, stream, _, _, has_top = here(size)[:5]
    rows_ref[...] = jnp.where(has_top == stream, here_ref[...], there_ref[...])


def add_rows(rows_ref, got_ref, sum_ref):
    sum_ref[...] = (rows_ref[...].astype(F32) + got_ref[...].astype(F32)).astype(BF16)


DIGITS = 10
POINT = 20


def digits_of(value):
    fixed = (value * float(1 << POINT)).astype(jnp.int32)
    size = jnp.abs(fixed)
    lane = iota(value.shape, 1)
    digits = jnp.zeros(value.shape, jnp.int32)
    for k in range(DIGITS):
        digits = jnp.where(lane == k, (size >> (3 * k)) & 7, digits)
    return jnp.where(fixed < 0, -digits, digits).astype(F32)


def value_of(digits):
    lane = iota(digits.shape, 1)
    half = DIGITS // 2
    weight = jnp.zeros(digits.shape, F32)
    for k in range(half):
        weight = jnp.where(jnp.logical_or(lane == k, lane == k + half), float(8**k), weight)
    low = jnp.sum(jnp.where(lane < half, digits * weight, 0.0))
    high = jnp.sum(jnp.where(jnp.logical_and(lane >= half, lane < DIGITS), digits * weight, 0.0))
    return (high * float(8**half) + low) * (1.0 / (1 << POINT))


def turn(core, place, block):
    return jnp.where(core == 0, place - block, block - place) & (RING - 1)


def block_at(core, place, distance):
    return jnp.where(core == 0, place - distance, place + distance) & (RING - 1)


def store_block(keep_ref, send_ref, rows, block, places, value):
    core, place = places
    mine = core == block // RING
    at = turn(block // RING, place, block % RING)

    @pl.when(mine)
    def _():
        keep_ref[at, rows, :] = value

    @pl.when(jnp.logical_not(mine))
    def _():
        send_ref[at, rows, :] = value


def feed_back(
    size, dq_ref, dd_ref, got_ref, xh2_ref, rs2_ref, affine_ref, wproj_ref, slope_ref, act_ref,
    xh1_ref, wdown_ref, wup_hbm,
    keep_ref, send_ref, tail_keep, tail_send, dfirst_ref, gproj_ref, small_ref,
    dinner_ref, wup_ref, sems,
):
    step = 512
    spans = [slice(c * step, (c + 1) * step) for c in range(FF // step)]
    copies = fetch([(wup_hbm, wup_ref)], sems)
    g1, s1, g2, s2 = [affine_ref[k : k + 1, :] for k in range(4)]
    _, stream, _, _, has_top, *places = here(size)
    is_query, docs_there = stream == 0, has_top == 0
    got = got_ref[...].astype(F32)
    d_vec = jnp.where(
        is_query,
        dq_ref[...].astype(F32) + got,
        jnp.where(docs_there, got, dd_ref[...].astype(F32)),
    )
    d_proj = d_vec.astype(BF16)
    xhat = xh2_ref[...]
    gain = g2
    second = (xhat * gain + s2).astype(BF16)
    gproj_ref[...] = mm_tn(second, d_proj)
    d_second = mm_nt(d_proj, wproj_ref[...])
    small_ref[...] = jnp.zeros_like(small_ref)
    small_ref[5:6, :] = col_sum(d_second * xhat)
    small_ref[6:7, :] = col_sum(d_second)
    d_sum = norm_back(d_second, xhat, rs2_ref[:, :1], gain)
    d_branch = d_sum.astype(BF16)
    small_ref[4:5, :] = col_sum(d_branch.astype(F32))
    d_first = d_sum
    for c in range(FF // step):
        cols = spans[c]
        d_act = mm_nt(d_branch, wdown_ref[cols, :])
        d_inner = (d_act * slope_ref[:, cols].astype(F32)).astype(BF16)
        dinner_ref[:, cols] = d_inner
        small_ref[c : c + 1, :] = col_sum(d_inner.astype(F32))
        grad = mm_tn(act_ref[:, cols], d_branch).astype(BF16)
        for k in range(step // DOWN):
            store_block(
                keep_ref, send_ref, slice(0, DOWN), c * (step // DOWN) + k, places,
                grad[k * DOWN : (k + 1) * DOWN, :],
            )
    copies[0].wait()
    first = (xh1_ref[...] * g1 + s1).astype(BF16)
    for c in range(FF // step):
        cols = slice(c * step, (c + 1) * step)
        d_first = d_first + mm_nt(dinner_ref[:, cols], wup_ref[:, cols])
        grad = mm_tn(first, dinner_ref[:, cols]).astype(BF16)
        for k in range(D // DOWN):
            block = c * (D // DOWN) + k
            start = k * DOWN
            store_block(
                keep_ref, send_ref, slice(DOWN, FIRST), block, places, grad[start : start + HEAD, :]
            )
            store_block(
                tail_keep, tail_send, slice(0, TAIL), block, places,
                grad[start + HEAD : start + DOWN, :],
            )
    dfirst_ref[...] = d_first


def attend_back(
    size, dfirst_ref, gproj_ref, small_ref, loss_ref, tail_keep, tail_send, xh1_ref, rs1_ref, affine_ref, mixed_ref, wout_ref,
    qkv_ref, probs_ref, rope_ref, x_ref,
    keep_ref, ahead_ref, send_ref, dsum_ref, djoined_ref, rest_ref,
):
    me, *_, core, place = here(size)
    d_first = dfirst_ref[...]
    xhat = xh1_ref[...]
    gain = affine_ref[0:1, :]
    gain_grad = col_sum(d_first * xhat)
    shift_grad = col_sum(d_first)
    d_sum = norm_back(d_first, xhat, rs1_ref[:, :1], gain)
    d_att = d_sum.astype(BF16)
    bias_out = col_sum(d_att.astype(F32))
    rest_ref[3 * D : 4 * D, :] = mm_tn(mixed_ref[...], d_att)
    d_mixed = mm_nt(d_att, wout_ref[...]).astype(BF16)
    cosine, sine = rope_ref[:, :128], rope_ref[:, 128:]
    low_half = iota((ROW, 128), 1) < HD

    scale = 1.0 / math.sqrt(HD)
    cosine, sine = cosine * scale, sine * scale
    swap = swapping()

    def unrotate(both):
        return (both[:, :128] * cosine - both[:, 128:] * sine).astype(BF16)

    for g in range(HEADS // 2):
        span = slice(g * 128, (g + 1) * 128)
        q_g = qkv_ref[:, g * 128 : (g + 1) * 128]
        k_g = qkv_ref[:, D + g * 128 : D + (g + 1) * 128]
        v_g = qkv_ref[:, 2 * D + g * 128 : 2 * D + (g + 1) * 128]
        m_g = d_mixed[:, span]
        q_both = jnp.concatenate([q_g, mm(q_g, swap).astype(BF16)], axis=1)
        k_both = jnp.concatenate([k_g, mm(k_g, swap).astype(BF16)], axis=1)
        d_q = jnp.zeros((ROW, 256), F32)
        d_k = jnp.zeros((ROW, 256), F32)
        d_v = jnp.zeros((ROW, 128), F32)
        zero = jnp.zeros((ROW, 128), BF16)
        zero_both = jnp.zeros((ROW, 256), BF16)
        for h in range(2):
            pick = low_half if h == 0 else jnp.logical_not(low_half)
            probs_low = probs_ref[2 * g + h]
            probs = probs_low.astype(F32)
            m_h = jnp.where(pick, m_g, zero)
            d_probs = mm_nt(m_h, v_g)
            d_v = d_v + mm_tn(probs_low, m_h)
            inner = jnp.sum(d_probs * probs, axis=1, keepdims=True)
            d_scores = (probs * (d_probs - inner)).astype(BF16)
            pick_both = jnp.concatenate([pick, pick], axis=1)
            d_q = d_q + mm(d_scores, jnp.where(pick_both, k_both, zero_both))
            d_k = d_k + mm_tn(d_scores, jnp.where(pick_both, q_both, zero_both))
        djoined_ref[:, g * 128 : (g + 1) * 128] = unrotate(d_q)
        djoined_ref[:, D + g * 128 : D + (g + 1) * 128] = unrotate(d_k)
        djoined_ref[:, 2 * D + g * 128 : 2 * D + (g + 1) * 128] = d_v.astype(BF16)
    x = x_ref[...]
    dsum_ref[...] = d_sum
    rest_ref[4 * D :, :] = jnp.zeros((8 * 2 * RING, D), F32)
    smalls = []
    for c in range(3):
        cols = slice(c * D, (c + 1) * D)
        d_part = djoined_ref[:, cols]
        rest_ref[c * D : (c + 1) * D, :] = mm_tn(x, d_part)
        smalls.append(col_sum(d_part.astype(F32)))
    smalls += [bias_out, gain_grad, shift_grad] + [small_ref[k : k + 1, :] for k in range(7)]
    counted = jnp.where((me & 3) == 0, 1.0, 0.0)
    lines = [digits_of(loss_ref[k : k + 1, :]) * counted for k in range(2)]
    smalls.append(jnp.concatenate(lines + [jnp.zeros((1, D - 256), F32)], axis=1))
    for k, row in enumerate(smalls):
        rest_ref[4 * D + 8 * k : 4 * D + 8 * k + 1, :] = row
    for k in range(RING):
        sent, at = (ahead_ref, AHEAD.index(k)) if k in AHEAD else (send_ref, LATER.index(k))
        for ref, index, tail_ref, owner in (
            (keep_ref, k, tail_keep, core), (sent, at, tail_send, 1 - core)
        ):
            block = owner * RING + block_at(owner, place, k)
            parts = []
            for c in range(4):
                start = pl.multiple_of(c * D + block * SHARE, SHARE)
                parts.append(rest_ref[pl.ds(start, SHARE), :])
            row = pl.multiple_of(block * SHARE, SHARE)
            parts.append(
                jnp.concatenate(
                    [gproj_ref[pl.ds(row + 8 * j, 8), :] for j in range(SHARE // 8)], axis=1
                )
            )
            parts.append(rest_ref[pl.ds(pl.multiple_of(4 * D + block * 8, 8), 8), :])
            ref[index, : REST // 16, :] = jnp.concatenate(parts, axis=0).astype(BF16)
            ref[index, REST // 16 :, :] = tail_ref[k]


def tokens_back(dsum_ref, djoined_ref, wqkv_ref, tokens_ref):
    tokens = dsum_ref[...]
    for c in range(3):
        cols = slice(c * D, (c + 1) * D)
        tokens = tokens + mm_nt(djoined_ref[:, cols], wqkv_ref[:, cols])
    tokens_ref[...] = tokens


def spread(size, jobs, last, *refs):
    core, place = here(size)[-2:]
    halves = refs[: 2 * len(jobs)]
    wide_one, wide_two, wide_qkv, wide_proj, small_ref, sems = refs[-6:]
    outs = refs[-21:-6] if last else refs[-11:-6]
    down_hbm, up_hbm, qkv_hbm, out_hbm, proj_hbm = outs[:5]
    copies = []

    def move(src, dst):
        copy = pltpu.make_async_copy(src, dst, sems.at[len(copies)])
        copy.start()
        copies.append(copy)

    at = 0
    for job, (mine, group) in enumerate(jobs):
        owner = core if mine else 1 - core
        one_ref, two_ref = halves[2 * job : 2 * job + 2]
        for p, distance in enumerate(GROUPS[group]):
            block = owner * RING + block_at(owner, place, distance)
            wide_one[at] = one_ref[p].astype(F32)
            rows = pl.ds(pl.multiple_of(block * DOWN, DOWN), DOWN)
            move(wide_one.at[at, :DOWN, :], down_hbm.at[rows, :])
            start = (block % (D // DOWN)) * DOWN
            columns = pl.ds(pl.multiple_of((block // (D // DOWN)) * D, D), D)
            rows = pl.ds(pl.multiple_of(start, DOWN), HEAD)
            move(wide_one.at[at, DOWN:, :], up_hbm.at[rows, columns])
            wide = two_ref[p].astype(F32)
            wide_two[at, :SHARE, :] = wide[3 * SHARE : 4 * SHARE, :]
            wide_two[at, SHARE:, :] = wide[REST // 16 :, :]
            rows = pl.ds(pl.multiple_of(start + HEAD, 16), TAIL)
            move(wide_two.at[at, SHARE:, :], up_hbm.at[rows, columns])
            rows = pl.ds(pl.multiple_of(block * SHARE, SHARE), SHARE)
            for c in range(3):
                wide_qkv[at, :, c * D : (c + 1) * D] = wide[c * SHARE : (c + 1) * SHARE, :]
            move(wide_qkv.at[at], qkv_hbm.at[rows, :])
            move(wide_two.at[at, :SHARE, :], out_hbm.at[rows, :])
            for j in range(SHARE // 8):
                wide_proj[at, 8 * j : 8 * j + 8, :] = wide[
                    4 * SHARE : 4 * SHARE + 8, j * PROJ : (j + 1) * PROJ
                ]
            move(wide_proj.at[at], proj_hbm.at[rows, :])
            at += 1
    if last:
        sources = refs[2 * len(jobs) : 2 * len(jobs) + 2 * len(GROUPS)]
        for k, ref in enumerate(sources):
            owner = core if k < len(GROUPS) else 1 - core
            for p, distance in enumerate(GROUPS[k % len(GROUPS)]):
                block = owner * RING + block_at(owner, place, distance)
                line = ref[p, 4 * SHARE : 4 * SHARE + 16, :].astype(F32)[8:, :]
                small_ref[pl.ds(pl.multiple_of(block * 8, 8), 8), :] = line
        rows = [small_ref[8 * k : 8 * k + 1, :] for k in range(14)]
        bqkv_ref, bout_ref, g1_ref, s1_ref, bup_ref, bdown_ref, g2_ref, s2_ref = outs[5:13]
        for k, ref in enumerate(outs[13:]):
            ref[0] = value_of(rows[13][:, k * 128 : (k + 1) * 128])
        for c in range(3):
            bqkv_ref[:, c * D : (c + 1) * D] = rows[c]
        bout_ref[...] = rows[3]
        g1_ref[...] = rows[4]
        s1_ref[...] = rows[5]
        for c in range(4):
            bup_ref[:, c * D : (c + 1) * D] = rows[6 + c]
        bdown_ref[...] = rows[10]
        g2_ref[...] = rows[11]
        s2_ref[...] = rows[12]
    for copy in copies:
        copy.wait()


def spread_call(size, jobs, halves, outs, others):
    last = len(others) > 0
    shapes = ((FF, D), (D, FF), (D, 3 * D), (D, D), (D, PROJ))
    widths = (3 * D, D, D, D, FF, D, D, D) if last else ()
    args = [*halves, *others, *outs]
    count = sum(len(GROUPS[group]) for _, group in jobs)
    before = len(halves) + len(others)
    return call(
        partial(spread, size, jobs, last),
        args,
        [VMEM] * before + [HBM] * len(outs),
        [pltpu.HBM(shape, F32) for shape in shapes]
        + [shape_of((1, width)) for width in widths]
        + [shape_of((1,))] * (2 * last),
        [
            pltpu.VMEM((count, FIRST, D), F32),
            pltpu.VMEM((count, SHARE + TAIL, D), F32),
            pltpu.VMEM((count, SHARE, 3 * D), F32),
            pltpu.VMEM((count, SHARE, PROJ), F32),
            pltpu.VMEM((16 * RING, D), F32),
            pltpu.SemaphoreType.DMA((6 * count,)),
        ],
        out_specs=[HBM] * 5 + [VMEM] * len(widths) + [SMEM] * (2 * last),
        aliases={before + k: k for k in range(len(outs))},
        cost=SPREAD_COST,
        room=14,
    )


def shape_of(shape, dtype=F32):
    return jax.ShapeDtypeStruct(tuple(shape), dtype)


def call(kernel, args, specs, outs, scratch=(), room=24, out_specs=None, aliases={}, cost=10**7):
    spaces = {id(HBM): pltpu.HBM, id(HELD): pltpu.VMEM}
    args = [
        pltpu.with_memory_space_constraint(arg, spaces[id(spec)]) if id(spec) in spaces else arg
        for arg, spec in zip(args, specs)
    ]
    return pl.pallas_call(
        kernel,
        out_shape=outs,
        in_specs=specs,
        out_specs=out_specs or [VMEM] * len(outs),
        scratch_shapes=list(scratch),
        input_output_aliases=aliases,
        compiler_params=pltpu.CompilerParams(vmem_limit_bytes=room * MIB),
        cost_estimate=pl.CostEstimate(
            flops=10 * cost, bytes_accessed=cost, transcendentals=0
        ),
    )(*args)


def swapped(value, mask, axis="dp"):
    size = lax.axis_size(axis)
    return lax.ppermute(value, axis, [(k, k ^ mask) for k in range(size)])


def added(a, b):
    return (a.astype(F32) + b.astype(F32)).astype(BF16)


def join_blocks(*refs):
    for k, ref in enumerate(refs[:-1]):
        refs[-1][k] = ref[0]


def ring_swap(value, onward):
    size = lax.axis_size("dp")
    pairs = []
    for k in range(size):
        at = CIRCLE.index((k >> 1) % RING)
        to = CIRCLE[(at + (1 if (k % 2 == 0) == onward else -1)) % RING]
        pairs.append((k, (k & ~(2 * RING - 1)) | (to << 1) | (k & 1)))
    return lax.ppermute(value, "dp", pairs)


def add_blocks(places, *refs):
    count = len(places)
    held_ref = refs[count] if any(place is not None for place in places) else None
    for k, place in enumerate(places):
        value = refs[k][...]
        if place is not None:
            value = (value.astype(F32) + held_ref[place : place + 1].astype(F32)).astype(BF16)
        refs[-count + k][...] = value


def first_blocks(places, keep_ref, pair_ref, *outs):
    for ref, (k, j) in zip(outs, places):
        ref[0] = (keep_ref[k].astype(F32) + pair_ref[j].astype(F32)).astype(BF16)


def later_blocks(places, keep_ref, pair_ref, out_ref):
    for k in AHEAD:
        out_ref[k] = jnp.zeros(out_ref.shape[1:], BF16)
    for k, j in places:
        out_ref[k] = (keep_ref[k].astype(F32) + pair_ref[j].astype(F32)).astype(BF16)


class Summed:
    def __init__(self, keep, sends, others):
        self.keep, self.others, self.hop = keep, others, 0
        self.pairs = [swapped(send, 1) for send in sends]
        self.sent, self.blocks, self.near, self.far = [], {}, [], []

    def blocks_call(self, blocks, places, held):
        return call(
            partial(add_blocks, places),
            (*blocks, *held),
            [VMEM] * (len(blocks) + len(held)),
            [shape_of(block.shape, BF16) for block in blocks],
            room=8,
            cost=STEP_COST,
        )

    def open(self, after):
        keep, pair, _ = lax.optimization_barrier((self.keep, self.pairs[0], after))
        shape = (1, *keep.shape[1:])
        places = [(k, AHEAD.index(k) if len(self.pairs) > 1 else k) for k in AHEAD]
        first, second = call(
            partial(first_blocks, places),
            (keep, pair),
            [VMEM] * 2,
            [shape_of(shape, BF16)] * 2,
            room=8,
            cost=STEP_COST,
        )
        self.sent = [(first, True), (second, False)]
        return second

    def total(self, after):
        keep, _ = lax.optimization_barrier((self.keep, after))
        later = [(k, LATER.index(k) if len(self.pairs) > 1 else k) for k in LATER]
        (self.keep,) = call(
            partial(later_blocks, later),
            (keep, self.pairs[-1]),
            [VMEM] * 2,
            [shape_of(keep.shape, BF16)],
            room=8,
            cost=STEP_COST,
        )
        return self.keep

    def step(self, after):
        half = RING // 2
        self.hop += 1
        hop = self.hop
        *got, _ = lax.optimization_barrier((*[ring_swap(*one) for one in self.sent], after))
        if hop < half:
            out = self.blocks_call(got, (half + hop, half - 1 - hop), [self.keep])
            self.part = out[1]
        elif hop == half:
            (own,) = self.blocks_call(got, (0,), [self.part])
            for mask in self.others:
                own = added(own, swapped(own, mask))
            self.blocks[0] = own
            out = [own, own]
        else:
            out = self.blocks_call(got, (None,) * len(got), [])
            hop -= half
            self.blocks[hop] = out[0]
            if hop < half:
                self.blocks[RING - hop] = out[1]
        if hop == half - 1:
            self.sent = [(out[0], True)]
        elif self.hop < 2 * half:
            self.sent = [(out[0], True), (out[1], False)]
        return out[0]

    def share(self, group, after):
        *blocks, _ = lax.optimization_barrier((*[self.blocks[k] for k in GROUPS[group]], after))
        shape = (len(blocks), *blocks[0].shape[1:])
        self.near += call(
            join_blocks, blocks, [VMEM] * len(blocks), [shape_of(shape, BF16)], room=8, cost=0
        )
        self.far.append(swapped(self.near[-1], 1))
        return self.near[-1]


def per_device(
    tokens, qkv_weight, qkv_bias, out_weight, out_bias, first_gain, first_shift, up_weight,
    up_bias, down_weight, down_bias, second_gain, second_shift, proj_weight, log_scale,
    doc_lengths, labels,
):
    size = lax.axis_size("dp")
    bits = [1 << k for k in range(size.bit_length() - 1)]
    near_masks, doc_masks = bits[:2], bits[2:]
    top_mask, doc_masks = doc_masks[-1], doc_masks[:-1]
    others = bits[4:]
    me = lax.axis_index("dp")
    stream = lax.axis_index("stream")
    is_query = stream == 0
    has_top = (me & top_mask) != 0
    lens = doc_lengths.T
    scale = log_scale.reshape(1)

    vec, *moved, qkv, rope, probs, mixed, xh1, rs1, affine = call(
        partial(encoder_forward, size),
        (
            lens, labels, jnp.asarray(rope_table()), tokens[0], qkv_weight[0], qkv_bias,
            out_weight[0], out_bias, first_gain, first_shift, up_weight[0], up_bias,
            down_weight[0], down_bias, second_gain, second_shift, proj_weight[0],
        ),
        [HBM] * 17,
        [shape_of((ROW + EXT, PROJ), BF16)]
        + [shape_of(*kind) for kind in MOVED]
        + [pltpu.HBM(*kind) for kind in KEPT],
        [pltpu.VMEM(*kind) for kind in KEPT]
        + [pltpu.SemaphoreType.DMA((len(KEPT),))]
        + [
            pltpu.VMEM(shape, BF16)
            for shape in (
                (ROW, 512), (ROW, D), (D, 3 * D), (1, 3 * D), (D, D), (1, D), (1, D), (1, D), (D, FF),
                (1, FF), (FF, D), (1, D), (1, D), (1, D), (D, PROJ),
            )
        ]
        + [
            pltpu.SMEM(lens.shape, jnp.int32),
            pltpu.SMEM(labels.shape, jnp.int32),
            pltpu.SemaphoreType.DMA((17,)),
        ],
        room=40,
        out_specs=[VMEM] * (1 + len(MOVED)) + [HBM] * len(KEPT),
    )
    act, slope, xh2, rs2 = call(
        move_kept,
        moved,
        [VMEM] * len(MOVED),
        [pltpu.HBM(*kind) for kind in MOVED],
        [pltpu.SemaphoreType.DMA((len(MOVED),))],
        room=8,
        out_specs=[HBM] * len(MOVED),
        cost=STEP_COST,
    )

    every, other_y = range(size), near_masks[1]
    other, _ = lax.optimization_barrier((swapped(vec, 1, "stream"), rs2))
    near = jnp.where(is_query, vec, other)
    rows = jnp.where(is_query, other, vec)[:ROW]
    moved = swapped(rows, top_mask)
    (rows,) = call(
        partial(pick_rows, size),
        (rows, moved),
        [VMEM] * 2,
        [shape_of((ROW, PROJ), BF16)],
        room=8,
        cost=STEP_COST,
    )
    got_y, _ = lax.optimization_barrier((swapped(near, other_y), rows))
    near = jnp.concatenate([near, got_y], axis=0)
    far = swapped(near, near_masks[0])
    pieces = []
    for k, mask in enumerate(doc_masks):
        pieces.append(rows)
        got = swapped(rows, mask)
        if k + 1 < len(doc_masks):
            rows = jnp.concatenate([rows, got], axis=0)
        else:
            pieces = [rows, got]
    doc_rows = sum(p.shape[0] for p in pieces) // ROW
    tokens_d = doc_rows * ROW
    tokens_q = 4 * ROW
    lanes = -(-3 * doc_rows * DOCS_ROW // 128) * 128
    room = 20 if doc_rows <= 4 else 56
    totals, el, hot, stats = call(
        partial(matching_stats, size, doc_masks, lanes),
        (scale, lens, near, far, *pieces),
        [SMEM] * 2 + [VMEM] * (2 + len(pieces)),
        [
            shape_of((tokens_q, lanes)),
            shape_of((tokens_q // QLEN, lanes)),
            shape_of((tokens_q // QLEN, lanes)),
            shape_of((tokens_q // QLEN, 128)),
        ],
        [pltpu.VMEM((PROJ, tokens_d), F32), pltpu.VMEM((3, PROJ, tokens_d), BF16)],
        room=room,
    )
    small_enough = doc_rows <= 4
    ready = call(
        matching_ready,
        (near, far, *pieces),
        [VMEM] * (2 + len(pieces)),
        [
            shape_of((3, tokens_q, PROJ), BF16),
            shape_of((3, PROJ, tokens_q), BF16),
            shape_of((tokens_q, 128)),
            shape_of((3, PROJ, tokens_d), BF16),
            shape_of((8, tokens_d)),
        ]
        + [shape_of((3, tokens_q, tokens_d), BF16)] * small_enough,
        [pltpu.VMEM((PROJ, tokens_d), F32)],
        room=room,
    )
    stats = stats + swapped(stats, near_masks[0])
    over_y = swapped(stats, other_y)
    over_x = swapped(stats, 1, "stream")
    pairs = [(k * size + r, (1 - k) * size + (r ^ other_y)) for k in range(2) for r in every]
    over_both = lax.ppermute(stats, ("stream", "dp"), pairs)
    dq, dq_send, keep, send, loss = call(
        partial(matching_back, size, doc_masks, lanes),
        (scale, lens, totals, el, hot, stats, over_y, over_x, over_both, *ready),
        [SMEM] * 2 + [VMEM] * (7 + len(ready)),
        [shape_of((tokens_q // 2, PROJ), BF16)] * 2
        + [shape_of((tokens_d // 2, PROJ), BF16)] * 2
        + [shape_of((8, 128))],
        [
            pltpu.VMEM((tokens_q, PROJ), F32),
            pltpu.VMEM((3, PROJ, tokens_d), F32),
            pltpu.VMEM((tokens_q // QLEN, 128), F32),
        ],
        room=room,
    )
    got_dq = swapped(dq_send, near_masks[0])
    for mask in reversed(doc_masks[1:]):
        total, half = added(keep, swapped(send, mask)), keep.shape[0] // 2
        keep, send = total[:half], total[half:]
    got_dd = swapped(send, doc_masks[0])
    def summed(rows, got, after=None):
        if after is not None:
            got, _ = lax.optimization_barrier((got, after))
        return call(
            add_rows, (rows, got), [VMEM] * 2, [shape_of(rows.shape, BF16)], room=8, cost=STEP_COST
        )[0]

    dq = summed(dq, got_dq)
    dd = summed(keep, got_dd, dq)
    dd = summed(dd, swapped(dd, top_mask))
    dq = summed(dq[:ROW], swapped(dq[ROW:], other_y), dd)
    got = swapped(jnp.where(is_query, dd, dq), 1, "stream")

    one_keep, one_send, tail_keep, tail_send, d_first, gproj, small = call(
        partial(feed_back, size),
        (
            dq, dd, got, xh2, rs2, affine, proj_weight[0], slope, act, xh1, down_weight[0],
            up_weight[0],
        ),
        [VMEM] * 3 + [HELD] * 8 + [HBM],
        [shape_of((RING, FIRST, D), BF16)] * 2
        + [shape_of((RING, TAIL, D), BF16)] * 2
        + [shape_of((ROW, D)), shape_of((D, PROJ)), shape_of((8, D))],
        [
            pltpu.VMEM((ROW, FF), BF16),
            pltpu.VMEM((D, FF), BF16),
            pltpu.SemaphoreType.DMA((1,)),
        ],
        room=24,
    )
    two_keep, two_ahead, two_send, d_sum, d_joined = call(
        partial(attend_back, size),
        (
            d_first, gproj, small, loss, tail_keep, tail_send, xh1, rs1, affine, mixed, out_weight[0], qkv, probs, rope,
            tokens[0],
        ),
        [VMEM] * 6 + [HELD] * 9,
        [shape_of((count, SECOND, D), BF16) for count in (RING, len(AHEAD), len(LATER))]
        + [shape_of((ROW, D)), shape_of((ROW, 3 * D), BF16)],
        [pltpu.VMEM((4 * D + 16 * RING, D), F32)],
        room=24,
    )
    one, two = [
        Summed(keep, sends, others)
        for keep, *sends in ((one_keep, one_send), (two_keep, two_ahead, two_send))
    ]
    token, outs = d_sum, ()
    for event in ORDER:
        kind, k, *group = event
        if kind == "tokens":
            d_sum, _ = lax.optimization_barrier((d_sum, token))
            (tokens_grad,) = call(
                tokens_back,
                (d_sum, d_joined, qkv_weight[0]),
                [VMEM] * 3,
                [shape_of((ROW, D))],
                room=8,
                cost=STEP_COST,
            )
            token = tokens_grad
            continue
        if kind == "spread":
            jobs = event[1]
            halves = [
                (piece.near if mine else piece.far)[group] for mine, group in jobs for piece in (one, two)
            ]
            *halves, _ = lax.optimization_barrier((*halves, token))
            others = [*two.near, *two.far] if event == ORDER[-1] else []
            outs = spread_call(size, jobs, halves, outs[:5], others)
            token = outs[0]
            continue
        piece = (one, two)[k]
        token = getattr(piece, kind)(*group, token)
    grad_down, grad_up, grad_qkv, grad_out, grad_proj = outs[:5]
    (
        grad_bqkv, grad_bout, grad_g1, grad_s1, grad_bup, grad_bdown, grad_g2, grad_s2, loss,
        scale_grad,
    ) = outs[5:]
    return (
        loss.reshape(()),
        tokens_grad[None],
        grad_qkv[None],
        grad_bqkv,
        grad_out[None],
        grad_bout,
        grad_g1,
        grad_s1,
        grad_up[None],
        grad_bup,
        grad_down[None],
        grad_bdown,
        grad_g2,
        grad_s2,
        grad_proj[None],
        scale_grad.reshape(()),
    )


def solution(mesh):
    return jax.shard_map(
        per_device,
        mesh=mesh,
        in_specs=(
            P("stream", "dp", None),
            P("stream", None, None),
            P("stream", None),
            P("stream", None, None),
            P("stream", None),
            P("stream", None),
            P("stream", None),
            P("stream", None, None),
            P("stream", None),
            P("stream", None, None),
            P("stream", None),
            P("stream", None),
            P("stream", None),
            P("stream", None, None),
            P(),
            P(),
            P("dp"),
        ),
        out_specs=(
            P(),
            P("stream", "dp", None),
            P("stream", None, None),
            P("stream", None),
            P("stream", None, None),
            P("stream", None),
            P("stream", None),
            P("stream", None),
            P("stream", None, None),
            P("stream", None),
            P("stream", None, None),
            P("stream", None),
            P("stream", None),
            P("stream", None),
            P("stream", None, None),
            P(),
        ),
        check_vma=False,
    )
```

```python
from functools import partial
import math

import jax
import jax.numpy as jnp
import numpy as np
from jax import lax
from jax.experimental import pallas as pl
from jax.experimental.pallas import tpu as pltpu
from jax.sharding import PartitionSpec as P

D = 512
HEADS = 8
HD = 64
FF = 2048
PROJ = 128
QLEN = 32
DOCS_ROW = 4
ROW = 256
EXT = 16
RANGES = (64, 96, 128)

SHARPNESS = 8.0
EPS_NORM = 1e-06
EPS_LAYER = 1e-05
LOG2E = 1.4426950408889634

F32 = jnp.float32
BF16 = jnp.bfloat16
REST = 2304
SHARE = 32
DOWN = FF // 16
HEAD = 80
TAIL = DOWN - HEAD
FIRST = DOWN + HEAD
SECOND = REST // 16 + TAIL
CIRCLE = (0, 2, 4, 6, 7, 5, 3, 1)
RING = len(CIRCLE)
AHEAD = (RING // 2, RING // 2 - 1)
LATER = tuple(k for k in range(RING) if k not in AHEAD)
GROUPS = ((0, 1, 2, 3, 5, 6, 7), (4,))
STEP_COST = 3 * 10**7
SPREAD_COST = 0
ROUND = (("step", 0), ("step", 1))
ORDER = (
    (("open", 0), ("open", 1), ("total", 0), ("total", 1), ("tokens", 0)) + ROUND * 7
    + (("share", 0), ("spread", ((True, 0),)), ("spread", ((False, 0),))) + ROUND
    + (("share", 1), ("spread", ((True, 1),)), ("spread", ((False, 1),)))
)
MIB = 1024 * 1024

VMEM = pl.BlockSpec(memory_space=pltpu.VMEM)
SMEM = pl.BlockSpec(memory_space=pltpu.SMEM)
HBM = pl.BlockSpec(memory_space=pltpu.HBM)
HELD = pl.BlockSpec(memory_space=pltpu.VMEM)


def mm(a, b):
    return lax.dot_general(a, b, (((1,), (0,)), ((), ())), preferred_element_type=F32)


def mm_nt(a, b):
    return lax.dot_general(a, b, (((1,), (1,)), ((), ())), preferred_element_type=F32)


def mm_tn(a, b):
    return lax.dot_general(a, b, (((0,), (0,)), ((), ())), preferred_element_type=F32)


def iota(shape, axis):
    return lax.broadcasted_iota(jnp.int32, shape, axis)


def rope_table():
    half = HD // 2
    freqs = (10000.0 ** (-np.arange(half, dtype=np.float32) / np.float32(half))).astype(np.float32)
    turned = np.arange(ROW, dtype=np.float32)[:, None] * freqs[None, :]
    cosine = np.cos(turned.astype(np.float64))
    sine = np.sin(turned.astype(np.float64))
    cosine = np.concatenate([cosine, cosine, cosine, cosine], axis=1).astype(np.float32)
    sine = np.concatenate([-sine, sine, -sine, sine], axis=1).astype(np.float32)
    parts = []
    for table in (cosine, sine):
        high = table.astype(jnp.bfloat16)
        low = (table - high.astype(np.float32)).astype(jnp.bfloat16)
        parts += [high, low]
    return np.concatenate(parts, axis=1)


def swapping():
    shape = (128, 128)
    return (iota(shape, 0) == (iota(shape, 1) ^ (HD // 2))).astype(F32).astype(BF16)


def bounds_of(lens_ref, row):
    ends, total = [], jnp.int32(0)
    for k in range(DOCS_ROW):
        total = total + lens_ref[k, row]
        ends.append(total)
    return ends


def segment_of(spot, ends):
    seg = jnp.zeros_like(spot)
    for end in ends:
        seg = seg + (spot >= end).astype(jnp.int32)
    return seg


def norm_rows(values):
    mean = jnp.mean(values, axis=1, keepdims=True)
    centred = values - mean
    spread = jnp.mean(centred * centred, axis=1, keepdims=True)
    rstd = lax.rsqrt(spread + EPS_LAYER)
    return centred * rstd, rstd


def norm_back(d_out, xhat, rstd, gain):
    scaled = d_out * gain
    first = jnp.mean(scaled, axis=1, keepdims=True)
    second = jnp.mean(scaled * xhat, axis=1, keepdims=True)
    return rstd * (scaled - first - xhat * second)


def col_sum(values):
    return jnp.sum(values, axis=0, keepdims=True)


def here(size):
    me, stream = lax.axis_index("dp"), lax.axis_index("stream")
    top = size // 2
    has_top = jnp.where((me & top) != 0, 1, 0)
    base = jnp.where(stream == 0, me & ~top, me | top)
    near_at = jnp.where((me & 2) != 0, 1, 0) + jnp.where((me & 1) != 0, 2, 0)
    chip = (me >> 1) % RING
    place = jnp.int32(0)
    for k, one in enumerate(CIRCLE):
        place = jnp.where(chip == one, k, place)
    return me, stream, base, near_at, has_top, me & 1, place


def fetch(pairs, sems):
    copies = [pltpu.make_async_copy(src, dst, sems.at[k]) for k, (src, dst) in enumerate(pairs)]
    for copy in copies:
        copy.start()
    return copies


KEPT = (
    ((ROW, 3 * D), BF16),
    ((ROW, 256), F32),
    ((HEADS, ROW, ROW), BF16),
    ((ROW, D), BF16),
    ((ROW, D), F32),
    ((ROW, 128), F32),
    ((8, D), F32),
)
MOVED = (((ROW, FF), BF16), ((ROW, FF), BF16), ((ROW, D), F32), ((ROW, 128), F32))


def move_kept(*refs):
    count = len(MOVED)
    for copy in fetch([*zip(refs[:count], refs[count:-1])], refs[-1]):
        copy.wait()


def encoder_forward(
    size, lens_hbm, labels_hbm, table_hbm, x_hbm, wqkv_hbm, bqkv_hbm, wout_hbm, bout_hbm,
    g1_hbm, s1_hbm, wup_hbm, bup_hbm, wdown_hbm, bdown_hbm, g2_hbm, s2_hbm, wproj_hbm,
    vec_ref, act_ref, slope_ref, xh2_ref, rs2_ref, qkv_hbm, rope_hbm, probs_hbm, mixed_hbm, xh1_hbm,
    rs1_hbm, affine_hbm,
    qkv_ref, rope_ref, probs_ref, mixed_ref, xh1_ref, rs1_ref, affine_ref, out_sems,
    table_ref, x_ref, wqkv_ref, bqkv_ref, wout_ref, bout_ref, g1_ref, s1_ref, wup_ref, bup_ref,
    wdown_ref, bdown_ref, g2_ref, s2_ref, wproj_ref, lens_ref, labels_ref, sems,
):
    me, stream = here(size)[:2]
    is_query = stream == 0
    scalars = fetch(((lens_hbm, lens_ref), (labels_hbm, labels_ref)), sems.at[pl.ds(15, 2)])
    copies = fetch(
        (
            (table_hbm, table_ref), (x_hbm, x_ref), (wqkv_hbm, wqkv_ref), (bqkv_hbm, bqkv_ref),
            (wout_hbm, wout_ref), (bout_hbm, bout_ref), (g1_hbm, g1_ref), (s1_hbm, s1_ref),
            (bup_hbm, bup_ref), (bdown_hbm, bdown_ref), (g2_hbm, g2_ref), (s2_hbm, s2_ref),
            (wup_hbm, wup_ref), (wdown_hbm, wdown_ref), (wproj_hbm, wproj_ref),
        ),
        sems,
    )
    kept = []

    def keep(src, dst):
        copy = pltpu.make_async_copy(src, dst, out_sems.at[len(kept)])
        copy.start()
        kept.append(copy)

    for copy in scalars:
        copy.wait()
    ends = bounds_of(lens_ref, me)

    def layout(spot):
        seg_doc = segment_of(spot, ends)
        start_doc = jnp.zeros_like(spot)
        for k in range(DOCS_ROW):
            start_doc = jnp.where(seg_doc == k + 1, ends[k], start_doc)
        seg_query = spot // QLEN
        seg = jnp.where(is_query, seg_query, seg_doc)
        start = jnp.where(is_query, seg_query * QLEN, start_doc)
        return seg, start

    shape = (ROW, ROW)
    seg_q, start_q = layout(iota(shape, 0))
    seg_k, _ = layout(iota(shape, 1))
    same = seg_q == seg_k
    onehot = (iota(shape, 1) == iota(shape, 0) - start_q).astype(F32).astype(BF16)
    for copy in copies[:4]:
        copy.wait()
    turned = mm(onehot, table_ref[...])
    cosine = turned[:, :128] + turned[:, 128:256]
    sine = turned[:, 256:384] + turned[:, 384:]
    rope_ref[:, :128] = cosine
    rope_ref[:, 128:] = sine
    keep(rope_ref, rope_hbm)

    x = x_ref[...]
    joined = mm(x, wqkv_ref[...]) + bqkv_ref[...].astype(F32)
    swap = swapping()
    swap = jnp.concatenate([swap, swap], axis=0)
    for g in range(2 * D // 128):
        block = joined[:, g * 128 : (g + 1) * 128]
        high = block.astype(BF16)
        low = (block - high.astype(F32)).astype(BF16)
        other = mm(jnp.concatenate([high, low], axis=1), swap)
        qkv_ref[:, g * 128 : (g + 1) * 128] = (block * cosine + other * sine).astype(BF16)
    qkv_ref[:, 2 * D :] = joined[:, 2 * D :].astype(BF16)
    keep(qkv_ref, qkv_hbm)

    low_half = iota((ROW, 128), 1) < HD
    for g in range(HEADS // 2):
        q_g = qkv_ref[:, g * 128 : (g + 1) * 128]
        k_g = qkv_ref[:, D + g * 128 : D + (g + 1) * 128]
        v_g = qkv_ref[:, 2 * D + g * 128 : 2 * D + (g + 1) * 128]
        v_ones = jnp.concatenate([v_g, jnp.ones((ROW, 128), BF16)], axis=1)
        outs = []
        for h in range(2):
            pick = low_half if h == 0 else jnp.logical_not(low_half)
            scores = mm_nt(jnp.where(pick, q_g, jnp.zeros_like(q_g)), k_g)
            scores = jnp.where(same, scores * (LOG2E / math.sqrt(HD)), -1e30)
            top = jnp.max(scores, axis=1, keepdims=True)
            exps = jnp.exp2(scores - top)
            both = mm(exps.astype(BF16), v_ones)
            inverse = 1.0 / both[:, 128:]
            probs_ref[2 * g + h] = (exps * jnp.concatenate([inverse, inverse], axis=1)).astype(BF16)
            outs.append(both[:, :128] * inverse)
        mixed_ref[:, g * 128 : (g + 1) * 128] = jnp.where(low_half, outs[0], outs[1]).astype(BF16)

    keep(probs_ref, probs_hbm)
    keep(mixed_ref, mixed_hbm)
    for copy in copies[4:12]:
        copy.wait()
    for k, ref in enumerate((g1_ref, s1_ref, g2_ref, s2_ref)):
        affine_ref[k : k + 1, :] = ref[...].astype(F32)
    affine_ref[4:, :] = jnp.zeros((4, D), F32)
    keep(affine_ref, affine_hbm)
    attended = mm(mixed_ref[...], wout_ref[...]) + bout_ref[...].astype(F32)
    xhat, rstd = norm_rows(x.astype(F32) + attended)
    xh1_ref[...] = xhat
    rs1_ref[...] = jnp.broadcast_to(rstd, (ROW, 128))
    keep(xh1_ref, xh1_hbm)
    keep(rs1_ref, rs1_hbm)
    first = xhat * g1_ref[...].astype(F32) + s1_ref[...].astype(F32)
    first_low = first.astype(BF16)
    branch = bdown_ref[...].astype(F32) + first
    step = 512
    copies[12].wait()
    for c in range(FF // step):
        cols = slice(c * step, (c + 1) * step)
        inner = mm(first_low, wup_ref[:, cols]) + bup_ref[:, cols].astype(F32)
        gate = 0.5 + 0.5 * lax.erf(inner * math.sqrt(0.5))
        bell = jnp.exp2(inner * inner * (-0.5 * LOG2E)) * (1.0 / math.sqrt(2.0 * math.pi))
        act = (inner * gate).astype(BF16)
        act_ref[:, cols] = act
        slope_ref[:, cols] = (gate + inner * bell).astype(BF16)
        if c == 0:
            copies[13].wait()
        branch = branch + mm(act, wdown_ref[cols, :])
    xhat, rstd = norm_rows(branch)
    xh2_ref[...] = xhat
    rs2_ref[...] = jnp.broadcast_to(rstd, (ROW, 128))
    second = xhat * g2_ref[...].astype(F32) + s2_ref[...].astype(F32)
    copies[14].wait()
    vec_ref[:ROW, :] = mm(second.astype(BF16), wproj_ref[...]).astype(BF16)
    line = iota((EXT, PROJ), 0)
    tag = jnp.zeros((EXT, PROJ), jnp.int32)
    for k in range(labels_ref.shape[0]):
        label = labels_ref[k]
        tag = jnp.where(line == k, label >> 6, tag)
        tag = jnp.where(line == k + 8, label & 63, tag)
    vec_ref[ROW:, :] = tag.astype(F32).astype(BF16)
    for copy in kept:
        copy.wait()


def prefix_norms(values, axis):
    place = iota(values.shape, axis)
    squared = values * values
    sums = [
        jnp.sum(jnp.where(place < cut, squared, 0.0), axis=axis, keepdims=True) for cut in RANGES
    ]
    return [lax.rsqrt(s + EPS_NORM) for s in sums]


def load_queries(near_ref, far_ref):
    span = ROW + EXT
    rows = []
    for ref in (near_ref, far_ref):
        for k in range(ref.shape[0] // span):
            rows.append(ref[k * span : k * span + ROW, :])
    return jnp.concatenate(rows, axis=0).astype(F32)


def unit_queries(queries, scale):
    lane = iota(queries.shape, 1)
    inverse = prefix_norms(queries, 1)
    unit = [
        jnp.where(lane < cut, queries * (inv * scale), 0.0) for cut, inv in zip(RANGES, inverse)
    ]
    return unit, inverse


def unit_docs(doc_refs, scratch_ref):
    at = 0
    for ref in doc_refs:
        for k in range(ref.shape[0] // ROW):
            scratch_ref[:, at * ROW : (at + 1) * ROW] = ref[
                k * ROW : (k + 1) * ROW, :
            ].astype(F32).T
            at += 1
    turned = scratch_ref[...]
    inverse = prefix_norms(turned, 0)
    place = iota(turned.shape, 0)
    unit = [jnp.where(place < cut, turned * inv, 0.0) for cut, inv in zip(RANGES, inverse)]
    return unit, inverse


def row_ids(base, masks, doc_rows):
    ids = []
    for p in range(doc_rows):
        offset = 0
        for k, mask in enumerate(masks):
            if (p >> k) & 1:
                offset ^= mask
        ids.append(base ^ offset)
    return ids


def doc_marks(lens_ref, ids, lanes, transposed):
    docs = len(ids) * DOCS_ROW
    shape = (lanes, ROW) if transposed else (ROW, lanes)
    spot, lane = (iota(shape, 1), iota(shape, 0)) if transposed else (iota(shape, 0), iota(shape, 1))
    marks = []
    for p, row in enumerate(ids):
        seg = segment_of(spot, bounds_of(lens_ref, row))
        local = jnp.where(seg < DOCS_ROW, seg + p * DOCS_ROW, -1 - lanes)
        marks.append(
            [(lane == local + m * docs).astype(F32).astype(BF16) for m in range(len(RANGES))]
        )
    return marks


def matching_stats(
    size, masks, lanes, scale_ref, lens_ref, near_ref, far_ref, *refs
):
    doc_refs = refs[:-6]
    totals_ref, el_ref, hot_ref, stats_ref, turn_ref, unit_ref = refs[-6:]
    base, near_at = here(size)[2:4]
    span = ROW + EXT
    queries = load_queries(near_ref, far_ref)
    count = queries.shape[0]
    unit_q, _ = unit_queries(queries, SHARPNESS * LOG2E)
    unit_q = [u.astype(BF16) for u in unit_q]
    unit_d, _ = unit_docs(doc_refs, turn_ref)
    for m in range(len(RANGES)):
        unit_ref[m] = unit_d[m].astype(BF16)
    doc_rows = turn_ref.shape[1] // ROW
    docs = doc_rows * DOCS_ROW
    ids = row_ids(base, masks, doc_rows)
    marks = doc_marks(lens_ref, ids, lanes, False)
    totals = jnp.zeros((count, lanes), F32)
    for p in range(doc_rows):
        for m in range(len(RANGES)):
            sims = mm(unit_q[m], unit_ref[m, :, p * ROW : (p + 1) * ROW])
            totals = totals + mm(jnp.exp2(sims).astype(BF16), marks[p][m])
    lane_t = iota((count, lanes), 1)
    totals = jnp.where(lane_t < len(RANGES) * docs, totals, 1.0)
    totals_ref[...] = totals
    shape = (8, lanes)
    lane = iota(shape, 1)
    length = jnp.ones(shape, jnp.int32)
    name = jnp.full(shape, -1, jnp.int32)
    for p in range(doc_rows):
        for k in range(DOCS_ROW):
            own = jnp.zeros(shape, jnp.bool_)
            for m in range(len(RANGES)):
                own = jnp.logical_or(own, lane == m * docs + p * DOCS_ROW + k)
            length = jnp.where(own, lens_ref[k, ids[p]], length)
            name = jnp.where(own, ids[p] * DOCS_ROW + k, name)
    log_length = jnp.log(length.astype(F32))
    matched = (jnp.log(totals) - log_length[:1]) * (1.0 / SHARPNESS)
    per_query = jnp.sum(matched.reshape(count // QLEN, QLEN, lanes), axis=1)
    scale = jnp.exp(jnp.full(shape, scale_ref[0], F32))[:1]
    logits = per_query * (scale * (1.0 / QLEN))
    groups = count // ROW
    tags = []
    for ref in (near_ref, far_ref):
        for k in range(ref.shape[0] // span):
            high = ref[k * span + ROW : k * span + ROW + 8, :].astype(F32).astype(jnp.int32)
            low = ref[k * span + ROW + 8 : k * span + ROW + 16, :].astype(F32).astype(jnp.int32)
            tag = high * 64 + low
            tags.append(jnp.concatenate([tag] * (lanes // 128), axis=1))
    tag = jnp.concatenate(tags, axis=0)
    lane_q = iota(logits.shape, 1)
    valid = lane_q < len(RANGES) * docs
    el = jnp.where(valid, jnp.exp(logits), 0.0)
    hot = jnp.where(jnp.logical_and(valid, jnp.concatenate([name] * groups, axis=0) == tag), 1.0, 0.0)
    el_ref[...] = el
    hot_ref[...] = hot
    place = iota((groups * 8, 128), 1)
    stats = jnp.zeros((groups * 8, 128), F32)
    for k, values in enumerate((el, el * logits, hot * logits)):
        for m in range(len(RANGES)):
            inside = jnp.logical_and(lane_q >= m * docs, lane_q < (m + 1) * docs)
            one = jnp.sum(jnp.where(inside, values, 0.0), axis=1, keepdims=True)
            stats = jnp.where(place == k * 3 + m, one, stats)
    for a in range(groups):
        at = pl.multiple_of((near_at ^ a) * 8, 8)
        stats_ref[pl.ds(at, 8), :] = stats[a * 8 : (a + 1) * 8, :]


def matching_back(
    size, masks, lanes, scale_ref, lens_ref, totals_ref, el_ref, hot_ref, own_ref, over_y, over_x, over_both, unitq_ref, qt_ref, invq_ref, unit_ref, invd_ref, *refs
):
    dq_ref, far_ref, keep_ref, send_ref, loss_ref, dot_ref, dt_ref, stats_ref = refs[-8:]
    _, stream, base, near_at = here(size)[:4]
    total_queries = size * (ROW // QLEN)
    temper = SHARPNESS * LOG2E
    count = unitq_ref.shape[1]
    inv_q = [invq_ref[:, m : m + 1] for m in range(len(RANGES))]
    inv_d = [invd_ref[m : m + 1, :] for m in range(len(RANGES))]
    unit_q = [unitq_ref[m] for m in range(len(RANGES))]
    doc_rows = unit_ref.shape[2] // ROW
    docs = doc_rows * DOCS_ROW
    ids = row_ids(base, masks, doc_rows)
    groups = count // ROW
    odd_y, odd_x = (near_at & 1) == 1, stream == 1
    parts = [own_ref[...], over_y[...], over_x[...], over_both[...]]
    parts = [jnp.where(odd_y, a, b) for a, b in ((parts[1], parts[0]), (parts[0], parts[1]),
                                                  (parts[3], parts[2]), (parts[2], parts[3]))]
    parts = [jnp.where(odd_x, parts[(k + 2) % 4], parts[k]) for k in range(4)]
    stats_ref[...] = (parts[0] + parts[1]) + (parts[2] + parts[3])
    rows = []
    for a in range(groups):
        at = pl.multiple_of((near_at ^ a) * 8, 8)
        rows.append(stats_ref[pl.ds(at, 8), :])
    stats = jnp.concatenate(rows, axis=0)
    place = iota(stats.shape, 1)

    def column(k):
        return jnp.sum(jnp.where(place == k, stats, 0.0), axis=1, keepdims=True)

    shape = (groups * 8, lanes)
    lane_q = iota(shape, 1)
    sums = jnp.ones(shape, F32)
    loss = jnp.zeros((groups * 8, 1), F32)
    moved = jnp.zeros((groups * 8, 1), F32)
    for m in range(len(RANGES)):
        whole, weighted, picked = column(m), column(3 + m), column(6 + m)
        inside = jnp.logical_and(lane_q >= m * docs, lane_q < (m + 1) * docs)
        sums = jnp.where(inside, whole, sums)
        loss = loss + (jnp.log(whole) - picked)
        moved = moved + (weighted / whole - picked)
    line = iota((8, 128), 0)
    loss = jnp.where(
        line == 0,
        jnp.sum(loss, axis=0, keepdims=True) * (1.0 / total_queries),
        jnp.where(line == 1, jnp.sum(moved, axis=0, keepdims=True) * (1.0 / total_queries), 0.0),
    )
    loss_ref[...] = loss
    marks = doc_marks(lens_ref, ids, lanes, True)
    scale = jnp.exp(jnp.full((8, lanes), scale_ref[0], F32))[:1]
    coeff = (el_ref[...] / sums - hot_ref[...]) * (scale * (1.0 / (QLEN * total_queries)))
    coeff = jnp.broadcast_to(coeff[:, None, :], (groups * 8, QLEN, lanes)).reshape(count, lanes)
    ratio = coeff / totals_ref[...]
    ratio_high = ratio.astype(BF16)
    ratio_low = (ratio - ratio_high.astype(F32)).astype(BF16)
    ratio = jnp.concatenate([ratio_high, ratio_low], axis=1)
    for m in range(len(RANGES)):
        grad = jnp.zeros((count, PROJ), F32)
        for p in range(doc_rows):
            block = unit_ref[m, :, p * ROW : (p + 1) * ROW]
            mark = marks[p][m]
            if len(refs) > 8:
                exps = refs[0][m, :, p * ROW : (p + 1) * ROW].astype(F32)
            else:
                exps = jnp.exp2(mm(unit_q[m], block))
            d_sims = (exps * mm(ratio, jnp.concatenate([mark, mark], axis=0))).astype(BF16)
            grad = grad + mm_nt(d_sims, block)
            dt_ref[m, :, p * ROW : (p + 1) * ROW] = mm(qt_ref[m], d_sims)
        unit = unit_q[m].astype(F32) * (1.0 / temper)
        along = jnp.sum(grad * unit, axis=1, keepdims=True)
        part = inv_q[m] * (grad - unit * along)
        if m == 0:
            dot_ref[...] = part
        else:
            dot_ref[...] += part
    dq_ref[...] = dot_ref[: count // 2, :].astype(BF16)
    far_ref[...] = dot_ref[count // 2 :, :].astype(BF16)
    total = jnp.zeros(unit_ref.shape[1:], F32)
    for m in range(len(RANGES)):
        grad = dt_ref[m] * (1.0 / temper)
        unit = unit_ref[m].astype(F32)
        along = jnp.sum(grad * unit, axis=0, keepdims=True)
        total = total + inv_d[m] * (grad - unit * along)
    for p in range(doc_rows):
        ref, at = (keep_ref, p) if p < doc_rows // 2 else (send_ref, p - doc_rows // 2)
        ref[at * ROW : (at + 1) * ROW, :] = total[:, p * ROW : (p + 1) * ROW].T.astype(BF16)


def matching_ready(near_ref, far_ref, *refs):
    doc_refs = refs[:-6] if refs[-2].shape[0] != len(RANGES) else refs[:-7]
    unitq_ref, qt_ref, invq_ref, unit_ref, invd_ref = refs[len(doc_refs) : len(doc_refs) + 5]
    turn_ref = refs[-1]
    queries = load_queries(near_ref, far_ref)
    unit_q, inv_q = unit_queries(queries, SHARPNESS * LOG2E)
    unit_d, inv_d = unit_docs(doc_refs, turn_ref)
    lane = iota(invq_ref.shape, 1)
    columns = jnp.zeros(invq_ref.shape, F32)
    invd_ref[...] = jnp.zeros_like(invd_ref)
    for m in range(len(RANGES)):
        unitq_ref[m] = unit_q[m].astype(BF16)
        unit_ref[m] = unit_d[m].astype(BF16)
        qt_ref[m] = unit_q[m].T.astype(BF16)
        columns = jnp.where(lane == m, inv_q[m], columns)
        invd_ref[m : m + 1, :] = inv_d[m]
        if len(refs) - len(doc_refs) > 6:
            refs[-2][m] = jnp.exp2(mm(unitq_ref[m], unit_ref[m])).astype(BF16)
    invq_ref[...] = columns


def pick_rows(size, here_ref, there_ref, rows_ref):
    _, stream, _, _, has_top = here(size)[:5]
    rows_ref[...] = jnp.where(has_top == stream, here_ref[...], there_ref[...])


def add_rows(rows_ref, got_ref, sum_ref):
    sum_ref[...] = (rows_ref[...].astype(F32) + got_ref[...].astype(F32)).astype(BF16)


DIGITS = 10
POINT = 20


def digits_of(value):
    fixed = (value * float(1 << POINT)).astype(jnp.int32)
    size = jnp.abs(fixed)
    lane = iota(value.shape, 1)
    digits = jnp.zeros(value.shape, jnp.int32)
    for k in range(DIGITS):
        digits = jnp.where(lane == k, (size >> (3 * k)) & 7, digits)
    return jnp.where(fixed < 0, -digits, digits).astype(F32)


def value_of(digits):
    lane = iota(digits.shape, 1)
    half = DIGITS // 2
    weight = jnp.zeros(digits.shape, F32)
    for k in range(half):
        weight = jnp.where(jnp.logical_or(lane == k, lane == k + half), float(8**k), weight)
    low = jnp.sum(jnp.where(lane < half, digits * weight, 0.0))
    high = jnp.sum(jnp.where(jnp.logical_and(lane >= half, lane < DIGITS), digits * weight, 0.0))
    return (high * float(8**half) + low) * (1.0 / (1 << POINT))


def turn(core, place, block):
    return jnp.where(core == 0, place - block, block - place) & (RING - 1)


def block_at(core, place, distance):
    return jnp.where(core == 0, place - distance, place + distance) & (RING - 1)


def store_block(keep_ref, send_ref, rows, block, places, value):
    core, place = places
    mine = core == block // RING
    at = turn(block // RING, place, block % RING)

    @pl.when(mine)
    def _():
        keep_ref[at, rows, :] = value

    @pl.when(jnp.logical_not(mine))
    def _():
        send_ref[at, rows, :] = value


def feed_back(
    size, dq_ref, dd_ref, got_ref, xh2_ref, rs2_ref, affine_ref, wproj_ref, slope_ref, act_ref,
    xh1_ref, wdown_ref, wup_hbm,
    keep_ref, send_ref, tail_keep, tail_send, dfirst_ref, gproj_ref, small_ref,
    dinner_ref, wup_ref, sems,
):
    step = 512
    spans = [slice(c * step, (c + 1) * step) for c in range(FF // step)]
    copies = fetch([(wup_hbm, wup_ref)], sems)
    g1, s1, g2, s2 = [affine_ref[k : k + 1, :] for k in range(4)]
    _, stream, _, _, has_top, *places = here(size)
    is_query, docs_there = stream == 0, has_top == 0
    got = got_ref[...].astype(F32)
    d_vec = jnp.where(
        is_query,
        dq_ref[...].astype(F32) + got,
        jnp.where(docs_there, got, dd_ref[...].astype(F32)),
    )
    d_proj = d_vec.astype(BF16)
    xhat = xh2_ref[...]
    gain = g2
    second = (xhat * gain + s2).astype(BF16)
    gproj_ref[...] = mm_tn(second, d_proj)
    d_second = mm_nt(d_proj, wproj_ref[...])
    small_ref[...] = jnp.zeros_like(small_ref)
    small_ref[5:6, :] = col_sum(d_second * xhat)
    small_ref[6:7, :] = col_sum(d_second)
    d_sum = norm_back(d_second, xhat, rs2_ref[:, :1], gain)
    d_branch = d_sum.astype(BF16)
    small_ref[4:5, :] = col_sum(d_branch.astype(F32))
    d_first = d_sum
    for c in range(FF // step):
        cols = spans[c]
        d_act = mm_nt(d_branch, wdown_ref[cols, :])
        d_inner = (d_act * slope_ref[:, cols].astype(F32)).astype(BF16)
        dinner_ref[:, cols] = d_inner
        small_ref[c : c + 1, :] = col_sum(d_inner.astype(F32))
        grad = mm_tn(act_ref[:, cols], d_branch).astype(BF16)
        for k in range(step // DOWN):
            store_block(
                keep_ref, send_ref, slice(0, DOWN), c * (step // DOWN) + k, places,
                grad[k * DOWN : (k + 1) * DOWN, :],
            )
    copies[0].wait()
    first = (xh1_ref[...] * g1 + s1).astype(BF16)
    for c in range(FF // step):
        cols = slice(c * step, (c + 1) * step)
        d_first = d_first + mm_nt(dinner_ref[:, cols], wup_ref[:, cols])
        grad = mm_tn(first, dinner_ref[:, cols]).astype(BF16)
        for k in range(D // DOWN):
            block = c * (D // DOWN) + k
            start = k * DOWN
            store_block(
                keep_ref, send_ref, slice(DOWN, FIRST), block, places, grad[start : start + HEAD, :]
            )
            store_block(
                tail_keep, tail_send, slice(0, TAIL), block, places,
                grad[start + HEAD : start + DOWN, :],
            )
    dfirst_ref[...] = d_first


def attend_back(
    size, dfirst_ref, gproj_ref, small_ref, loss_ref, tail_keep, tail_send, xh1_ref, rs1_ref, affine_ref, mixed_ref, wout_ref,
    qkv_ref, probs_ref, rope_ref, x_ref,
    keep_ref, ahead_ref, send_ref, dsum_ref, djoined_ref, rest_ref,
):
    me, *_, core, place = here(size)
    d_first = dfirst_ref[...]
    xhat = xh1_ref[...]
    gain = affine_ref[0:1, :]
    gain_grad = col_sum(d_first * xhat)
    shift_grad = col_sum(d_first)
    d_sum = norm_back(d_first, xhat, rs1_ref[:, :1], gain)
    d_att = d_sum.astype(BF16)
    bias_out = col_sum(d_att.astype(F32))
    rest_ref[3 * D : 4 * D, :] = mm_tn(mixed_ref[...], d_att)
    d_mixed = mm_nt(d_att, wout_ref[...]).astype(BF16)
    cosine, sine = rope_ref[:, :128], rope_ref[:, 128:]
    low_half = iota((ROW, 128), 1) < HD

    scale = 1.0 / math.sqrt(HD)
    cosine, sine = cosine * scale, sine * scale
    swap = swapping()

    def unrotate(both):
        return (both[:, :128] * cosine - both[:, 128:] * sine).astype(BF16)

    for g in range(HEADS // 2):
        span = slice(g * 128, (g + 1) * 128)
        q_g = qkv_ref[:, g * 128 : (g + 1) * 128]
        k_g = qkv_ref[:, D + g * 128 : D + (g + 1) * 128]
        v_g = qkv_ref[:, 2 * D + g * 128 : 2 * D + (g + 1) * 128]
        m_g = d_mixed[:, span]
        q_both = jnp.concatenate([q_g, mm(q_g, swap).astype(BF16)], axis=1)
        k_both = jnp.concatenate([k_g, mm(k_g, swap).astype(BF16)], axis=1)
        d_q = jnp.zeros((ROW, 256), F32)
        d_k = jnp.zeros((ROW, 256), F32)
        d_v = jnp.zeros((ROW, 128), F32)
        zero = jnp.zeros((ROW, 128), BF16)
        zero_both = jnp.zeros((ROW, 256), BF16)
        for h in range(2):
            pick = low_half if h == 0 else jnp.logical_not(low_half)
            probs_low = probs_ref[2 * g + h]
            probs = probs_low.astype(F32)
            m_h = jnp.where(pick, m_g, zero)
            d_probs = mm_nt(m_h, v_g)
            d_v = d_v + mm_tn(probs_low, m_h)
            inner = jnp.sum(d_probs * probs, axis=1, keepdims=True)
            d_scores = (probs * (d_probs - inner)).astype(BF16)
            pick_both = jnp.concatenate([pick, pick], axis=1)
            d_q = d_q + mm(d_scores, jnp.where(pick_both, k_both, zero_both))
            d_k = d_k + mm_tn(d_scores, jnp.where(pick_both, q_both, zero_both))
        djoined_ref[:, g * 128 : (g + 1) * 128] = unrotate(d_q)
        djoined_ref[:, D + g * 128 : D + (g + 1) * 128] = unrotate(d_k)
        djoined_ref[:, 2 * D + g * 128 : 2 * D + (g + 1) * 128] = d_v.astype(BF16)
    x = x_ref[...]
    dsum_ref[...] = d_sum
    rest_ref[4 * D :, :] = jnp.zeros((8 * 2 * RING, D), F32)
    smalls = []
    for c in range(3):
        cols = slice(c * D, (c + 1) * D)
        d_part = djoined_ref[:, cols]
        rest_ref[c * D : (c + 1) * D, :] = mm_tn(x, d_part)
        smalls.append(col_sum(d_part.astype(F32)))
    smalls += [bias_out, gain_grad, shift_grad] + [small_ref[k : k + 1, :] for k in range(7)]
    counted = jnp.where((me & 3) == 0, 1.0, 0.0)
    lines = [digits_of(loss_ref[k : k + 1, :]) * counted for k in range(2)]
    smalls.append(jnp.concatenate(lines + [jnp.zeros((1, D - 256), F32)], axis=1))
    for k, row in enumerate(smalls):
        rest_ref[4 * D + 8 * k : 4 * D + 8 * k + 1, :] = row
    for k in range(RING):
        sent, at = (ahead_ref, AHEAD.index(k)) if k in AHEAD else (send_ref, LATER.index(k))
        for ref, index, tail_ref, owner in (
            (keep_ref, k, tail_keep, core), (sent, at, tail_send, 1 - core)
        ):
            block = owner * RING + block_at(owner, place, k)
            parts = []
            for c in range(4):
                start = pl.multiple_of(c * D + block * SHARE, SHARE)
                parts.append(rest_ref[pl.ds(start, SHARE), :])
            row = pl.multiple_of(block * SHARE, SHARE)
            parts.append(
                jnp.concatenate(
                    [gproj_ref[pl.ds(row + 8 * j, 8), :] for j in range(SHARE // 8)], axis=1
                )
            )
            parts.append(rest_ref[pl.ds(pl.multiple_of(4 * D + block * 8, 8), 8), :])
            ref[index, : REST // 16, :] = jnp.concatenate(parts, axis=0).astype(BF16)
            ref[index, REST // 16 :, :] = tail_ref[k]


def tokens_back(dsum_ref, djoined_ref, wqkv_ref, tokens_ref):
    tokens = dsum_ref[...]
    for c in range(3):
        cols = slice(c * D, (c + 1) * D)
        tokens = tokens + mm_nt(djoined_ref[:, cols], wqkv_ref[:, cols])
    tokens_ref[...] = tokens


def spread(size, jobs, last, *refs):
    core, place = here(size)[-2:]
    halves = refs[: len(jobs)]
    wide_one, wide_two, wide_qkv, wide_proj, small_ref, sems = refs[-6:]
    outs = refs[-21:-6] if last else refs[-11:-6]
    down_hbm, up_hbm, qkv_hbm, out_hbm, proj_hbm = outs[:5]
    copies = []

    def move(src, dst):
        copy = pltpu.make_async_copy(src, dst, sems.at[len(copies)])
        copy.start()
        copies.append(copy)

    at = 0
    for job, (mine, group) in enumerate(jobs):
        owner = core if mine else 1 - core
        both_ref = halves[job]
        for p, distance in enumerate(GROUPS[group]):
            block = owner * RING + block_at(owner, place, distance)
            wide_one[at] = both_ref[p, :FIRST, :].astype(F32)
            rows = pl.ds(pl.multiple_of(block * DOWN, DOWN), DOWN)
            move(wide_one.at[at, :DOWN, :], down_hbm.at[rows, :])
            start = (block % (D // DOWN)) * DOWN
            columns = pl.ds(pl.multiple_of((block // (D // DOWN)) * D, D), D)
            rows = pl.ds(pl.multiple_of(start, DOWN), HEAD)
            move(wide_one.at[at, DOWN:, :], up_hbm.at[rows, columns])
            wide = both_ref[p, FIRST:, :].astype(F32)
            wide_two[at, :SHARE, :] = wide[3 * SHARE : 4 * SHARE, :]
            wide_two[at, SHARE:, :] = wide[REST // 16 :, :]
            rows = pl.ds(pl.multiple_of(start + HEAD, 16), TAIL)
            move(wide_two.at[at, SHARE:, :], up_hbm.at[rows, columns])
            rows = pl.ds(pl.multiple_of(block * SHARE, SHARE), SHARE)
            for c in range(3):
                wide_qkv[at, :, c * D : (c + 1) * D] = wide[c * SHARE : (c + 1) * SHARE, :]
            move(wide_qkv.at[at], qkv_hbm.at[rows, :])
            move(wide_two.at[at, :SHARE, :], out_hbm.at[rows, :])
            for j in range(SHARE // 8):
                wide_proj[at, 8 * j : 8 * j + 8, :] = wide[
                    4 * SHARE : 4 * SHARE + 8, j * PROJ : (j + 1) * PROJ
                ]
            move(wide_proj.at[at], proj_hbm.at[rows, :])
            at += 1
    if last:
        sources = refs[len(jobs) : len(jobs) + 2 * len(GROUPS)]
        for k, ref in enumerate(sources):
            owner = core if k < len(GROUPS) else 1 - core
            for p, distance in enumerate(GROUPS[k % len(GROUPS)]):
                block = owner * RING + block_at(owner, place, distance)
                start = FIRST + 4 * SHARE
                line = ref[p, start : start + 16, :].astype(F32)[8:, :]
                small_ref[pl.ds(pl.multiple_of(block * 8, 8), 8), :] = line
        rows = [small_ref[8 * k : 8 * k + 1, :] for k in range(14)]
        bqkv_ref, bout_ref, g1_ref, s1_ref, bup_ref, bdown_ref, g2_ref, s2_ref = outs[5:13]
        for k, ref in enumerate(outs[13:]):
            ref[0] = value_of(rows[13][:, k * 128 : (k + 1) * 128])
        for c in range(3):
            bqkv_ref[:, c * D : (c + 1) * D] = rows[c]
        bout_ref[...] = rows[3]
        g1_ref[...] = rows[4]
        s1_ref[...] = rows[5]
        for c in range(4):
            bup_ref[:, c * D : (c + 1) * D] = rows[6 + c]
        bdown_ref[...] = rows[10]
        g2_ref[...] = rows[11]
        s2_ref[...] = rows[12]
    for copy in copies:
        copy.wait()


def spread_call(size, jobs, halves, outs, others):
    last = len(others) > 0
    shapes = ((FF, D), (D, FF), (D, 3 * D), (D, D), (D, PROJ))
    widths = (3 * D, D, D, D, FF, D, D, D) if last else ()
    args = [*halves, *others, *outs]
    count = sum(len(GROUPS[group]) for _, group in jobs)
    before = len(halves) + len(others)
    return call(
        partial(spread, size, jobs, last),
        args,
        [VMEM] * before + [HBM] * len(outs),
        [pltpu.HBM(shape, F32) for shape in shapes]
        + [shape_of((1, width)) for width in widths]
        + [shape_of((1,))] * (2 * last),
        [
            pltpu.VMEM((count, FIRST, D), F32),
            pltpu.VMEM((count, SHARE + TAIL, D), F32),
            pltpu.VMEM((count, SHARE, 3 * D), F32),
            pltpu.VMEM((count, SHARE, PROJ), F32),
            pltpu.VMEM((16 * RING, D), F32),
            pltpu.SemaphoreType.DMA((6 * count,)),
        ],
        out_specs=[HBM] * 5 + [VMEM] * len(widths) + [SMEM] * (2 * last),
        aliases={before + k: k for k in range(len(outs))},
        cost=SPREAD_COST,
        room=14,
    )


def shape_of(shape, dtype=F32):
    return jax.ShapeDtypeStruct(tuple(shape), dtype)


def call(kernel, args, specs, outs, scratch=(), room=24, out_specs=None, aliases={}, cost=10**7):
    spaces = {id(HBM): pltpu.HBM, id(HELD): pltpu.VMEM}
    args = [
        pltpu.with_memory_space_constraint(arg, spaces[id(spec)]) if id(spec) in spaces else arg
        for arg, spec in zip(args, specs)
    ]
    return pl.pallas_call(
        kernel,
        out_shape=outs,
        in_specs=specs,
        out_specs=out_specs or [VMEM] * len(outs),
        scratch_shapes=list(scratch),
        input_output_aliases=aliases,
        compiler_params=pltpu.CompilerParams(vmem_limit_bytes=room * MIB),
        cost_estimate=pl.CostEstimate(
            flops=10 * cost, bytes_accessed=cost, transcendentals=0
        ),
    )(*args)


def swapped(value, mask, axis="dp"):
    size = lax.axis_size(axis)
    return lax.ppermute(value, axis, [(k, k ^ mask) for k in range(size)])


def added(a, b):
    return (a.astype(F32) + b.astype(F32)).astype(BF16)


def join_blocks(*refs):
    half = (len(refs) - 1) // 2
    for k in range(half):
        refs[-1][k, :FIRST, :] = refs[k][0]
        refs[-1][k, FIRST:, :] = refs[half + k][0]


def ring_swap(value, onward):
    size = lax.axis_size("dp")
    pairs = []
    for k in range(size):
        at = CIRCLE.index((k >> 1) % RING)
        to = CIRCLE[(at + (1 if (k % 2 == 0) == onward else -1)) % RING]
        pairs.append((k, (k & ~(2 * RING - 1)) | (to << 1) | (k & 1)))
    return lax.ppermute(value, "dp", pairs)


def add_blocks(places, *refs):
    count = len(places)
    held_ref = refs[count] if any(place is not None for place in places) else None
    for k, place in enumerate(places):
        value = refs[k][...]
        if place is not None:
            value = (value.astype(F32) + held_ref[place : place + 1].astype(F32)).astype(BF16)
        refs[-count + k][...] = value


def first_blocks(places, keep_ref, pair_ref, *outs):
    for ref, (k, j) in zip(outs, places):
        ref[0] = (keep_ref[k].astype(F32) + pair_ref[j].astype(F32)).astype(BF16)


def later_blocks(places, keep_ref, pair_ref, out_ref):
    for k in AHEAD:
        out_ref[k] = jnp.zeros(out_ref.shape[1:], BF16)
    for k, j in places:
        out_ref[k] = (keep_ref[k].astype(F32) + pair_ref[j].astype(F32)).astype(BF16)


class Summed:
    def __init__(self, keep, sends, others):
        self.keep, self.others, self.hop = keep, others, 0
        self.pairs = [swapped(send, 1) for send in sends]
        self.sent, self.blocks = [], {}

    def blocks_call(self, blocks, places, held):
        return call(
            partial(add_blocks, places),
            (*blocks, *held),
            [VMEM] * (len(blocks) + len(held)),
            [shape_of(block.shape, BF16) for block in blocks],
            room=8,
            cost=STEP_COST,
        )

    def open(self, after):
        keep, pair, _ = lax.optimization_barrier((self.keep, self.pairs[0], after))
        shape = (1, *keep.shape[1:])
        places = [(k, AHEAD.index(k) if len(self.pairs) > 1 else k) for k in AHEAD]
        first, second = call(
            partial(first_blocks, places),
            (keep, pair),
            [VMEM] * 2,
            [shape_of(shape, BF16)] * 2,
            room=8,
            cost=STEP_COST,
        )
        self.sent = [(first, True), (second, False)]
        return second

    def total(self, after):
        keep, _ = lax.optimization_barrier((self.keep, after))
        later = [(k, LATER.index(k) if len(self.pairs) > 1 else k) for k in LATER]
        (self.keep,) = call(
            partial(later_blocks, later),
            (keep, self.pairs[-1]),
            [VMEM] * 2,
            [shape_of(keep.shape, BF16)],
            room=8,
            cost=STEP_COST,
        )
        return self.keep

    def step(self, after):
        half = RING // 2
        self.hop += 1
        hop = self.hop
        *got, _ = lax.optimization_barrier((*[ring_swap(*one) for one in self.sent], after))
        if hop < half:
            out = self.blocks_call(got, (half + hop, half - 1 - hop), [self.keep])
            self.part = out[1]
        elif hop == half:
            (own,) = self.blocks_call(got, (0,), [self.part])
            for mask in self.others:
                own = added(own, swapped(own, mask))
            self.blocks[0] = own
            out = [own, own]
        else:
            out = self.blocks_call(got, (None,) * len(got), [])
            hop -= half
            self.blocks[hop] = out[0]
            if hop < half:
                self.blocks[RING - hop] = out[1]
        if hop == half - 1:
            self.sent = [(out[0], True)]
        elif self.hop < 2 * half:
            self.sent = [(out[0], True), (out[1], False)]
        return out[0]


def share(pieces, group, after):
    blocks = [piece.blocks[k] for piece in pieces for k in GROUPS[group]]
    *blocks, _ = lax.optimization_barrier((*blocks, after))
    shape = (len(GROUPS[group]), FIRST + SECOND, D)
    (near,) = call(
        join_blocks, blocks, [VMEM] * len(blocks), [shape_of(shape, BF16)], room=8, cost=0
    )
    return near, swapped(near, 1)


def per_device(
    tokens, qkv_weight, qkv_bias, out_weight, out_bias, first_gain, first_shift, up_weight,
    up_bias, down_weight, down_bias, second_gain, second_shift, proj_weight, log_scale,
    doc_lengths, labels,
):
    size = lax.axis_size("dp")
    bits = [1 << k for k in range(size.bit_length() - 1)]
    near_masks, doc_masks = bits[:2], bits[2:]
    top_mask, doc_masks = doc_masks[-1], doc_masks[:-1]
    others = bits[4:]
    me = lax.axis_index("dp")
    stream = lax.axis_index("stream")
    is_query = stream == 0
    has_top = (me & top_mask) != 0
    lens = doc_lengths.T
    scale = log_scale.reshape(1)

    vec, *moved, qkv, rope, probs, mixed, xh1, rs1, affine = call(
        partial(encoder_forward, size),
        (
            lens, labels, jnp.asarray(rope_table()), tokens[0], qkv_weight[0], qkv_bias,
            out_weight[0], out_bias, first_gain, first_shift, up_weight[0], up_bias,
            down_weight[0], down_bias, second_gain, second_shift, proj_weight[0],
        ),
        [HBM] * 17,
        [shape_of((ROW + EXT, PROJ), BF16)]
        + [shape_of(*kind) for kind in MOVED]
        + [pltpu.HBM(*kind) for kind in KEPT],
        [pltpu.VMEM(*kind) for kind in KEPT]
        + [pltpu.SemaphoreType.DMA((len(KEPT),))]
        + [
            pltpu.VMEM(shape, BF16)
            for shape in (
                (ROW, 512), (ROW, D), (D, 3 * D), (1, 3 * D), (D, D), (1, D), (1, D), (1, D), (D, FF),
                (1, FF), (FF, D), (1, D), (1, D), (1, D), (D, PROJ),
            )
        ]
        + [
            pltpu.SMEM(lens.shape, jnp.int32),
            pltpu.SMEM(labels.shape, jnp.int32),
            pltpu.SemaphoreType.DMA((17,)),
        ],
        room=40,
        out_specs=[VMEM] * (1 + len(MOVED)) + [HBM] * len(KEPT),
    )
    act, slope, xh2, rs2 = call(
        move_kept,
        moved,
        [VMEM] * len(MOVED),
        [pltpu.HBM(*kind) for kind in MOVED],
        [pltpu.SemaphoreType.DMA((len(MOVED),))],
        room=8,
        out_specs=[HBM] * len(MOVED),
        cost=STEP_COST,
    )

    every, other_y = range(size), near_masks[1]
    other, _ = lax.optimization_barrier((swapped(vec, 1, "stream"), rs2))
    near = jnp.where(is_query, vec, other)
    rows = jnp.where(is_query, other, vec)[:ROW]
    moved = swapped(rows, top_mask)
    (rows,) = call(
        partial(pick_rows, size),
        (rows, moved),
        [VMEM] * 2,
        [shape_of((ROW, PROJ), BF16)],
        room=8,
        cost=STEP_COST,
    )
    got_y, _ = lax.optimization_barrier((swapped(near, other_y), rows))
    near = jnp.concatenate([near, got_y], axis=0)
    far = swapped(near, near_masks[0])
    pieces = []
    for k, mask in enumerate(doc_masks):
        pieces.append(rows)
        got = swapped(rows, mask)
        if k + 1 < len(doc_masks):
            rows = jnp.concatenate([rows, got], axis=0)
        else:
            pieces = [rows, got]
    doc_rows = sum(p.shape[0] for p in pieces) // ROW
    tokens_d = doc_rows * ROW
    tokens_q = 4 * ROW
    lanes = -(-3 * doc_rows * DOCS_ROW // 128) * 128
    room = 20 if doc_rows <= 4 else 56
    totals, el, hot, stats = call(
        partial(matching_stats, size, doc_masks, lanes),
        (scale, lens, near, far, *pieces),
        [SMEM] * 2 + [VMEM] * (2 + len(pieces)),
        [
            shape_of((tokens_q, lanes)),
            shape_of((tokens_q // QLEN, lanes)),
            shape_of((tokens_q // QLEN, lanes)),
            shape_of((tokens_q // QLEN, 128)),
        ],
        [pltpu.VMEM((PROJ, tokens_d), F32), pltpu.VMEM((3, PROJ, tokens_d), BF16)],
        room=room,
    )
    small_enough = doc_rows <= 4
    ready = call(
        matching_ready,
        (near, far, *pieces),
        [VMEM] * (2 + len(pieces)),
        [
            shape_of((3, tokens_q, PROJ), BF16),
            shape_of((3, PROJ, tokens_q), BF16),
            shape_of((tokens_q, 128)),
            shape_of((3, PROJ, tokens_d), BF16),
            shape_of((8, tokens_d)),
        ]
        + [shape_of((3, tokens_q, tokens_d), BF16)] * small_enough,
        [pltpu.VMEM((PROJ, tokens_d), F32)],
        room=room,
    )
    stats = stats + swapped(stats, near_masks[0])
    over_y = swapped(stats, other_y)
    over_x = swapped(stats, 1, "stream")
    pairs = [(k * size + r, (1 - k) * size + (r ^ other_y)) for k in range(2) for r in every]
    over_both = lax.ppermute(stats, ("stream", "dp"), pairs)
    dq, dq_send, keep, send, loss = call(
        partial(matching_back, size, doc_masks, lanes),
        (scale, lens, totals, el, hot, stats, over_y, over_x, over_both, *ready),
        [SMEM] * 2 + [VMEM] * (7 + len(ready)),
        [shape_of((tokens_q // 2, PROJ), BF16)] * 2
        + [shape_of((tokens_d // 2, PROJ), BF16)] * 2
        + [shape_of((8, 128))],
        [
            pltpu.VMEM((tokens_q, PROJ), F32),
            pltpu.VMEM((3, PROJ, tokens_d), F32),
            pltpu.VMEM((tokens_q // QLEN, 128), F32),
        ],
        room=room,
    )
    got_dq = swapped(dq_send, near_masks[0])
    for mask in reversed(doc_masks[1:]):
        total, half = added(keep, swapped(send, mask)), keep.shape[0] // 2
        keep, send = total[:half], total[half:]
    got_dd = swapped(send, doc_masks[0])
    def summed(rows, got, after=None):
        if after is not None:
            got, _ = lax.optimization_barrier((got, after))
        return call(
            add_rows, (rows, got), [VMEM] * 2, [shape_of(rows.shape, BF16)], room=8, cost=STEP_COST
        )[0]

    dq = summed(dq, got_dq)
    dd = summed(keep, got_dd, dq)
    dd = summed(dd, swapped(dd, top_mask))
    dq = summed(dq[:ROW], swapped(dq[ROW:], other_y), dd)
    got = swapped(jnp.where(is_query, dd, dq), 1, "stream")

    one_keep, one_send, tail_keep, tail_send, d_first, gproj, small = call(
        partial(feed_back, size),
        (
            dq, dd, got, xh2, rs2, affine, proj_weight[0], slope, act, xh1, down_weight[0],
            up_weight[0],
        ),
        [VMEM] * 3 + [HELD] * 8 + [HBM],
        [shape_of((RING, FIRST, D), BF16)] * 2
        + [shape_of((RING, TAIL, D), BF16)] * 2
        + [shape_of((ROW, D)), shape_of((D, PROJ)), shape_of((8, D))],
        [
            pltpu.VMEM((ROW, FF), BF16),
            pltpu.VMEM((D, FF), BF16),
            pltpu.SemaphoreType.DMA((1,)),
        ],
        room=24,
    )
    two_keep, two_ahead, two_send, d_sum, d_joined = call(
        partial(attend_back, size),
        (
            d_first, gproj, small, loss, tail_keep, tail_send, xh1, rs1, affine, mixed, out_weight[0], qkv, probs, rope,
            tokens[0],
        ),
        [VMEM] * 6 + [HELD] * 9,
        [shape_of((count, SECOND, D), BF16) for count in (RING, len(AHEAD), len(LATER))]
        + [shape_of((ROW, D)), shape_of((ROW, 3 * D), BF16)],
        [pltpu.VMEM((4 * D + 16 * RING, D), F32)],
        room=24,
    )
    one, two = [
        Summed(keep, sends, others)
        for keep, *sends in ((one_keep, one_send), (two_keep, two_ahead, two_send))
    ]
    token, outs, shared = d_sum, (), []
    for event in ORDER:
        kind, k, *group = event
        if kind == "tokens":
            d_sum, _ = lax.optimization_barrier((d_sum, token))
            (tokens_grad,) = call(
                tokens_back,
                (d_sum, d_joined, qkv_weight[0]),
                [VMEM] * 3,
                [shape_of((ROW, D))],
                room=8,
                cost=STEP_COST,
            )
            token = tokens_grad
            continue
        if kind == "spread":
            jobs = event[1]
            halves = [shared[group][0 if mine else 1] for mine, group in jobs]
            *halves, _ = lax.optimization_barrier((*halves, token))
            others = [pair[j] for j in range(2) for pair in shared] if event == ORDER[-1] else []
            outs = spread_call(size, jobs, halves, outs[:5], others)
            token = outs[0]
            continue
        if kind == "share":
            shared.append(share((one, two), k, token))
            token = shared[-1][0]
            continue
        piece = (one, two)[k]
        token = getattr(piece, kind)(*group, token)
    grad_down, grad_up, grad_qkv, grad_out, grad_proj = outs[:5]
    (
        grad_bqkv, grad_bout, grad_g1, grad_s1, grad_bup, grad_bdown, grad_g2, grad_s2, loss,
        scale_grad,
    ) = outs[5:]
    return (
        loss.reshape(()),
        tokens_grad[None],
        grad_qkv[None],
        grad_bqkv,
        grad_out[None],
        grad_bout,
        grad_g1,
        grad_s1,
        grad_up[None],
        grad_bup,
        grad_down[None],
        grad_bdown,
        grad_g2,
        grad_s2,
        grad_proj[None],
        scale_grad.reshape(()),
    )


def solution(mesh):
    return jax.shard_map(
        per_device,
        mesh=mesh,
        in_specs=(
            P("stream", "dp", None),
            P("stream", None, None),
            P("stream", None),
            P("stream", None, None),
            P("stream", None),
            P("stream", None),
            P("stream", None),
            P("stream", None, None),
            P("stream", None),
            P("stream", None, None),
            P("stream", None),
            P("stream", None),
            P("stream", None),
            P("stream", None, None),
            P(),
            P(),
            P("dp"),
        ),
        out_specs=(
            P(),
            P("stream", "dp", None),
            P("stream", None, None),
            P("stream", None),
            P("stream", None, None),
            P("stream", None),
            P("stream", None),
            P("stream", None),
            P("stream", None, None),
            P("stream", None),
            P("stream", None, None),
            P("stream", None),
            P("stream", None),
            P("stream", None),
            P("stream", None, None),
            P(),
        ),
        check_vma=False,
    )
```

```python
from functools import partial
import math

import jax
import jax.numpy as jnp
import numpy as np
from jax import lax
from jax.experimental import pallas as pl
from jax.experimental.pallas import tpu as pltpu
from jax.sharding import PartitionSpec as P

D = 512
HEADS = 8
HD = 64
FF = 2048
PROJ = 128
QLEN = 32
DOCS_ROW = 4
ROW = 256
EXT = 16
RANGES = (64, 96, 128)

SHARPNESS = 8.0
EPS_NORM = 1e-06
EPS_LAYER = 1e-05
LOG2E = 1.4426950408889634

F32 = jnp.float32
BF16 = jnp.bfloat16
REST = 2304
SHARE = 32
DOWN = FF // 16
HEAD = 80
TAIL = DOWN - HEAD
FIRST = DOWN + HEAD
SECOND = REST // 16 + TAIL
CIRCLE = (0, 2, 4, 6, 7, 5, 3, 1)
RING = len(CIRCLE)
AHEAD = (RING // 2, RING // 2 - 1)
LATER = tuple(k for k in range(RING) if k not in AHEAD)
GROUPS = ((0, 1, 2, 3, 5, 6, 7), (4,))
STEP_COST = 3 * 10**7
SPREAD_COST = 0
ROUND = (("step", 0), ("step", 1))
ORDER = (
    (("open", 0), ("open", 1), ("total", 0), ("total", 1), ("tokens", 0)) + ROUND * 7
    + (("share", 0), ("spread", ((True, 0),)), ("spread", ((False, 0),))) + ROUND
    + (("share", 1), ("spread", ((True, 1),)), ("spread", ((False, 1),)))
)
MIB = 1024 * 1024

VMEM = pl.BlockSpec(memory_space=pltpu.VMEM)
SMEM = pl.BlockSpec(memory_space=pltpu.SMEM)
HBM = pl.BlockSpec(memory_space=pltpu.HBM)
HELD = pl.BlockSpec(memory_space=pltpu.VMEM)


def mm(a, b):
    return lax.dot_general(a, b, (((1,), (0,)), ((), ())), preferred_element_type=F32)


def mm_nt(a, b):
    return lax.dot_general(a, b, (((1,), (1,)), ((), ())), preferred_element_type=F32)


def mm_tn(a, b):
    return lax.dot_general(a, b, (((0,), (0,)), ((), ())), preferred_element_type=F32)


def iota(shape, axis):
    return lax.broadcasted_iota(jnp.int32, shape, axis)


def rope_table():
    half = HD // 2
    freqs = (10000.0 ** (-np.arange(half, dtype=np.float32) / np.float32(half))).astype(np.float32)
    turned = np.arange(ROW, dtype=np.float32)[:, None] * freqs[None, :]
    cosine = np.cos(turned.astype(np.float64))
    sine = np.sin(turned.astype(np.float64))
    cosine = np.concatenate([cosine, cosine, cosine, cosine], axis=1).astype(np.float32)
    sine = np.concatenate([-sine, sine, -sine, sine], axis=1).astype(np.float32)
    parts = []
    for table in (cosine, sine):
        high = table.astype(jnp.bfloat16)
        low = (table - high.astype(np.float32)).astype(jnp.bfloat16)
        parts += [high, low]
    return np.concatenate(parts, axis=1)


def swapping():
    shape = (128, 128)
    return (iota(shape, 0) == (iota(shape, 1) ^ (HD // 2))).astype(F32).astype(BF16)


def bounds_of(lens_ref, row):
    ends, total = [], jnp.int32(0)
    for k in range(DOCS_ROW):
        total = total + lens_ref[k, row]
        ends.append(total)
    return ends


def segment_of(spot, ends):
    seg = jnp.zeros_like(spot)
    for end in ends:
        seg = seg + (spot >= end).astype(jnp.int32)
    return seg


def norm_rows(values):
    mean = jnp.mean(values, axis=1, keepdims=True)
    centred = values - mean
    spread = jnp.mean(centred * centred, axis=1, keepdims=True)
    rstd = lax.rsqrt(spread + EPS_LAYER)
    return centred * rstd, rstd


def norm_back(d_out, xhat, rstd, gain):
    scaled = d_out * gain
    first = jnp.mean(scaled, axis=1, keepdims=True)
    second = jnp.mean(scaled * xhat, axis=1, keepdims=True)
    return rstd * (scaled - first - xhat * second)


def col_sum(values):
    return jnp.sum(values, axis=0, keepdims=True)


def here(size):
    me, stream = lax.axis_index("dp"), lax.axis_index("stream")
    top = size // 2
    has_top = jnp.where((me & top) != 0, 1, 0)
    base = jnp.where(stream == 0, me & ~top, me | top)
    near_at = jnp.where((me & 2) != 0, 1, 0) + jnp.where((me & 1) != 0, 2, 0)
    chip = (me >> 1) % RING
    place = jnp.int32(0)
    for k, one in enumerate(CIRCLE):
        place = jnp.where(chip == one, k, place)
    return me, stream, base, near_at, has_top, me & 1, place


def fetch(pairs, sems):
    copies = [pltpu.make_async_copy(src, dst, sems.at[k]) for k, (src, dst) in enumerate(pairs)]
    for copy in copies:
        copy.start()
    return copies


KEPT = (
    ((ROW, 3 * D), BF16),
    ((ROW, 256), F32),
    ((HEADS, ROW, ROW), BF16),
    ((ROW, D), BF16),
    ((ROW, D), F32),
    ((ROW, 128), F32),
    ((8, D), F32),
)
MOVED = (((ROW, FF), BF16), ((ROW, FF), BF16), ((ROW, D), F32), ((ROW, 128), F32))


def move_kept(*refs):
    count = len(MOVED)
    for copy in fetch([*zip(refs[:count], refs[count:-1])], refs[-1]):
        copy.wait()


def encoder_forward(
    size, lens_hbm, labels_hbm, table_hbm, x_hbm, wqkv_hbm, bqkv_hbm, wout_hbm, bout_hbm,
    g1_hbm, s1_hbm, wup_hbm, bup_hbm, wdown_hbm, bdown_hbm, g2_hbm, s2_hbm, wproj_hbm,
    vec_ref, act_ref, slope_ref, xh2_ref, rs2_ref, qkv_hbm, rope_hbm, probs_hbm, mixed_hbm, xh1_hbm,
    rs1_hbm, affine_hbm,
    qkv_ref, rope_ref, probs_ref, mixed_ref, xh1_ref, rs1_ref, affine_ref, out_sems,
    table_ref, x_ref, wqkv_ref, bqkv_ref, wout_ref, bout_ref, g1_ref, s1_ref, wup_ref, bup_ref,
    wdown_ref, bdown_ref, g2_ref, s2_ref, wproj_ref, lens_ref, labels_ref, sems,
):
    me, stream = here(size)[:2]
    is_query = stream == 0
    scalars = fetch(((lens_hbm, lens_ref), (labels_hbm, labels_ref)), sems.at[pl.ds(15, 2)])
    copies = fetch(
        (
            (table_hbm, table_ref), (x_hbm, x_ref), (wqkv_hbm, wqkv_ref), (bqkv_hbm, bqkv_ref),
            (wout_hbm, wout_ref), (bout_hbm, bout_ref), (g1_hbm, g1_ref), (s1_hbm, s1_ref),
            (bup_hbm, bup_ref), (bdown_hbm, bdown_ref), (g2_hbm, g2_ref), (s2_hbm, s2_ref),
            (wup_hbm, wup_ref), (wdown_hbm, wdown_ref), (wproj_hbm, wproj_ref),
        ),
        sems,
    )
    kept = []

    def keep(src, dst):
        copy = pltpu.make_async_copy(src, dst, out_sems.at[len(kept)])
        copy.start()
        kept.append(copy)

    for copy in scalars:
        copy.wait()
    ends = bounds_of(lens_ref, me)

    def layout(spot):
        seg_doc = segment_of(spot, ends)
        start_doc = jnp.zeros_like(spot)
        for k in range(DOCS_ROW):
            start_doc = jnp.where(seg_doc == k + 1, ends[k], start_doc)
        seg_query = spot // QLEN
        seg = jnp.where(is_query, seg_query, seg_doc)
        start = jnp.where(is_query, seg_query * QLEN, start_doc)
        return seg, start

    shape = (ROW, ROW)
    seg_q, start_q = layout(iota(shape, 0))
    seg_k, _ = layout(iota(shape, 1))
    same = seg_q == seg_k
    onehot = (iota(shape, 1) == iota(shape, 0) - start_q).astype(F32).astype(BF16)
    for copy in copies[:4]:
        copy.wait()
    turned = mm(onehot, table_ref[...])
    cosine = turned[:, :128] + turned[:, 128:256]
    sine = turned[:, 256:384] + turned[:, 384:]
    rope_ref[:, :128] = cosine
    rope_ref[:, 128:] = sine
    keep(rope_ref, rope_hbm)

    x = x_ref[...]
    joined = mm(x, wqkv_ref[...]) + bqkv_ref[...].astype(F32)
    swap = swapping()
    swap = jnp.concatenate([swap, swap], axis=0)
    for g in range(2 * D // 128):
        block = joined[:, g * 128 : (g + 1) * 128]
        high = block.astype(BF16)
        low = (block - high.astype(F32)).astype(BF16)
        other = mm(jnp.concatenate([high, low], axis=1), swap)
        qkv_ref[:, g * 128 : (g + 1) * 128] = (block * cosine + other * sine).astype(BF16)
    qkv_ref[:, 2 * D :] = joined[:, 2 * D :].astype(BF16)
    keep(qkv_ref, qkv_hbm)

    low_half = iota((ROW, 128), 1) < HD
    for g in range(HEADS // 2):
        q_g = qkv_ref[:, g * 128 : (g + 1) * 128]
        k_g = qkv_ref[:, D + g * 128 : D + (g + 1) * 128]
        v_g = qkv_ref[:, 2 * D + g * 128 : 2 * D + (g + 1) * 128]
        v_ones = jnp.concatenate([v_g, jnp.ones((ROW, 128), BF16)], axis=1)
        outs = []
        for h in range(2):
            pick = low_half if h == 0 else jnp.logical_not(low_half)
            scores = mm_nt(jnp.where(pick, q_g, jnp.zeros_like(q_g)), k_g)
            scores = jnp.where(same, scores * (LOG2E / math.sqrt(HD)), -1e30)
            top = jnp.max(scores, axis=1, keepdims=True)
            exps = jnp.exp2(scores - top)
            both = mm(exps.astype(BF16), v_ones)
            inverse = 1.0 / both[:, 128:]
            probs_ref[2 * g + h] = (exps * jnp.concatenate([inverse, inverse], axis=1)).astype(BF16)
            outs.append(both[:, :128] * inverse)
        mixed_ref[:, g * 128 : (g + 1) * 128] = jnp.where(low_half, outs[0], outs[1]).astype(BF16)

    keep(probs_ref, probs_hbm)
    keep(mixed_ref, mixed_hbm)
    for copy in copies[4:12]:
        copy.wait()
    for k, ref in enumerate((g1_ref, s1_ref, g2_ref, s2_ref)):
        affine_ref[k : k + 1, :] = ref[...].astype(F32)
    affine_ref[4:, :] = jnp.zeros((4, D), F32)
    keep(affine_ref, affine_hbm)
    attended = mm(mixed_ref[...], wout_ref[...]) + bout_ref[...].astype(F32)
    xhat, rstd = norm_rows(x.astype(F32) + attended)
    xh1_ref[...] = xhat
    rs1_ref[...] = jnp.broadcast_to(rstd, (ROW, 128))
    keep(xh1_ref, xh1_hbm)
    keep(rs1_ref, rs1_hbm)
    first = xhat * g1_ref[...].astype(F32) + s1_ref[...].astype(F32)
    first_low = first.astype(BF16)
    branch = bdown_ref[...].astype(F32) + first
    step = 512
    copies[12].wait()
    for c in range(FF // step):
        cols = slice(c * step, (c + 1) * step)
        inner = mm(first_low, wup_ref[:, cols]) + bup_ref[:, cols].astype(F32)
        gate = 0.5 + 0.5 * lax.erf(inner * math.sqrt(0.5))
        bell = jnp.exp2(inner * inner * (-0.5 * LOG2E)) * (1.0 / math.sqrt(2.0 * math.pi))
        act = (inner * gate).astype(BF16)
        act_ref[:, cols] = act
        slope_ref[:, cols] = (gate + inner * bell).astype(BF16)
        if c == 0:
            copies[13].wait()
        branch = branch + mm(act, wdown_ref[cols, :])
    xhat, rstd = norm_rows(branch)
    xh2_ref[...] = xhat
    rs2_ref[...] = jnp.broadcast_to(rstd, (ROW, 128))
    second = xhat * g2_ref[...].astype(F32) + s2_ref[...].astype(F32)
    copies[14].wait()
    vec_ref[:ROW, :] = mm(second.astype(BF16), wproj_ref[...]).astype(BF16)
    line = iota((EXT, PROJ), 0)
    tag = jnp.zeros((EXT, PROJ), jnp.int32)
    for k in range(labels_ref.shape[0]):
        label = labels_ref[k]
        tag = jnp.where(line == k, label >> 6, tag)
        tag = jnp.where(line == k + 8, label & 63, tag)
    vec_ref[ROW:, :] = tag.astype(F32).astype(BF16)
    for copy in kept:
        copy.wait()


def prefix_norms(values, axis):
    place = iota(values.shape, axis)
    squared = values * values
    sums = [
        jnp.sum(jnp.where(place < cut, squared, 0.0), axis=axis, keepdims=True) for cut in RANGES
    ]
    return [lax.rsqrt(s + EPS_NORM) for s in sums]


def load_queries(near_ref, far_ref):
    span = ROW + EXT
    rows = []
    for ref in (near_ref, far_ref):
        for k in range(ref.shape[0] // span):
            rows.append(ref[k * span : k * span + ROW, :])
    return jnp.concatenate(rows, axis=0).astype(F32)


def unit_queries(queries, scale):
    lane = iota(queries.shape, 1)
    inverse = prefix_norms(queries, 1)
    unit = [
        jnp.where(lane < cut, queries * (inv * scale), 0.0) for cut, inv in zip(RANGES, inverse)
    ]
    return unit, inverse


def unit_docs(doc_refs, scratch_ref):
    at = 0
    for ref in doc_refs:
        for k in range(ref.shape[0] // ROW):
            scratch_ref[:, at * ROW : (at + 1) * ROW] = ref[
                k * ROW : (k + 1) * ROW, :
            ].astype(F32).T
            at += 1
    turned = scratch_ref[...]
    inverse = prefix_norms(turned, 0)
    place = iota(turned.shape, 0)
    unit = [jnp.where(place < cut, turned * inv, 0.0) for cut, inv in zip(RANGES, inverse)]
    return unit, inverse


def row_ids(base, masks, doc_rows):
    ids = []
    for p in range(doc_rows):
        offset = 0
        for k, mask in enumerate(masks):
            if (p >> k) & 1:
                offset ^= mask
        ids.append(base ^ offset)
    return ids


def doc_marks(lens_ref, ids, lanes, transposed):
    docs = len(ids) * DOCS_ROW
    shape = (lanes, ROW) if transposed else (ROW, lanes)
    spot, lane = (iota(shape, 1), iota(shape, 0)) if transposed else (iota(shape, 0), iota(shape, 1))
    marks = []
    for p, row in enumerate(ids):
        seg = segment_of(spot, bounds_of(lens_ref, row))
        local = jnp.where(seg < DOCS_ROW, seg + p * DOCS_ROW, -1 - lanes)
        marks.append(
            [(lane == local + m * docs).astype(F32).astype(BF16) for m in range(len(RANGES))]
        )
    return marks


def matching_stats(
    size, masks, lanes, scale_ref, lens_ref, near_ref, far_ref, *refs
):
    doc_refs = refs[:-7]
    totals_ref, el_ref, hot_ref, factor_ref, stats_ref, turn_ref, unit_ref = refs[-7:]
    base, near_at = here(size)[2:4]
    span = ROW + EXT
    queries = load_queries(near_ref, far_ref)
    count = queries.shape[0]
    unit_q, _ = unit_queries(queries, SHARPNESS * LOG2E)
    unit_q = [u.astype(BF16) for u in unit_q]
    unit_d, _ = unit_docs(doc_refs, turn_ref)
    for m in range(len(RANGES)):
        unit_ref[m] = unit_d[m].astype(BF16)
    doc_rows = turn_ref.shape[1] // ROW
    docs = doc_rows * DOCS_ROW
    ids = row_ids(base, masks, doc_rows)
    marks = doc_marks(lens_ref, ids, lanes, False)
    totals = jnp.zeros((count, lanes), F32)
    for p in range(doc_rows):
        for m in range(len(RANGES)):
            sims = mm(unit_q[m], unit_ref[m, :, p * ROW : (p + 1) * ROW])
            totals = totals + mm(jnp.exp2(sims).astype(BF16), marks[p][m])
    lane_t = iota((count, lanes), 1)
    totals = jnp.where(lane_t < len(RANGES) * docs, totals, 1.0)
    totals_ref[...] = totals
    shape = (8, lanes)
    lane = iota(shape, 1)
    length = jnp.ones(shape, jnp.int32)
    name = jnp.full(shape, -1, jnp.int32)
    for p in range(doc_rows):
        for k in range(DOCS_ROW):
            own = jnp.zeros(shape, jnp.bool_)
            for m in range(len(RANGES)):
                own = jnp.logical_or(own, lane == m * docs + p * DOCS_ROW + k)
            length = jnp.where(own, lens_ref[k, ids[p]], length)
            name = jnp.where(own, ids[p] * DOCS_ROW + k, name)
    log_length = jnp.log(length.astype(F32))
    matched = (jnp.log(totals) - log_length[:1]) * (1.0 / SHARPNESS)
    per_query = jnp.sum(matched.reshape(count // QLEN, QLEN, lanes), axis=1)
    scale = jnp.exp(jnp.full(shape, scale_ref[0], F32))
    factor_ref[...] = scale
    scale = scale[:1]
    logits = per_query * (scale * (1.0 / QLEN))
    groups = count // ROW
    tags = []
    for ref in (near_ref, far_ref):
        for k in range(ref.shape[0] // span):
            high = ref[k * span + ROW : k * span + ROW + 8, :].astype(F32).astype(jnp.int32)
            low = ref[k * span + ROW + 8 : k * span + ROW + 16, :].astype(F32).astype(jnp.int32)
            tag = high * 64 + low
            tags.append(jnp.concatenate([tag] * (lanes // 128), axis=1))
    tag = jnp.concatenate(tags, axis=0)
    lane_q = iota(logits.shape, 1)
    valid = lane_q < len(RANGES) * docs
    el = jnp.where(valid, jnp.exp(logits), 0.0)
    hot = jnp.where(jnp.logical_and(valid, jnp.concatenate([name] * groups, axis=0) == tag), 1.0, 0.0)
    el_ref[...] = el
    hot_ref[...] = hot
    place = iota((groups * 8, 128), 1)
    stats = jnp.zeros((groups * 8, 128), F32)
    for k, values in enumerate((el, el * logits, hot * logits)):
        for m in range(len(RANGES)):
            inside = jnp.logical_and(lane_q >= m * docs, lane_q < (m + 1) * docs)
            one = jnp.sum(jnp.where(inside, values, 0.0), axis=1, keepdims=True)
            stats = jnp.where(place == k * 3 + m, one, stats)
    for a in range(groups):
        at = pl.multiple_of((near_at ^ a) * 8, 8)
        stats_ref[pl.ds(at, 8), :] = stats[a * 8 : (a + 1) * 8, :]


def matching_back(
    size, masks, lanes, totals_ref, el_ref, hot_ref, factor_ref, own_ref, over_y, over_x, over_both, unitq_ref, qt_ref, invq_ref, unit_ref, invd_ref, marks_ref, *refs
):
    dq_ref, far_ref, keep_ref, send_ref, loss_ref, dot_ref, dt_ref, stats_ref = refs[-8:]
    _, stream, base, near_at = here(size)[:4]
    total_queries = size * (ROW // QLEN)
    temper = SHARPNESS * LOG2E
    count = unitq_ref.shape[1]
    inv_q = [invq_ref[:, m : m + 1] for m in range(len(RANGES))]
    inv_d = [invd_ref[m : m + 1, :] for m in range(len(RANGES))]
    unit_q = [unitq_ref[m] for m in range(len(RANGES))]
    doc_rows = unit_ref.shape[2] // ROW
    docs = doc_rows * DOCS_ROW
    groups = count // ROW
    odd_y, odd_x = (near_at & 1) == 1, stream == 1
    parts = [own_ref[...], over_y[...], over_x[...], over_both[...]]
    parts = [jnp.where(odd_y, a, b) for a, b in ((parts[1], parts[0]), (parts[0], parts[1]),
                                                  (parts[3], parts[2]), (parts[2], parts[3]))]
    parts = [jnp.where(odd_x, parts[(k + 2) % 4], parts[k]) for k in range(4)]
    stats_ref[...] = (parts[0] + parts[1]) + (parts[2] + parts[3])
    rows = []
    for a in range(groups):
        at = pl.multiple_of((near_at ^ a) * 8, 8)
        rows.append(stats_ref[pl.ds(at, 8), :])
    stats = jnp.concatenate(rows, axis=0)
    place = iota(stats.shape, 1)

    def column(k):
        return jnp.sum(jnp.where(place == k, stats, 0.0), axis=1, keepdims=True)

    shape = (groups * 8, lanes)
    lane_q = iota(shape, 1)
    sums = jnp.ones(shape, F32)
    loss = jnp.zeros((groups * 8, 1), F32)
    moved = jnp.zeros((groups * 8, 1), F32)
    for m in range(len(RANGES)):
        whole, weighted, picked = column(m), column(3 + m), column(6 + m)
        inside = jnp.logical_and(lane_q >= m * docs, lane_q < (m + 1) * docs)
        sums = jnp.where(inside, whole, sums)
        loss = loss + (jnp.log(whole) - picked)
        moved = moved + (weighted / whole - picked)
    line = iota((8, 128), 0)
    loss = jnp.where(
        line == 0,
        jnp.sum(loss, axis=0, keepdims=True) * (1.0 / total_queries),
        jnp.where(line == 1, jnp.sum(moved, axis=0, keepdims=True) * (1.0 / total_queries), 0.0),
    )
    loss_ref[...] = loss
    scale = factor_ref[:1, :]
    coeff = (el_ref[...] / sums - hot_ref[...]) * (scale * (1.0 / (QLEN * total_queries)))
    coeff = jnp.broadcast_to(coeff[:, None, :], (groups * 8, QLEN, lanes)).reshape(count, lanes)
    ratio = coeff / totals_ref[...]
    ratio_high = ratio.astype(BF16)
    ratio_low = (ratio - ratio_high.astype(F32)).astype(BF16)
    ratio = jnp.concatenate([ratio_high, ratio_low], axis=1)
    for m in range(len(RANGES)):
        grad = jnp.zeros((count, PROJ), F32)
        for p in range(doc_rows):
            block = unit_ref[m, :, p * ROW : (p + 1) * ROW]
            mark = marks_ref[p * len(RANGES) + m]
            if len(refs) > 8:
                exps = refs[0][m, :, p * ROW : (p + 1) * ROW].astype(F32)
            else:
                exps = jnp.exp2(mm(unit_q[m], block))
            d_sims = (exps * mm(ratio, jnp.concatenate([mark, mark], axis=0))).astype(BF16)
            grad = grad + mm_nt(d_sims, block)
            dt_ref[m, :, p * ROW : (p + 1) * ROW] = mm(qt_ref[m], d_sims)
        unit = unit_q[m].astype(F32) * (1.0 / temper)
        along = jnp.sum(grad * unit, axis=1, keepdims=True)
        part = inv_q[m] * (grad - unit * along)
        if m == 0:
            dot_ref[...] = part
        else:
            dot_ref[...] += part
    dq_ref[...] = dot_ref[: count // 2, :].astype(BF16)
    far_ref[...] = dot_ref[count // 2 :, :].astype(BF16)
    total = jnp.zeros(unit_ref.shape[1:], F32)
    for m in range(len(RANGES)):
        grad = dt_ref[m] * (1.0 / temper)
        unit = unit_ref[m].astype(F32)
        along = jnp.sum(grad * unit, axis=0, keepdims=True)
        total = total + inv_d[m] * (grad - unit * along)
    for p in range(doc_rows):
        ref, at = (keep_ref, p) if p < doc_rows // 2 else (send_ref, p - doc_rows // 2)
        ref[at * ROW : (at + 1) * ROW, :] = total[:, p * ROW : (p + 1) * ROW].T.astype(BF16)


def matching_ready(size, masks, lanes, lens_ref, near_ref, far_ref, *refs):
    doc_refs = refs[:-7] if refs[-2].shape[0] != len(RANGES) else refs[:-8]
    unitq_ref, qt_ref, invq_ref, unit_ref, invd_ref, marks_ref = refs[len(doc_refs) : len(doc_refs) + 6]
    turn_ref = refs[-1]
    ids = row_ids(here(size)[2], masks, unit_ref.shape[2] // ROW)
    for p, marks in enumerate(doc_marks(lens_ref, ids, lanes, True)):
        for m, mark in enumerate(marks):
            marks_ref[p * len(RANGES) + m] = mark
    queries = load_queries(near_ref, far_ref)
    unit_q, inv_q = unit_queries(queries, SHARPNESS * LOG2E)
    unit_d, inv_d = unit_docs(doc_refs, turn_ref)
    lane = iota(invq_ref.shape, 1)
    columns = jnp.zeros(invq_ref.shape, F32)
    invd_ref[...] = jnp.zeros_like(invd_ref)
    for m in range(len(RANGES)):
        unitq_ref[m] = unit_q[m].astype(BF16)
        unit_ref[m] = unit_d[m].astype(BF16)
        qt_ref[m] = unit_q[m].T.astype(BF16)
        columns = jnp.where(lane == m, inv_q[m], columns)
        invd_ref[m : m + 1, :] = inv_d[m]
        if len(refs) - len(doc_refs) > 7:
            refs[-2][m] = jnp.exp2(mm(unitq_ref[m], unit_ref[m])).astype(BF16)
    invq_ref[...] = columns


def pick_rows(size, here_ref, there_ref, rows_ref):
    _, stream, _, _, has_top = here(size)[:5]
    rows_ref[...] = jnp.where(has_top == stream, here_ref[...], there_ref[...])


def add_rows(rows_ref, got_ref, sum_ref):
    sum_ref[...] = (rows_ref[...].astype(F32) + got_ref[...].astype(F32)).astype(BF16)


DIGITS = 10
POINT = 20


def digits_of(value):
    fixed = (value * float(1 << POINT)).astype(jnp.int32)
    size = jnp.abs(fixed)
    lane = iota(value.shape, 1)
    digits = jnp.zeros(value.shape, jnp.int32)
    for k in range(DIGITS):
        digits = jnp.where(lane == k, (size >> (3 * k)) & 7, digits)
    return jnp.where(fixed < 0, -digits, digits).astype(F32)


def value_of(digits):
    lane = iota(digits.shape, 1)
    half = DIGITS // 2
    weight = jnp.zeros(digits.shape, F32)
    for k in range(half):
        weight = jnp.where(jnp.logical_or(lane == k, lane == k + half), float(8**k), weight)
    low = jnp.sum(jnp.where(lane < half, digits * weight, 0.0))
    high = jnp.sum(jnp.where(jnp.logical_and(lane >= half, lane < DIGITS), digits * weight, 0.0))
    return (high * float(8**half) + low) * (1.0 / (1 << POINT))


def turn(core, place, block):
    return jnp.where(core == 0, place - block, block - place) & (RING - 1)


def block_at(core, place, distance):
    return jnp.where(core == 0, place - distance, place + distance) & (RING - 1)


def store_block(keep_ref, send_ref, rows, block, places, value):
    core, place = places
    mine = core == block // RING
    at = turn(block // RING, place, block % RING)

    @pl.when(mine)
    def _():
        keep_ref[at, rows, :] = value

    @pl.when(jnp.logical_not(mine))
    def _():
        send_ref[at, rows, :] = value


def feed_back(
    size, dq_ref, dd_ref, got_ref, xh2_ref, rs2_ref, affine_ref, wproj_ref, slope_ref, act_ref,
    xh1_ref, wdown_ref, wup_hbm,
    keep_ref, send_ref, tail_keep, tail_send, dfirst_ref, gproj_ref, small_ref,
    dinner_ref, wup_ref, sems,
):
    step = 512
    spans = [slice(c * step, (c + 1) * step) for c in range(FF // step)]
    copies = fetch([(wup_hbm, wup_ref)], sems)
    g1, s1, g2, s2 = [affine_ref[k : k + 1, :] for k in range(4)]
    _, stream, _, _, has_top, *places = here(size)
    is_query, docs_there = stream == 0, has_top == 0
    got = got_ref[...].astype(F32)
    d_vec = jnp.where(
        is_query,
        dq_ref[...].astype(F32) + got,
        jnp.where(docs_there, got, dd_ref[...].astype(F32)),
    )
    d_proj = d_vec.astype(BF16)
    xhat = xh2_ref[...]
    gain = g2
    second = (xhat * gain + s2).astype(BF16)
    gproj_ref[...] = mm_tn(second, d_proj)
    d_second = mm_nt(d_proj, wproj_ref[...])
    small_ref[...] = jnp.zeros_like(small_ref)
    small_ref[5:6, :] = col_sum(d_second * xhat)
    small_ref[6:7, :] = col_sum(d_second)
    d_sum = norm_back(d_second, xhat, rs2_ref[:, :1], gain)
    d_branch = d_sum.astype(BF16)
    small_ref[4:5, :] = col_sum(d_branch.astype(F32))
    d_first = d_sum
    for c in range(FF // step):
        cols = spans[c]
        d_act = mm_nt(d_branch, wdown_ref[cols, :])
        d_inner = (d_act * slope_ref[:, cols].astype(F32)).astype(BF16)
        dinner_ref[:, cols] = d_inner
        small_ref[c : c + 1, :] = col_sum(d_inner.astype(F32))
        grad = mm_tn(act_ref[:, cols], d_branch).astype(BF16)
        for k in range(step // DOWN):
            store_block(
                keep_ref, send_ref, slice(0, DOWN), c * (step // DOWN) + k, places,
                grad[k * DOWN : (k + 1) * DOWN, :],
            )
    copies[0].wait()
    first = (xh1_ref[...] * g1 + s1).astype(BF16)
    for c in range(FF // step):
        cols = slice(c * step, (c + 1) * step)
        d_first = d_first + mm_nt(dinner_ref[:, cols], wup_ref[:, cols])
        grad = mm_tn(first, dinner_ref[:, cols]).astype(BF16)
        for k in range(D // DOWN):
            block = c * (D // DOWN) + k
            start = k * DOWN
            store_block(
                keep_ref, send_ref, slice(DOWN, FIRST), block, places, grad[start : start + HEAD, :]
            )
            store_block(
                tail_keep, tail_send, slice(0, TAIL), block, places,
                grad[start + HEAD : start + DOWN, :],
            )
    dfirst_ref[...] = d_first


def attend_back(
    size, dfirst_ref, gproj_ref, small_ref, loss_ref, tail_keep, tail_send, xh1_ref, rs1_ref, affine_ref, mixed_ref, wout_ref,
    qkv_ref, probs_ref, rope_ref, x_ref,
    keep_ref, ahead_ref, send_ref, dsum_ref, djoined_ref, rest_ref,
):
    me, *_, core, place = here(size)
    d_first = dfirst_ref[...]
    xhat = xh1_ref[...]
    gain = affine_ref[0:1, :]
    gain_grad = col_sum(d_first * xhat)
    shift_grad = col_sum(d_first)
    d_sum = norm_back(d_first, xhat, rs1_ref[:, :1], gain)
    d_att = d_sum.astype(BF16)
    bias_out = col_sum(d_att.astype(F32))
    rest_ref[3 * D : 4 * D, :] = mm_tn(mixed_ref[...], d_att)
    d_mixed = mm_nt(d_att, wout_ref[...]).astype(BF16)
    cosine, sine = rope_ref[:, :128], rope_ref[:, 128:]
    low_half = iota((ROW, 128), 1) < HD

    scale = 1.0 / math.sqrt(HD)
    cosine, sine = cosine * scale, sine * scale
    swap = swapping()

    def unrotate(both):
        return (both[:, :128] * cosine - both[:, 128:] * sine).astype(BF16)

    for g in range(HEADS // 2):
        span = slice(g * 128, (g + 1) * 128)
        q_g = qkv_ref[:, g * 128 : (g + 1) * 128]
        k_g = qkv_ref[:, D + g * 128 : D + (g + 1) * 128]
        v_g = qkv_ref[:, 2 * D + g * 128 : 2 * D + (g + 1) * 128]
        m_g = d_mixed[:, span]
        q_both = jnp.concatenate([q_g, mm(q_g, swap).astype(BF16)], axis=1)
        k_both = jnp.concatenate([k_g, mm(k_g, swap).astype(BF16)], axis=1)
        d_q = jnp.zeros((ROW, 256), F32)
        d_k = jnp.zeros((ROW, 256), F32)
        d_v = jnp.zeros((ROW, 128), F32)
        zero = jnp.zeros((ROW, 128), BF16)
        zero_both = jnp.zeros((ROW, 256), BF16)
        for h in range(2):
            pick = low_half if h == 0 else jnp.logical_not(low_half)
            probs_low = probs_ref[2 * g + h]
            probs = probs_low.astype(F32)
            m_h = jnp.where(pick, m_g, zero)
            d_probs = mm_nt(m_h, v_g)
            d_v = d_v + mm_tn(probs_low, m_h)
            inner = jnp.sum(d_probs * probs, axis=1, keepdims=True)
            d_scores = (probs * (d_probs - inner)).astype(BF16)
            pick_both = jnp.concatenate([pick, pick], axis=1)
            d_q = d_q + mm(d_scores, jnp.where(pick_both, k_both, zero_both))
            d_k = d_k + mm_tn(d_scores, jnp.where(pick_both, q_both, zero_both))
        djoined_ref[:, g * 128 : (g + 1) * 128] = unrotate(d_q)
        djoined_ref[:, D + g * 128 : D + (g + 1) * 128] = unrotate(d_k)
        djoined_ref[:, 2 * D + g * 128 : 2 * D + (g + 1) * 128] = d_v.astype(BF16)
    x = x_ref[...]
    dsum_ref[...] = d_sum
    rest_ref[4 * D :, :] = jnp.zeros((8 * 2 * RING, D), F32)
    smalls = []
    for c in range(3):
        cols = slice(c * D, (c + 1) * D)
        d_part = djoined_ref[:, cols]
        rest_ref[c * D : (c + 1) * D, :] = mm_tn(x, d_part)
        smalls.append(col_sum(d_part.astype(F32)))
    smalls += [bias_out, gain_grad, shift_grad] + [small_ref[k : k + 1, :] for k in range(7)]
    counted = jnp.where((me & 3) == 0, 1.0, 0.0)
    lines = [digits_of(loss_ref[k : k + 1, :]) * counted for k in range(2)]
    smalls.append(jnp.concatenate(lines + [jnp.zeros((1, D - 256), F32)], axis=1))
    for k, row in enumerate(smalls):
        rest_ref[4 * D + 8 * k : 4 * D + 8 * k + 1, :] = row
    for k in range(RING):
        sent, at = (ahead_ref, AHEAD.index(k)) if k in AHEAD else (send_ref, LATER.index(k))
        for ref, index, tail_ref, owner in (
            (keep_ref, k, tail_keep, core), (sent, at, tail_send, 1 - core)
        ):
            block = owner * RING + block_at(owner, place, k)
            parts = []
            for c in range(4):
                start = pl.multiple_of(c * D + block * SHARE, SHARE)
                parts.append(rest_ref[pl.ds(start, SHARE), :])
            row = pl.multiple_of(block * SHARE, SHARE)
            parts.append(
                jnp.concatenate(
                    [gproj_ref[pl.ds(row + 8 * j, 8), :] for j in range(SHARE // 8)], axis=1
                )
            )
            parts.append(rest_ref[pl.ds(pl.multiple_of(4 * D + block * 8, 8), 8), :])
            ref[index, : REST // 16, :] = jnp.concatenate(parts, axis=0).astype(BF16)
            ref[index, REST // 16 :, :] = tail_ref[k]


def tokens_back(dsum_ref, djoined_ref, wqkv_ref, tokens_ref):
    tokens = dsum_ref[...]
    for c in range(3):
        cols = slice(c * D, (c + 1) * D)
        tokens = tokens + mm_nt(djoined_ref[:, cols], wqkv_ref[:, cols])
    tokens_ref[...] = tokens


def spread(size, jobs, last, *refs):
    core, place = here(size)[-2:]
    halves = refs[: len(jobs)]
    wide_one, wide_two, wide_qkv, wide_proj, small_ref, sems = refs[-6:]
    outs = refs[-21:-6] if last else refs[-11:-6]
    down_hbm, up_hbm, qkv_hbm, out_hbm, proj_hbm = outs[:5]
    copies = []

    def move(src, dst):
        copy = pltpu.make_async_copy(src, dst, sems.at[len(copies)])
        copy.start()
        copies.append(copy)

    at = 0
    for job, (mine, group) in enumerate(jobs):
        owner = core if mine else 1 - core
        both_ref = halves[job]
        for p, distance in enumerate(GROUPS[group]):
            block = owner * RING + block_at(owner, place, distance)
            wide_one[at] = both_ref[p, :FIRST, :].astype(F32)
            rows = pl.ds(pl.multiple_of(block * DOWN, DOWN), DOWN)
            move(wide_one.at[at, :DOWN, :], down_hbm.at[rows, :])
            start = (block % (D // DOWN)) * DOWN
            columns = pl.ds(pl.multiple_of((block // (D // DOWN)) * D, D), D)
            rows = pl.ds(pl.multiple_of(start, DOWN), HEAD)
            move(wide_one.at[at, DOWN:, :], up_hbm.at[rows, columns])
            wide = both_ref[p, FIRST:, :].astype(F32)
            wide_two[at, :SHARE, :] = wide[3 * SHARE : 4 * SHARE, :]
            wide_two[at, SHARE:, :] = wide[REST // 16 :, :]
            rows = pl.ds(pl.multiple_of(start + HEAD, 16), TAIL)
            move(wide_two.at[at, SHARE:, :], up_hbm.at[rows, columns])
            rows = pl.ds(pl.multiple_of(block * SHARE, SHARE), SHARE)
            for c in range(3):
                wide_qkv[at, :, c * D : (c + 1) * D] = wide[c * SHARE : (c + 1) * SHARE, :]
            move(wide_qkv.at[at], qkv_hbm.at[rows, :])
            move(wide_two.at[at, :SHARE, :], out_hbm.at[rows, :])
            for j in range(SHARE // 8):
                wide_proj[at, 8 * j : 8 * j + 8, :] = wide[
                    4 * SHARE : 4 * SHARE + 8, j * PROJ : (j + 1) * PROJ
                ]
            move(wide_proj.at[at], proj_hbm.at[rows, :])
            at += 1
    if last:
        sources = refs[len(jobs) : len(jobs) + 2 * len(GROUPS)]
        for k, ref in enumerate(sources):
            owner = core if k < len(GROUPS) else 1 - core
            for p, distance in enumerate(GROUPS[k % len(GROUPS)]):
                block = owner * RING + block_at(owner, place, distance)
                start = FIRST + 4 * SHARE
                line = ref[p, start : start + 16, :].astype(F32)[8:, :]
                small_ref[pl.ds(pl.multiple_of(block * 8, 8), 8), :] = line
        rows = [small_ref[8 * k : 8 * k + 1, :] for k in range(14)]
        bqkv_ref, bout_ref, g1_ref, s1_ref, bup_ref, bdown_ref, g2_ref, s2_ref = outs[5:13]
        for k, ref in enumerate(outs[13:]):
            ref[0] = value_of(rows[13][:, k * 128 : (k + 1) * 128])
        for c in range(3):
            bqkv_ref[:, c * D : (c + 1) * D] = rows[c]
        bout_ref[...] = rows[3]
        g1_ref[...] = rows[4]
        s1_ref[...] = rows[5]
        for c in range(4):
            bup_ref[:, c * D : (c + 1) * D] = rows[6 + c]
        bdown_ref[...] = rows[10]
        g2_ref[...] = rows[11]
        s2_ref[...] = rows[12]
    for copy in copies:
        copy.wait()


def spread_call(size, jobs, halves, outs, others):
    last = len(others) > 0
    shapes = ((FF, D), (D, FF), (D, 3 * D), (D, D), (D, PROJ))
    widths = (3 * D, D, D, D, FF, D, D, D) if last else ()
    args = [*halves, *others, *outs]
    count = sum(len(GROUPS[group]) for _, group in jobs)
    before = len(halves) + len(others)
    return call(
        partial(spread, size, jobs, last),
        args,
        [VMEM] * before + [HBM] * len(outs),
        [pltpu.HBM(shape, F32) for shape in shapes]
        + [shape_of((1, width)) for width in widths]
        + [shape_of((1,))] * (2 * last),
        [
            pltpu.VMEM((count, FIRST, D), F32),
            pltpu.VMEM((count, SHARE + TAIL, D), F32),
            pltpu.VMEM((count, SHARE, 3 * D), F32),
            pltpu.VMEM((count, SHARE, PROJ), F32),
            pltpu.VMEM((16 * RING, D), F32),
            pltpu.SemaphoreType.DMA((6 * count,)),
        ],
        out_specs=[HBM] * 5 + [VMEM] * len(widths) + [SMEM] * (2 * last),
        aliases={before + k: k for k in range(len(outs))},
        cost=SPREAD_COST,
        room=14,
    )


def shape_of(shape, dtype=F32):
    return jax.ShapeDtypeStruct(tuple(shape), dtype)


def call(kernel, args, specs, outs, scratch=(), room=24, out_specs=None, aliases={}, cost=10**7):
    spaces = {id(HBM): pltpu.HBM, id(HELD): pltpu.VMEM}
    args = [
        pltpu.with_memory_space_constraint(arg, spaces[id(spec)]) if id(spec) in spaces else arg
        for arg, spec in zip(args, specs)
    ]
    return pl.pallas_call(
        kernel,
        out_shape=outs,
        in_specs=specs,
        out_specs=out_specs or [VMEM] * len(outs),
        scratch_shapes=list(scratch),
        input_output_aliases=aliases,
        compiler_params=pltpu.CompilerParams(vmem_limit_bytes=room * MIB),
        cost_estimate=pl.CostEstimate(
            flops=10 * cost, bytes_accessed=cost, transcendentals=0
        ),
    )(*args)


def swapped(value, mask, axis="dp"):
    size = lax.axis_size(axis)
    return lax.ppermute(value, axis, [(k, k ^ mask) for k in range(size)])


def added(a, b):
    return (a.astype(F32) + b.astype(F32)).astype(BF16)


def join_blocks(*refs):
    half = (len(refs) - 1) // 2
    for k in range(half):
        refs[-1][k, :FIRST, :] = refs[k][0]
        refs[-1][k, FIRST:, :] = refs[half + k][0]


def ring_swap(value, onward):
    size = lax.axis_size("dp")
    pairs = []
    for k in range(size):
        at = CIRCLE.index((k >> 1) % RING)
        to = CIRCLE[(at + (1 if (k % 2 == 0) == onward else -1)) % RING]
        pairs.append((k, (k & ~(2 * RING - 1)) | (to << 1) | (k & 1)))
    return lax.ppermute(value, "dp", pairs)


def add_blocks(places, *refs):
    count = len(places)
    held_ref = refs[count] if any(place is not None for place in places) else None
    for k, place in enumerate(places):
        value = refs[k][...]
        if place is not None:
            value = (value.astype(F32) + held_ref[place : place + 1].astype(F32)).astype(BF16)
        refs[-count + k][...] = value


def first_blocks(places, keep_ref, pair_ref, *outs):
    for ref, (k, j) in zip(outs, places):
        ref[0] = (keep_ref[k].astype(F32) + pair_ref[j].astype(F32)).astype(BF16)


def later_blocks(places, keep_ref, pair_ref, out_ref):
    for k in AHEAD:
        out_ref[k] = jnp.zeros(out_ref.shape[1:], BF16)
    for k, j in places:
        out_ref[k] = (keep_ref[k].astype(F32) + pair_ref[j].astype(F32)).astype(BF16)


class Summed:
    def __init__(self, keep, sends, others):
        self.keep, self.others, self.hop = keep, others, 0
        self.pairs = [swapped(send, 1) for send in sends]
        self.sent, self.blocks = [], {}

    def blocks_call(self, blocks, places, held):
        return call(
            partial(add_blocks, places),
            (*blocks, *held),
            [VMEM] * (len(blocks) + len(held)),
            [shape_of(block.shape, BF16) for block in blocks],
            room=8,
            cost=STEP_COST,
        )

    def open(self, after):
        keep, pair, _ = lax.optimization_barrier((self.keep, self.pairs[0], after))
        shape = (1, *keep.shape[1:])
        places = [(k, AHEAD.index(k) if len(self.pairs) > 1 else k) for k in AHEAD]
        first, second = call(
            partial(first_blocks, places),
            (keep, pair),
            [VMEM] * 2,
            [shape_of(shape, BF16)] * 2,
            room=8,
            cost=STEP_COST,
        )
        self.sent = [(first, True), (second, False)]
        return second

    def total(self, after):
        keep, _ = lax.optimization_barrier((self.keep, after))
        later = [(k, LATER.index(k) if len(self.pairs) > 1 else k) for k in LATER]
        (self.keep,) = call(
            partial(later_blocks, later),
            (keep, self.pairs[-1]),
            [VMEM] * 2,
            [shape_of(keep.shape, BF16)],
            room=8,
            cost=STEP_COST,
        )
        return self.keep

    def step(self, after):
        half = RING // 2
        self.hop += 1
        hop = self.hop
        *got, _ = lax.optimization_barrier((*[ring_swap(*one) for one in self.sent], after))
        if hop < half:
            out = self.blocks_call(got, (half + hop, half - 1 - hop), [self.keep])
            self.part = out[1]
        elif hop == half:
            (own,) = self.blocks_call(got, (0,), [self.part])
            for mask in self.others:
                own = added(own, swapped(own, mask))
            self.blocks[0] = own
            out = [own, own]
        else:
            out = self.blocks_call(got, (None,) * len(got), [])
            hop -= half
            self.blocks[hop] = out[0]
            if hop < half:
                self.blocks[RING - hop] = out[1]
        if hop == half - 1:
            self.sent = [(out[0], True)]
        elif self.hop < 2 * half:
            self.sent = [(out[0], True), (out[1], False)]
        return out[0]


def share(pieces, group, after):
    blocks = [piece.blocks[k] for piece in pieces for k in GROUPS[group]]
    *blocks, _ = lax.optimization_barrier((*blocks, after))
    shape = (len(GROUPS[group]), FIRST + SECOND, D)
    (near,) = call(
        join_blocks, blocks, [VMEM] * len(blocks), [shape_of(shape, BF16)], room=8, cost=0
    )
    return near, swapped(near, 1)


def per_device(
    tokens, qkv_weight, qkv_bias, out_weight, out_bias, first_gain, first_shift, up_weight,
    up_bias, down_weight, down_bias, second_gain, second_shift, proj_weight, log_scale,
    doc_lengths, labels,
):
    size = lax.axis_size("dp")
    bits = [1 << k for k in range(size.bit_length() - 1)]
    near_masks, doc_masks = bits[:2], bits[2:]
    top_mask, doc_masks = doc_masks[-1], doc_masks[:-1]
    others = bits[4:]
    me = lax.axis_index("dp")
    stream = lax.axis_index("stream")
    is_query = stream == 0
    has_top = (me & top_mask) != 0
    lens = doc_lengths.T
    scale = log_scale.reshape(1)

    vec, *moved, qkv, rope, probs, mixed, xh1, rs1, affine = call(
        partial(encoder_forward, size),
        (
            lens, labels, jnp.asarray(rope_table()), tokens[0], qkv_weight[0], qkv_bias,
            out_weight[0], out_bias, first_gain, first_shift, up_weight[0], up_bias,
            down_weight[0], down_bias, second_gain, second_shift, proj_weight[0],
        ),
        [HBM] * 17,
        [shape_of((ROW + EXT, PROJ), BF16)]
        + [shape_of(*kind) for kind in MOVED]
        + [pltpu.HBM(*kind) for kind in KEPT],
        [pltpu.VMEM(*kind) for kind in KEPT]
        + [pltpu.SemaphoreType.DMA((len(KEPT),))]
        + [
            pltpu.VMEM(shape, BF16)
            for shape in (
                (ROW, 512), (ROW, D), (D, 3 * D), (1, 3 * D), (D, D), (1, D), (1, D), (1, D), (D, FF),
                (1, FF), (FF, D), (1, D), (1, D), (1, D), (D, PROJ),
            )
        ]
        + [
            pltpu.SMEM(lens.shape, jnp.int32),
            pltpu.SMEM(labels.shape, jnp.int32),
            pltpu.SemaphoreType.DMA((17,)),
        ],
        room=40,
        out_specs=[VMEM] * (1 + len(MOVED)) + [HBM] * len(KEPT),
    )
    act, slope, xh2, rs2 = call(
        move_kept,
        moved,
        [VMEM] * len(MOVED),
        [pltpu.HBM(*kind) for kind in MOVED],
        [pltpu.SemaphoreType.DMA((len(MOVED),))],
        room=8,
        out_specs=[HBM] * len(MOVED),
        cost=STEP_COST,
    )

    every, other_y = range(size), near_masks[1]
    other, _ = lax.optimization_barrier((swapped(vec, 1, "stream"), rs2))
    near = jnp.where(is_query, vec, other)
    rows = jnp.where(is_query, other, vec)[:ROW]
    moved = swapped(rows, top_mask)
    (rows,) = call(
        partial(pick_rows, size),
        (rows, moved),
        [VMEM] * 2,
        [shape_of((ROW, PROJ), BF16)],
        room=8,
        cost=STEP_COST,
    )
    got_y, _ = lax.optimization_barrier((swapped(near, other_y), rows))
    near = jnp.concatenate([near, got_y], axis=0)
    far = swapped(near, near_masks[0])
    pieces = []
    for k, mask in enumerate(doc_masks):
        pieces.append(rows)
        got = swapped(rows, mask)
        if k + 1 < len(doc_masks):
            rows = jnp.concatenate([rows, got], axis=0)
        else:
            pieces = [rows, got]
    doc_rows = sum(p.shape[0] for p in pieces) // ROW
    tokens_d = doc_rows * ROW
    tokens_q = 4 * ROW
    lanes = -(-3 * doc_rows * DOCS_ROW // 128) * 128
    room = 20 if doc_rows <= 4 else 56
    totals, el, hot, factor, stats = call(
        partial(matching_stats, size, doc_masks, lanes),
        (scale, lens, near, far, *pieces),
        [SMEM] * 2 + [VMEM] * (2 + len(pieces)),
        [
            shape_of((tokens_q, lanes)),
            shape_of((tokens_q // QLEN, lanes)),
            shape_of((tokens_q // QLEN, lanes)),
            shape_of((8, lanes)),
            shape_of((tokens_q // QLEN, 128)),
        ],
        [pltpu.VMEM((PROJ, tokens_d), F32), pltpu.VMEM((3, PROJ, tokens_d), BF16)],
        room=room,
    )
    small_enough = doc_rows <= 4
    ready = call(
        partial(matching_ready, size, doc_masks, lanes),
        (lens, near, far, *pieces),
        [SMEM] + [VMEM] * (2 + len(pieces)),
        [
            shape_of((3, tokens_q, PROJ), BF16),
            shape_of((3, PROJ, tokens_q), BF16),
            shape_of((tokens_q, 128)),
            shape_of((3, PROJ, tokens_d), BF16),
            shape_of((8, tokens_d)),
            shape_of((3 * doc_rows, lanes, ROW), BF16),
        ]
        + [shape_of((3, tokens_q, tokens_d), BF16)] * small_enough,
        [pltpu.VMEM((PROJ, tokens_d), F32)],
        room=room,
    )
    stats = stats + swapped(stats, near_masks[0])
    over_y = swapped(stats, other_y)
    over_x = swapped(stats, 1, "stream")
    pairs = [(k * size + r, (1 - k) * size + (r ^ other_y)) for k in range(2) for r in every]
    over_both = lax.ppermute(stats, ("stream", "dp"), pairs)
    dq, dq_send, keep, send, loss = call(
        partial(matching_back, size, doc_masks, lanes),
        (totals, el, hot, factor, stats, over_y, over_x, over_both, *ready),
        [VMEM] * (8 + len(ready)),
        [shape_of((tokens_q // 2, PROJ), BF16)] * 2
        + [shape_of((tokens_d // 2, PROJ), BF16)] * 2
        + [shape_of((8, 128))],
        [
            pltpu.VMEM((tokens_q, PROJ), F32),
            pltpu.VMEM((3, PROJ, tokens_d), F32),
            pltpu.VMEM((tokens_q // QLEN, 128), F32),
        ],
        room=room,
    )
    got_dq = swapped(dq_send, near_masks[0])
    for mask in reversed(doc_masks[1:]):
        total, half = added(keep, swapped(send, mask)), keep.shape[0] // 2
        keep, send = total[:half], total[half:]
    got_dd = swapped(send, doc_masks[0])
    def summed(rows, got, after=None):
        if after is not None:
            got, _ = lax.optimization_barrier((got, after))
        return call(
            add_rows, (rows, got), [VMEM] * 2, [shape_of(rows.shape, BF16)], room=8, cost=STEP_COST
        )[0]

    dq = summed(dq, got_dq)
    dd = summed(keep, got_dd, dq)
    dd = summed(dd, swapped(dd, top_mask))
    dq = summed(dq[:ROW], swapped(dq[ROW:], other_y), dd)
    got = swapped(jnp.where(is_query, dd, dq), 1, "stream")

    one_keep, one_send, tail_keep, tail_send, d_first, gproj, small = call(
        partial(feed_back, size),
        (
            dq, dd, got, xh2, rs2, affine, proj_weight[0], slope, act, xh1, down_weight[0],
            up_weight[0],
        ),
        [VMEM] * 3 + [HELD] * 8 + [HBM],
        [shape_of((RING, FIRST, D), BF16)] * 2
        + [shape_of((RING, TAIL, D), BF16)] * 2
        + [shape_of((ROW, D)), shape_of((D, PROJ)), shape_of((8, D))],
        [
            pltpu.VMEM((ROW, FF), BF16),
            pltpu.VMEM((D, FF), BF16),
            pltpu.SemaphoreType.DMA((1,)),
        ],
        room=24,
    )
    two_keep, two_ahead, two_send, d_sum, d_joined = call(
        partial(attend_back, size),
        (
            d_first, gproj, small, loss, tail_keep, tail_send, xh1, rs1, affine, mixed, out_weight[0], qkv, probs, rope,
            tokens[0],
        ),
        [VMEM] * 6 + [HELD] * 9,
        [shape_of((count, SECOND, D), BF16) for count in (RING, len(AHEAD), len(LATER))]
        + [shape_of((ROW, D)), shape_of((ROW, 3 * D), BF16)],
        [pltpu.VMEM((4 * D + 16 * RING, D), F32)],
        room=24,
    )
    one, two = [
        Summed(keep, sends, others)
        for keep, *sends in ((one_keep, one_send), (two_keep, two_ahead, two_send))
    ]
    token, outs, shared = d_sum, (), []
    for event in ORDER:
        kind, k, *group = event
        if kind == "tokens":
            d_sum, _ = lax.optimization_barrier((d_sum, token))
            (tokens_grad,) = call(
                tokens_back,
                (d_sum, d_joined, qkv_weight[0]),
                [VMEM] * 3,
                [shape_of((ROW, D))],
                room=8,
                cost=STEP_COST,
            )
            token = tokens_grad
            continue
        if kind == "spread":
            jobs = event[1]
            halves = [shared[group][0 if mine else 1] for mine, group in jobs]
            *halves, _ = lax.optimization_barrier((*halves, token))
            others = [pair[j] for j in range(2) for pair in shared] if event == ORDER[-1] else []
            outs = spread_call(size, jobs, halves, outs[:5], others)
            token = outs[0]
            continue
        if kind == "share":
            shared.append(share((one, two), k, token))
            token = shared[-1][0]
            continue
        piece = (one, two)[k]
        token = getattr(piece, kind)(*group, token)
    grad_down, grad_up, grad_qkv, grad_out, grad_proj = outs[:5]
    (
        grad_bqkv, grad_bout, grad_g1, grad_s1, grad_bup, grad_bdown, grad_g2, grad_s2, loss,
        scale_grad,
    ) = outs[5:]
    return (
        loss.reshape(()),
        tokens_grad[None],
        grad_qkv[None],
        grad_bqkv,
        grad_out[None],
        grad_bout,
        grad_g1,
        grad_s1,
        grad_up[None],
        grad_bup,
        grad_down[None],
        grad_bdown,
        grad_g2,
        grad_s2,
        grad_proj[None],
        scale_grad.reshape(()),
    )


def solution(mesh):
    return jax.shard_map(
        per_device,
        mesh=mesh,
        in_specs=(
            P("stream", "dp", None),
            P("stream", None, None),
            P("stream", None),
            P("stream", None, None),
            P("stream", None),
            P("stream", None),
            P("stream", None),
            P("stream", None, None),
            P("stream", None),
            P("stream", None, None),
            P("stream", None),
            P("stream", None),
            P("stream", None),
            P("stream", None, None),
            P(),
            P(),
            P("dp"),
        ),
        out_specs=(
            P(),
            P("stream", "dp", None),
            P("stream", None, None),
            P("stream", None),
            P("stream", None, None),
            P("stream", None),
            P("stream", None),
            P("stream", None),
            P("stream", None, None),
            P("stream", None),
            P("stream", None, None),
            P("stream", None),
            P("stream", None),
            P("stream", None),
            P("stream", None, None),
            P(),
        ),
        check_vma=False,
    )
```
